32 devices in a mesh: seq: 16 (over z, y, x), grp: 2 (over core).
Axes of the slice: x: 2, y: 2, z: 4, core: 2. Of those that a mesh axis runs over, the one named last changes fastest.
Arguments:
- tokens: bfloat16 [2, 2048, 768], P('grp', 'seq'), may hold values from -6 to 6
- cotangent: bfloat16 [2, 2048, 768], P('grp', 'seq'), may hold values from -6 to 6
- holes: int32 [2, 2048], P('grp', 'seq'), may hold values 0 or 1
- slide_lengths: int32 [2, 8], P('grp'), may hold values from 1 to 1984, 2048 in all within a row
- master: float32 [2, 3542400], P('grp', 'seq'), may hold values from -2 to 2
- first_moment: float32 [2, 3542400], P('grp', 'seq'), may hold values from -32 to 32
- second_moment: float32 [2, 3542400], P('grp', 'seq'), may hold values from 2.048 to 2048
Outputs:
- output: bfloat16 [2, 2048, 768], P('grp', 'seq')
- input_grad: float32 [2, 2048, 768], P('grp', 'seq')
- new_moment: float32 [2, 3542400], P('grp', 'seq')
- new_second: float32 [2, 3542400], P('grp', 'seq')
- new_master: float32 [2, 3542400], P('grp', 'seq')
The draws below stay inside these ranges and needn't reach their ends.
All inputs are finite; a program needn't handle non-finite values. No bound on the sum of `holes` on one device may be relied on, other than what follows from the above.
Results may differ from the reference program's by a relative error of at most 0.018.
Values may be sent and summed in bfloat16 or wider, within the bound.
A program may use at most 128 MiB of HBM per device.

```python
import math
import jax
import jax.numpy as jnp
import numpy as np
from jax import lax

D = 768
FF = 3072
HEADS = 16
HEAD = 48
TOK_DEV = 128
NSLIDE = 8
STEP = 10
SEQLEN = 2048
TOKS = 4096
HALF = 3542400
N_SEQ = 16
N_GRP = 2


def bounds_drawn():
    qkv_edge = 3 * D * D // 2
    out_edge = qkv_edge + D * D // 2
    up_edge = out_edge + D * FF // 2
    down_edge = up_edge + FF * D // 2
    gain_edge = down_edge + D
    return (qkv_edge, out_edge, up_edge, down_edge, gain_edge)


def per_segment_drawn(flat_index, values):
    edge_list = bounds_drawn()
    result = jnp.full(flat_index.shape, values[5], jnp.float32)
    for position in range(4, -1, -1):
        result = jnp.where(flat_index < edge_list[position], jnp.float32(values[position]), result)
    return result


def grad_scale(flat_index):
    return per_segment_drawn(flat_index, (0.5, 0.2, 0.5, 0.6, 1.0, 1.0)) * math.sqrt(TOKS)


def draw_master(key, part):
    key = jax.random.fold_in(key, 1)
    flat_index = jnp.arange(HALF, dtype=jnp.int32)
    spread = per_segment_drawn(flat_index, (math.sqrt(2.0 / D), math.sqrt(24.0 / D), math.sqrt(1.0 / D), math.sqrt(1.0 / FF), 0.15, 0.3))
    centre = per_segment_drawn(flat_index, (0.0, 0.0, 0.0, 0.0, 1.0, 0.0))
    uniform_noise = jax.random.uniform(key, (2, HALF), jnp.float32, -1.0, 1.0) * math.sqrt(3.0)
    return centre[None, :] + spread[None, :] * uniform_noise


def draw_first_moment(key, part):
    key = jax.random.fold_in(key, 2)
    flat_index = jnp.arange(HALF, dtype=jnp.int32)
    normal_noise = jnp.clip(jax.random.normal(key, (2, HALF), jnp.float32), -4.0, 4.0)
    return normal_noise * grad_scale(flat_index)[None, :] * (0.1 / 0.9)


def draw_second_moment(key, part):
    key = jax.random.fold_in(key, 3)
    flat_index = jnp.arange(HALF, dtype=jnp.int32)
    uniform_noise = jax.random.uniform(key, (2, HALF), jnp.float32, 0.0, 1.0)
    scale = grad_scale(flat_index)[None, :]
    return 0.05 / 0.95 * scale * scale * 0.5 * jnp.exp(uniform_noise * math.log(16.0))


def plant(values, key, low, high):
    longest = values.shape.index(max(values.shape))
    spots = []
    for shift in (0, 1):
        where = [jax.random.randint(jax.random.fold_in(key, axis), (), 0, length) for axis, length in enumerate(values.shape)]
        where[longest] = (where[longest] + shift) % values.shape[longest]
        spots.append(tuple(where))
    return values.at[spots[0]].set(low).at[spots[1]].set(high)


def shard_levels(stream_key, extent, shards, low, top_value):
    gain = 1.0
    for dim, parts in shards:
        draws = jax.random.uniform(jax.random.fold_in(jax.random.fold_in(stream_key, 6), dim), (parts,), jnp.float32, low / len(shards), top_value / len(shards))
        gain = gain * jnp.repeat(jnp.exp(draws), extent[dim] // parts).reshape((-1,) + (1,) * (len(extent) - 1 - dim))
    return gain


def length_profile(count, total, limit, slope):
    loads = [(1 << 20) // math.isqrt(grade ** slope) + 1 for grade in range(2, count + 1)]
    surplus, given = total - limit - (count - 1), [1] * (count - 1)
    while surplus > 0:
        movable = [i for i in range(count - 1) if given[i] < limit]
        mass, budget = sum([loads[i] for i in movable]), surplus
        for i in movable:
            more = min(limit - given[i], max(1, budget * loads[i] // mass), surplus)
            given[i] = given[i] + more
            surplus = surplus - more
    return np.array([limit] + given)


def uneven(stream_key, number_of, total, bound, lean):
    if number_of == 2:
        one = jax.random.randint(stream_key, (), max(1, total - bound), min(bound, total - 1) + 1)
        return jnp.stack([one, total - one])
    tallies = jnp.asarray(length_profile(number_of, total, bound, lean), jnp.int32)
    couples = (number_of - 1) // 2
    source_of, receiver = tallies[1:1 + 2 * couples:2], tallies[2:2 + 2 * couples:2]
    room = jnp.minimum(source_of - 1, bound - receiver)
    moved = jax.random.randint(jax.random.fold_in(stream_key, 1), (couples,), 0, 1 << 20) % (room + 1)
    tallies = tallies.at[1:1 + 2 * couples:2].set(source_of - moved).at[2:2 + 2 * couples:2].set(receiver + moved)
    return tallies[jax.random.permutation(jax.random.fold_in(stream_key, 2), number_of)]


def gaussian(rng, dims, deviation, most, cuts=(), kind=jnp.bfloat16):
    loudness = shard_levels(rng, dims, cuts, -0.22, 0.18) if cuts else 1.0
    values = jax.random.normal(rng, dims, jnp.float32) * deviation * loudness
    return jnp.minimum(jnp.maximum(values, -most), most).astype(kind)


def setup_inputs(seed: int = 0) -> dict:
    key_list = jax.random.split(jax.random.key(seed), 8)
    return {
        "tokens": gaussian(key_list[0], (N_GRP, SEQLEN, D), 1.0, 6.0, ((0, 2), (1, 16))),
        "cotangent": gaussian(key_list[1], (N_GRP, SEQLEN, D), 1.0, 6.0, ((0, 2), (1, 16))),
        "holes": plant((jax.random.randint(key_list[2], (N_GRP, SEQLEN), 0, 4) < 3).astype(jnp.int32), jax.random.fold_in(key_list[2], 1), 0, 1),
        "slide_lengths": jax.vmap(lambda own: uneven(own, NSLIDE, SEQLEN, SEQLEN - TOK_DEV // 2, 0))(jax.random.split(key_list[3], N_GRP)).reshape((N_GRP, NSLIDE)).astype(jnp.int32),
        "master": draw_master(jax.random.fold_in(key_list[7], 71), 0),
        "first_moment": draw_first_moment(jax.random.fold_in(key_list[7], 71), 0),
        "second_moment": draw_second_moment(jax.random.fold_in(key_list[7], 71), 0),
    }


EPS_NORM = 1e-05
EPS_ADAM = 1e-08
BETA_ONE = 0.9
BETA_TWO = 0.95
HIGH = lax.Precision.HIGHEST

@jax.custom_vjp
def low(v):
    return lax.optimization_barrier(v.astype(jnp.bfloat16)).astype(jnp.float32)

@jax.custom_vjp
def low_back(v):
    return v

def low_keep(v):
    return (low(v), None)

def low_pass(kept, grad):
    return (grad,)

def back_keep(v):
    return (v, None)

def back_low(kept, grad):
    return (low(grad),)
low.defvjp(low_keep, low_pass)
low_back.defvjp(back_keep, back_low)

def bounds():
    qkv_edge = 3 * D * D // 2
    out_edge = qkv_edge + D * D // 2
    up_edge = out_edge + D * FF // 2
    down_edge = up_edge + FF * D // 2
    gain_edge = down_edge + D
    return (qkv_edge, out_edge, up_edge, down_edge, gain_edge)

def per_segment(flat_index, values):
    edge_list = bounds()
    result = jnp.full(flat_index.shape, values[5], jnp.float32)
    for position in range(4, -1, -1):
        result = jnp.where(flat_index < edge_list[position], jnp.float32(values[position]), result)
    return result

def unpack(flat):
    edge_list = bounds()

    def joined(start, stop, shape):
        return jnp.concatenate([flat[0, start:stop].reshape(shape), flat[1, start:stop].reshape(shape)], axis=-1)
    w_qkv = joined(0, edge_list[0], (D, 3 * D // 2))
    w_out = joined(edge_list[0], edge_list[1], (D, D // 2))
    w_up = joined(edge_list[1], edge_list[2], (D, FF // 2))
    w_down = joined(edge_list[2], edge_list[3], (FF, D // 2))
    gain_rows = joined(edge_list[3], edge_list[4], (2, D // 2))
    shift_rows = joined(edge_list[4], edge_list[4] + 3 * D // 2, (3, D // 2))
    bias_up = joined(edge_list[4] + 3 * D // 2, HALF, (FF // 2,))
    return (w_qkv, w_out, w_up, w_down, gain_rows, shift_rows, bias_up)

def normalize(values):
    centered = values - lax.optimization_barrier(jnp.mean(values, axis=-1, keepdims=True))
    return centered * lax.rsqrt(lax.optimization_barrier(jnp.mean(centered * centered, axis=-1, keepdims=True)) + EPS_NORM)

def slide_index(positions, slide_ends):
    return lax.optimization_barrier(jnp.sum((positions[:, None] >= slide_ends[None, :]).astype(jnp.int32), axis=1))

def block_attend(packed, slides, present):
    token_count = packed.shape[0]
    queries = packed[:, :D].reshape(token_count, HEADS, HEAD)
    keyset = packed[:, D:2 * D].reshape(token_count, HEADS, HEAD)
    valueset = packed[:, 2 * D:].reshape(token_count, HEADS, HEAD)
    scores = jnp.einsum('qhe,khe->hqk', queries, keyset, precision=HIGH) * HEAD ** (-0.5)
    scores = low_back(scores)
    allowed = (slides[:, None] == slides[None, :]) & (present[None, :] > 0) | jnp.eye(token_count, dtype=bool)
    scores = jnp.where(allowed[None], scores, -1000000000.0)
    totals = jax.nn.logsumexp(scores, axis=-1)
    attention = jnp.exp(scores - totals[:, :, None])
    result = jnp.einsum('hqk,khe->qhe', low(attention), valueset, precision=HIGH)
    return (result.reshape(token_count, D), totals.T)

def apply_block(pieces):
    return jax.checkpoint(block_attend)(pieces[0], pieces[1], pieces[2])

def layer(flat, inputs, slides, present):
    params = low(flat)
    w_qkv, w_out, w_up, w_down, gain_rows, shift_rows, bias_up = unpack(params)
    normed = low(normalize(inputs) * gain_rows[0] + shift_rows[0])
    projected = low(low_back(jnp.dot(normed, w_qkv, precision=HIGH, preferred_element_type=jnp.float32)))
    blocks = SEQLEN // TOK_DEV
    near_out, near_lse = lax.map(apply_block, (projected.reshape(blocks, TOK_DEV, 3 * D), slides.reshape(blocks, TOK_DEV), present.reshape(blocks, TOK_DEV)))
    near_out = low_back(near_out.reshape(SEQLEN, D))
    near_lse = near_lse.reshape(SEQLEN, HEADS)
    far_in = low_back(projected).reshape(TOK_DEV, N_SEQ, 3 * D).transpose(1, 0, 2)
    far_out, far_lse = lax.map(apply_block, (far_in, slides.reshape(TOK_DEV, N_SEQ).T, present.reshape(TOK_DEV, N_SEQ).T))
    far_out = low_back(far_out.transpose(1, 0, 2).reshape(SEQLEN, D))
    far_lse = far_lse.transpose(1, 0, 2).reshape(SEQLEN, HEADS)
    near_share = jax.nn.sigmoid(near_lse - far_lse)[:, :, None]
    mixture = near_share * near_out.reshape(SEQLEN, HEADS, HEAD) + (1.0 - near_share) * far_out.reshape(SEQLEN, HEADS, HEAD)
    mixture = low(mixture.reshape(SEQLEN, D))
    attended = low_back(jnp.dot(mixture, w_out, precision=HIGH, preferred_element_type=jnp.float32))
    middle = inputs + attended
    second_in = low(normalize(middle) * gain_rows[1] + shift_rows[1])
    hidden = low_back(jnp.dot(second_in, w_up, precision=HIGH, preferred_element_type=jnp.float32) + bias_up)
    activated = low(jax.nn.gelu(hidden, approximate=True))
    downward = low_back(jnp.dot(activated, w_down, precision=HIGH, preferred_element_type=jnp.float32) + shift_rows[2])
    return middle + downward

def adam_update(weights, moment, second, gradient, flat_index):
    step_rates = per_segment(flat_index, (0.7 * (2.0 / D) ** 0.5, 0.7 * (24.0 / D) ** 0.5, 0.7 * (1.0 / D) ** 0.5, 0.7 * (1.0 / FF) ** 0.5, 0.15, 0.2))
    decays = per_segment(flat_index, (0.1, 0.1, 0.1, 0.1, 0.0, 0.0))
    new_moment = BETA_ONE * moment + (1.0 - BETA_ONE) * gradient
    new_second = BETA_TWO * second + (1.0 - BETA_TWO) * gradient * gradient
    fix_one = 1.0 - BETA_ONE ** STEP
    fix_two = 1.0 - BETA_TWO ** STEP
    update = new_moment / fix_one / (jnp.sqrt(new_second / fix_two) + EPS_ADAM)
    return (new_moment, new_second, weights - step_rates * (update + decays * weights))

def reference(tokens, cotangent, holes, slide_lengths, master, first_moment, second_moment):
    positions = jnp.arange(SEQLEN, dtype=jnp.int32)
    gradient = jnp.zeros(master.shape, jnp.float32)
    outputs = []
    input_grads = []
    for group_index in range(N_GRP):
        slide_ends = jnp.cumsum(slide_lengths[group_index]).astype(jnp.int32)
        slides = slide_index(positions, slide_ends)
        present = holes[group_index]

        def run_layer(flat, inputs):
            return layer(flat, inputs, slides, present)
        result, pullback = jax.vjp(run_layer, master, tokens[group_index].astype(jnp.float32))
        flat_grad, token_grad = pullback(cotangent[group_index].astype(jnp.float32))
        gradient = gradient + flat_grad
        outputs.append(result.astype(jnp.bfloat16))
        input_grads.append(token_grad)
    flat_index = jnp.arange(HALF, dtype=jnp.int32)
    new_moment, new_second, new_master = adam_update(master, first_moment, second_moment, gradient, flat_index)
    return (jnp.stack(outputs), jnp.stack(input_grads), new_moment, new_second, new_master)
```

```python
from functools import partial

import jax
import jax.numpy as jnp
from jax import lax
from jax.experimental import pallas as pl
from jax.experimental.pallas import tpu as pltpu
from jax.sharding import PartitionSpec as P

D = 768
FF = 3072
HEADS = 16
HEAD = 48
STEP = 10


EPS_NORM = 1e-05
EPS_ADAM = 1e-08
BETA_ONE = 0.9
BETA_TWO = 0.95


def as_sent(array):
    return jax.tree.map(lambda a: a.astype(jnp.bfloat16) if a.dtype == jnp.float32 else a, array)


def bounds():
    qkv_edge = 3 * D * D // 2
    out_edge = qkv_edge + D * D // 2
    up_edge = out_edge + D * FF // 2
    down_edge = up_edge + FF * D // 2
    gain_edge = down_edge + D
    return (qkv_edge, out_edge, up_edge, down_edge, gain_edge)


def per_segment(flat_index, values):
    edge_list = bounds()
    result = jnp.full(flat_index.shape, values[5], jnp.float32)
    for position in range(4, -1, -1):
        result = jnp.where(flat_index < edge_list[position], jnp.float32(values[position]), result)
    return result


def unpack(flat):
    edge_list = bounds()
    total = flat.shape[1]

    def joined(start, stop, shape):
        return jnp.concatenate(
            [flat[0, start:stop].reshape(shape), flat[1, start:stop].reshape(shape)], axis=-1
        )

    w_qkv = joined(0, edge_list[0], (D, 3 * D // 2))
    w_out = joined(edge_list[0], edge_list[1], (D, D // 2))
    w_up = joined(edge_list[1], edge_list[2], (D, FF // 2))
    w_down = joined(edge_list[2], edge_list[3], (FF, D // 2))
    gain_rows = joined(edge_list[3], edge_list[4], (2, D // 2))
    shift_rows = joined(edge_list[4], edge_list[4] + 3 * D // 2, (3, D // 2))
    bias_up = joined(edge_list[4] + 3 * D // 2, total, (FF // 2,))
    return (w_qkv, w_out, w_up, w_down, gain_rows, shift_rows, bias_up)


def normalize(values):
    centered = values - jnp.mean(values, axis=-1, keepdims=True)
    inverse = lax.rsqrt(jnp.mean(centered * centered, axis=-1, keepdims=True) + EPS_NORM)
    return (centered * inverse, inverse)


def norm_back(grad_hat, normed_hat, inverse):
    return inverse * (
        grad_hat
        - jnp.mean(grad_hat, axis=-1, keepdims=True)
        - normed_hat * jnp.mean(grad_hat * normed_hat, axis=-1, keepdims=True)
    )


def contract_rows(left, right):
    return lax.dot_general(
        left, right, (((0,), (0,)), ((), ())), preferred_element_type=jnp.float32
    )


def contract_cols(left, right):
    return lax.dot_general(
        left, right, (((1,), (1,)), ((), ())), preferred_element_type=jnp.float32
    )


def slide_index(positions, slide_ends):
    return jnp.sum((positions[:, None] >= slide_ends[None, :]).astype(jnp.int32), axis=1)


def split_heads(block_rows):
    return block_rows.reshape(block_rows.shape[0], HEADS, HEAD).transpose(1, 0, 2)


def join_heads(stacked):
    return stacked.transpose(1, 0, 2).reshape(stacked.shape[1], HEADS * HEAD)


def allowance(slides, present):
    token_count = slides.shape[0]
    same_slide = (slides[:, None] == slides[None, :]) & (present[None, :] > 0)
    return same_slide | jnp.eye(token_count, dtype=bool)


def attend(packed, slides, present):
    allowed = allowance(slides, present)
    scale = HEAD ** (-0.5)

    def one_head(pieces):
        query_head, key_head, value_head = pieces
        scores = contract_cols(query_head, key_head) * scale
        scores = jnp.where(allowed, scores, -1000000000.0)
        row_max = jnp.max(scores, axis=-1, keepdims=True)
        exponent = jnp.exp(scores - row_max)
        denominator = jnp.sum(exponent, axis=-1, keepdims=True)
        attention = (exponent / denominator).astype(jnp.bfloat16)
        result = jnp.dot(attention, value_head, preferred_element_type=jnp.float32)
        return (result, (row_max + jnp.log(denominator))[:, 0])

    outs, lses = lax.map(
        one_head,
        (
            split_heads(packed[:, :D]),
            split_heads(packed[:, D : 2 * D]),
            split_heads(packed[:, 2 * D :]),
        ),
    )
    return (join_heads(outs), lses.T)


def attend_back(packed, slides, present, lse_rows, out_grad, lse_grad):
    allowed = allowance(slides, present)
    scale = HEAD ** (-0.5)

    def one_head(pieces):
        query_head, key_head, value_head, lse_head, grad_head, extra_lse = pieces
        scores = contract_cols(query_head, key_head) * scale
        scores = jnp.where(allowed, scores, -1000000000.0)
        attention = jnp.exp(scores - lse_head[:, None])
        prob_grad = contract_cols(grad_head, value_head)
        inner_sum = jnp.sum(attention * prob_grad, axis=-1, keepdims=True)
        score_grad = (attention * (prob_grad - inner_sum + extra_lse[:, None])).astype(jnp.bfloat16)
        query_grad = jnp.dot(score_grad, key_head, preferred_element_type=jnp.float32) * scale
        key_grad = contract_rows(score_grad, query_head) * scale
        value_grad = contract_rows(attention.astype(jnp.bfloat16), grad_head)
        return (query_grad, key_grad, value_grad)

    query_grad, key_grad, value_grad = lax.map(
        one_head,
        (
            split_heads(packed[:, :D]),
            split_heads(packed[:, D : 2 * D]),
            split_heads(packed[:, 2 * D :]),
            lse_rows.T,
            split_heads(out_grad),
            lse_grad.T,
        ),
    )
    return jnp.concatenate(
        [join_heads(query_grad), join_heads(key_grad), join_heads(value_grad)], axis=1
    )


def adam_update(weights, moment, second, gradient, flat_index):
    step_rates = per_segment(
        flat_index,
        (
            0.7 * (2.0 / D) ** 0.5,
            0.7 * (24.0 / D) ** 0.5,
            0.7 * (1.0 / D) ** 0.5,
            0.7 * (1.0 / FF) ** 0.5,
            0.15,
            0.2,
        ),
    )
    decays = per_segment(flat_index, (0.1, 0.1, 0.1, 0.1, 0.0, 0.0))
    new_moment = BETA_ONE * moment + (1.0 - BETA_ONE) * gradient
    new_second = BETA_TWO * second + (1.0 - BETA_TWO) * gradient * gradient
    fix_one = 1.0 - BETA_ONE**STEP
    fix_two = 1.0 - BETA_TWO**STEP
    update = new_moment / fix_one / (jnp.sqrt(new_second / fix_two) + EPS_ADAM)
    return (new_moment, new_second, weights - step_rates * (update + decays * weights))


def column_halves(values):
    return values.reshape(values.shape[0], 2, values.shape[1] // 2)


def plain_on_device(tokens, cotangent, holes, slide_lengths, master, first_moment, second_moment):
    own_half = lax.all_gather(master.astype(jnp.bfloat16), "seq", axis=1, tiled=True)
    whole_flat = lax.all_gather(own_half, "grp", axis=0, tiled=True)
    w_qkv, w_out, w_up, w_down, gain_rows, shift_rows, bias_up = unpack(whole_flat)
    gain_rows = gain_rows.astype(jnp.float32)
    shift_rows = shift_rows.astype(jnp.float32)
    bias_up = bias_up.astype(jnp.float32)
    inputs = tokens[0].astype(jnp.float32)
    row_count = inputs.shape[0]
    seq_ways = lax.axis_size("seq")
    seq_place = lax.axis_index("seq")
    row_steps = jnp.arange(row_count, dtype=jnp.int32)
    slide_ends = jnp.cumsum(slide_lengths[0])
    near_slides = slide_index(seq_place * row_count + row_steps, slide_ends)
    far_slides = slide_index(seq_place + seq_ways * row_steps, slide_ends)
    near_present = holes[0]
    strided_shape = (row_count // seq_ways, seq_ways)

    def to_strided(packed):
        moved, moved_mask = (
            lax.all_to_all(
                packed.reshape(strided_shape + (3 * D,)),
                "seq",
                split_axis=1,
                concat_axis=0,
                tiled=True,
            ),
            lax.all_to_all(
                near_present.astype(jnp.bfloat16).reshape(strided_shape + (1,)),
                "seq",
                split_axis=1,
                concat_axis=0,
                tiled=True,
            ),
        )
        return (moved.reshape(row_count, 3 * D), moved_mask.reshape(row_count).astype(jnp.int32))

    normed_one, inverse_one = normalize(inputs)
    normed = (normed_one * gain_rows[0] + shift_rows[0]).astype(jnp.bfloat16)
    projected = jnp.dot(normed, w_qkv, preferred_element_type=jnp.float32).astype(jnp.bfloat16)
    near_out, near_lse = attend(projected, near_slides, near_present)
    far_proj, far_present = to_strided(projected)
    far_local, far_local_lse = attend(far_proj, far_slides, far_present)
    returned = (
        lax.all_to_all(
            far_local.reshape(row_count, 1, D).astype(jnp.bfloat16),
            "seq",
            split_axis=0,
            concat_axis=1,
            tiled=True,
        ).astype(jnp.float32),
        lax.all_to_all(
            far_local_lse.reshape(row_count, 1, HEADS).astype(jnp.bfloat16),
            "seq",
            split_axis=0,
            concat_axis=1,
            tiled=True,
        ).astype(jnp.float32),
    )
    far_out = returned[0].reshape(row_count, D)
    far_lse = returned[1].reshape(row_count, HEADS)
    near_share = jax.nn.sigmoid(near_lse - far_lse)
    near_heads = near_out.reshape(row_count, HEADS, HEAD)
    far_heads = far_out.reshape(row_count, HEADS, HEAD)
    mixture = (
        (near_share[:, :, None] * near_heads + (1.0 - near_share[:, :, None]) * far_heads)
        .reshape(row_count, D)
        .astype(jnp.bfloat16)
    )
    middle = inputs + jnp.dot(mixture, w_out, preferred_element_type=jnp.float32)
    normed_two, inverse_two = normalize(middle)
    second_in = (normed_two * gain_rows[1] + shift_rows[1]).astype(jnp.bfloat16)
    hidden = jnp.dot(second_in, w_up, preferred_element_type=jnp.float32) + bias_up
    activated = jax.nn.gelu(hidden, approximate=True).astype(jnp.bfloat16)
    output = middle + jnp.dot(activated, w_down, preferred_element_type=jnp.float32) + shift_rows[2]
    upstream = cotangent[0].astype(jnp.float32)
    down_grad = upstream.astype(jnp.bfloat16)
    grad_act = contract_cols(down_grad, w_down)
    gelu_pull = jax.vjp(partial(jax.nn.gelu, approximate=True), hidden)[1]
    hidden_grad = gelu_pull(grad_act)[0].astype(jnp.bfloat16)
    second_grad = contract_cols(hidden_grad, w_up)
    grad_gain_two = jnp.sum(second_grad * normed_two, axis=0)
    grad_shift_two = jnp.sum(second_grad, axis=0)
    middle_grad = upstream + norm_back(second_grad * gain_rows[1], normed_two, inverse_two)
    attend_grad = middle_grad.astype(jnp.bfloat16)
    mix_grad = contract_cols(attend_grad, w_out).reshape(row_count, HEADS, HEAD)
    near_lse_grad = (
        near_share * (1.0 - near_share) * jnp.sum((near_heads - far_heads) * mix_grad, axis=-1)
    )
    near_grad = (near_share[:, :, None] * mix_grad).reshape(row_count, D).astype(jnp.bfloat16)
    far_grad = ((1.0 - near_share[:, :, None]) * mix_grad).reshape(row_count, D)
    sent = (
        lax.all_to_all(
            as_sent(far_grad.reshape(strided_shape + (D,))),
            "seq",
            split_axis=1,
            concat_axis=0,
            tiled=True,
        ),
        lax.all_to_all(
            as_sent((-near_lse_grad).reshape(strided_shape + (HEADS,))),
            "seq",
            split_axis=1,
            concat_axis=0,
            tiled=True,
        ),
    )
    far_back = sent[0].reshape(row_count, D).astype(jnp.bfloat16)
    far_lse_grad = sent[1].reshape(row_count, HEADS)
    again_proj, again_present = to_strided(projected)
    again_lse = attend(again_proj, far_slides, again_present)[1]
    far_proj_grad = attend_back(
        again_proj, far_slides, again_present, again_lse, far_back, far_lse_grad
    ).astype(jnp.bfloat16)
    far_home = lax.all_to_all(
        far_proj_grad.reshape(row_count, 1, 3 * D), "seq", split_axis=0, concat_axis=1, tiled=True
    ).reshape(row_count, 3 * D)
    near_proj_grad = attend_back(
        projected, near_slides, near_present, near_lse, near_grad, near_lse_grad
    )
    proj_grad = (near_proj_grad + far_home.astype(jnp.float32)).astype(jnp.bfloat16)
    first_grad = contract_cols(proj_grad, w_qkv)
    grad_gain_one = jnp.sum(first_grad * normed_one, axis=0)
    grad_shift_one = jnp.sum(first_grad, axis=0)
    input_grad = middle_grad + norm_back(first_grad * gain_rows[0], normed_one, inverse_one)
    both_rows = (
        lax.all_gather(normed, "grp", axis=0, tiled=True),
        lax.all_gather(mixture, "grp", axis=0, tiled=True),
        lax.all_gather(second_in, "grp", axis=0, tiled=True),
        lax.all_gather(activated, "grp", axis=0, tiled=True),
    )
    moved = (
        lax.all_to_all(column_halves(proj_grad), "grp", split_axis=1, concat_axis=0, tiled=True),
        lax.all_to_all(column_halves(attend_grad), "grp", split_axis=1, concat_axis=0, tiled=True),
        lax.all_to_all(column_halves(hidden_grad), "grp", split_axis=1, concat_axis=0, tiled=True),
        lax.all_to_all(column_halves(down_grad), "grp", split_axis=1, concat_axis=0, tiled=True),
    )
    proj_mine = moved[0].reshape(2 * row_count, 3 * D // 2)
    attend_mine = moved[1].reshape(2 * row_count, D // 2)
    hidden_mine = moved[2].reshape(2 * row_count, FF // 2)
    down_mine = moved[3].reshape(2 * row_count, D // 2)
    norm_sums = lax.psum(
        jnp.stack([grad_gain_one, grad_gain_two, grad_shift_one, grad_shift_two]), "grp"
    )
    half_width = D // 2
    norm_half = lax.dynamic_slice_in_dim(
        norm_sums, lax.axis_index("grp") * half_width, half_width, 1
    )
    grad_w_qkv = contract_rows(both_rows[0], proj_mine)
    grad_w_out = contract_rows(both_rows[1], attend_mine)
    grad_w_up = contract_rows(both_rows[2], hidden_mine)
    grad_w_down = contract_rows(both_rows[3], down_mine)
    grad_bias_down = jnp.sum(down_mine.astype(jnp.float32), axis=0)
    grad_bias_up = jnp.sum(hidden_mine.astype(jnp.float32), axis=0)
    gradient = jnp.concatenate(
        [
            grad_w_qkv.reshape(-1),
            grad_w_out.reshape(-1),
            grad_w_up.reshape(-1),
            grad_w_down.reshape(-1),
            norm_half[0],
            norm_half[1],
            norm_half[2],
            norm_half[3],
            grad_bias_down,
            grad_bias_up,
        ]
    )
    reduced = lax.psum_scatter(gradient, "seq", scatter_dimension=0, tiled=True)
    shard_size = master.shape[1]
    flat_index = lax.axis_index("seq") * shard_size + jnp.arange(shard_size, dtype=jnp.int32)
    new_moment, new_second, new_master = adam_update(
        master[0], first_moment[0], second_moment[0], reduced, flat_index
    )
    return (
        output[None].astype(jnp.bfloat16),
        input_grad[None],
        new_moment[None],
        new_second[None],
        new_master[None],
    )


LANES = 128
BF16 = jnp.bfloat16
F32 = jnp.float32
MAT_ROWS = (3 * D * D + D * D + D * FF + FF * D) // 2 // LANES
SMALL_ROWS = 32
UNIT = 576
PAIR = 2
TILES = (3 * D // 2 // LANES, D // 2 // LANES, FF // 2 // LANES, D // 2 // LANES)
DEPTHS = (D, D, D, FF)
MESH = pl.DeviceIdType.MESH
VMEM_BYTES = 60 * 2**20
NEG = -1000000000.0


def matrix_starts():
    starts = [0]
    for tiles, depth in zip(TILES, DEPTHS):
        starts.append(starts[-1] + tiles * depth)
    return starts


def place():
    return lax.axis_index("seq"), lax.axis_index("grp")


def enter(ways):
    s, g = place()
    barrier = pltpu.get_barrier_semaphore()

    def greet(step, carry):
        pl.semaphore_signal(
            barrier, inc=1, device_id=(lax.rem(s + step, ways), g), device_id_type=MESH
        )
        return carry

    lax.fori_loop(1, ways, greet, 0)
    pl.semaphore_signal(barrier, inc=1, device_id=(s, 1 - g), device_id_type=MESH)
    pl.semaphore_wait(barrier, ways)


def remote(src, dst, send_sem, recv_sem, to):
    return pltpu.make_async_remote_copy(
        src_ref=src,
        dst_ref=dst,
        send_sem=send_sem,
        recv_sem=recv_sem,
        device_id=to,
        device_id_type=MESH,
    )


def unit_tiles(unit, body):
    edges = [start // UNIT for start in matrix_starts()]
    kinds = {}
    for index, tiles in enumerate(TILES):
        inside = (unit >= edges[index]) & (unit < edges[index + 1])
        kinds[tiles] = kinds[tiles] | inside if tiles in kinds else inside
    for tiles, inside in kinds.items():
        pl.when(inside)(lambda tiles=tiles: body(tiles))


def gather_kernel(
    ways, flat, whole, small, extended, aligned, tail,
    tail_send, tail_recv, slot_send, slot_recv, pair_send, pair_recv, small_send, small_recv,
):
    s, g = place()
    planes = ways // 4
    z, y, x = s // 4, lax.rem(s // 2, 2), lax.rem(s, 2)
    own = MAT_ROWS // ways
    half = own // 2
    flat_rows = flat.shape[0]
    entries = (MAT_ROWS * LANES + bounds_total()) // ways - own * LANES
    last_row, last_lane = divmod(own * LANES + entries, LANES)
    lanes = lax.broadcasted_iota(jnp.int32, (SMALL_ROWS, LANES), 1)
    gap = LANES - last_lane
    older = pltpu.roll(flat[last_row - SMALL_ROWS : last_row, :], gap, 1)
    newer = pltpu.roll(flat[last_row - SMALL_ROWS + 1 : last_row + 1, :], gap, 1)
    tail[...] = jnp.where(lanes < gap, older, newer)
    enter(ways)
    follow = remote(
        tail, extended.at[pl.ds(0, SMALL_ROWS)], tail_send, tail_recv, (lax.rem(s + 1, ways), g)
    )
    follow.start()
    extended[SMALL_ROWS : SMALL_ROWS + flat_rows, :] = flat[...]
    extended[SMALL_ROWS + flat_rows :, :] = jnp.zeros(
        (extended.shape[0] - SMALL_ROWS - flat_rows, LANES), F32
    )
    follow.wait()
    shift = entries * s
    row_shift, lane_shift = shift // LANES, lax.rem(shift, LANES)
    step_rows = 176
    step_lanes = lax.broadcasted_iota(jnp.int32, (step_rows, LANES), 1)

    def align(step, carry):
        start = step * step_rows
        here = extended[pl.ds(SMALL_ROWS + start - row_shift, step_rows), :]
        before = extended[pl.ds(SMALL_ROWS - 1 + start - row_shift, step_rows), :]
        aligned[pl.ds(pl.multiple_of(start, 8), step_rows), :] = jnp.where(
            step_lanes >= lane_shift,
            pltpu.roll(here, lane_shift, 1),
            pltpu.roll(before, lane_shift, 1),
        )
        return carry

    lax.fori_loop(0, (own + SMALL_ROWS) // step_rows, align, 0)
    base = s * own

    def fill(unit, carry):
        first = unit * UNIT

        def tiled(tiles):
            for group in range(UNIT // (16 * tiles)):
                for tile in range(tiles):
                    rows = aligned[pl.ds(first + group * 16 * tiles + tile, 16, stride=tiles), :]
                    at = base + first + 16 * (group * tiles + tile)
                    whole[g, pl.ds(pl.multiple_of(at, 16), 16), :] = rows.astype(BF16)

        unit_tiles(s * (own // UNIT) + unit, tiled)
        return carry

    lax.fori_loop(0, own // UNIT, fill, 0)

    def slot(plane, row, column, part):
        at = ((plane * 2 + row) * 2 + column) * own + part * half
        return whole.at[g, pl.ds(pl.multiple_of(at, 16), half)]

    def copy(plane, row, column, part, kind, to):
        where = slot(plane, row, column, part)
        return remote(
            where,
            where,
            slot_send.at[part, plane, kind],
            slot_recv.at[part, (plane * 2 + row) * 2 + column],
            to,
        )

    def chip(plane, row, column):
        return ((plane * 2 + row) * 2 + column, g)

    def spread(plane, act):
        for part in range(2):
            if act == "start":
                pl.when(z != plane)(copy(plane, y, x, part, 0, chip(z, y, x)).wait_recv)
            up = copy(plane, y, x, part, 0, chip(z + 1, y, x))
            down = copy(plane, y, x, part, 1, chip(z - 1, y, x))
            to_x = copy(plane, y, x, part, 2, chip(z, y, 1 - x))
            to_y = copy(plane, y, x, part, 3, chip(z, 1 - y, x))
            act_on = (lambda c: c.start) if act == "start" else (lambda c: c.wait_send)
            pl.when((z >= plane) & (z < planes - 1))(act_on(up))
            pl.when((z <= plane) & (z > 0))(act_on(down))
            act_on(to_y if part == 0 else to_x)()
            act_on(to_x if part == 0 else to_y)()

    def turn(plane, act):
        first = copy(plane, 1 - y, x, 0, 4, chip(z, y, 1 - x))
        second = copy(plane, y, 1 - x, 1, 4, chip(z, 1 - y, x))
        for onward in (first, second):
            if act == "start":
                onward.wait_recv()
                onward.start()
            else:
                onward.wait_send()

    def across(plane):
        block = whole.at[g, pl.ds(plane * 4 * own, 4 * own)]
        return remote(block, block, pair_send.at[plane], pair_recv.at[plane], (s, 1 - g))

    def finish(plane):
        copy(plane, y, 1 - x, 0, 0, chip(z, y, x)).wait_recv()
        copy(plane, 1 - y, 1 - x, 0, 0, chip(z, y, x)).wait_recv()
        copy(plane, 1 - y, x, 1, 0, chip(z, y, x)).wait_recv()
        copy(plane, 1 - y, 1 - x, 1, 0, chip(z, y, x)).wait_recv()
        across(plane).start()

    def small_to(index):
        return remote(small.at[g], small.at[g], small_send.at[index], small_recv.at[0], (index, g))

    small_pair = remote(
        small.at[g], small.at[g], small_send.at[ways - 1], small_recv.at[1], (s, 1 - g)
    )

    @pl.when(s == ways - 1)
    def _():
        small[g] = aligned[own : own + SMALL_ROWS, :].astype(BF16)

    def tell(index, carry):
        small_to(index).start()
        return carry

    def told(index, carry):
        small_to(index).wait_send()
        return carry

    spread(0, "start")

    @pl.when(s == ways - 1)
    def _():
        lax.fori_loop(0, ways - 1, tell, 0)

    turn(0, "start")
    for plane in range(1, planes):
        spread(plane, "start")
        turn(plane, "start")
        if plane == 1:
            pl.when(s != ways - 1)(small_to(s).wait_recv)
            small_pair.start()
        finish(plane - 1)
    finish(planes - 1)
    for plane in range(planes):
        across(plane).wait()
    for plane in range(planes):
        spread(plane, "wait")
        turn(plane, "wait")
    small_pair.wait()

    @pl.when(s == ways - 1)
    def _():
        lax.fori_loop(0, ways - 1, told, 0)


def bounds_total():
    return 5 * D // 2 + FF // 2


def gather_params(flat, ways):
    own = MAT_ROWS // ways
    planes = ways // 4
    dma = pltpu.SemaphoreType.DMA
    return pl.pallas_call(
        partial(gather_kernel, ways),
        out_shape=(
            jax.ShapeDtypeStruct((2, MAT_ROWS, LANES), BF16),
            jax.ShapeDtypeStruct((2, SMALL_ROWS, LANES), BF16),
        ),
        in_specs=[pl.BlockSpec(memory_space=pltpu.VMEM)],
        out_specs=(
            pl.BlockSpec(memory_space=pltpu.VMEM),
            pl.BlockSpec(memory_space=pltpu.VMEM),
        ),
        scratch_shapes=[
            pltpu.VMEM((own + 2 * SMALL_ROWS, LANES), F32),
            pltpu.VMEM((own + SMALL_ROWS, LANES), F32),
            pltpu.VMEM((SMALL_ROWS, LANES), F32),
            dma, dma,
            dma((2, planes, 5)),
            dma((2, ways)),
            dma((planes,)), dma((planes,)),
            dma((ways,)), dma((2,)),
        ],
        compiler_params=pltpu.CompilerParams(
            collective_id=1, has_side_effects=True, vmem_limit_bytes=VMEM_BYTES
        ),
        name="gather_params",
    )(flat)


def dot(left, right):
    return jnp.dot(left, right, preferred_element_type=F32)


def dot_cols(left, right):
    return contract_cols(left, right)


def dot_rows(left, right):
    return contract_rows(left, right)


def tile_view(ref, index):
    rows = 16 * TILES[index]
    start = matrix_starts()[index]
    return ref.reshape(ref.shape[:-2] + (MAT_ROWS // rows, rows, LANES)), start // rows


def tile_groups(index):
    tiles = TILES[index]
    groups, at = [], 0
    while at < tiles:
        width = 3 if tiles - at == 3 else 2
        groups.append((at, width))
        at += width
    return groups


def weight(ref, index, half, row, rows, tile, width):
    view, base = tile_view(ref, index)
    first = base + row // 16
    pieces = [
        view[half, first : first + rows // 16, 16 * t : 16 * t + 16, :].reshape(rows, LANES)
        for t in range(tile, tile + width)
    ]
    return jnp.concatenate(pieces, axis=1)


def heads_of(rows):
    row = lax.broadcasted_iota(jnp.int32, (rows, D), 0) * HEAD
    column = lax.broadcasted_iota(jnp.int32, (rows, D), 1)
    return ((column >= row) & (column < row + HEAD)).astype(F32)


def to_columns(per_head):
    return jnp.dot(
        per_head, heads_of(HEADS), precision=lax.Precision.HIGHEST, preferred_element_type=F32
    )


def to_heads(columns):
    return lax.dot_general(
        columns,
        heads_of(HEADS),
        (((1,), (1,)), ((), ())),
        precision=lax.Precision.HIGHEST,
        preferred_element_type=F32,
    )


def pack_blocks(ref, values, extra):
    blocks = values.shape[0] // 8
    split = values.reshape(blocks, 8, D)
    ref[:, :, : D // 2] = jnp.concatenate(
        [split[:, :, : D // 2], split[:, :, D // 2 :]], axis=1
    ).astype(BF16)
    if extra is not None:
        high = extra.astype(BF16).astype(F32)
        low = extra - high
        pieces = jnp.concatenate(
            [high.reshape(blocks, 8, HEADS), low.reshape(blocks, 8, HEADS)], axis=1
        )
        ref[:, :, D // 2 : D // 2 + HEADS] = pieces.astype(BF16)


def unpack_values(ref):
    blocks = ref.shape[0]
    values = ref[:, :, : D // 2].astype(F32)
    return jnp.concatenate(
        [values[:, :8, :].reshape(blocks * 8, D // 2), values[:, 8:, :].reshape(blocks * 8, D // 2)],
        axis=1,
    )


def unpack_extra(ref):
    blocks = ref.shape[0]
    pieces = ref[:, :, D // 2 :].astype(F32)
    both = pieces[:, :8, :] + pieces[:, 8:, :]
    return both.reshape(blocks * 8, LANES)[:, :HEADS]


def slide_masks(ends_ref, s, ways, near_keys, far_keys):
    rows = near_keys.shape[1]
    ends, end = [], 0
    for index in range(ends_ref.shape[1]):
        end = end + ends_ref[0, index]
        ends.append(end)

    def slides(positions):
        total = jnp.zeros(positions.shape, jnp.int32)
        for end in ends:
            total = total + (positions >= end).astype(jnp.int32)
        return total

    across = rows // ways
    result = []
    for far, keys in ((False, near_keys), (True, far_keys)):
        found = []
        for dim in (0, 1):
            at = lax.broadcasted_iota(jnp.int32, (rows, rows), dim)
            if far:
                position = s + ways * at
            else:
                position = rows * s + ways * lax.rem(at, across) + at // across
            found.append(slides(position))
        query = lax.broadcasted_iota(jnp.int32, (rows, rows), 0)
        key = lax.broadcasted_iota(jnp.int32, (rows, rows), 1)
        allowed = ((found[0] == found[1]) & (keys > 0.5)) | (query == key)
        result.append(allowed.astype(F32))
    return result


def layer_kernel(
    ways, tokens, cotangent, holes, lengths, whole, small,
    output, input_grad, grads, small_grads,
    turning, send_blocks, recv_blocks, masks, normed, normed_hat, inverse, projected, attended, lses,
    mixture, second_in, activated, slope, second_hat, second_inverse, middle_grad,
    qkv_grad, out_grad, up_grad, down_grad, near_grad, far_grad, lse_grads,
    their_normed, their_mixture, their_second, their_activated,
    their_qkv, their_out, their_up, their_down, small_parts, their_small,
    block_send, block_recv, pair_send, pair_recv,
):
    s, g = place()
    rows = tokens.shape[0]
    across = rows // ways
    tiles = D // LANES

    def exchange(index):
        def start(step, carry):
            to = lax.rem(s + step, ways)
            remote(
                send_blocks.at[index, to],
                recv_blocks.at[index, s],
                block_send.at[index],
                block_recv.at[index],
                (to, g),
            ).start()
            return carry

        recv_blocks[index, s] = send_blocks[index, s]
        lax.fori_loop(1, ways, start, 0)

    def exchanged(index):
        remote(
            send_blocks.at[index, pl.ds(0, ways - 1)],
            recv_blocks.at[index, pl.ds(0, ways - 1)],
            block_send.at[index],
            block_recv.at[index],
            (s, 1 - g),
        ).wait()

    pairs = []

    def hand_over(src, dst):
        index = len(pairs)
        copy = remote(src, dst, pair_send.at[index], pair_recv.at[index], (s, 1 - g))
        copy.start()
        pairs.append(copy)

    def by_residue(value):
        for tile in range(tiles):
            turning[tile] = value[:, tile * LANES : (tile + 1) * LANES]
        return jnp.concatenate(
            [
                jnp.concatenate(
                    [turning[tile, pl.ds(i, across, stride=ways), :] for i in range(ways)], axis=0
                )
                for tile in range(tiles)
            ],
            axis=1,
        )

    def in_order(value):
        for tile in range(tiles):
            for i in range(ways):
                turning[tile, pl.ds(i, across, stride=ways), :] = value[
                    across * i : across * (i + 1), tile * LANES : (tile + 1) * LANES
                ]
        return jnp.concatenate([turning[tile] for tile in range(tiles)], axis=1)

    def small_row(first, count):
        return jnp.concatenate(
            [small[half, first + r : first + r + 1, :] for half in range(2) for r in range(count)],
            axis=1,
        ).astype(F32)

    third = D // 2 // LANES
    gain_one, gain_two = small_row(0, third), small_row(third, third)
    shift_one, shift_two = small_row(2 * third, third), small_row(3 * third, third)
    shift_down = small_row(4 * third, third)
    bias_up = small_row(5 * third, FF // 2 // LANES)

    inputs = by_residue(tokens[...].astype(F32))
    lane = lax.broadcasted_iota(jnp.int32, (rows, rows), 1)
    row = lax.broadcasted_iota(jnp.int32, (rows, rows), 0)
    flags = holes[...].astype(F32)
    to_column = (row == lane).astype(F32)
    own_column = jnp.sum(to_column * flags, axis=1, keepdims=True)
    turned_at = ways * lax.rem(row, across) + row // across
    turned_column = jnp.sum((turned_at == lane).astype(F32) * flags, axis=1, keepdims=True)
    turned_row_at = ways * lax.rem(lane, across) + lane // across
    turned_row = jnp.sum((turned_row_at == row).astype(F32) * own_column, axis=0, keepdims=True)
    enter(ways)
    pack_blocks(send_blocks.at[0], inputs, jnp.broadcast_to(turned_column, (rows, HEADS)) * 1.0)
    exchange(0)
    upstream = by_residue(cotangent[...].astype(F32))
    half_width = D // 2
    for half in range(2):
        down_grad[half] = upstream[:, half * half_width : (half + 1) * half_width].astype(BF16)
    hand_over(down_grad.at[1 - g], their_down)

    exchanged(0)
    far_inputs = unpack_values(recv_blocks.at[0])
    far_column = unpack_extra(recv_blocks.at[0])[:, :1]
    far_row = jnp.sum(to_column * far_column, axis=0, keepdims=True)
    near_mask, far_mask = slide_masks(lengths, s, ways, turned_row, far_row)
    masks[0] = near_mask
    masks[1] = far_mask
    hat, scale = normalize(jnp.concatenate([inputs, far_inputs], axis=0))
    normed[...] = (hat * gain_one + shift_one).astype(BF16)
    normed_hat[...] = hat[:rows]
    inverse[...] = scale[:rows]
    hand_over(normed, their_normed)
    for half in range(2):
        for tile, width in tile_groups(0):
            at = half * 3 * half_width + tile * LANES
            projected[:, at : at + width * LANES] = dot(
                normed[...], weight(whole, 0, half, 0, D, tile, width)
            ).astype(BF16)

    temper = HEAD ** (-0.5)

    def scores(which, head):
        at = slice(which * rows, (which + 1) * rows)
        query = projected[at, head * HEAD : (head + 1) * HEAD]
        key = projected[at, D + head * HEAD : D + (head + 1) * HEAD]
        value = projected[at, 2 * D + head * HEAD : 2 * D + (head + 1) * HEAD]
        found = jnp.where(masks[which] > 0.5, dot_cols(query, key) * temper, NEG)
        return query, key, value, found

    def attend_set(which):
        results, totals = [], []
        for head in range(HEADS):
            _, _, value, found = scores(which, head)
            top = jnp.max(found, axis=1, keepdims=True)
            weights = jnp.exp(found - top)
            total = jnp.sum(weights, axis=1, keepdims=True)
            results.append(dot(weights.astype(BF16), value) * (1.0 / total))
            totals.append(top + jnp.log(total))
        attended[which] = jnp.concatenate(results, axis=1)
        lses[which] = jnp.concatenate(totals, axis=1)

    attend_set(1)
    pack_blocks(send_blocks.at[1], attended[1], lses[1])
    exchange(1)
    attend_set(0)
    exchanged(1)
    far_out = unpack_values(recv_blocks.at[1])
    near_out = attended[0]
    share = jax.nn.sigmoid(lses[0] - unpack_extra(recv_blocks.at[1]))
    shares = to_columns(share)
    difference = near_out - far_out
    mixture[...] = (shares * near_out + (1.0 - shares) * far_out).astype(BF16)
    hand_over(mixture, their_mixture)
    middle = inputs + jnp.concatenate(
        [dot(mixture[...], weight(whole, 1, half, 0, D, 0, third)) for half in range(2)], axis=1
    )
    hat, scale = normalize(middle)
    second_hat[...] = hat
    second_inverse[...] = scale
    second_in[...] = (hat * gain_two + shift_two).astype(BF16)
    hand_over(second_in, their_second)
    root = (2.0 / 3.141592653589793) ** 0.5
    for half in range(2):
        for tile, width in tile_groups(2):
            at = half * FF // 2 + tile * LANES
            to = slice(at, at + width * LANES)
            v = dot(second_in[...], weight(whole, 2, half, 0, D, tile, width)) + bias_up[:, to]
            square = v * v
            t = jnp.tanh(root * (v + 0.044715 * v * square))
            activated[:, to] = (0.5 * v * (1.0 + t)).astype(BF16)
            slope[:, to] = 0.5 * (1.0 + t) + 0.5 * v * (1.0 - t * t) * (
                root * (1.0 + 3 * 0.044715 * square)
            )
    hand_over(activated, their_activated)
    result = middle + shift_down + jnp.concatenate(
        [dot(activated[...], weight(whole, 3, half, 0, FF, 0, third)) for half in range(2)], axis=1
    )
    output[...] = in_order(result).astype(BF16)

    block = 256
    up_sums = []
    for start in range(0, FF, block):
        to = slice(start, start + block)
        pulled = sum(
            dot_cols(down_grad[half], weight(whole, 3, half, start, block, 0, third))
            for half in range(2)
        )
        grad = (pulled * slope[:, to]).astype(BF16)
        half, at = divmod(start, FF // 2)
        up_grad[half, :, at : at + block] = grad
        up_sums.append(jnp.sum(grad.astype(F32), axis=0, keepdims=True))
    hand_over(up_grad.at[1 - g], their_up)
    second_grad = jnp.concatenate(
        [
            sum(
                dot_cols(up_grad[half], weight(whole, 2, half, start, block, 0, TILES[2]))
                for half in range(2)
            )
            for start in range(0, D, block)
        ],
        axis=1,
    )
    hat = second_hat[...]
    gain_two_sum = jnp.sum(second_grad * hat, axis=0, keepdims=True)
    shift_two_sum = jnp.sum(second_grad, axis=0, keepdims=True)
    gained = upstream + norm_back(second_grad * gain_two, hat, second_inverse[...])
    middle_grad[...] = gained
    for half in range(2):
        out_grad[half] = gained[:, half * half_width : (half + 1) * half_width].astype(BF16)
    hand_over(out_grad.at[1 - g], their_out)
    mix_grad = jnp.concatenate(
        [
            sum(
                dot_cols(out_grad[half], weight(whole, 1, half, start, block, 0, third))
                for half in range(2)
            )
            for start in range(0, D, block)
        ],
        axis=1,
    )
    near_lse_grad = share * (1.0 - share) * to_heads(difference * mix_grad)
    lse_grads[0] = near_lse_grad
    near_grad[...] = (shares * mix_grad).astype(BF16)
    pack_blocks(send_blocks.at[2], (1.0 - shares) * mix_grad, -near_lse_grad)
    exchange(2)

    def attend_set_back(which, out_grads):
        lists = ([], [], [])
        for head in range(HEADS):
            query, key, value, found = scores(which, head)
            weights = jnp.exp(found - lses[which, :, head : head + 1])
            pulled = out_grads[:, head * HEAD : (head + 1) * HEAD]
            weight_grad = dot_cols(pulled, value)
            inner = jnp.sum(weights * weight_grad, axis=1, keepdims=True)
            extra = lse_grads[which, :, head : head + 1] - inner
            score_grad = (weights * (weight_grad + extra)).astype(BF16)
            lists[0].append(dot(score_grad, key) * temper)
            lists[1].append(dot_rows(score_grad, query) * temper)
            lists[2].append(dot_rows(weights.astype(BF16), pulled))
        at = slice(which * rows, (which + 1) * rows)
        query_grad, key_grad, value_grad = (jnp.concatenate(one, axis=1).astype(BF16) for one in lists)
        qkv_grad[0, at, :D] = query_grad
        qkv_grad[0, at, D:] = key_grad[:, :half_width]
        qkv_grad[1, at, :half_width] = key_grad[:, half_width:]
        qkv_grad[1, at, half_width:] = value_grad

    attend_set_back(0, near_grad)
    exchanged(2)
    far_grad[...] = unpack_values(recv_blocks.at[2]).astype(BF16)
    lse_grads[1] = unpack_extra(recv_blocks.at[2])
    attend_set_back(1, far_grad)
    hand_over(qkv_grad.at[1 - g], their_qkv)
    first_grad = jnp.concatenate(
        [
            sum(
                dot_cols(qkv_grad[half], weight(whole, 0, half, start, block, 0, TILES[0]))
                for half in range(2)
            )
            for start in range(0, D, block)
        ],
        axis=1,
    )
    pack_blocks(send_blocks.at[3], first_grad[rows:], None)
    exchange(3)

    def weight_grad(index, mine, theirs, grad, their_grad, first, count):
        left = jnp.concatenate(
            [mine[:, first : first + count], theirs[:, first : first + count]], axis=0
        )
        view, base = tile_view(grads, index)
        at = base + first // 16
        for tile, width in tile_groups(index):
            to = slice(tile * LANES, (tile + width) * LANES)
            right = jnp.concatenate([grad[g, :, to], their_grad[:, to]], axis=0)
            found = dot_rows(left, right).astype(BF16)
            for t in range(width):
                view[at : at + count // 16, 16 * (tile + t) : 16 * (tile + t) + 16, :] = found[
                    :, t * LANES : (t + 1) * LANES
                ].reshape(count // 16, 16, LANES)

    for copy in pairs:
        copy.wait()
    for first in range(0, FF, D):
        weight_grad(3, activated, their_activated, down_grad, their_down, first, D)
    weight_grad(2, second_in, their_second, up_grad, their_up, 0, D)
    weight_grad(1, mixture, their_mixture, out_grad, their_out, 0, D)
    weight_grad(0, normed, their_normed, qkv_grad, their_qkv, 0, D)

    exchanged(3)
    first_grad = first_grad[:rows] + unpack_values(recv_blocks.at[3])
    hat = normed_hat[...]
    gain_one_sum = jnp.sum(first_grad * hat, axis=0, keepdims=True)
    shift_one_sum = jnp.sum(first_grad, axis=0, keepdims=True)
    input_grad[...] = in_order(
        middle_grad[...] + norm_back(first_grad * gain_one, hat, inverse[...])
    )
    down_sums = [
        jnp.sum(down_grad[half].astype(F32), axis=0, keepdims=True) for half in range(2)
    ]
    up_sum = jnp.concatenate(up_sums, axis=1)
    for half in range(2):
        to = slice(half * half_width, (half + 1) * half_width)
        listed = (
            gain_one_sum[:, to], gain_two_sum[:, to], shift_one_sum[:, to], shift_two_sum[:, to],
            down_sums[half], up_sum[:, half * FF // 2 : (half + 1) * FF // 2],
        )
        at = 0
        for vector in listed:
            count = vector.shape[1] // LANES
            small_parts[half, at : at + count, :] = vector.reshape(count, LANES)
            at += count
        small_parts[half, at:, :] = jnp.zeros((SMALL_ROWS - at, LANES), F32)
    hand_over(small_parts.at[1 - g], their_small)
    pairs[-1].wait()
    small_grads[...] = small_parts[g] + their_small[...]


def run_layer(tokens, cotangent, holes, lengths, whole, small, ways):
    rows = tokens.shape[0]
    vmem = pl.BlockSpec(memory_space=pltpu.VMEM)
    dma = pltpu.SemaphoreType.DMA
    half = D // 2
    shapes = [
        ((D // LANES, rows, LANES), F32),
        ((4, ways, 16, half + LANES), BF16),
        ((4, ways, 16, half + LANES), BF16),
        ((2, rows, rows), F32),
        ((2 * rows, D), BF16),
        ((rows, D), F32),
        ((rows, 1), F32),
        ((2 * rows, 3 * D), BF16),
        ((2, rows, D), F32),
        ((2, rows, HEADS), F32),
        ((rows, D), BF16),
        ((rows, D), BF16),
        ((rows, FF), BF16),
        ((rows, FF), F32),
        ((rows, D), F32),
        ((rows, 1), F32),
        ((rows, D), F32),
        ((2, 2 * rows, 3 * half), BF16),
        ((2, rows, half), BF16),
        ((2, rows, FF // 2), BF16),
        ((2, rows, half), BF16),
        ((rows, D), BF16),
        ((rows, D), BF16),
        ((2, rows, HEADS), F32),
        ((2 * rows, D), BF16),
        ((rows, D), BF16),
        ((rows, D), BF16),
        ((rows, FF), BF16),
        ((2 * rows, 3 * half), BF16),
        ((rows, half), BF16),
        ((rows, FF // 2), BF16),
        ((rows, half), BF16),
        ((2, SMALL_ROWS, LANES), F32),
        ((SMALL_ROWS, LANES), F32),
    ]
    return pl.pallas_call(
        partial(layer_kernel, ways),
        out_shape=(
            jax.ShapeDtypeStruct((rows, D), BF16),
            jax.ShapeDtypeStruct((rows, D), F32),
            jax.ShapeDtypeStruct((MAT_ROWS, LANES), BF16),
            jax.ShapeDtypeStruct((SMALL_ROWS, LANES), F32),
        ),
        in_specs=[vmem, vmem, vmem, pl.BlockSpec(memory_space=pltpu.SMEM), vmem, vmem],
        out_specs=(vmem,) * 4,
        scratch_shapes=[pltpu.VMEM(*shape) for shape in shapes]
        + [dma((4,)), dma((4,)), dma((9,)), dma((9,))],
        compiler_params=pltpu.CompilerParams(
            collective_id=2, has_side_effects=True, vmem_limit_bytes=VMEM_BYTES
        ),
        name="run_layer",
    )(tokens, cotangent, holes, lengths, whole, small)


def reduce_kernel(
    ways, grads_in, small_in, flat, grads, by_x, by_y, up_blocks, down_blocks, total, laid, follow_rows,
    small_all, x_send, x_recv, y_send, y_recv, z_send, up_recv, down_recv, tail_sem, small_sem,
    load_sem,
):
    s, g = place()
    planes = ways // 4
    z, y, x = s // 4, lax.rem(s // 2, 2), lax.rem(s, 2)
    own = MAT_ROWS // ways
    half = own // 2
    load = pltpu.make_async_copy(grads_in, grads, load_sem)
    load.start()
    enter(ways)
    load.wait()

    def at(plane, row, column, part):
        first = ((plane * 2 + row) * 2 + column) * own + part * half
        return pl.ds(pl.multiple_of(first, 16), half)

    def chip(plane, row, column):
        return ((plane * 2 + row) * 2 + column, g)

    def first_copies(plane):
        for k in range(2):
            yield remote(
                grads.at[at(plane, k, 1 - x, 0)], by_x.at[plane, 0, k],
                x_send.at[plane, 0, k], x_recv.at[plane, 0, k], chip(z, y, 1 - x),
            )
            yield remote(
                grads.at[at(plane, 1 - y, k, 1)], by_x.at[plane, 1, k],
                x_send.at[plane, 1, k], x_recv.at[plane, 1, k], chip(z, 1 - y, x),
            )

    def first_wait(plane, part, k):
        remote(
            by_x.at[plane, part, k], by_x.at[plane, part, k],
            x_send.at[plane, part, k], x_recv.at[plane, part, k], chip(z, y, x),
        ).wait_recv()

    def second_copies(plane):
        yield remote(
            grads.at[at(plane, 1 - y, x, 0)], by_y.at[plane, 0],
            y_send.at[plane, 0], y_recv.at[plane, 0], chip(z, 1 - y, x),
        )
        yield remote(
            grads.at[at(plane, y, 1 - x, 1)], by_y.at[plane, 1],
            y_send.at[plane, 1], y_recv.at[plane, 1], chip(z, y, 1 - x),
        )

    def add(where, block):
        grads[where, :] = (grads[where, :].astype(F32) + block[...].astype(F32)).astype(BF16)

    def second(plane):
        for part, other in ((0, 1 - y), (1, 1 - x)):
            first_wait(plane, part, other)
            where = at(plane, other, x, 0) if part == 0 else at(plane, y, other, 1)
            add(where, by_x.at[plane, part, other])
        for copy in second_copies(plane):
            copy.start()
        for part, mine in ((0, y), (1, x)):
            first_wait(plane, part, mine)
            add(at(plane, y, x, part), by_x.at[plane, part, mine])

    def line_copies(plane, part):
        where = grads.at[at(plane, y, x, part)]
        up = remote(
            where, up_blocks.at[plane, part], z_send.at[plane, part], up_recv.at[plane, part],
            chip(z + 1, y, x),
        )
        down = remote(
            where, down_blocks.at[plane, part], z_send.at[plane, part], down_recv.at[plane, part],
            chip(z - 1, y, x),
        )
        return up, down

    def line(plane):
        for part, copy in enumerate(second_copies(plane)):
            copy.wait_recv()
            where = at(plane, y, x, part)
            add(where, by_y.at[plane, part])
            up, down = line_copies(plane, part)

            def take_up(where=where, up=up, part=part):
                up.wait_recv()
                add(where, up_blocks.at[plane, part])

            def take_down(where=where, down=down, part=part):
                down.wait_recv()
                add(where, down_blocks.at[plane, part])

            pl.when((z < plane) & (z > 0))(take_up)
            pl.when((z > plane) & (z < planes - 1))(take_down)
            pl.when(z < plane)(up.start)
            pl.when(z > plane)(down.start)

    def settle(plane):
        def at_home():
            for part in range(2):
                up, down = line_copies(plane, part)
                to = slice(part * half, (part + 1) * half)
                total[to, :] = grads[at(plane, y, x, part), :].astype(F32)
                if plane > 0:
                    up.wait_recv()
                    total[to, :] += up_blocks[plane, part].astype(F32)
                if plane < planes - 1:
                    down.wait_recv()
                    total[to, :] += down_blocks[plane, part].astype(F32)

        pl.when(z == plane)(at_home)

    small_copy = remote(
        small_in, small_all.at[s], small_sem.at[0], small_sem.at[1], (ways - 1, g)
    )
    pl.when(s != ways - 1)(small_copy.start)
    order = list(range(planes - 1, -1, -1))
    for plane in order:
        for copy in first_copies(plane):
            copy.start()
    for plane in order:
        second(plane)
    for plane in order:
        line(plane)
    for plane in order:
        settle(plane)

    def lay(unit, carry):
        first = unit * UNIT

        def tiled(tiles):
            for group in range(UNIT // (16 * tiles)):
                for tile in range(tiles):
                    rows = total[pl.ds(first + 16 * (group * tiles + tile), 16), :]
                    laid[pl.ds(first + group * 16 * tiles + tile, 16, stride=tiles), :] = rows

        unit_tiles(s * (own // UNIT) + unit, tiled)
        return carry

    lax.fori_loop(0, own // UNIT, lay, 0)

    @pl.when(s == ways - 1)
    def _():
        remote(
            small_all.at[pl.ds(0, ways - 1)], small_all.at[pl.ds(0, ways - 1)],
            small_sem.at[0], small_sem.at[1], (0, g),
        ).wait_recv()
        small_all[ways - 1] = small_in[...]
        laid[own : own + SMALL_ROWS, :] = jnp.sum(small_all[...], axis=0)

    pl.when(s != ways - 1)(small_copy.wait_send)
    follow = remote(
        laid.at[pl.ds(0, SMALL_ROWS)], follow_rows, tail_sem.at[0], tail_sem.at[1],
        (lax.rem(s + ways - 1, ways), g),
    )
    follow.start()
    follow.wait()

    @pl.when(s != ways - 1)
    def _():
        laid[own : own + SMALL_ROWS, :] = follow_rows[...]

    flat_rows = flat.shape[0]
    laid[own + SMALL_ROWS :, :] = jnp.zeros(
        (laid.shape[0] - own - SMALL_ROWS, LANES), F32
    )
    entries = (MAT_ROWS * LANES + bounds_total()) // ways - own * LANES
    shift = entries * s
    row_shift, lane_shift = shift // LANES, lax.rem(shift, LANES)
    back = lax.rem(LANES - lane_shift, LANES)
    step_rows = 56
    lanes = lax.broadcasted_iota(jnp.int32, (step_rows, LANES), 1)

    def align(step, carry):
        start = step * step_rows
        here = laid[pl.ds(start + row_shift, step_rows), :]
        after = laid[pl.ds(start + row_shift + 1, step_rows), :]
        flat[pl.ds(pl.multiple_of(start, 8), step_rows), :] = jnp.where(
            lanes < LANES - lane_shift, pltpu.roll(here, back, 1), pltpu.roll(after, back, 1)
        )
        return carry

    lax.fori_loop(0, flat_rows // step_rows, align, 0)
    for plane in order:
        for copy in first_copies(plane):
            copy.wait_send()
        for copy in second_copies(plane):
            copy.wait_send()
        for part in range(2):
            pl.when(z != plane)(line_copies(plane, part)[0].wait_send)


def reduce_grads(grads, small, flat_rows, ways):
    own = MAT_ROWS // ways
    half = own // 2
    planes = ways // 4
    dma = pltpu.SemaphoreType.DMA
    vmem = pl.BlockSpec(memory_space=pltpu.VMEM)
    return pl.pallas_call(
        partial(reduce_kernel, ways),
        out_shape=jax.ShapeDtypeStruct((flat_rows, LANES), F32),
        in_specs=[pl.BlockSpec(memory_space=pl.ANY), vmem],
        out_specs=vmem,
        scratch_shapes=[
            pltpu.VMEM((MAT_ROWS, LANES), BF16),
            pltpu.VMEM((planes, 2, 2, half, LANES), BF16),
            pltpu.VMEM((planes, 2, half, LANES), BF16),
            pltpu.VMEM((planes, 2, half, LANES), BF16),
            pltpu.VMEM((planes, 2, half, LANES), BF16),
            pltpu.VMEM((own, LANES), F32),
            pltpu.VMEM((own + 2 * SMALL_ROWS, LANES), F32),
            pltpu.VMEM((SMALL_ROWS, LANES), F32),
            pltpu.VMEM((ways, SMALL_ROWS, LANES), F32),
            dma((planes, 2, 2)), dma((planes, 2, 2)),
            dma((planes, 2)), dma((planes, 2)),
            dma((planes, 2)), dma((planes, 2)), dma((planes, 2)),
            dma((2,)), dma((2,)), dma,
        ],
        compiler_params=pltpu.CompilerParams(
            collective_id=3, has_side_effects=True, vmem_limit_bytes=VMEM_BYTES
        ),
        name="reduce_grads",
    )(grads, small)


def on_device(tokens, cotangent, holes, slide_lengths, master, first_moment, second_moment):
    ways = lax.axis_size("seq")
    shard_size = master.shape[1]
    flat_rows = -(-shard_size // (8 * LANES)) * 8
    flat = jnp.pad(master[0], (0, flat_rows * LANES - shard_size)).reshape(flat_rows, LANES)
    whole, small = gather_params(flat, ways)
    output, input_grad, grads, small_grads = run_layer(
        tokens[0], cotangent[0], holes, slide_lengths, whole, small, ways
    )
    reduced = reduce_grads(grads, small_grads, flat_rows, ways).reshape(-1)[:shard_size]
    flat_index = lax.axis_index("seq") * shard_size + jnp.arange(shard_size, dtype=jnp.int32)
    new_moment, new_second, new_master = adam_update(
        master[0], first_moment[0], second_moment[0], reduced, flat_index
    )
    return (output[None], input_grad[None], new_moment[None], new_second[None], new_master[None])


def even(mesh):
    ways = mesh.shape["seq"]
    return ways % 4 == 0 and MAT_ROWS % (ways * UNIT) == 0 and ways * 8 == LANES


def solution(mesh):
    return jax.shard_map(
        on_device if even(mesh) else plain_on_device,
        mesh=mesh,
        in_specs=(
            P("grp", "seq", None),
            P("grp", "seq", None),
            P("grp", "seq"),
            P("grp", None),
            P("grp", "seq"),
            P("grp", "seq"),
            P("grp", "seq"),
        ),
        out_specs=(
            P("grp", "seq", None),
            P("grp", "seq", None),
            P("grp", "seq"),
            P("grp", "seq"),
            P("grp", "seq"),
        ),
        check_vma=False,
    )
```

```python
from functools import partial

import jax
import jax.numpy as jnp
from jax import lax
from jax.experimental import pallas as pl
from jax.experimental.pallas import tpu as pltpu
from jax.sharding import PartitionSpec as P

D = 768
FF = 3072
HEADS = 16
HEAD = 48
STEP = 10


EPS_NORM = 1e-05
EPS_ADAM = 1e-08
BETA_ONE = 0.9
BETA_TWO = 0.95


def as_sent(array):
    return jax.tree.map(lambda a: a.astype(jnp.bfloat16) if a.dtype == jnp.float32 else a, array)


def bounds():
    qkv_edge = 3 * D * D // 2
    out_edge = qkv_edge + D * D // 2
    up_edge = out_edge + D * FF // 2
    down_edge = up_edge + FF * D // 2
    gain_edge = down_edge + D
    return (qkv_edge, out_edge, up_edge, down_edge, gain_edge)


def per_segment(flat_index, values):
    edge_list = bounds()
    result = jnp.full(flat_index.shape, values[5], jnp.float32)
    for position in range(4, -1, -1):
        result = jnp.where(flat_index < edge_list[position], jnp.float32(values[position]), result)
    return result


def unpack(flat):
    edge_list = bounds()
    total = flat.shape[1]

    def joined(start, stop, shape):
        return jnp.concatenate(
            [flat[0, start:stop].reshape(shape), flat[1, start:stop].reshape(shape)], axis=-1
        )

    w_qkv = joined(0, edge_list[0], (D, 3 * D // 2))
    w_out = joined(edge_list[0], edge_list[1], (D, D // 2))
    w_up = joined(edge_list[1], edge_list[2], (D, FF // 2))
    w_down = joined(edge_list[2], edge_list[3], (FF, D // 2))
    gain_rows = joined(edge_list[3], edge_list[4], (2, D // 2))
    shift_rows = joined(edge_list[4], edge_list[4] + 3 * D // 2, (3, D // 2))
    bias_up = joined(edge_list[4] + 3 * D // 2, total, (FF // 2,))
    return (w_qkv, w_out, w_up, w_down, gain_rows, shift_rows, bias_up)


def normalize(values):
    centered = values - jnp.mean(values, axis=-1, keepdims=True)
    inverse = lax.rsqrt(jnp.mean(centered * centered, axis=-1, keepdims=True) + EPS_NORM)
    return (centered * inverse, inverse)


def norm_back(grad_hat, normed_hat, inverse):
    return inverse * (
        grad_hat
        - jnp.mean(grad_hat, axis=-1, keepdims=True)
        - normed_hat * jnp.mean(grad_hat * normed_hat, axis=-1, keepdims=True)
    )


def contract_rows(left, right):
    return lax.dot_general(
        left, right, (((0,), (0,)), ((), ())), preferred_element_type=jnp.float32
    )


def contract_cols(left, right):
    return lax.dot_general(
        left, right, (((1,), (1,)), ((), ())), preferred_element_type=jnp.float32
    )


def slide_index(positions, slide_ends):
    return jnp.sum((positions[:, None] >= slide_ends[None, :]).astype(jnp.int32), axis=1)


def split_heads(block_rows):
    return block_rows.reshape(block_rows.shape[0], HEADS, HEAD).transpose(1, 0, 2)


def join_heads(stacked):
    return stacked.transpose(1, 0, 2).reshape(stacked.shape[1], HEADS * HEAD)


def allowance(slides, present):
    token_count = slides.shape[0]
    same_slide = (slides[:, None] == slides[None, :]) & (present[None, :] > 0)
    return same_slide | jnp.eye(token_count, dtype=bool)


def attend(packed, slides, present):
    allowed = allowance(slides, present)
    scale = HEAD ** (-0.5)

    def one_head(pieces):
        query_head, key_head, value_head = pieces
        scores = contract_cols(query_head, key_head) * scale
        scores = jnp.where(allowed, scores, -1000000000.0)
        row_max = jnp.max(scores, axis=-1, keepdims=True)
        exponent = jnp.exp(scores - row_max)
        denominator = jnp.sum(exponent, axis=-1, keepdims=True)
        attention = (exponent / denominator).astype(jnp.bfloat16)
        result = jnp.dot(attention, value_head, preferred_element_type=jnp.float32)
        return (result, (row_max + jnp.log(denominator))[:, 0])

    outs, lses = lax.map(
        one_head,
        (
            split_heads(packed[:, :D]),
            split_heads(packed[:, D : 2 * D]),
            split_heads(packed[:, 2 * D :]),
        ),
    )
    return (join_heads(outs), lses.T)


def attend_back(packed, slides, present, lse_rows, out_grad, lse_grad):
    allowed = allowance(slides, present)
    scale = HEAD ** (-0.5)

    def one_head(pieces):
        query_head, key_head, value_head, lse_head, grad_head, extra_lse = pieces
        scores = contract_cols(query_head, key_head) * scale
        scores = jnp.where(allowed, scores, -1000000000.0)
        attention = jnp.exp(scores - lse_head[:, None])
        prob_grad = contract_cols(grad_head, value_head)
        inner_sum = jnp.sum(attention * prob_grad, axis=-1, keepdims=True)
        score_grad = (attention * (prob_grad - inner_sum + extra_lse[:, None])).astype(jnp.bfloat16)
        query_grad = jnp.dot(score_grad, key_head, preferred_element_type=jnp.float32) * scale
        key_grad = contract_rows(score_grad, query_head) * scale
        value_grad = contract_rows(attention.astype(jnp.bfloat16), grad_head)
        return (query_grad, key_grad, value_grad)

    query_grad, key_grad, value_grad = lax.map(
        one_head,
        (
            split_heads(packed[:, :D]),
            split_heads(packed[:, D : 2 * D]),
            split_heads(packed[:, 2 * D :]),
            lse_rows.T,
            split_heads(out_grad),
            lse_grad.T,
        ),
    )
    return jnp.concatenate(
        [join_heads(query_grad), join_heads(key_grad), join_heads(value_grad)], axis=1
    )


def adam_update(weights, moment, second, gradient, flat_index):
    step_rates = per_segment(
        flat_index,
        (
            0.7 * (2.0 / D) ** 0.5,
            0.7 * (24.0 / D) ** 0.5,
            0.7 * (1.0 / D) ** 0.5,
            0.7 * (1.0 / FF) ** 0.5,
            0.15,
            0.2,
        ),
    )
    decays = per_segment(flat_index, (0.1, 0.1, 0.1, 0.1, 0.0, 0.0))
    new_moment = BETA_ONE * moment + (1.0 - BETA_ONE) * gradient
    new_second = BETA_TWO * second + (1.0 - BETA_TWO) * gradient * gradient
    fix_one = 1.0 - BETA_ONE**STEP
    fix_two = 1.0 - BETA_TWO**STEP
    update = new_moment / fix_one / (jnp.sqrt(new_second / fix_two) + EPS_ADAM)
    return (new_moment, new_second, weights - step_rates * (update + decays * weights))


def column_halves(values):
    return values.reshape(values.shape[0], 2, values.shape[1] // 2)


def plain_on_device(tokens, cotangent, holes, slide_lengths, master, first_moment, second_moment):
    own_half = lax.all_gather(master.astype(jnp.bfloat16), "seq", axis=1, tiled=True)
    whole_flat = lax.all_gather(own_half, "grp", axis=0, tiled=True)
    w_qkv, w_out, w_up, w_down, gain_rows, shift_rows, bias_up = unpack(whole_flat)
    gain_rows = gain_rows.astype(jnp.float32)
    shift_rows = shift_rows.astype(jnp.float32)
    bias_up = bias_up.astype(jnp.float32)
    inputs = tokens[0].astype(jnp.float32)
    row_count = inputs.shape[0]
    seq_ways = lax.axis_size("seq")
    seq_place = lax.axis_index("seq")
    row_steps = jnp.arange(row_count, dtype=jnp.int32)
    slide_ends = jnp.cumsum(slide_lengths[0])
    near_slides = slide_index(seq_place * row_count + row_steps, slide_ends)
    far_slides = slide_index(seq_place + seq_ways * row_steps, slide_ends)
    near_present = holes[0]
    strided_shape = (row_count // seq_ways, seq_ways)

    def to_strided(packed):
        moved, moved_mask = (
            lax.all_to_all(
                packed.reshape(strided_shape + (3 * D,)),
                "seq",
                split_axis=1,
                concat_axis=0,
                tiled=True,
            ),
            lax.all_to_all(
                near_present.astype(jnp.bfloat16).reshape(strided_shape + (1,)),
                "seq",
                split_axis=1,
                concat_axis=0,
                tiled=True,
            ),
        )
        return (moved.reshape(row_count, 3 * D), moved_mask.reshape(row_count).astype(jnp.int32))

    normed_one, inverse_one = normalize(inputs)
    normed = (normed_one * gain_rows[0] + shift_rows[0]).astype(jnp.bfloat16)
    projected = jnp.dot(normed, w_qkv, preferred_element_type=jnp.float32).astype(jnp.bfloat16)
    near_out, near_lse = attend(projected, near_slides, near_present)
    far_proj, far_present = to_strided(projected)
    far_local, far_local_lse = attend(far_proj, far_slides, far_present)
    returned = (
        lax.all_to_all(
            far_local.reshape(row_count, 1, D).astype(jnp.bfloat16),
            "seq",
            split_axis=0,
            concat_axis=1,
            tiled=True,
        ).astype(jnp.float32),
        lax.all_to_all(
            far_local_lse.reshape(row_count, 1, HEADS).astype(jnp.bfloat16),
            "seq",
            split_axis=0,
            concat_axis=1,
            tiled=True,
        ).astype(jnp.float32),
    )
    far_out = returned[0].reshape(row_count, D)
    far_lse = returned[1].reshape(row_count, HEADS)
    near_share = jax.nn.sigmoid(near_lse - far_lse)
    near_heads = near_out.reshape(row_count, HEADS, HEAD)
    far_heads = far_out.reshape(row_count, HEADS, HEAD)
    mixture = (
        (near_share[:, :, None] * near_heads + (1.0 - near_share[:, :, None]) * far_heads)
        .reshape(row_count, D)
        .astype(jnp.bfloat16)
    )
    middle = inputs + jnp.dot(mixture, w_out, preferred_element_type=jnp.float32)
    normed_two, inverse_two = normalize(middle)
    second_in = (normed_two * gain_rows[1] + shift_rows[1]).astype(jnp.bfloat16)
    hidden = jnp.dot(second_in, w_up, preferred_element_type=jnp.float32) + bias_up
    activated = jax.nn.gelu(hidden, approximate=True).astype(jnp.bfloat16)
    output = middle + jnp.dot(activated, w_down, preferred_element_type=jnp.float32) + shift_rows[2]
    upstream = cotangent[0].astype(jnp.float32)
    down_grad = upstream.astype(jnp.bfloat16)
    grad_act = contract_cols(down_grad, w_down)
    gelu_pull = jax.vjp(partial(jax.nn.gelu, approximate=True), hidden)[1]
    hidden_grad = gelu_pull(grad_act)[0].astype(jnp.bfloat16)
    second_grad = contract_cols(hidden_grad, w_up)
    grad_gain_two = jnp.sum(second_grad * normed_two, axis=0)
    grad_shift_two = jnp.sum(second_grad, axis=0)
    middle_grad = upstream + norm_back(second_grad * gain_rows[1], normed_two, inverse_two)
    attend_grad = middle_grad.astype(jnp.bfloat16)
    mix_grad = contract_cols(attend_grad, w_out).reshape(row_count, HEADS, HEAD)
    near_lse_grad = (
        near_share * (1.0 - near_share) * jnp.sum((near_heads - far_heads) * mix_grad, axis=-1)
    )
    near_grad = (near_share[:, :, None] * mix_grad).reshape(row_count, D).astype(jnp.bfloat16)
    far_grad = ((1.0 - near_share[:, :, None]) * mix_grad).reshape(row_count, D)
    sent = (
        lax.all_to_all(
            as_sent(far_grad.reshape(strided_shape + (D,))),
            "seq",
            split_axis=1,
            concat_axis=0,
            tiled=True,
        ),
        lax.all_to_all(
            as_sent((-near_lse_grad).reshape(strided_shape + (HEADS,))),
            "seq",
            split_axis=1,
            concat_axis=0,
            tiled=True,
        ),
    )
    far_back = sent[0].reshape(row_count, D).astype(jnp.bfloat16)
    far_lse_grad = sent[1].reshape(row_count, HEADS)
    again_proj, again_present = to_strided(projected)
    again_lse = attend(again_proj, far_slides, again_present)[1]
    far_proj_grad = attend_back(
        again_proj, far_slides, again_present, again_lse, far_back, far_lse_grad
    ).astype(jnp.bfloat16)
    far_home = lax.all_to_all(
        far_proj_grad.reshape(row_count, 1, 3 * D), "seq", split_axis=0, concat_axis=1, tiled=True
    ).reshape(row_count, 3 * D)
    near_proj_grad = attend_back(
        projected, near_slides, near_present, near_lse, near_grad, near_lse_grad
    )
    proj_grad = (near_proj_grad + far_home.astype(jnp.float32)).astype(jnp.bfloat16)
    first_grad = contract_cols(proj_grad, w_qkv)
    grad_gain_one = jnp.sum(first_grad * normed_one, axis=0)
    grad_shift_one = jnp.sum(first_grad, axis=0)
    input_grad = middle_grad + norm_back(first_grad * gain_rows[0], normed_one, inverse_one)
    both_rows = (
        lax.all_gather(normed, "grp", axis=0, tiled=True),
        lax.all_gather(mixture, "grp", axis=0, tiled=True),
        lax.all_gather(second_in, "grp", axis=0, tiled=True),
        lax.all_gather(activated, "grp", axis=0, tiled=True),
    )
    moved = (
        lax.all_to_all(column_halves(proj_grad), "grp", split_axis=1, concat_axis=0, tiled=True),
        lax.all_to_all(column_halves(attend_grad), "grp", split_axis=1, concat_axis=0, tiled=True),
        lax.all_to_all(column_halves(hidden_grad), "grp", split_axis=1, concat_axis=0, tiled=True),
        lax.all_to_all(column_halves(down_grad), "grp", split_axis=1, concat_axis=0, tiled=True),
    )
    proj_mine = moved[0].reshape(2 * row_count, 3 * D // 2)
    attend_mine = moved[1].reshape(2 * row_count, D // 2)
    hidden_mine = moved[2].reshape(2 * row_count, FF // 2)
    down_mine = moved[3].reshape(2 * row_count, D // 2)
    norm_sums = lax.psum(
        jnp.stack([grad_gain_one, grad_gain_two, grad_shift_one, grad_shift_two]), "grp"
    )
    half_width = D // 2
    norm_half = lax.dynamic_slice_in_dim(
        norm_sums, lax.axis_index("grp") * half_width, half_width, 1
    )
    grad_w_qkv = contract_rows(both_rows[0], proj_mine)
    grad_w_out = contract_rows(both_rows[1], attend_mine)
    grad_w_up = contract_rows(both_rows[2], hidden_mine)
    grad_w_down = contract_rows(both_rows[3], down_mine)
    grad_bias_down = jnp.sum(down_mine.astype(jnp.float32), axis=0)
    grad_bias_up = jnp.sum(hidden_mine.astype(jnp.float32), axis=0)
    gradient = jnp.concatenate(
        [
            grad_w_qkv.reshape(-1),
            grad_w_out.reshape(-1),
            grad_w_up.reshape(-1),
            grad_w_down.reshape(-1),
            norm_half[0],
            norm_half[1],
            norm_half[2],
            norm_half[3],
            grad_bias_down,
            grad_bias_up,
        ]
    )
    reduced = lax.psum_scatter(gradient, "seq", scatter_dimension=0, tiled=True)
    shard_size = master.shape[1]
    flat_index = lax.axis_index("seq") * shard_size + jnp.arange(shard_size, dtype=jnp.int32)
    new_moment, new_second, new_master = adam_update(
        master[0], first_moment[0], second_moment[0], reduced, flat_index
    )
    return (
        output[None].astype(jnp.bfloat16),
        input_grad[None],
        new_moment[None],
        new_second[None],
        new_master[None],
    )


LANES = 128
BF16 = jnp.bfloat16
F32 = jnp.float32
MAT_ROWS = (3 * D * D + D * D + D * FF + FF * D) // 2 // LANES
SMALL_ROWS = 32
UNIT = 576
PAIR = 2
TILES = (3 * D // 2 // LANES, D // 2 // LANES, FF // 2 // LANES, D // 2 // LANES)
DEPTHS = (D, D, D, FF)
MESH = pl.DeviceIdType.MESH
VMEM_BYTES = 60 * 2**20
NEG = -1000000000.0


def matrix_starts():
    starts = [0]
    for tiles, depth in zip(TILES, DEPTHS):
        starts.append(starts[-1] + tiles * depth)
    return starts


def place():
    return lax.axis_index("seq"), lax.axis_index("grp")


def greet_all(ways):
    s, g = place()
    barrier = pltpu.get_barrier_semaphore()

    def greet(step, carry):
        pl.semaphore_signal(
            barrier, inc=1, device_id=(lax.rem(s + step, ways), g), device_id_type=MESH
        )
        return carry

    lax.fori_loop(1, ways, greet, 0)
    pl.semaphore_signal(barrier, inc=1, device_id=(s, 1 - g), device_id_type=MESH)
    return barrier


def remote(src, dst, send_sem, recv_sem, to):
    return pltpu.make_async_remote_copy(
        src_ref=src,
        dst_ref=dst,
        send_sem=send_sem,
        recv_sem=recv_sem,
        device_id=to,
        device_id_type=MESH,
    )


def unit_tiles(unit, body):
    edges = [start // UNIT for start in matrix_starts()]
    kinds = {}
    for index, tiles in enumerate(TILES):
        inside = (unit >= edges[index]) & (unit < edges[index + 1])
        kinds[tiles] = kinds[tiles] | inside if tiles in kinds else inside
    for tiles, inside in kinds.items():
        pl.when(inside)(lambda tiles=tiles: body(tiles))


def dot(left, right):
    return jnp.dot(left, right, preferred_element_type=F32)


def dot_cols(left, right):
    return contract_cols(left, right)


def dot_rows(left, right):
    return contract_rows(left, right)


def tile_view(ref, index):
    rows = 16 * TILES[index]
    start = matrix_starts()[index]
    return ref.reshape(ref.shape[:-2] + (MAT_ROWS // rows, rows, LANES)), start // rows


def tile_groups(index):
    tiles = TILES[index]
    groups, at = [], 0
    while at < tiles:
        width = 3 if tiles - at == 3 else 2
        groups.append((at, width))
        at += width
    return groups


def weight(ref, index, half, row, rows, tile, width):
    view, base = tile_view(ref, index)
    first = base + row // 16
    pieces = [
        view[half, first : first + rows // 16, 16 * t : 16 * t + 16, :].reshape(rows, LANES)
        for t in range(tile, tile + width)
    ]
    return jnp.concatenate(pieces, axis=1)


def heads_of(rows):
    row = lax.broadcasted_iota(jnp.int32, (rows, D), 0) * HEAD
    column = lax.broadcasted_iota(jnp.int32, (rows, D), 1)
    return ((column >= row) & (column < row + HEAD)).astype(F32)


def to_columns(per_head):
    return jnp.dot(
        per_head, heads_of(HEADS), precision=lax.Precision.HIGHEST, preferred_element_type=F32
    )


def to_heads(columns):
    return lax.dot_general(
        columns,
        heads_of(HEADS),
        (((1,), (1,)), ((), ())),
        precision=lax.Precision.HIGHEST,
        preferred_element_type=F32,
    )


def pack_blocks(ref, values, extra):
    blocks = values.shape[0] // 8
    split = values.reshape(blocks, 8, D)
    ref[:, :, : D // 2] = jnp.concatenate(
        [split[:, :, : D // 2], split[:, :, D // 2 :]], axis=1
    ).astype(BF16)
    if extra is not None:
        high = extra.astype(BF16).astype(F32)
        low = extra - high
        pieces = jnp.concatenate(
            [high.reshape(blocks, 8, HEADS), low.reshape(blocks, 8, HEADS)], axis=1
        )
        ref[:, :, D // 2 : D // 2 + HEADS] = pieces.astype(BF16)


def unpack_values(ref):
    blocks = ref.shape[0]
    values = ref[:, :, : D // 2].astype(F32)
    return jnp.concatenate(
        [values[:, :8, :].reshape(blocks * 8, D // 2), values[:, 8:, :].reshape(blocks * 8, D // 2)],
        axis=1,
    )


def unpack_extra(ref):
    blocks = ref.shape[0]
    pieces = ref[:, :, D // 2 :].astype(F32)
    both = pieces[:, :8, :] + pieces[:, 8:, :]
    return both.reshape(blocks * 8, LANES)[:, :HEADS]


def slide_masks(ends_ref, s, ways, near_keys, far_keys):
    rows = near_keys.shape[1]
    ends, end = [], 0
    for index in range(ends_ref.shape[1]):
        end = end + ends_ref[0, index]
        ends.append(end)

    def slides(positions):
        total = jnp.zeros(positions.shape, jnp.int32)
        for end in ends:
            total = total + (positions >= end).astype(jnp.int32)
        return total

    across = rows // ways
    result = []
    for far, keys in ((False, near_keys), (True, far_keys)):
        found = []
        for dim in (0, 1):
            at = lax.broadcasted_iota(jnp.int32, (rows, rows), dim)
            if far:
                position = s + ways * at
            else:
                position = rows * s + ways * lax.rem(at, across) + at // across
            found.append(slides(position))
        query = lax.broadcasted_iota(jnp.int32, (rows, rows), 0)
        key = lax.broadcasted_iota(jnp.int32, (rows, rows), 1)
        allowed = ((found[0] == found[1]) & (keys > 0.5)) | (query == key)
        result.append(allowed.astype(F32))
    return result


def step_kernel(
    ways, tokens, cotangent, holes, lengths, flat,
    output, input_grad, flat_grad,
    whole, grads, small, extended, aligned, tail,
    turning, send_blocks, recv_blocks, masks, normed, normed_hat, inverse, projected, attended, lses,
    mixture, second_in, activated, slope, second_hat, second_inverse, middle_grad,
    qkv_grad, out_grad, up_grad, down_grad, near_grad, far_grad, lse_grads,
    their_normed, their_mixture, their_second, their_activated,
    their_qkv, their_out, their_up, their_down, small_parts, their_small,
    by_x, by_y, by_z, total, laid, follow_rows, small_all,
    tail_sem, slot_send, slot_recv, core_send, core_recv, small_send, small_recv,
    block_send, block_recv, pair_send, pair_recv,
    x_send, x_recv, y_send, y_recv, z_send, z_recv, end_sem, sum_sem,
):
    s, g = place()
    planes = ways // 4
    z, y, x = s // 4, lax.rem(s // 2, 2), lax.rem(s, 2)
    own = MAT_ROWS // ways
    half_own = own // 2
    rows = tokens.shape[0]
    across = rows // ways
    tiles = D // LANES
    half_width = D // 2
    third = half_width // LANES
    entries = (MAT_ROWS * LANES + bounds_total()) // ways - own * LANES
    shift = entries * s
    row_shift, lane_shift = shift // LANES, lax.rem(shift, LANES)

    def chip(plane, row, column):
        return ((plane * 2 + row) * 2 + column, g)

    def part_at(plane, row, column, part):
        first = ((plane * 2 + row) * 2 + column) * own + part * half_own
        return pl.ds(pl.multiple_of(first, 16), half_own)


    last_row, last_lanes = divmod(own * LANES + entries, LANES)

    def take_flat():
        end = SMALL_ROWS + flat.shape[0]
        extended[SMALL_ROWS:end, :] = flat[...]
        extended[end:, :] = jnp.zeros((extended.shape[0] - end, LANES), F32)

    def follow_copy():
        return remote(
            tail, extended.at[pl.ds(0, SMALL_ROWS)], tail_sem.at[0], tail_sem.at[1],
            (lax.rem(s + 1, ways), g),
        )

    def send_tail():
        lanes = lax.broadcasted_iota(jnp.int32, (SMALL_ROWS, LANES), 1)
        gap = LANES - last_lanes
        older = pltpu.roll(flat[last_row - SMALL_ROWS : last_row, :], gap, 1)
        newer = pltpu.roll(flat[last_row - SMALL_ROWS + 1 : last_row + 1, :], gap, 1)
        tail[...] = jnp.where(lanes < gap, older, newer)
        follow_copy().start()

    def align_own():
        follow_copy().wait()
        step_rows = 176
        step_lanes = lax.broadcasted_iota(jnp.int32, (step_rows, LANES), 1)

        def align(step, carry):
            start = step * step_rows
            here = extended[pl.ds(SMALL_ROWS + start - row_shift, step_rows), :]
            before = extended[pl.ds(SMALL_ROWS - 1 + start - row_shift, step_rows), :]
            aligned[pl.ds(pl.multiple_of(start, 8), step_rows), :] = jnp.where(
                step_lanes >= lane_shift,
                pltpu.roll(here, lane_shift, 1),
                pltpu.roll(before, lane_shift, 1),
            )
            return carry

        lax.fori_loop(0, (own + SMALL_ROWS) // step_rows, align, 0)

        def fill(unit, carry):
            first = unit * UNIT

            def tiled(count):
                for group in range(UNIT // (16 * count)):
                    for tile in range(count):
                        block = aligned[pl.ds(first + group * 16 * count + tile, 16, stride=count), :]
                        at = s * own + first + 16 * (group * count + tile)
                        whole[g, pl.ds(pl.multiple_of(at, 16), 16), :] = block.astype(BF16)

            unit_tiles(s * (own // UNIT) + unit, tiled)
            return carry

        lax.fori_loop(0, own // UNIT, fill, 0)

    order = [z]
    for step in range(1, planes):
        listed = [[p for p in ([0] + [q for q in range(at + 1, planes)] + [q for q in range(at - 1, 0, -1)]) if p != at]
                  for at in range(planes)]
        plane = jnp.int32(listed[0][step - 1])
        for at in range(1, planes):
            plane = jnp.where(z == at, listed[at][step - 1], plane)
        order.append(plane)

    def slot_copy(plane, row, column, part, kind, to):
        where = whole.at[g, part_at(plane, row, column, part)]
        return remote(
            where,
            where,
            slot_send.at[part, plane, kind],
            slot_recv.at[part, (plane * 2 + row) * 2 + column],
            to,
        )

    def line_up(plane, part):
        return slot_copy(plane, y, x, part, 0, chip(z + 1, y, x))

    def line_down(plane, part):
        return slot_copy(plane, y, x, part, 1, chip(z - 1, y, x))

    def in_plane(plane, part):
        to_x = slot_copy(plane, y, x, part, 2, chip(z, y, 1 - x))
        to_y = slot_copy(plane, y, x, part, 3, chip(z, 1 - y, x))
        return (to_y, to_x) if part == 0 else (to_x, to_y)

    def turned(plane):
        return (
            slot_copy(plane, 1 - y, x, 0, 4, chip(z, y, 1 - x)),
            slot_copy(plane, y, 1 - x, 1, 4, chip(z, 1 - y, x)),
        )

    def spread_own():
        for part in range(2):
            pl.when(z > 0)(lambda part=part: line_down(z, part).start())
            pl.when(z == 0)(lambda part=part: line_up(z, part).start())
            for copy in in_plane(z, part):
                copy.start()

    def spread_own_up():
        for part in range(2):
            pl.when((z > 0) & (z < planes - 1))(lambda part=part: line_up(z, part).start())

    def spread(step):
        plane = order[step]
        for part in range(2):
            slot_copy(plane, y, x, part, 0, chip(z, y, x)).wait_recv()
            pl.when((z > plane) & (z < planes - 1))(lambda part=part: line_up(plane, part).start())
            pl.when((z < plane) & (z > 0))(lambda part=part: line_down(plane, part).start())
            for copy in in_plane(plane, part):
                copy.start()

    def turn(step):
        for copy in turned(order[step]):
            copy.wait_recv()
            copy.start()

    def across_copy(plane):
        block = whole.at[g, pl.ds(pl.multiple_of(plane * 4 * own, 16), 4 * own)]
        return remote(block, block, core_send.at[plane], core_recv.at[plane], (s, 1 - g))

    def across_recv(plane):
        block = whole.at[1 - g, pl.ds(pl.multiple_of(plane * 4 * own, 16), 4 * own)]
        return remote(block, block, core_send.at[plane], core_recv.at[plane], (s, 1 - g))

    def finish(step):
        plane = order[step]
        slot_copy(plane, y, 1 - x, 0, 0, chip(z, y, x)).wait_recv()
        slot_copy(plane, 1 - y, 1 - x, 0, 0, chip(z, y, x)).wait_recv()
        slot_copy(plane, 1 - y, x, 1, 0, chip(z, y, x)).wait_recv()
        slot_copy(plane, 1 - y, 1 - x, 1, 0, chip(z, y, x)).wait_recv()
        across_copy(plane).start()

    def arrived(step):
        across_recv(order[step]).wait_recv()

    def gather_sent():
        for plane in range(planes):
            for part in range(2):
                pl.when((z >= plane) & (z < planes - 1))(
                    lambda part=part, plane=plane: line_up(plane, part).wait_send()
                )
                pl.when((z <= plane) & (z > 0))(
                    lambda part=part, plane=plane: line_down(plane, part).wait_send()
                )
                for copy in in_plane(plane, part):
                    copy.wait_send()
            for copy in turned(plane):
                copy.wait_send()
            across_copy(plane).wait_send()

    def small_to(index):
        return remote(small.at[g], small.at[g], small_send.at[index], small_recv.at[0], (index, g))

    def small_across():
        return remote(
            small.at[g], small.at[g], small_send.at[ways - 1], small_recv.at[1], (s, 1 - g)
        )

    def small_out():
        def tell(index, carry):
            small_to(index).start()
            return carry

        @pl.when(s == ways - 1)
        def _():
            small[g] = aligned[own : own + SMALL_ROWS, :].astype(BF16)
            lax.fori_loop(0, ways - 1, tell, 0)

    def small_in():
        pl.when(s != ways - 1)(lambda: small_to(s).wait_recv())
        small_across().start()
        remote(
            small.at[1 - g], small.at[1 - g], small_send.at[ways - 1], small_recv.at[1], (s, 1 - g)
        ).wait_recv()

    def small_sent():
        def told(index, carry):
            small_to(index).wait_send()
            return carry

        @pl.when(s == ways - 1)
        def _():
            lax.fori_loop(0, ways - 1, told, 0)

        small_across().wait_send()


    def first_copies(plane):
        for k in range(2):
            yield remote(
                grads.at[part_at(plane, k, 1 - x, 0)], by_x.at[plane, 0, k],
                x_send.at[plane, 0, k], x_recv.at[plane, 0, k], chip(z, y, 1 - x),
            )
            yield remote(
                grads.at[part_at(plane, 1 - y, k, 1)], by_x.at[plane, 1, k],
                x_send.at[plane, 1, k], x_recv.at[plane, 1, k], chip(z, 1 - y, x),
            )

    def first_wait(plane, part, k):
        remote(
            by_x.at[plane, part, k], by_x.at[plane, part, k],
            x_send.at[plane, part, k], x_recv.at[plane, part, k], chip(z, y, x),
        ).wait_recv()

    def second_copies(plane):
        yield remote(
            grads.at[part_at(plane, 1 - y, x, 0)], by_y.at[plane, 0],
            y_send.at[plane, 0], y_recv.at[plane, 0], chip(z, 1 - y, x),
        )
        yield remote(
            grads.at[part_at(plane, y, 1 - x, 1)], by_y.at[plane, 1],
            y_send.at[plane, 1], y_recv.at[plane, 1], chip(z, y, 1 - x),
        )

    def add(where, block):
        grads[where, :] = (grads[where, :].astype(F32) + block[...].astype(F32)).astype(BF16)

    def reduce_first(plane):
        for copy in first_copies(plane):
            copy.start()

    def reduce_second(plane):
        copies = list(second_copies(plane))
        for part, other in ((0, 1 - y), (1, 1 - x)):
            first_wait(plane, part, other)
            where = part_at(plane, other, x, 0) if part == 0 else part_at(plane, y, other, 1)
            add(where, by_x.at[plane, part, other])
            copies[part].start()
        for part, mine in ((0, y), (1, x)):
            first_wait(plane, part, mine)
            add(part_at(plane, y, x, part), by_x.at[plane, part, mine])

    def home_copy(plane, part, step):
        return remote(
            grads.at[part_at(plane, y, x, part)], by_z.at[step - 1, part],
            z_send.at[plane, part], z_recv.at[step - 1, part], chip(plane, y, x),
        )

    def reduce_third(plane):
        for part, copy in enumerate(second_copies(plane)):
            copy.wait_recv()
            add(part_at(plane, y, x, part), by_y.at[plane, part])

            @pl.when(z != plane)
            def _(part=part):
                home_copy(plane, part, lax.rem(planes + plane - z, planes)).start()

    def reduce_sent():
        for plane in range(planes):
            for copy in first_copies(plane):
                copy.wait_send()
            for copy in second_copies(plane):
                copy.wait_send()
            for part in range(2):

                @pl.when(z != plane)
                def _(part=part, plane=plane):
                    home_copy(plane, part, lax.rem(planes + plane - z, planes)).wait_send()

    def reduce_last():
        for part in range(2):
            to = slice(part * half_own, (part + 1) * half_own)
            total[to, :] = grads[part_at(z, y, x, part), :].astype(F32)
            for step in range(1, planes):
                home_copy(z, part, step).wait_recv()
                total[to, :] += by_z[step - 1, part].astype(F32)

    def small_home():
        return remote(
            small_parts.at[g], small_all.at[s], sum_sem.at[0], sum_sem.at[1], (ways - 1, g)
        )

    def settle():
        def lay(unit, carry):
            first = unit * UNIT

            def tiled(count):
                for group in range(UNIT // (16 * count)):
                    for tile in range(count):
                        block = total[
                            pl.ds(pl.multiple_of(first + 16 * (group * count + tile), 16), 16), :
                        ]
                        laid[pl.ds(first + group * 16 * count + tile, 16, stride=count), :] = block

            unit_tiles(s * (own // UNIT) + unit, tiled)
            return carry

        lax.fori_loop(0, own // UNIT, lay, 0)
        follow = remote(
            laid.at[pl.ds(0, SMALL_ROWS)], follow_rows, end_sem.at[0], end_sem.at[1],
            (lax.rem(s + ways - 1, ways), g),
        )
        follow.start()

        @pl.when(s == ways - 1)
        def _():
            remote(
                small_all.at[pl.ds(0, ways - 1)], small_all.at[pl.ds(0, ways - 1)],
                sum_sem.at[0], sum_sem.at[1], (0, g),
            ).wait_recv()
            small_all[ways - 1] = small_parts[g]
            laid[own : own + SMALL_ROWS, :] = jnp.sum(small_all[...], axis=0)

        laid[own + SMALL_ROWS :, :] = jnp.zeros((laid.shape[0] - own - SMALL_ROWS, LANES), F32)
        follow.wait()

        @pl.when(s != ways - 1)
        def _():
            laid[own : own + SMALL_ROWS, :] = follow_rows[...]

        back = lax.rem(LANES - lane_shift, LANES)
        step_rows = 56
        lanes = lax.broadcasted_iota(jnp.int32, (step_rows, LANES), 1)

        def align(step, carry):
            start = step * step_rows
            here = laid[pl.ds(start + row_shift, step_rows), :]
            after = laid[pl.ds(start + row_shift + 1, step_rows), :]
            flat_grad[pl.ds(pl.multiple_of(start, 8), step_rows), :] = jnp.where(
                lanes < LANES - lane_shift, pltpu.roll(here, back, 1), pltpu.roll(after, back, 1)
            )
            return carry

        lax.fori_loop(0, flat_grad.shape[0] // step_rows, align, 0)


    def exchange(index):
        def start(step, carry):
            to = lax.rem(s + step, ways)
            remote(
                send_blocks.at[index, to],
                recv_blocks.at[index, s],
                block_send.at[index],
                block_recv.at[index],
                (to, g),
            ).start()
            return carry

        recv_blocks[index, s] = send_blocks[index, s]
        lax.fori_loop(1, ways, start, 0)

    def exchanged(index):
        remote(
            send_blocks.at[index, pl.ds(0, ways - 1)],
            recv_blocks.at[index, pl.ds(0, ways - 1)],
            block_send.at[index],
            block_recv.at[index],
            (s, 1 - g),
        ).wait()

    pairs = {}

    def hand_over(name, src, dst):
        index = len(pairs)
        pairs[name] = remote(src, dst, pair_send.at[index], pair_recv.at[index], (s, 1 - g))
        pairs[name].start()

    def by_residue(value):
        for tile in range(tiles):
            turning[tile] = value[:, tile * LANES : (tile + 1) * LANES]
        return jnp.concatenate(
            [
                jnp.concatenate(
                    [turning[tile, pl.ds(i, across, stride=ways), :] for i in range(ways)], axis=0
                )
                for tile in range(tiles)
            ],
            axis=1,
        )

    def in_order(value):
        for tile in range(tiles):
            for i in range(ways):
                turning[tile, pl.ds(i, across, stride=ways), :] = value[
                    across * i : across * (i + 1), tile * LANES : (tile + 1) * LANES
                ]
        return jnp.concatenate([turning[tile] for tile in range(tiles)], axis=1)

    def small_row(first, count):
        return jnp.concatenate(
            [small[half, first + r : first + r + 1, :] for half in range(2) for r in range(count)],
            axis=1,
        ).astype(F32)

    temper = HEAD ** (-0.5)

    def scores(which, head):
        at = slice(which * rows, (which + 1) * rows)
        query = projected[at, head * HEAD : (head + 1) * HEAD]
        key = projected[at, D + head * HEAD : D + (head + 1) * HEAD]
        value = projected[at, 2 * D + head * HEAD : 2 * D + (head + 1) * HEAD]
        found = jnp.where(masks[which] > 0.5, dot_cols(query, key) * temper, NEG)
        return query, key, value, found

    def attend_set(which, between):
        results, totals = [], []
        for head in range(HEADS):
            _, _, value, found = scores(which, head)
            top = jnp.max(found, axis=1, keepdims=True)
            weights = jnp.exp(found - top)
            summed = jnp.sum(weights, axis=1, keepdims=True)
            results.append(dot(weights.astype(BF16), value) * (1.0 / summed))
            totals.append(top + jnp.log(summed))
            if head in between:
                between[head]()
        attended[which] = jnp.concatenate(results, axis=1)
        lses[which] = jnp.concatenate(totals, axis=1)

    def attend_set_back(which, out_grads, between):
        lists = ([], [], [])
        for head in range(HEADS):
            query, key, value, found = scores(which, head)
            weights = jnp.exp(found - lses[which, :, head : head + 1])
            pulled = out_grads[:, head * HEAD : (head + 1) * HEAD]
            weight_grad = dot_cols(pulled, value)
            inner = jnp.sum(weights * weight_grad, axis=1, keepdims=True)
            extra = lse_grads[which, :, head : head + 1] - inner
            score_grad = (weights * (weight_grad + extra)).astype(BF16)
            lists[0].append(dot(score_grad, key) * temper)
            lists[1].append(dot_rows(score_grad, query) * temper)
            lists[2].append(dot_rows(weights.astype(BF16), pulled))
            if head in between:
                between[head]()
        at = slice(which * rows, (which + 1) * rows)
        query_grad, key_grad, value_grad = (jnp.concatenate(one, axis=1).astype(BF16) for one in lists)
        qkv_grad[0, at, :D] = query_grad
        qkv_grad[0, at, D:] = key_grad[:, :half_width]
        qkv_grad[1, at, :half_width] = key_grad[:, half_width:]
        qkv_grad[1, at, half_width:] = value_grad

    def weight_grad(index, mine, theirs, grad, their_grad, first, count):
        left = jnp.concatenate(
            [mine[:, first : first + count], theirs[:, first : first + count]], axis=0
        )
        view, base = tile_view(grads, index)
        at = base + first // 16
        for tile, width in tile_groups(index):
            to = slice(tile * LANES, (tile + width) * LANES)
            right = jnp.concatenate([grad[g, :, to], their_grad[:, to]], axis=0)
            found = dot_rows(left, right).astype(BF16)
            for t in range(width):
                view[at : at + count // 16, 16 * (tile + t) : 16 * (tile + t) + 16, :] = found[
                    :, t * LANES : (t + 1) * LANES
                ].reshape(count // 16, 16, LANES)


    barrier = greet_all(ways)
    inputs = by_residue(tokens[...].astype(F32))
    lane = lax.broadcasted_iota(jnp.int32, (rows, rows), 1)
    row = lax.broadcasted_iota(jnp.int32, (rows, rows), 0)
    flags = holes[...].astype(F32)
    to_column = (row == lane).astype(F32)
    own_column = jnp.sum(to_column * flags, axis=1, keepdims=True)
    turned_at = ways * lax.rem(row, across) + row // across
    turned_column = jnp.sum((turned_at == lane).astype(F32) * flags, axis=1, keepdims=True)
    turned_row_at = ways * lax.rem(lane, across) + lane // across
    turned_row = jnp.sum((turned_row_at == row).astype(F32) * own_column, axis=0, keepdims=True)
    pack_blocks(send_blocks.at[0], inputs, jnp.broadcast_to(turned_column, (rows, HEADS)) * 1.0)
    take_flat()
    pl.semaphore_wait(barrier, ways)
    send_tail()
    exchange(0)
    align_own()
    spread_own()
    small_out()

    upstream = by_residue(cotangent[...].astype(F32))
    for half in range(2):
        down_grad[half] = upstream[:, half * half_width : (half + 1) * half_width].astype(BF16)
    hand_over("down_grad", down_grad.at[1 - g], their_down)
    exchanged(0)
    spread(1)
    spread_own_up()
    far_inputs = unpack_values(recv_blocks.at[0])
    far_column = unpack_extra(recv_blocks.at[0])[:, :1]
    far_row = jnp.sum(to_column * far_column, axis=0, keepdims=True)
    near_mask, far_mask = slide_masks(lengths, s, ways, turned_row, far_row)
    masks[0] = near_mask
    masks[1] = far_mask
    turn(0)
    hat, scale = normalize(jnp.concatenate([inputs, far_inputs], axis=0))
    small_in()
    gain_one, gain_two = small_row(0, third), small_row(third, third)
    shift_one, shift_two = small_row(2 * third, third), small_row(3 * third, third)
    shift_down = small_row(4 * third, third)
    bias_up = small_row(5 * third, FF // 2 // LANES)
    normed[...] = (hat * gain_one + shift_one).astype(BF16)
    normed_hat[...] = hat[:rows]
    inverse[...] = scale[:rows]
    hand_over("normed", normed, their_normed)
    spread(2)
    turn(1)
    finish(0)
    finish(1)
    spread(3)
    arrived(0)
    arrived(1)
    for half in range(2):
        for tile, width in tile_groups(0):
            at = half * 3 * half_width + tile * LANES
            projected[:, at : at + width * LANES] = dot(
                normed[...], weight(whole, 0, half, 0, D, tile, width)
            ).astype(BF16)
    attend_set(1, {})
    pack_blocks(send_blocks.at[1], attended[1], lses[1])
    exchange(1)
    turn(2)
    attend_set(0, {HEADS // 2: lambda: finish(2)})
    turn(3)
    exchanged(1)
    far_out = unpack_values(recv_blocks.at[1])
    near_out = attended[0]
    share = jax.nn.sigmoid(lses[0] - unpack_extra(recv_blocks.at[1]))
    shares = to_columns(share)
    difference = near_out - far_out
    mixture[...] = (shares * near_out + (1.0 - shares) * far_out).astype(BF16)
    hand_over("mixture", mixture, their_mixture)
    finish(3)
    arrived(2)
    arrived(3)
    middle = inputs + jnp.concatenate(
        [dot(mixture[...], weight(whole, 1, half, 0, D, 0, third)) for half in range(2)], axis=1
    )
    hat, scale = normalize(middle)
    second_hat[...] = hat
    second_inverse[...] = scale
    second_in[...] = (hat * gain_two + shift_two).astype(BF16)
    hand_over("second_in", second_in, their_second)
    root = (2.0 / 3.141592653589793) ** 0.5
    for half in range(2):
        for tile, width in tile_groups(2):
            at = half * FF // 2 + tile * LANES
            to = slice(at, at + width * LANES)
            v = dot(second_in[...], weight(whole, 2, half, 0, D, tile, width)) + bias_up[:, to]
            square = v * v
            t = jnp.tanh(root * (v + 0.044715 * v * square))
            activated[:, to] = (0.5 * v * (1.0 + t)).astype(BF16)
            slope[:, to] = 0.5 * (1.0 + t) + 0.5 * v * (1.0 - t * t) * (
                root * (1.0 + 3 * 0.044715 * square)
            )
    hand_over("activated", activated, their_activated)

    block = 256
    up_sums = []
    for start in range(0, FF, block):
        to = slice(start, start + block)
        pulled = sum(
            dot_cols(down_grad[half], weight(whole, 3, half, start, block, 0, third))
            for half in range(2)
        )
        grad = (pulled * slope[:, to]).astype(BF16)
        half, at = divmod(start, FF // 2)
        up_grad[half, :, at : at + block] = grad
        up_sums.append(jnp.sum(grad.astype(F32), axis=0, keepdims=True))
    hand_over("up_grad", up_grad.at[1 - g], their_up)
    pairs["down_grad"].wait()
    pairs["activated"].wait()
    for first in range(0, FF, D):
        weight_grad(3, activated, their_activated, down_grad, their_down, first, D)
    reduce_first(3)
    second_grad = jnp.concatenate(
        [
            sum(
                dot_cols(up_grad[half], weight(whole, 2, half, start, block, 0, TILES[2]))
                for half in range(2)
            )
            for start in range(0, D, block)
        ],
        axis=1,
    )
    hat = second_hat[...]
    gain_two_sum = jnp.sum(second_grad * hat, axis=0, keepdims=True)
    shift_two_sum = jnp.sum(second_grad, axis=0, keepdims=True)
    gained = upstream + norm_back(second_grad * gain_two, hat, second_inverse[...])
    middle_grad[...] = gained
    for half in range(2):
        out_grad[half] = gained[:, half * half_width : (half + 1) * half_width].astype(BF16)
    hand_over("out_grad", out_grad.at[1 - g], their_out)
    mix_grad = jnp.concatenate(
        [
            sum(
                dot_cols(out_grad[half], weight(whole, 1, half, start, block, 0, third))
                for half in range(2)
            )
            for start in range(0, D, block)
        ],
        axis=1,
    )
    near_lse_grad = share * (1.0 - share) * to_heads(difference * mix_grad)
    lse_grads[0] = near_lse_grad
    near_grad[...] = (shares * mix_grad).astype(BF16)
    pack_blocks(send_blocks.at[2], (1.0 - shares) * mix_grad, -near_lse_grad)
    exchange(2)
    pairs["second_in"].wait()
    pairs["up_grad"].wait()
    weight_grad(2, second_in, their_second, up_grad, their_up, 0, D)
    reduce_first(2)
    pairs["mixture"].wait()
    pairs["out_grad"].wait()
    weight_grad(1, mixture, their_mixture, out_grad, their_out, 0, D)
    reduce_first(1)
    reduce_second(3)
    result = middle + shift_down + jnp.concatenate(
        [dot(activated[...], weight(whole, 3, half, 0, FF, 0, third)) for half in range(2)], axis=1
    )
    output[...] = in_order(result).astype(BF16)

    attend_set_back(0, near_grad, {HEADS // 2: lambda: reduce_third(3)})
    reduce_second(2)
    exchanged(2)
    far_grad[...] = unpack_values(recv_blocks.at[2]).astype(BF16)
    lse_grads[1] = unpack_extra(recv_blocks.at[2])
    attend_set_back(1, far_grad, {HEADS // 2: lambda: reduce_third(2)})
    hand_over("qkv_grad", qkv_grad.at[1 - g], their_qkv)
    reduce_second(1)
    first_grad = jnp.concatenate(
        [
            sum(
                dot_cols(qkv_grad[half], weight(whole, 0, half, start, block, 0, TILES[0]))
                for half in range(2)
            )
            for start in range(0, D, block)
        ],
        axis=1,
    )
    pack_blocks(send_blocks.at[3], first_grad[rows:], None)
    exchange(3)
    pairs["normed"].wait()
    pairs["qkv_grad"].wait()
    weight_grad(0, normed, their_normed, qkv_grad, their_qkv, 0, D)
    reduce_first(0)
    reduce_third(1)

    exchanged(3)
    first_grad = first_grad[:rows] + unpack_values(recv_blocks.at[3])
    hat = normed_hat[...]
    gain_one_sum = jnp.sum(first_grad * hat, axis=0, keepdims=True)
    shift_one_sum = jnp.sum(first_grad, axis=0, keepdims=True)
    input_grad[...] = in_order(
        middle_grad[...] + norm_back(first_grad * gain_one, hat, inverse[...])
    )
    down_sums = [
        jnp.sum(down_grad[half].astype(F32), axis=0, keepdims=True) for half in range(2)
    ]
    up_sum = jnp.concatenate(up_sums, axis=1)
    for half in range(2):
        to = slice(half * half_width, (half + 1) * half_width)
        listed = (
            gain_one_sum[:, to], gain_two_sum[:, to], shift_one_sum[:, to], shift_two_sum[:, to],
            down_sums[half], up_sum[:, half * FF // 2 : (half + 1) * FF // 2],
        )
        at = 0
        for vector in listed:
            count = vector.shape[1] // LANES
            small_parts[half, at : at + count, :] = vector.reshape(count, LANES)
            at += count
        small_parts[half, at:, :] = jnp.zeros((SMALL_ROWS - at, LANES), F32)
    hand_over("small", small_parts.at[1 - g], their_small)
    pairs["small"].wait()
    small_parts[g] = small_parts[g] + their_small[...]
    pl.when(s != ways - 1)(lambda: small_home().start())
    reduce_second(0)
    reduce_third(0)
    reduce_last()
    settle()
    pl.when(s != ways - 1)(lambda: small_home().wait_send())
    gather_sent()
    small_sent()
    reduce_sent()


def bounds_total():
    return 5 * D // 2 + FF // 2


def run_step(tokens, cotangent, holes, lengths, flat, ways):
    rows = tokens.shape[0]
    flat_rows = flat.shape[0]
    own = MAT_ROWS // ways
    half_own = own // 2
    planes = ways // 4
    vmem = pl.BlockSpec(memory_space=pltpu.VMEM)
    dma = pltpu.SemaphoreType.DMA
    half = D // 2
    shapes = [
        ((2, MAT_ROWS, LANES), BF16),
        ((MAT_ROWS, LANES), BF16),
        ((2, SMALL_ROWS, LANES), BF16),
        ((own + 2 * SMALL_ROWS, LANES), F32),
        ((own + SMALL_ROWS, LANES), F32),
        ((SMALL_ROWS, LANES), F32),
        ((D // LANES, rows, LANES), F32),
        ((4, ways, 16, half + LANES), BF16),
        ((4, ways, 16, half + LANES), BF16),
        ((2, rows, rows), F32),
        ((2 * rows, D), BF16),
        ((rows, D), F32),
        ((rows, 1), F32),
        ((2 * rows, 3 * D), BF16),
        ((2, rows, D), F32),
        ((2, rows, HEADS), F32),
        ((rows, D), BF16),
        ((rows, D), BF16),
        ((rows, FF), BF16),
        ((rows, FF), F32),
        ((rows, D), F32),
        ((rows, 1), F32),
        ((rows, D), F32),
        ((2, 2 * rows, 3 * half), BF16),
        ((2, rows, half), BF16),
        ((2, rows, FF // 2), BF16),
        ((2, rows, half), BF16),
        ((rows, D), BF16),
        ((rows, D), BF16),
        ((2, rows, HEADS), F32),
        ((2 * rows, D), BF16),
        ((rows, D), BF16),
        ((rows, D), BF16),
        ((rows, FF), BF16),
        ((2 * rows, 3 * half), BF16),
        ((rows, half), BF16),
        ((rows, FF // 2), BF16),
        ((rows, half), BF16),
        ((2, SMALL_ROWS, LANES), F32),
        ((SMALL_ROWS, LANES), F32),
        ((planes, 2, 2, half_own, LANES), BF16),
        ((planes, 2, half_own, LANES), BF16),
        ((planes - 1, 2, half_own, LANES), BF16),
        ((own, LANES), F32),
        ((own + 2 * SMALL_ROWS, LANES), F32),
        ((SMALL_ROWS, LANES), F32),
        ((ways, SMALL_ROWS, LANES), F32),
    ]
    return pl.pallas_call(
        partial(step_kernel, ways),
        out_shape=(
            jax.ShapeDtypeStruct((rows, D), BF16),
            jax.ShapeDtypeStruct((rows, D), F32),
            jax.ShapeDtypeStruct((flat_rows, LANES), F32),
        ),
        in_specs=[
            vmem, vmem, vmem, pl.BlockSpec(memory_space=pltpu.SMEM), vmem,
        ],
        out_specs=(vmem,) * 3,
        scratch_shapes=[pltpu.VMEM(*shape) for shape in shapes]
        + [
            dma((2,)),
            dma((2, planes, 5)), dma((2, ways)),
            dma((planes,)), dma((planes,)),
            dma((ways,)), dma((2,)),
            dma((4,)), dma((4,)), dma((9,)), dma((9,)),
            dma((planes, 2, 2)), dma((planes, 2, 2)),
            dma((planes, 2)), dma((planes, 2)),
            dma((planes, 2)), dma((planes - 1, 2)),
            dma((2,)), dma((2,)),
        ],
        compiler_params=pltpu.CompilerParams(
            collective_id=1, has_side_effects=True, vmem_limit_bytes=VMEM_BYTES
        ),
        name="run_step",
    )(tokens, cotangent, holes, lengths, flat)


def rows_kernel(entries, flat, last, sems):
    full, rest = divmod(entries.shape[1], LANES)
    bulk = pltpu.make_async_copy(
        entries.at[:, pl.ds(0, full * LANES)].reshape(full, LANES), flat.at[pl.ds(0, full)], sems.at[0]
    )
    end = pltpu.make_async_copy(entries.at[:, pl.ds(full * LANES, rest)], last, sems.at[1])
    bulk.start()
    end.start()
    bulk.wait()
    end.wait()
    flat[full:, :] = jnp.zeros((flat.shape[0] - full, LANES), F32)
    flat[full : full + 1, :rest] = last[...]


def to_rows(entries):
    size = entries.shape[1]
    return pl.pallas_call(
        rows_kernel,
        out_shape=jax.ShapeDtypeStruct((-(-size // (8 * LANES)) * 8, LANES), F32),
        in_specs=[pl.BlockSpec(memory_space=pl.ANY)],
        out_specs=pl.BlockSpec(memory_space=pltpu.VMEM),
        scratch_shapes=[pltpu.VMEM((1, size % LANES), F32), pltpu.SemaphoreType.DMA((2,))],
        name="to_rows",
    )(entries)


def adam_kernel(
    gradient, master, first_moment, second_moment, new_moment, new_second, new_master,
    kept, last, load_sem, store_sem,
):
    size = master.shape[1]
    full, rest = divmod(size, LANES)
    chunks = 4
    chunk = -(-full // (8 * chunks)) * 8
    spans = [(c * chunk, min(chunk, full - c * chunk)) for c in range(chunks)]
    sources, targets = (first_moment, second_moment, master), (new_moment, new_second, new_master)

    def piece(array, first, count):
        return array.at[:, pl.ds(first * LANES, count * LANES)].reshape(count, LANES)

    def load(which, index):
        first, count = spans[index]
        return pltpu.make_async_copy(
            piece(sources[which], first, count), kept.at[which, pl.ds(first, count)],
            load_sem.at[which, index],
        )

    def store(which, index):
        first, count = spans[index]
        return pltpu.make_async_copy(
            kept.at[which, pl.ds(first, count)], piece(targets[which], first, count),
            store_sem.at[which, index],
        )

    def load_last(which):
        return pltpu.make_async_copy(
            sources[which].at[:, pl.ds(full * LANES, rest)], last.at[which], load_sem.at[which, chunks]
        )

    def store_last(which):
        return pltpu.make_async_copy(
            last.at[which], targets[which].at[:, pl.ds(full * LANES, rest)], store_sem.at[which, chunks]
        )

    for index in range(chunks):
        for which in range(3):
            load(which, index).start()
    for which in range(3):
        load_last(which).start()
    origin = lax.axis_index("seq") * size

    def update(first, count, moment, second, weights):
        at = (
            origin
            + (first + lax.broadcasted_iota(jnp.int32, (count, LANES), 0)) * LANES
            + lax.broadcasted_iota(jnp.int32, (count, LANES), 1)
        )
        return adam_update(weights, moment, second, gradient[pl.ds(first, count), :], at)

    step = 8

    for index, (first, count) in enumerate(spans):
        for which in range(3):
            load(which, index).wait()

        def run(at, carry, first=first):
            where = pl.multiple_of(first + at * step, 8)
            span = pl.ds(where, step)
            found = update(where, step, kept[0, span, :], kept[1, span, :], kept[2, span, :])
            for which in range(3):
                kept[which, span, :] = found[which]
            return carry

        lax.fori_loop(0, -(-count // step), run, 0, unroll=2)
        for which in range(3):
            store(which, index).start()
    for which in range(3):
        load_last(which).wait()
    moment, second, weights = (last[which] for which in range(3))
    at = origin + full * LANES + lax.broadcasted_iota(jnp.int32, (1, rest), 1)
    found = adam_update(weights, moment, second, gradient[full : full + 1, :rest], at)
    for which in range(3):
        last[which] = found[which]
        store_last(which).start()
    for which in range(3):
        for index in range(chunks):
            store(which, index).wait()
        store_last(which).wait()


def run_adam(gradient, master, first_moment, second_moment):
    size = master.shape[1]
    anywhere = pl.BlockSpec(memory_space=pl.ANY)
    return pl.pallas_call(
        adam_kernel,
        out_shape=(jax.ShapeDtypeStruct((1, size), F32),) * 3,
        in_specs=[pl.BlockSpec(memory_space=pltpu.VMEM), anywhere, anywhere, anywhere],
        out_specs=(anywhere,) * 3,
        scratch_shapes=[
            pltpu.VMEM((3,) + gradient.shape, F32),
            pltpu.VMEM((3, 1, size % LANES), F32),
            pltpu.SemaphoreType.DMA((3, 5)),
            pltpu.SemaphoreType.DMA((3, 5)),
        ],
        compiler_params=pltpu.CompilerParams(vmem_limit_bytes=VMEM_BYTES),
        name="run_adam",
    )(gradient, master, first_moment, second_moment)


def on_device(tokens, cotangent, holes, slide_lengths, master, first_moment, second_moment):
    ways = lax.axis_size("seq")
    output, input_grad, gradient = run_step(
        tokens[0], cotangent[0], holes, slide_lengths, to_rows(master), ways
    )
    new_moment, new_second, new_master = run_adam(gradient, master, first_moment, second_moment)
    return (output[None], input_grad[None], new_moment, new_second, new_master)


def even(mesh):
    ways = mesh.shape["seq"]
    return ways % 4 == 0 and MAT_ROWS % (ways * UNIT) == 0 and ways * 8 == LANES


def solution(mesh):
    return jax.shard_map(
        on_device if even(mesh) else plain_on_device,
        mesh=mesh,
        in_specs=(
            P("grp", "seq", None),
            P("grp", "seq", None),
            P("grp", "seq"),
            P("grp", None),
            P("grp", "seq"),
            P("grp", "seq"),
            P("grp", "seq"),
        ),
        out_specs=(
            P("grp", "seq", None),
            P("grp", "seq", None),
            P("grp", "seq"),
            P("grp", "seq"),
            P("grp", "seq"),
        ),
        check_vma=False,
    )
```

```python
from functools import partial

import jax
import jax.numpy as jnp
from jax import lax
from jax.experimental import pallas as pl
from jax.experimental.pallas import tpu as pltpu
from jax.sharding import PartitionSpec as P

D = 768
FF = 3072
HEADS = 16
HEAD = 48
STEP = 10


EPS_NORM = 1e-05
EPS_ADAM = 1e-08
BETA_ONE = 0.9
BETA_TWO = 0.95


def as_sent(array):
    return jax.tree.map(lambda a: a.astype(jnp.bfloat16) if a.dtype == jnp.float32 else a, array)


def bounds():
    qkv_edge = 3 * D * D // 2
    out_edge = qkv_edge + D * D // 2
    up_edge = out_edge + D * FF // 2
    down_edge = up_edge + FF * D // 2
    gain_edge = down_edge + D
    return (qkv_edge, out_edge, up_edge, down_edge, gain_edge)


def per_segment(flat_index, values):
    edge_list = bounds()
    result = jnp.full(flat_index.shape, values[5], jnp.float32)
    for position in range(4, -1, -1):
        result = jnp.where(flat_index < edge_list[position], jnp.float32(values[position]), result)
    return result


def unpack(flat):
    edge_list = bounds()
    total = flat.shape[1]

    def joined(start, stop, shape):
        return jnp.concatenate(
            [flat[0, start:stop].reshape(shape), flat[1, start:stop].reshape(shape)], axis=-1
        )

    w_qkv = joined(0, edge_list[0], (D, 3 * D // 2))
    w_out = joined(edge_list[0], edge_list[1], (D, D // 2))
    w_up = joined(edge_list[1], edge_list[2], (D, FF // 2))
    w_down = joined(edge_list[2], edge_list[3], (FF, D // 2))
    gain_rows = joined(edge_list[3], edge_list[4], (2, D // 2))
    shift_rows = joined(edge_list[4], edge_list[4] + 3 * D // 2, (3, D // 2))
    bias_up = joined(edge_list[4] + 3 * D // 2, total, (FF // 2,))
    return (w_qkv, w_out, w_up, w_down, gain_rows, shift_rows, bias_up)


def normalize(values):
    centered = values - jnp.mean(values, axis=-1, keepdims=True)
    inverse = lax.rsqrt(jnp.mean(centered * centered, axis=-1, keepdims=True) + EPS_NORM)
    return (centered * inverse, inverse)


def norm_back(grad_hat, normed_hat, inverse):
    return inverse * (
        grad_hat
        - jnp.mean(grad_hat, axis=-1, keepdims=True)
        - normed_hat * jnp.mean(grad_hat * normed_hat, axis=-1, keepdims=True)
    )


def contract_rows(left, right):
    return lax.dot_general(
        left, right, (((0,), (0,)), ((), ())), preferred_element_type=jnp.float32
    )


def contract_cols(left, right):
    return lax.dot_general(
        left, right, (((1,), (1,)), ((), ())), preferred_element_type=jnp.float32
    )


def slide_index(positions, slide_ends):
    return jnp.sum((positions[:, None] >= slide_ends[None, :]).astype(jnp.int32), axis=1)


def split_heads(block_rows):
    return block_rows.reshape(block_rows.shape[0], HEADS, HEAD).transpose(1, 0, 2)


def join_heads(stacked):
    return stacked.transpose(1, 0, 2).reshape(stacked.shape[1], HEADS * HEAD)


def allowance(slides, present):
    token_count = slides.shape[0]
    same_slide = (slides[:, None] == slides[None, :]) & (present[None, :] > 0)
    return same_slide | jnp.eye(token_count, dtype=bool)


def attend(packed, slides, present):
    allowed = allowance(slides, present)
    scale = HEAD ** (-0.5)

    def one_head(pieces):
        query_head, key_head, value_head = pieces
        scores = contract_cols(query_head, key_head) * scale
        scores = jnp.where(allowed, scores, -1000000000.0)
        row_max = jnp.max(scores, axis=-1, keepdims=True)
        exponent = jnp.exp(scores - row_max)
        denominator = jnp.sum(exponent, axis=-1, keepdims=True)
        attention = (exponent / denominator).astype(jnp.bfloat16)
        result = jnp.dot(attention, value_head, preferred_element_type=jnp.float32)
        return (result, (row_max + jnp.log(denominator))[:, 0])

    outs, lses = lax.map(
        one_head,
        (
            split_heads(packed[:, :D]),
            split_heads(packed[:, D : 2 * D]),
            split_heads(packed[:, 2 * D :]),
        ),
    )
    return (join_heads(outs), lses.T)


def attend_back(packed, slides, present, lse_rows, out_grad, lse_grad):
    allowed = allowance(slides, present)
    scale = HEAD ** (-0.5)

    def one_head(pieces):
        query_head, key_head, value_head, lse_head, grad_head, extra_lse = pieces
        scores = contract_cols(query_head, key_head) * scale
        scores = jnp.where(allowed, scores, -1000000000.0)
        attention = jnp.exp(scores - lse_head[:, None])
        prob_grad = contract_cols(grad_head, value_head)
        inner_sum = jnp.sum(attention * prob_grad, axis=-1, keepdims=True)
        score_grad = (attention * (prob_grad - inner_sum + extra_lse[:, None])).astype(jnp.bfloat16)
        query_grad = jnp.dot(score_grad, key_head, preferred_element_type=jnp.float32) * scale
        key_grad = contract_rows(score_grad, query_head) * scale
        value_grad = contract_rows(attention.astype(jnp.bfloat16), grad_head)
        return (query_grad, key_grad, value_grad)

    query_grad, key_grad, value_grad = lax.map(
        one_head,
        (
            split_heads(packed[:, :D]),
            split_heads(packed[:, D : 2 * D]),
            split_heads(packed[:, 2 * D :]),
            lse_rows.T,
            split_heads(out_grad),
            lse_grad.T,
        ),
    )
    return jnp.concatenate(
        [join_heads(query_grad), join_heads(key_grad), join_heads(value_grad)], axis=1
    )


def adam_update(weights, moment, second, gradient, flat_index):
    step_rates = per_segment(
        flat_index,
        (
            0.7 * (2.0 / D) ** 0.5,
            0.7 * (24.0 / D) ** 0.5,
            0.7 * (1.0 / D) ** 0.5,
            0.7 * (1.0 / FF) ** 0.5,
            0.15,
            0.2,
        ),
    )
    decays = per_segment(flat_index, (0.1, 0.1, 0.1, 0.1, 0.0, 0.0))
    new_moment = BETA_ONE * moment + (1.0 - BETA_ONE) * gradient
    new_second = BETA_TWO * second + (1.0 - BETA_TWO) * gradient * gradient
    fix_one = 1.0 - BETA_ONE**STEP
    fix_two = 1.0 - BETA_TWO**STEP
    update = new_moment / fix_one / (jnp.sqrt(new_second / fix_two) + EPS_ADAM)
    return (new_moment, new_second, weights - step_rates * (update + decays * weights))


def column_halves(values):
    return values.reshape(values.shape[0], 2, values.shape[1] // 2)


def plain_on_device(tokens, cotangent, holes, slide_lengths, master, first_moment, second_moment):
    own_half = lax.all_gather(master.astype(jnp.bfloat16), "seq", axis=1, tiled=True)
    whole_flat = lax.all_gather(own_half, "grp", axis=0, tiled=True)
    w_qkv, w_out, w_up, w_down, gain_rows, shift_rows, bias_up = unpack(whole_flat)
    gain_rows = gain_rows.astype(jnp.float32)
    shift_rows = shift_rows.astype(jnp.float32)
    bias_up = bias_up.astype(jnp.float32)
    inputs = tokens[0].astype(jnp.float32)
    row_count = inputs.shape[0]
    seq_ways = lax.axis_size("seq")
    seq_place = lax.axis_index("seq")
    row_steps = jnp.arange(row_count, dtype=jnp.int32)
    slide_ends = jnp.cumsum(slide_lengths[0])
    near_slides = slide_index(seq_place * row_count + row_steps, slide_ends)
    far_slides = slide_index(seq_place + seq_ways * row_steps, slide_ends)
    near_present = holes[0]
    strided_shape = (row_count // seq_ways, seq_ways)

    def to_strided(packed):
        moved, moved_mask = (
            lax.all_to_all(
                packed.reshape(strided_shape + (3 * D,)),
                "seq",
                split_axis=1,
                concat_axis=0,
                tiled=True,
            ),
            lax.all_to_all(
                near_present.astype(jnp.bfloat16).reshape(strided_shape + (1,)),
                "seq",
                split_axis=1,
                concat_axis=0,
                tiled=True,
            ),
        )
        return (moved.reshape(row_count, 3 * D), moved_mask.reshape(row_count).astype(jnp.int32))

    normed_one, inverse_one = normalize(inputs)
    normed = (normed_one * gain_rows[0] + shift_rows[0]).astype(jnp.bfloat16)
    projected = jnp.dot(normed, w_qkv, preferred_element_type=jnp.float32).astype(jnp.bfloat16)
    near_out, near_lse = attend(projected, near_slides, near_present)
    far_proj, far_present = to_strided(projected)
    far_local, far_local_lse = attend(far_proj, far_slides, far_present)
    returned = (
        lax.all_to_all(
            far_local.reshape(row_count, 1, D).astype(jnp.bfloat16),
            "seq",
            split_axis=0,
            concat_axis=1,
            tiled=True,
        ).astype(jnp.float32),
        lax.all_to_all(
            far_local_lse.reshape(row_count, 1, HEADS).astype(jnp.bfloat16),
            "seq",
            split_axis=0,
            concat_axis=1,
            tiled=True,
        ).astype(jnp.float32),
    )
    far_out = returned[0].reshape(row_count, D)
    far_lse = returned[1].reshape(row_count, HEADS)
    near_share = jax.nn.sigmoid(near_lse - far_lse)
    near_heads = near_out.reshape(row_count, HEADS, HEAD)
    far_heads = far_out.reshape(row_count, HEADS, HEAD)
    mixture = (
        (near_share[:, :, None] * near_heads + (1.0 - near_share[:, :, None]) * far_heads)
        .reshape(row_count, D)
        .astype(jnp.bfloat16)
    )
    middle = inputs + jnp.dot(mixture, w_out, preferred_element_type=jnp.float32)
    normed_two, inverse_two = normalize(middle)
    second_in = (normed_two * gain_rows[1] + shift_rows[1]).astype(jnp.bfloat16)
    hidden = jnp.dot(second_in, w_up, preferred_element_type=jnp.float32) + bias_up
    activated = jax.nn.gelu(hidden, approximate=True).astype(jnp.bfloat16)
    output = middle + jnp.dot(activated, w_down, preferred_element_type=jnp.float32) + shift_rows[2]
    upstream = cotangent[0].astype(jnp.float32)
    down_grad = upstream.astype(jnp.bfloat16)
    grad_act = contract_cols(down_grad, w_down)
    gelu_pull = jax.vjp(partial(jax.nn.gelu, approximate=True), hidden)[1]
    hidden_grad = gelu_pull(grad_act)[0].astype(jnp.bfloat16)
    second_grad = contract_cols(hidden_grad, w_up)
    grad_gain_two = jnp.sum(second_grad * normed_two, axis=0)
    grad_shift_two = jnp.sum(second_grad, axis=0)
    middle_grad = upstream + norm_back(second_grad * gain_rows[1], normed_two, inverse_two)
    attend_grad = middle_grad.astype(jnp.bfloat16)
    mix_grad = contract_cols(attend_grad, w_out).reshape(row_count, HEADS, HEAD)
    near_lse_grad = (
        near_share * (1.0 - near_share) * jnp.sum((near_heads - far_heads) * mix_grad, axis=-1)
    )
    near_grad = (near_share[:, :, None] * mix_grad).reshape(row_count, D).astype(jnp.bfloat16)
    far_grad = ((1.0 - near_share[:, :, None]) * mix_grad).reshape(row_count, D)
    sent = (
        lax.all_to_all(
            as_sent(far_grad.reshape(strided_shape + (D,))),
            "seq",
            split_axis=1,
            concat_axis=0,
            tiled=True,
        ),
        lax.all_to_all(
            as_sent((-near_lse_grad).reshape(strided_shape + (HEADS,))),
            "seq",
            split_axis=1,
            concat_axis=0,
            tiled=True,
        ),
    )
    far_back = sent[0].reshape(row_count, D).astype(jnp.bfloat16)
    far_lse_grad = sent[1].reshape(row_count, HEADS)
    again_proj, again_present = to_strided(projected)
    again_lse = attend(again_proj, far_slides, again_present)[1]
    far_proj_grad = attend_back(
        again_proj, far_slides, again_present, again_lse, far_back, far_lse_grad
    ).astype(jnp.bfloat16)
    far_home = lax.all_to_all(
        far_proj_grad.reshape(row_count, 1, 3 * D), "seq", split_axis=0, concat_axis=1, tiled=True
    ).reshape(row_count, 3 * D)
    near_proj_grad = attend_back(
        projected, near_slides, near_present, near_lse, near_grad, near_lse_grad
    )
    proj_grad = (near_proj_grad + far_home.astype(jnp.float32)).astype(jnp.bfloat16)
    first_grad = contract_cols(proj_grad, w_qkv)
    grad_gain_one = jnp.sum(first_grad * normed_one, axis=0)
    grad_shift_one = jnp.sum(first_grad, axis=0)
    input_grad = middle_grad + norm_back(first_grad * gain_rows[0], normed_one, inverse_one)
    both_rows = (
        lax.all_gather(normed, "grp", axis=0, tiled=True),
        lax.all_gather(mixture, "grp", axis=0, tiled=True),
        lax.all_gather(second_in, "grp", axis=0, tiled=True),
        lax.all_gather(activated, "grp", axis=0, tiled=True),
    )
    moved = (
        lax.all_to_all(column_halves(proj_grad), "grp", split_axis=1, concat_axis=0, tiled=True),
        lax.all_to_all(column_halves(attend_grad), "grp", split_axis=1, concat_axis=0, tiled=True),
        lax.all_to_all(column_halves(hidden_grad), "grp", split_axis=1, concat_axis=0, tiled=True),
        lax.all_to_all(column_halves(down_grad), "grp", split_axis=1, concat_axis=0, tiled=True),
    )
    proj_mine = moved[0].reshape(2 * row_count, 3 * D // 2)
    attend_mine = moved[1].reshape(2 * row_count, D // 2)
    hidden_mine = moved[2].reshape(2 * row_count, FF // 2)
    down_mine = moved[3].reshape(2 * row_count, D // 2)
    norm_sums = lax.psum(
        jnp.stack([grad_gain_one, grad_gain_two, grad_shift_one, grad_shift_two]), "grp"
    )
    half_width = D // 2
    norm_half = lax.dynamic_slice_in_dim(
        norm_sums, lax.axis_index("grp") * half_width, half_width, 1
    )
    grad_w_qkv = contract_rows(both_rows[0], proj_mine)
    grad_w_out = contract_rows(both_rows[1], attend_mine)
    grad_w_up = contract_rows(both_rows[2], hidden_mine)
    grad_w_down = contract_rows(both_rows[3], down_mine)
    grad_bias_down = jnp.sum(down_mine.astype(jnp.float32), axis=0)
    grad_bias_up = jnp.sum(hidden_mine.astype(jnp.float32), axis=0)
    gradient = jnp.concatenate(
        [
            grad_w_qkv.reshape(-1),
            grad_w_out.reshape(-1),
            grad_w_up.reshape(-1),
            grad_w_down.reshape(-1),
            norm_half[0],
            norm_half[1],
            norm_half[2],
            norm_half[3],
            grad_bias_down,
            grad_bias_up,
        ]
    )
    reduced = lax.psum_scatter(gradient, "seq", scatter_dimension=0, tiled=True)
    shard_size = master.shape[1]
    flat_index = lax.axis_index("seq") * shard_size + jnp.arange(shard_size, dtype=jnp.int32)
    new_moment, new_second, new_master = adam_update(
        master[0], first_moment[0], second_moment[0], reduced, flat_index
    )
    return (
        output[None].astype(jnp.bfloat16),
        input_grad[None],
        new_moment[None],
        new_second[None],
        new_master[None],
    )


LANES = 128
BF16 = jnp.bfloat16
F32 = jnp.float32
MAT_ROWS = (3 * D * D + D * D + D * FF + FF * D) // 2 // LANES
SMALL_ROWS = 32
UNIT = 576
PAIR = 2
TILES = (3 * D // 2 // LANES, D // 2 // LANES, FF // 2 // LANES, D // 2 // LANES)
DEPTHS = (D, D, D, FF)
MESH = pl.DeviceIdType.MESH
VMEM_BYTES = 60 * 2**20
NEG = -1000000000.0
ORDERS = ((1, 2, 3), (0, 2, 3), (3, 0, 1), (2, 0, 1))
PIECES = 2


def matrix_starts():
    starts = [0]
    for tiles, depth in zip(TILES, DEPTHS):
        starts.append(starts[-1] + tiles * depth)
    return starts


def place():
    return lax.axis_index("seq"), lax.axis_index("grp")


def greet_all(ways):
    s, g = place()
    barrier = pltpu.get_barrier_semaphore()

    def greet(step, carry):
        pl.semaphore_signal(
            barrier, inc=1, device_id=(lax.rem(s + step, ways), g), device_id_type=MESH
        )
        return carry

    lax.fori_loop(1, ways, greet, 0)
    pl.semaphore_signal(barrier, inc=1, device_id=(s, 1 - g), device_id_type=MESH)
    return barrier


def remote(src, dst, send_sem, recv_sem, to):
    return pltpu.make_async_remote_copy(
        src_ref=src,
        dst_ref=dst,
        send_sem=send_sem,
        recv_sem=recv_sem,
        device_id=to,
        device_id_type=MESH,
    )


def unit_tiles(unit, body):
    edges = [start // UNIT for start in matrix_starts()]
    kinds = {}
    for index, tiles in enumerate(TILES):
        inside = (unit >= edges[index]) & (unit < edges[index + 1])
        kinds[tiles] = kinds[tiles] | inside if tiles in kinds else inside
    for tiles, inside in kinds.items():
        pl.when(inside)(lambda tiles=tiles: body(tiles))


def dot(left, right):
    return jnp.dot(left, right, preferred_element_type=F32)


def dot_cols(left, right):
    return contract_cols(left, right)


def dot_rows(left, right):
    return contract_rows(left, right)


def tile_view(ref, index):
    rows = 16 * TILES[index]
    start = matrix_starts()[index]
    return ref.reshape(ref.shape[:-2] + (MAT_ROWS // rows, rows, LANES)), start // rows


def tile_groups(index):
    tiles = TILES[index]
    groups, at = [], 0
    while at < tiles:
        width = 3 if tiles - at == 3 else 2
        groups.append((at, width))
        at += width
    return groups


def weight(ref, index, half, row, rows, tile, width):
    view, base = tile_view(ref, index)
    first = base + row // 16
    pieces = [
        view[half, first : first + rows // 16, 16 * t : 16 * t + 16, :].reshape(rows, LANES)
        for t in range(tile, tile + width)
    ]
    return jnp.concatenate(pieces, axis=1)


def heads_of(rows):
    row = lax.broadcasted_iota(jnp.int32, (rows, D), 0) * HEAD
    column = lax.broadcasted_iota(jnp.int32, (rows, D), 1)
    return ((column >= row) & (column < row + HEAD)).astype(F32)


def to_columns(per_head):
    return jnp.dot(
        per_head, heads_of(HEADS), precision=lax.Precision.HIGHEST, preferred_element_type=F32
    )


def to_heads(columns):
    return lax.dot_general(
        columns,
        heads_of(HEADS),
        (((1,), (1,)), ((), ())),
        precision=lax.Precision.HIGHEST,
        preferred_element_type=F32,
    )


def pack_blocks(ref, values, extra):
    blocks = values.shape[0] // 8
    split = values.reshape(blocks, 8, D)
    ref[:, :, : D // 2] = jnp.concatenate(
        [split[:, :, : D // 2], split[:, :, D // 2 :]], axis=1
    ).astype(BF16)
    if extra is not None:
        high = extra.astype(BF16).astype(F32)
        low = extra - high
        pieces = jnp.concatenate(
            [high.reshape(blocks, 8, HEADS), low.reshape(blocks, 8, HEADS)], axis=1
        )
        ref[:, :, D // 2 : D // 2 + HEADS] = pieces.astype(BF16)


def unpack_values(ref):
    blocks = ref.shape[0]
    values = ref[:, :, : D // 2].astype(F32)
    return jnp.concatenate(
        [values[:, :8, :].reshape(blocks * 8, D // 2), values[:, 8:, :].reshape(blocks * 8, D // 2)],
        axis=1,
    )


def unpack_extra(ref):
    blocks = ref.shape[0]
    pieces = ref[:, :, D // 2 :].astype(F32)
    both = pieces[:, :8, :] + pieces[:, 8:, :]
    return both.reshape(blocks * 8, LANES)[:, :HEADS]


def slide_masks(ends_ref, s, ways, near_keys, far_keys):
    rows = near_keys.shape[1]
    ends, end = [], 0
    for index in range(ends_ref.shape[1]):
        end = end + ends_ref[0, index]
        ends.append(end)

    def slides(positions):
        total = jnp.zeros(positions.shape, jnp.int32)
        for end in ends:
            total = total + (positions >= end).astype(jnp.int32)
        return total

    across = rows // ways
    result = []
    for far, keys in ((False, near_keys), (True, far_keys)):
        found = []
        for dim in (0, 1):
            at = lax.broadcasted_iota(jnp.int32, (rows, rows), dim)
            if far:
                position = s + ways * at
            else:
                position = rows * s + ways * lax.rem(at, across) + at // across
            found.append(slides(position))
        query = lax.broadcasted_iota(jnp.int32, (rows, rows), 0)
        key = lax.broadcasted_iota(jnp.int32, (rows, rows), 1)
        allowed = ((found[0] == found[1]) & (keys > 0.5)) | (query == key)
        result.append(allowed.astype(F32))
    return result


def step_kernel(
    ways, tokens, cotangent, holes, lengths, flat,
    output, input_grad, flat_grad,
    whole, grads, small, extended, aligned, tail,
    turning, send_blocks, recv_blocks, masks, normed, normed_hat, inverse, projected, attended, lses,
    mixture, second_in, activated, slope, second_hat, second_inverse, middle_grad,
    qkv_grad, out_grad, up_grad, down_grad, near_grad, far_grad, lse_grads,
    their_normed, their_mixture, their_second, their_activated,
    their_qkv, their_out, their_up, their_down, small_parts, their_small,
    by_x, by_y, by_z, total, laid, follow_rows, small_all,
    tail_sem, slot_send, slot_recv, core_send, core_recv, small_send, small_recv,
    block_send, block_recv, pair_send, pair_recv,
    x_send, x_recv, y_send, y_recv, z_send, z_recv, end_sem, sum_sem,
):
    s, g = place()
    planes = ways // 4
    z, y, x = s // 4, lax.rem(s // 2, 2), lax.rem(s, 2)
    own = MAT_ROWS // ways
    half_own = own // 2
    rows = tokens.shape[0]
    across = rows // ways
    tiles = D // LANES
    half_width = D // 2
    third_rows = half_width // LANES
    entries = (MAT_ROWS * LANES + bounds_total()) // ways - own * LANES
    shift = entries * s
    row_shift, lane_shift = shift // LANES, lax.rem(shift, LANES)

    def chip(plane, row, column):
        return ((plane * 2 + row) * 2 + column, g)

    def part_at(plane, row, column, part):
        first = ((plane * 2 + row) * 2 + column) * own + part * half_own
        return pl.ds(pl.multiple_of(first, 16), half_own)


    last_row, last_lanes = divmod(own * LANES + entries, LANES)

    def take_flat():
        end = SMALL_ROWS + flat.shape[0]
        extended[SMALL_ROWS:end, :] = flat[...]
        extended[end:, :] = jnp.zeros((extended.shape[0] - end, LANES), F32)

    def follow_copy():
        return remote(
            tail, extended.at[pl.ds(0, SMALL_ROWS)], tail_sem.at[0], tail_sem.at[1],
            (lax.rem(s + 1, ways), g),
        )

    def send_tail():
        lanes = lax.broadcasted_iota(jnp.int32, (SMALL_ROWS, LANES), 1)
        gap = LANES - last_lanes
        older = pltpu.roll(flat[last_row - SMALL_ROWS : last_row, :], gap, 1)
        newer = pltpu.roll(flat[last_row - SMALL_ROWS + 1 : last_row + 1, :], gap, 1)
        tail[...] = jnp.where(lanes < gap, older, newer)
        follow_copy().start()

    def align_own():
        follow_copy().wait()
        step_rows = 176
        step_lanes = lax.broadcasted_iota(jnp.int32, (step_rows, LANES), 1)

        def align(step, carry):
            start = step * step_rows
            here = extended[pl.ds(SMALL_ROWS + start - row_shift, step_rows), :]
            before = extended[pl.ds(SMALL_ROWS - 1 + start - row_shift, step_rows), :]
            aligned[pl.ds(pl.multiple_of(start, 8), step_rows), :] = jnp.where(
                step_lanes >= lane_shift,
                pltpu.roll(here, lane_shift, 1),
                pltpu.roll(before, lane_shift, 1),
            )
            return carry

        lax.fori_loop(0, (own + SMALL_ROWS) // step_rows, align, 0)

        def fill(unit, carry):
            first = unit * UNIT

            def tiled(count):
                for group in range(UNIT // (16 * count)):
                    for tile in range(count):
                        block = aligned[pl.ds(first + group * 16 * count + tile, 16, stride=count), :]
                        at = s * own + first + 16 * (group * count + tile)
                        whole[g, pl.ds(pl.multiple_of(at, 16), 16), :] = block.astype(BF16)

            unit_tiles(s * (own // UNIT) + unit, tiled)
            return carry

        lax.fori_loop(0, own // UNIT, fill, 0)

    order = [z]
    for step in range(1, planes):
        plane = jnp.int32(ORDERS[0][step - 1])
        for at in range(1, planes):
            plane = jnp.where(z == at, ORDERS[at][step - 1], plane)
        order.append(plane)

    def slot_copy(plane, row, column, part, kind, to):
        where = whole.at[g, part_at(plane, row, column, part)]
        return remote(
            where,
            where,
            slot_send.at[part, plane, kind],
            slot_recv.at[part, (plane * 2 + row) * 2 + column],
            to,
        )

    def line_up(plane, part):
        return slot_copy(plane, y, x, part, 0, chip(z + 1, y, x))

    def line_down(plane, part):
        return slot_copy(plane, y, x, part, 1, chip(z - 1, y, x))

    def to_x(plane, part):
        return slot_copy(plane, y, x, part, 2, chip(z, y, 1 - x))

    def to_y(plane, part):
        return slot_copy(plane, y, x, part, 3, chip(z, 1 - y, x))

    def turned(plane):
        return (
            slot_copy(plane, 1 - y, x, 0, 4, chip(z, y, 1 - x)),
            slot_copy(plane, y, 1 - x, 1, 4, chip(z, 1 - y, x)),
        )

    def spread_own():
        to_y(z, 0).start()
        to_x(z, 1).start()
        for part in range(2):
            pl.when((z != 1) & (z < planes - 1))(lambda part=part: line_up(z, part).start())
            pl.when(z > 0)(lambda part=part: line_down(z, part).start())
        to_x(z, 0).start()
        to_y(z, 1).start()

    def spread_own_up():
        for part in range(2):
            pl.when((z == 1) & (z < planes - 1))(lambda part=part: line_up(z, part).start())

    def spread(step):
        plane = order[step]
        for part in range(2):
            slot_copy(plane, y, x, part, 0, chip(z, y, x)).wait_recv()
            pl.when((z > plane) & (z < planes - 1))(lambda part=part: line_up(plane, part).start())
            pl.when((z < plane) & (z > 0))(lambda part=part: line_down(plane, part).start())
            if part == 0:
                to_y(plane, 0).start()
        to_x(plane, 1).start()
        to_x(plane, 0).start()
        to_y(plane, 1).start()

    def turn(step):
        for copy in turned(order[step]):
            copy.wait_recv()
            copy.start()

    def across_copy(plane):
        block = whole.at[g, pl.ds(pl.multiple_of(plane * 4 * own, 16), 4 * own)]
        return remote(block, block, core_send.at[plane], core_recv.at[plane], (s, 1 - g))

    def across_recv(plane):
        block = whole.at[1 - g, pl.ds(pl.multiple_of(plane * 4 * own, 16), 4 * own)]
        return remote(block, block, core_send.at[plane], core_recv.at[plane], (s, 1 - g))

    def finish(step):
        plane = order[step]
        slot_copy(plane, y, 1 - x, 0, 0, chip(z, y, x)).wait_recv()
        slot_copy(plane, 1 - y, 1 - x, 0, 0, chip(z, y, x)).wait_recv()
        slot_copy(plane, 1 - y, x, 1, 0, chip(z, y, x)).wait_recv()
        slot_copy(plane, 1 - y, 1 - x, 1, 0, chip(z, y, x)).wait_recv()
        across_copy(plane).start()

    def arrived(step):
        across_recv(order[step]).wait_recv()

    def gather_sent():
        for plane in range(planes):
            for part in range(2):
                pl.when((z >= plane) & (z < planes - 1))(
                    lambda part=part, plane=plane: line_up(plane, part).wait_send()
                )
                pl.when((z <= plane) & (z > 0))(
                    lambda part=part, plane=plane: line_down(plane, part).wait_send()
                )
                to_x(plane, part).wait_send()
                to_y(plane, part).wait_send()
            for copy in turned(plane):
                copy.wait_send()
            across_copy(plane).wait_send()

    def small_to(index):
        return remote(small.at[g], small.at[g], small_send.at[index], small_recv.at[0], (index, g))

    def small_across():
        return remote(
            small.at[g], small.at[g], small_send.at[ways - 1], small_recv.at[1], (s, 1 - g)
        )

    def small_out():
        def tell(index, carry):
            small_to(index).start()
            return carry

        @pl.when(s == ways - 1)
        def _():
            small[g] = aligned[own : own + SMALL_ROWS, :].astype(BF16)
            lax.fori_loop(0, ways - 1, tell, 0)

    def small_in():
        pl.when(s != ways - 1)(lambda: small_to(s).wait_recv())
        small_across().start()
        remote(
            small.at[1 - g], small.at[1 - g], small_send.at[ways - 1], small_recv.at[1], (s, 1 - g)
        ).wait_recv()

    def small_sent():
        def told(index, carry):
            small_to(index).wait_send()
            return carry

        @pl.when(s == ways - 1)
        def _():
            lax.fori_loop(0, ways - 1, told, 0)

        small_across().wait_send()


    piece_rows = half_own // PIECES

    def piece_at(plane, row, column, part, piece):
        first = ((plane * 2 + row) * 2 + column) * own + part * half_own + piece * piece_rows
        return pl.ds(pl.multiple_of(first, 16), piece_rows)

    def first_copy(plane, part, k, piece):
        where = (k, 1 - x) if part == 0 else (1 - y, k)
        return remote(
            grads.at[piece_at(plane, *where, part, piece)], by_x.at[plane, part, k, piece],
            x_send.at[plane, part, k, piece], x_recv.at[plane, part, k, piece],
            chip(z, y, 1 - x) if part == 0 else chip(z, 1 - y, x),
        )

    def second_copy(plane, part, piece):
        where = (1 - y, x) if part == 0 else (y, 1 - x)
        return remote(
            grads.at[piece_at(plane, *where, part, piece)], by_y.at[plane, part, piece],
            y_send.at[plane, part, piece], y_recv.at[plane, part, piece],
            chip(z, 1 - y, x) if part == 0 else chip(z, y, 1 - x),
        )

    def line_copy(plane, part, piece, way):
        return remote(
            grads.at[piece_at(plane, y, x, part, piece)], by_z.at[way, plane, part, piece],
            z_send.at[plane, part, piece], z_recv.at[way, plane, part, piece],
            chip(z + 1 - 2 * way, y, x),
        )

    def add(where, block):
        grads[where, :] = (grads[where, :].astype(F32) + block[...].astype(F32)).astype(BF16)

    def each():
        return [(part, piece) for piece in range(PIECES) for part in range(2)]

    def reduce_first(plane):
        for part, piece in each():
            first_copy(plane, part, (1 - y, 1 - x)[part], piece).start()
        for part, piece in each():
            first_copy(plane, part, (y, x)[part], piece).start()

    def reduce_second(plane):
        for part, piece in each():
            other = (1 - y, 1 - x)[part]
            first_copy(plane, part, other, piece).wait_recv()
            where = (other, x) if part == 0 else (y, other)
            add(piece_at(plane, *where, part, piece), by_x.at[plane, part, other, piece])
            second_copy(plane, part, piece).start()
        for part, piece in each():
            mine = (y, x)[part]
            first_copy(plane, part, mine, piece).wait_recv()
            add(piece_at(plane, y, x, part, piece), by_x.at[plane, part, mine, piece])

    def third(plane, part, piece):
        second_copy(plane, part, piece).wait_recv()
        add(piece_at(plane, y, x, part, piece), by_y.at[plane, part, piece])
        if plane > 0:
            pl.when(z == 0)(lambda: line_copy(plane, part, piece, 0).start())
        if plane < planes - 1:
            pl.when(z == planes - 1)(lambda: line_copy(plane, part, piece, 1).start())

    def relay(plane, part, piece):
        for way in range(2):

            def take(way=way):
                line_copy(plane, part, piece, way).wait_recv()
                add(piece_at(plane, y, x, part, piece), by_z.at[way, plane, part, piece])
                line_copy(plane, part, piece, way).start()

            if way == 0 and plane > 1:
                pl.when((z > 0) & (z < plane))(take)
            if way == 1 and plane < planes - 2:
                pl.when((z > plane) & (z < planes - 1))(take)

    def reduce_third(plane):
        for part, piece in each():
            third(plane, part, piece)

    def reduce_relay(plane):
        for part, piece in each():
            relay(plane, part, piece)

    def reduce_end(plane):
        for part, piece in each():
            third(plane, part, piece)
            relay(plane, part, piece)

    def reduce_sent():
        for plane in range(planes):
            for part, piece in each():
                for k in range(2):
                    first_copy(plane, part, k, piece).wait_send()
                second_copy(plane, part, piece).wait_send()
                pl.when(z != plane)(
                    lambda plane=plane, part=part, piece=piece: line_copy(
                        plane, part, piece, 0
                    ).wait_send()
                )

    def reduce_last():
        for part, piece in each():
            first = part * half_own + piece * piece_rows
            to = slice(first, first + piece_rows)
            total[to, :] = grads[piece_at(z, y, x, part, piece), :].astype(F32)
            for way in range(2):

                def take(way=way, part=part, piece=piece, to=to):
                    line_copy(z, part, piece, way).wait_recv()
                    total[to, :] += by_z[way, z, part, piece].astype(F32)

                pl.when((z > 0) if way == 0 else (z < planes - 1))(take)

    def small_home():
        return remote(
            small_parts.at[g], small_all.at[s], sum_sem.at[0], sum_sem.at[1], (ways - 1, g)
        )

    def settle():
        def lay(unit, carry):
            first = unit * UNIT

            def tiled(count):
                for group in range(UNIT // (16 * count)):
                    for tile in range(count):
                        block = total[
                            pl.ds(pl.multiple_of(first + 16 * (group * count + tile), 16), 16), :
                        ]
                        laid[pl.ds(first + group * 16 * count + tile, 16, stride=count), :] = block

            unit_tiles(s * (own // UNIT) + unit, tiled)
            return carry

        lax.fori_loop(0, own // UNIT, lay, 0)
        follow = remote(
            laid.at[pl.ds(0, SMALL_ROWS)], follow_rows, end_sem.at[0], end_sem.at[1],
            (lax.rem(s + ways - 1, ways), g),
        )
        follow.start()

        @pl.when(s == ways - 1)
        def _():
            remote(
                small_all.at[pl.ds(0, ways - 1)], small_all.at[pl.ds(0, ways - 1)],
                sum_sem.at[0], sum_sem.at[1], (0, g),
            ).wait_recv()
            small_all[ways - 1] = small_parts[g]
            laid[own : own + SMALL_ROWS, :] = jnp.sum(small_all[...], axis=0)

        laid[own + SMALL_ROWS :, :] = jnp.zeros((laid.shape[0] - own - SMALL_ROWS, LANES), F32)
        follow.wait()

        @pl.when(s != ways - 1)
        def _():
            laid[own : own + SMALL_ROWS, :] = follow_rows[...]

        back = lax.rem(LANES - lane_shift, LANES)
        step_rows = 56
        lanes = lax.broadcasted_iota(jnp.int32, (step_rows, LANES), 1)

        def align(step, carry):
            start = step * step_rows
            here = laid[pl.ds(start + row_shift, step_rows), :]
            after = laid[pl.ds(start + row_shift + 1, step_rows), :]
            flat_grad[pl.ds(pl.multiple_of(start, 8), step_rows), :] = jnp.where(
                lanes < LANES - lane_shift, pltpu.roll(here, back, 1), pltpu.roll(after, back, 1)
            )
            return carry

        lax.fori_loop(0, flat_grad.shape[0] // step_rows, align, 0)


    def exchange(index):
        def start(step, carry):
            to = lax.rem(s + step, ways)
            remote(
                send_blocks.at[index, to],
                recv_blocks.at[index, s],
                block_send.at[index],
                block_recv.at[index],
                (to, g),
            ).start()
            return carry

        recv_blocks[index, s] = send_blocks[index, s]
        lax.fori_loop(1, ways, start, 0)

    def exchanged(index):
        remote(
            send_blocks.at[index, pl.ds(0, ways - 1)],
            recv_blocks.at[index, pl.ds(0, ways - 1)],
            block_send.at[index],
            block_recv.at[index],
            (s, 1 - g),
        ).wait()

    pairs = {}

    def hand_over(name, src, dst):
        index = len(pairs)
        pairs[name] = remote(src, dst, pair_send.at[index], pair_recv.at[index], (s, 1 - g))
        pairs[name].start()

    def by_residue(value):
        for tile in range(tiles):
            turning[tile] = value[:, tile * LANES : (tile + 1) * LANES]
        return jnp.concatenate(
            [
                jnp.concatenate(
                    [turning[tile, pl.ds(i, across, stride=ways), :] for i in range(ways)], axis=0
                )
                for tile in range(tiles)
            ],
            axis=1,
        )

    def in_order(value):
        for tile in range(tiles):
            for i in range(ways):
                turning[tile, pl.ds(i, across, stride=ways), :] = value[
                    across * i : across * (i + 1), tile * LANES : (tile + 1) * LANES
                ]
        return jnp.concatenate([turning[tile] for tile in range(tiles)], axis=1)

    def small_row(first, count):
        return jnp.concatenate(
            [small[half, first + r : first + r + 1, :] for half in range(2) for r in range(count)],
            axis=1,
        ).astype(F32)

    temper = HEAD ** (-0.5)

    def scores(which, head):
        at = slice(which * rows, (which + 1) * rows)
        query = projected[at, head * HEAD : (head + 1) * HEAD]
        key = projected[at, D + head * HEAD : D + (head + 1) * HEAD]
        value = projected[at, 2 * D + head * HEAD : 2 * D + (head + 1) * HEAD]
        found = jnp.where(masks[which] > 0.5, dot_cols(query, key) * temper, NEG)
        return query, key, value, found

    def attend_set(which, between):
        results, totals = [], []
        for head in range(HEADS):
            _, _, value, found = scores(which, head)
            top = jnp.max(found, axis=1, keepdims=True)
            weights = jnp.exp(found - top)
            summed = jnp.sum(weights, axis=1, keepdims=True)
            results.append(dot(weights.astype(BF16), value) * (1.0 / summed))
            totals.append(top + jnp.log(summed))
            if head in between:
                between[head]()
        attended[which] = jnp.concatenate(results, axis=1)
        lses[which] = jnp.concatenate(totals, axis=1)

    def attend_set_back(which, out_grads, between):
        lists = ([], [], [])
        for head in range(HEADS):
            query, key, value, found = scores(which, head)
            weights = jnp.exp(found - lses[which, :, head : head + 1])
            pulled = out_grads[:, head * HEAD : (head + 1) * HEAD]
            weight_grad = dot_cols(pulled, value)
            inner = jnp.sum(weights * weight_grad, axis=1, keepdims=True)
            extra = lse_grads[which, :, head : head + 1] - inner
            score_grad = (weights * (weight_grad + extra)).astype(BF16)
            lists[0].append(dot(score_grad, key) * temper)
            lists[1].append(dot_rows(score_grad, query) * temper)
            lists[2].append(dot_rows(weights.astype(BF16), pulled))
            if head in between:
                between[head]()
        at = slice(which * rows, (which + 1) * rows)
        query_grad, key_grad, value_grad = (jnp.concatenate(one, axis=1).astype(BF16) for one in lists)
        qkv_grad[0, at, :D] = query_grad
        qkv_grad[0, at, D:] = key_grad[:, :half_width]
        qkv_grad[1, at, :half_width] = key_grad[:, half_width:]
        qkv_grad[1, at, half_width:] = value_grad

    def weight_grad(index, mine, theirs, grad, their_grad, first, count):
        left = jnp.concatenate(
            [mine[:, first : first + count], theirs[:, first : first + count]], axis=0
        )
        view, base = tile_view(grads, index)
        at = base + first // 16
        for tile, width in tile_groups(index):
            to = slice(tile * LANES, (tile + width) * LANES)
            right = jnp.concatenate([grad[g, :, to], their_grad[:, to]], axis=0)
            found = dot_rows(left, right).astype(BF16)
            for t in range(width):
                view[at : at + count // 16, 16 * (tile + t) : 16 * (tile + t) + 16, :] = found[
                    :, t * LANES : (t + 1) * LANES
                ].reshape(count // 16, 16, LANES)


    barrier = greet_all(ways)
    inputs = by_residue(tokens[...].astype(F32))
    lane = lax.broadcasted_iota(jnp.int32, (rows, rows), 1)
    row = lax.broadcasted_iota(jnp.int32, (rows, rows), 0)
    flags = holes[...].astype(F32)
    to_column = (row == lane).astype(F32)
    own_column = jnp.sum(to_column * flags, axis=1, keepdims=True)
    turned_at = ways * lax.rem(row, across) + row // across
    turned_column = jnp.sum((turned_at == lane).astype(F32) * flags, axis=1, keepdims=True)
    turned_row_at = ways * lax.rem(lane, across) + lane // across
    turned_row = jnp.sum((turned_row_at == row).astype(F32) * own_column, axis=0, keepdims=True)
    pack_blocks(send_blocks.at[0], inputs, jnp.broadcast_to(turned_column, (rows, HEADS)) * 1.0)
    take_flat()
    pl.semaphore_wait(barrier, ways)
    send_tail()
    exchange(0)
    align_own()
    spread_own()
    small_out()

    upstream = by_residue(cotangent[...].astype(F32))
    for half in range(2):
        down_grad[half] = upstream[:, half * half_width : (half + 1) * half_width].astype(BF16)
    hand_over("down_grad", down_grad.at[1 - g], their_down)
    turn(0)
    spread(1)
    spread_own_up()
    exchanged(0)
    far_inputs = unpack_values(recv_blocks.at[0])
    far_column = unpack_extra(recv_blocks.at[0])[:, :1]
    far_row = jnp.sum(to_column * far_column, axis=0, keepdims=True)
    near_mask, far_mask = slide_masks(lengths, s, ways, turned_row, far_row)
    masks[0] = near_mask
    masks[1] = far_mask
    hat, scale = normalize(jnp.concatenate([inputs, far_inputs], axis=0))
    small_in()
    gain_one, gain_two = small_row(0, third_rows), small_row(third_rows, third_rows)
    shift_one, shift_two = small_row(2 * third_rows, third_rows), small_row(3 * third_rows, third_rows)
    shift_down = small_row(4 * third_rows, third_rows)
    bias_up = small_row(5 * third_rows, FF // 2 // LANES)
    normed[...] = (hat * gain_one + shift_one).astype(BF16)
    normed_hat[...] = hat[:rows]
    inverse[...] = scale[:rows]
    hand_over("normed", normed, their_normed)
    finish(0)
    turn(1)
    spread(2)
    finish(1)
    spread(3)
    turn(2)
    finish(2)
    arrived(0)
    arrived(1)
    arrived(2)
    for half in range(2):
        for tile, width in tile_groups(0):
            at = half * 3 * half_width + tile * LANES
            projected[:, at : at + width * LANES] = dot(
                normed[...], weight(whole, 0, half, 0, D, tile, width)
            ).astype(BF16)
    turn(3)
    attend_set(1, {})
    pack_blocks(send_blocks.at[1], attended[1], lses[1])
    exchange(1)
    attend_set(0, {})
    finish(3)
    exchanged(1)
    far_out = unpack_values(recv_blocks.at[1])
    near_out = attended[0]
    share = jax.nn.sigmoid(lses[0] - unpack_extra(recv_blocks.at[1]))
    shares = to_columns(share)
    difference = near_out - far_out
    mixture[...] = (shares * near_out + (1.0 - shares) * far_out).astype(BF16)
    hand_over("mixture", mixture, their_mixture)
    arrived(3)
    middle = inputs + jnp.concatenate(
        [dot(mixture[...], weight(whole, 1, half, 0, D, 0, third_rows)) for half in range(2)], axis=1
    )
    hat, scale = normalize(middle)
    second_hat[...] = hat
    second_inverse[...] = scale
    second_in[...] = (hat * gain_two + shift_two).astype(BF16)
    hand_over("second_in", second_in, their_second)
    root = (2.0 / 3.141592653589793) ** 0.5
    for half in range(2):
        for tile, width in tile_groups(2):
            at = half * FF // 2 + tile * LANES
            to = slice(at, at + width * LANES)
            v = dot(second_in[...], weight(whole, 2, half, 0, D, tile, width)) + bias_up[:, to]
            square = v * v
            t = jnp.tanh(root * (v + 0.044715 * v * square))
            activated[:, to] = (0.5 * v * (1.0 + t)).astype(BF16)
            slope[:, to] = 0.5 * (1.0 + t) + 0.5 * v * (1.0 - t * t) * (
                root * (1.0 + 3 * 0.044715 * square)
            )
    hand_over("activated", activated, their_activated)

    block = 256
    up_sums = []
    for start in range(0, FF, block):
        to = slice(start, start + block)
        pulled = sum(
            dot_cols(down_grad[half], weight(whole, 3, half, start, block, 0, third_rows))
            for half in range(2)
        )
        grad = (pulled * slope[:, to]).astype(BF16)
        half, at = divmod(start, FF // 2)
        up_grad[half, :, at : at + block] = grad
        up_sums.append(jnp.sum(grad.astype(F32), axis=0, keepdims=True))
    hand_over("up_grad", up_grad.at[1 - g], their_up)
    pairs["down_grad"].wait()
    pairs["activated"].wait()
    for first in range(0, FF, D):
        weight_grad(3, activated, their_activated, down_grad, their_down, first, D)
    reduce_first(3)
    second_grad = jnp.concatenate(
        [
            sum(
                dot_cols(up_grad[half], weight(whole, 2, half, start, block, 0, TILES[2]))
                for half in range(2)
            )
            for start in range(0, D, block)
        ],
        axis=1,
    )
    hat = second_hat[...]
    gain_two_sum = jnp.sum(second_grad * hat, axis=0, keepdims=True)
    shift_two_sum = jnp.sum(second_grad, axis=0, keepdims=True)
    gained = upstream + norm_back(second_grad * gain_two, hat, second_inverse[...])
    middle_grad[...] = gained
    for half in range(2):
        out_grad[half] = gained[:, half * half_width : (half + 1) * half_width].astype(BF16)
    hand_over("out_grad", out_grad.at[1 - g], their_out)
    mix_grad = jnp.concatenate(
        [
            sum(
                dot_cols(out_grad[half], weight(whole, 1, half, start, block, 0, third_rows))
                for half in range(2)
            )
            for start in range(0, D, block)
        ],
        axis=1,
    )
    near_lse_grad = share * (1.0 - share) * to_heads(difference * mix_grad)
    lse_grads[0] = near_lse_grad
    near_grad[...] = (shares * mix_grad).astype(BF16)
    pack_blocks(send_blocks.at[2], (1.0 - shares) * mix_grad, -near_lse_grad)
    exchange(2)
    pairs["second_in"].wait()
    pairs["up_grad"].wait()
    weight_grad(2, second_in, their_second, up_grad, their_up, 0, D)
    reduce_first(2)
    pairs["mixture"].wait()
    pairs["out_grad"].wait()
    weight_grad(1, mixture, their_mixture, out_grad, their_out, 0, D)
    result = middle + shift_down + jnp.concatenate(
        [dot(activated[...], weight(whole, 3, half, 0, FF, 0, third_rows)) for half in range(2)], axis=1
    )
    output[...] = in_order(result).astype(BF16)

    attend_set_back(0, near_grad, {})
    reduce_second(3)
    exchanged(2)
    far_grad[...] = unpack_values(recv_blocks.at[2]).astype(BF16)
    lse_grads[1] = unpack_extra(recv_blocks.at[2])
    attend_set_back(1, far_grad, {})
    hand_over("qkv_grad", qkv_grad.at[1 - g], their_qkv)
    reduce_second(2)
    first_grad = jnp.concatenate(
        [
            sum(
                dot_cols(qkv_grad[half], weight(whole, 0, half, start, block, 0, TILES[0]))
                for half in range(2)
            )
            for start in range(0, D, block)
        ],
        axis=1,
    )
    pack_blocks(send_blocks.at[3], first_grad[rows:], None)
    exchange(3)
    pairs["normed"].wait()
    pairs["qkv_grad"].wait()
    weight_grad(0, normed, their_normed, qkv_grad, their_qkv, 0, D)
    reduce_first(0)
    reduce_third(3)
    reduce_first(1)
    reduce_relay(3)
    reduce_third(2)
    exchanged(3)
    first_grad = first_grad[:rows] + unpack_values(recv_blocks.at[3])
    hat = normed_hat[...]
    gain_one_sum = jnp.sum(first_grad * hat, axis=0, keepdims=True)
    shift_one_sum = jnp.sum(first_grad, axis=0, keepdims=True)
    input_grad[...] = in_order(
        middle_grad[...] + norm_back(first_grad * gain_one, hat, inverse[...])
    )
    down_sums = [
        jnp.sum(down_grad[half].astype(F32), axis=0, keepdims=True) for half in range(2)
    ]
    up_sum = jnp.concatenate(up_sums, axis=1)
    for half in range(2):
        to = slice(half * half_width, (half + 1) * half_width)
        listed = (
            gain_one_sum[:, to], gain_two_sum[:, to], shift_one_sum[:, to], shift_two_sum[:, to],
            down_sums[half], up_sum[:, half * FF // 2 : (half + 1) * FF // 2],
        )
        at = 0
        for vector in listed:
            count = vector.shape[1] // LANES
            small_parts[half, at : at + count, :] = vector.reshape(count, LANES)
            at += count
        small_parts[half, at:, :] = jnp.zeros((SMALL_ROWS - at, LANES), F32)
    hand_over("small", small_parts.at[1 - g], their_small)
    pairs["small"].wait()
    small_parts[g] = small_parts[g] + their_small[...]
    pl.when(s != ways - 1)(lambda: small_home().start())
    reduce_second(0)
    reduce_relay(2)
    reduce_second(1)
    reduce_third(0)
    reduce_relay(0)
    reduce_end(1)
    reduce_last()
    settle()
    pl.when(s != ways - 1)(lambda: small_home().wait_send())
    gather_sent()
    small_sent()
    reduce_sent()


def bounds_total():
    return 5 * D // 2 + FF // 2


def run_step(tokens, cotangent, holes, lengths, flat, ways):
    rows = tokens.shape[0]
    flat_rows = flat.shape[0]
    own = MAT_ROWS // ways
    half_own = own // 2
    planes = ways // 4
    vmem = pl.BlockSpec(memory_space=pltpu.VMEM)
    dma = pltpu.SemaphoreType.DMA
    half = D // 2
    shapes = [
        ((2, MAT_ROWS, LANES), BF16),
        ((MAT_ROWS, LANES), BF16),
        ((2, SMALL_ROWS, LANES), BF16),
        ((own + 2 * SMALL_ROWS, LANES), F32),
        ((own + SMALL_ROWS, LANES), F32),
        ((SMALL_ROWS, LANES), F32),
        ((D // LANES, rows, LANES), F32),
        ((4, ways, 16, half + LANES), BF16),
        ((4, ways, 16, half + LANES), BF16),
        ((2, rows, rows), F32),
        ((2 * rows, D), BF16),
        ((rows, D), F32),
        ((rows, 1), F32),
        ((2 * rows, 3 * D), BF16),
        ((2, rows, D), F32),
        ((2, rows, HEADS), F32),
        ((rows, D), BF16),
        ((rows, D), BF16),
        ((rows, FF), BF16),
        ((rows, FF), F32),
        ((rows, D), F32),
        ((rows, 1), F32),
        ((rows, D), F32),
        ((2, 2 * rows, 3 * half), BF16),
        ((2, rows, half), BF16),
        ((2, rows, FF // 2), BF16),
        ((2, rows, half), BF16),
        ((rows, D), BF16),
        ((rows, D), BF16),
        ((2, rows, HEADS), F32),
        ((2 * rows, D), BF16),
        ((rows, D), BF16),
        ((rows, D), BF16),
        ((rows, FF), BF16),
        ((2 * rows, 3 * half), BF16),
        ((rows, half), BF16),
        ((rows, FF // 2), BF16),
        ((rows, half), BF16),
        ((2, SMALL_ROWS, LANES), F32),
        ((SMALL_ROWS, LANES), F32),
        ((planes, 2, 2, PIECES, half_own // PIECES, LANES), BF16),
        ((planes, 2, PIECES, half_own // PIECES, LANES), BF16),
        ((2, planes, 2, PIECES, half_own // PIECES, LANES), BF16),
        ((own, LANES), F32),
        ((own + 2 * SMALL_ROWS, LANES), F32),
        ((SMALL_ROWS, LANES), F32),
        ((ways, SMALL_ROWS, LANES), F32),
    ]
    return pl.pallas_call(
        partial(step_kernel, ways),
        out_shape=(
            jax.ShapeDtypeStruct((rows, D), BF16),
            jax.ShapeDtypeStruct((rows, D), F32),
            jax.ShapeDtypeStruct((flat_rows, LANES), F32),
        ),
        in_specs=[
            vmem, vmem, vmem, pl.BlockSpec(memory_space=pltpu.SMEM), vmem,
        ],
        out_specs=(vmem,) * 3,
        scratch_shapes=[pltpu.VMEM(*shape) for shape in shapes]
        + [
            dma((2,)),
            dma((2, planes, 5)), dma((2, ways)),
            dma((planes,)), dma((planes,)),
            dma((ways,)), dma((2,)),
            dma((4,)), dma((4,)), dma((9,)), dma((9,)),
            dma((planes, 2, 2, PIECES)), dma((planes, 2, 2, PIECES)),
            dma((planes, 2, PIECES)), dma((planes, 2, PIECES)),
            dma((planes, 2, PIECES)), dma((2, planes, 2, PIECES)),
            dma((2,)), dma((2,)),
        ],
        compiler_params=pltpu.CompilerParams(
            collective_id=1, has_side_effects=True, vmem_limit_bytes=VMEM_BYTES
        ),
        name="run_step",
    )(tokens, cotangent, holes, lengths, flat)


def rows_kernel(entries, flat, last, sems):
    full, rest = divmod(entries.shape[1], LANES)
    bulk = pltpu.make_async_copy(
        entries.at[:, pl.ds(0, full * LANES)].reshape(full, LANES), flat.at[pl.ds(0, full)], sems.at[0]
    )
    end = pltpu.make_async_copy(entries.at[:, pl.ds(full * LANES, rest)], last, sems.at[1])
    bulk.start()
    end.start()
    bulk.wait()
    end.wait()
    flat[full:, :] = jnp.zeros((flat.shape[0] - full, LANES), F32)
    flat[full : full + 1, :rest] = last[...]


def to_rows(entries):
    size = entries.shape[1]
    return pl.pallas_call(
        rows_kernel,
        out_shape=jax.ShapeDtypeStruct((-(-size // (8 * LANES)) * 8, LANES), F32),
        in_specs=[pl.BlockSpec(memory_space=pl.ANY)],
        out_specs=pl.BlockSpec(memory_space=pltpu.VMEM),
        scratch_shapes=[pltpu.VMEM((1, size % LANES), F32), pltpu.SemaphoreType.DMA((2,))],
        name="to_rows",
    )(entries)


def adam_kernel(
    gradient, master, first_moment, second_moment, new_moment, new_second, new_master,
    kept, last, load_sem, store_sem,
):
    size = master.shape[1]
    full, rest = divmod(size, LANES)
    chunks = 4
    chunk = -(-full // (8 * chunks)) * 8
    spans = [(c * chunk, min(chunk, full - c * chunk)) for c in range(chunks)]
    sources, targets = (first_moment, second_moment, master), (new_moment, new_second, new_master)

    def piece(array, first, count):
        return array.at[:, pl.ds(first * LANES, count * LANES)].reshape(count, LANES)

    def load(which, index):
        first, count = spans[index]
        return pltpu.make_async_copy(
            piece(sources[which], first, count), kept.at[which, pl.ds(first, count)],
            load_sem.at[which, index],
        )

    def store(which, index):
        first, count = spans[index]
        return pltpu.make_async_copy(
            kept.at[which, pl.ds(first, count)], piece(targets[which], first, count),
            store_sem.at[which, index],
        )

    def load_last(which):
        return pltpu.make_async_copy(
            sources[which].at[:, pl.ds(full * LANES, rest)], last.at[which], load_sem.at[which, chunks]
        )

    def store_last(which):
        return pltpu.make_async_copy(
            last.at[which], targets[which].at[:, pl.ds(full * LANES, rest)], store_sem.at[which, chunks]
        )

    for index in range(chunks):
        for which in range(3):
            load(which, index).start()
    for which in range(3):
        load_last(which).start()
    origin = lax.axis_index("seq") * size

    def update(first, count, moment, second, weights):
        at = (
            origin
            + (first + lax.broadcasted_iota(jnp.int32, (count, LANES), 0)) * LANES
            + lax.broadcasted_iota(jnp.int32, (count, LANES), 1)
        )
        return adam_update(weights, moment, second, gradient[pl.ds(first, count), :], at)

    step = 8

    for index, (first, count) in enumerate(spans):
        for which in range(3):
            load(which, index).wait()

        def run(at, carry, first=first):
            where = pl.multiple_of(first + at * step, 8)
            span = pl.ds(where, step)
            found = update(where, step, kept[0, span, :], kept[1, span, :], kept[2, span, :])
            for which in range(3):
                kept[which, span, :] = found[which]
            return carry

        lax.fori_loop(0, -(-count // step), run, 0, unroll=2)
        for which in range(3):
            store(which, index).start()
    for which in range(3):
        load_last(which).wait()
    moment, second, weights = (last[which] for which in range(3))
    at = origin + full * LANES + lax.broadcasted_iota(jnp.int32, (1, rest), 1)
    found = adam_update(weights, moment, second, gradient[full : full + 1, :rest], at)
    for which in range(3):
        last[which] = found[which]
        store_last(which).start()
    for which in range(3):
        for index in range(chunks):
            store(which, index).wait()
        store_last(which).wait()


def run_adam(gradient, master, first_moment, second_moment):
    size = master.shape[1]
    anywhere = pl.BlockSpec(memory_space=pl.ANY)
    return pl.pallas_call(
        adam_kernel,
        out_shape=(jax.ShapeDtypeStruct((1, size), F32),) * 3,
        in_specs=[pl.BlockSpec(memory_space=pltpu.VMEM), anywhere, anywhere, anywhere],
        out_specs=(anywhere,) * 3,
        scratch_shapes=[
            pltpu.VMEM((3,) + gradient.shape, F32),
            pltpu.VMEM((3, 1, size % LANES), F32),
            pltpu.SemaphoreType.DMA((3, 5)),
            pltpu.SemaphoreType.DMA((3, 5)),
        ],
        compiler_params=pltpu.CompilerParams(vmem_limit_bytes=VMEM_BYTES),
        name="run_adam",
    )(gradient, master, first_moment, second_moment)


def on_device(tokens, cotangent, holes, slide_lengths, master, first_moment, second_moment):
    ways = lax.axis_size("seq")
    output, input_grad, gradient = run_step(
        tokens[0], cotangent[0], holes, slide_lengths, to_rows(master), ways
    )
    new_moment, new_second, new_master = run_adam(gradient, master, first_moment, second_moment)
    return (output[None], input_grad[None], new_moment, new_second, new_master)


def even(mesh):
    ways = mesh.shape["seq"]
    return ways % 4 == 0 and MAT_ROWS % (ways * UNIT) == 0 and ways * 8 == LANES


def solution(mesh):
    return jax.shard_map(
        on_device if even(mesh) else plain_on_device,
        mesh=mesh,
        in_specs=(
            P("grp", "seq", None),
            P("grp", "seq", None),
            P("grp", "seq"),
            P("grp", None),
            P("grp", "seq"),
            P("grp", "seq"),
            P("grp", "seq"),
        ),
        out_specs=(
            P("grp", "seq", None),
            P("grp", "seq", None),
            P("grp", "seq"),
            P("grp", "seq"),
            P("grp", "seq"),
        ),
        check_vma=False,
    )
```

```python
from functools import partial
from types import SimpleNamespace

import jax
import jax.numpy as jnp
from jax import lax
from jax.experimental import pallas as pl
from jax.experimental.pallas import tpu as pltpu
from jax.sharding import PartitionSpec as P

D = 768
FF = 3072
HEADS = 16
HEAD = 48
STEP = 10


EPS_NORM = 1e-05
EPS_ADAM = 1e-08
BETA_ONE = 0.9
BETA_TWO = 0.95


def as_sent(array):
    return jax.tree.map(lambda a: a.astype(jnp.bfloat16) if a.dtype == jnp.float32 else a, array)


def bounds():
    qkv_edge = 3 * D * D // 2
    out_edge = qkv_edge + D * D // 2
    up_edge = out_edge + D * FF // 2
    down_edge = up_edge + FF * D // 2
    gain_edge = down_edge + D
    return (qkv_edge, out_edge, up_edge, down_edge, gain_edge)


def per_segment(flat_index, values):
    edge_list = bounds()
    result = jnp.full(flat_index.shape, values[5], jnp.float32)
    for position in range(4, -1, -1):
        result = jnp.where(flat_index < edge_list[position], jnp.float32(values[position]), result)
    return result


def unpack(flat):
    edge_list = bounds()
    total = flat.shape[1]

    def joined(start, stop, shape):
        return jnp.concatenate(
            [flat[0, start:stop].reshape(shape), flat[1, start:stop].reshape(shape)], axis=-1
        )

    w_qkv = joined(0, edge_list[0], (D, 3 * D // 2))
    w_out = joined(edge_list[0], edge_list[1], (D, D // 2))
    w_up = joined(edge_list[1], edge_list[2], (D, FF // 2))
    w_down = joined(edge_list[2], edge_list[3], (FF, D // 2))
    gain_rows = joined(edge_list[3], edge_list[4], (2, D // 2))
    shift_rows = joined(edge_list[4], edge_list[4] + 3 * D // 2, (3, D // 2))
    bias_up = joined(edge_list[4] + 3 * D // 2, total, (FF // 2,))
    return (w_qkv, w_out, w_up, w_down, gain_rows, shift_rows, bias_up)


def normalize(values):
    centered = values - jnp.mean(values, axis=-1, keepdims=True)
    inverse = lax.rsqrt(jnp.mean(centered * centered, axis=-1, keepdims=True) + EPS_NORM)
    return (centered * inverse, inverse)


def norm_back(grad_hat, normed_hat, inverse):
    return inverse * (
        grad_hat
        - jnp.mean(grad_hat, axis=-1, keepdims=True)
        - normed_hat * jnp.mean(grad_hat * normed_hat, axis=-1, keepdims=True)
    )


def contract_rows(left, right):
    return lax.dot_general(
        left, right, (((0,), (0,)), ((), ())), preferred_element_type=jnp.float32
    )


def contract_cols(left, right):
    return lax.dot_general(
        left, right, (((1,), (1,)), ((), ())), preferred_element_type=jnp.float32
    )


def slide_index(positions, slide_ends):
    return jnp.sum((positions[:, None] >= slide_ends[None, :]).astype(jnp.int32), axis=1)


def split_heads(block_rows):
    return block_rows.reshape(block_rows.shape[0], HEADS, HEAD).transpose(1, 0, 2)


def join_heads(stacked):
    return stacked.transpose(1, 0, 2).reshape(stacked.shape[1], HEADS * HEAD)


def allowance(slides, present):
    token_count = slides.shape[0]
    same_slide = (slides[:, None] == slides[None, :]) & (present[None, :] > 0)
    return same_slide | jnp.eye(token_count, dtype=bool)


def attend(packed, slides, present):
    allowed = allowance(slides, present)
    scale = HEAD ** (-0.5)

    def one_head(pieces):
        query_head, key_head, value_head = pieces
        scores = contract_cols(query_head, key_head) * scale
        scores = jnp.where(allowed, scores, -1000000000.0)
        row_max = jnp.max(scores, axis=-1, keepdims=True)
        exponent = jnp.exp(scores - row_max)
        denominator = jnp.sum(exponent, axis=-1, keepdims=True)
        attention = (exponent / denominator).astype(jnp.bfloat16)
        result = jnp.dot(attention, value_head, preferred_element_type=jnp.float32)
        return (result, (row_max + jnp.log(denominator))[:, 0])

    outs, lses = lax.map(
        one_head,
        (
            split_heads(packed[:, :D]),
            split_heads(packed[:, D : 2 * D]),
            split_heads(packed[:, 2 * D :]),
        ),
    )
    return (join_heads(outs), lses.T)


def attend_back(packed, slides, present, lse_rows, out_grad, lse_grad):
    allowed = allowance(slides, present)
    scale = HEAD ** (-0.5)

    def one_head(pieces):
        query_head, key_head, value_head, lse_head, grad_head, extra_lse = pieces
        scores = contract_cols(query_head, key_head) * scale
        scores = jnp.where(allowed, scores, -1000000000.0)
        attention = jnp.exp(scores - lse_head[:, None])
        prob_grad = contract_cols(grad_head, value_head)
        inner_sum = jnp.sum(attention * prob_grad, axis=-1, keepdims=True)
        score_grad = (attention * (prob_grad - inner_sum + extra_lse[:, None])).astype(jnp.bfloat16)
        query_grad = jnp.dot(score_grad, key_head, preferred_element_type=jnp.float32) * scale
        key_grad = contract_rows(score_grad, query_head) * scale
        value_grad = contract_rows(attention.astype(jnp.bfloat16), grad_head)
        return (query_grad, key_grad, value_grad)

    query_grad, key_grad, value_grad = lax.map(
        one_head,
        (
            split_heads(packed[:, :D]),
            split_heads(packed[:, D : 2 * D]),
            split_heads(packed[:, 2 * D :]),
            lse_rows.T,
            split_heads(out_grad),
            lse_grad.T,
        ),
    )
    return jnp.concatenate(
        [join_heads(query_grad), join_heads(key_grad), join_heads(value_grad)], axis=1
    )


def adam_update(weights, moment, second, gradient, flat_index):
    step_rates = per_segment(
        flat_index,
        (
            0.7 * (2.0 / D) ** 0.5,
            0.7 * (24.0 / D) ** 0.5,
            0.7 * (1.0 / D) ** 0.5,
            0.7 * (1.0 / FF) ** 0.5,
            0.15,
            0.2,
        ),
    )
    decays = per_segment(flat_index, (0.1, 0.1, 0.1, 0.1, 0.0, 0.0))
    new_moment = BETA_ONE * moment + (1.0 - BETA_ONE) * gradient
    new_second = BETA_TWO * second + (1.0 - BETA_TWO) * gradient * gradient
    fix_one = 1.0 - BETA_ONE**STEP
    fix_two = 1.0 - BETA_TWO**STEP
    update = new_moment / fix_one / (jnp.sqrt(new_second / fix_two) + EPS_ADAM)
    return (new_moment, new_second, weights - step_rates * (update + decays * weights))


def column_halves(values):
    return values.reshape(values.shape[0], 2, values.shape[1] // 2)


def plain_on_device(tokens, cotangent, holes, slide_lengths, master, first_moment, second_moment):
    own_half = lax.all_gather(master.astype(jnp.bfloat16), "seq", axis=1, tiled=True)
    whole_flat = lax.all_gather(own_half, "grp", axis=0, tiled=True)
    w_qkv, w_out, w_up, w_down, gain_rows, shift_rows, bias_up = unpack(whole_flat)
    gain_rows = gain_rows.astype(jnp.float32)
    shift_rows = shift_rows.astype(jnp.float32)
    bias_up = bias_up.astype(jnp.float32)
    inputs = tokens[0].astype(jnp.float32)
    row_count = inputs.shape[0]
    seq_ways = lax.axis_size("seq")
    seq_place = lax.axis_index("seq")
    row_steps = jnp.arange(row_count, dtype=jnp.int32)
    slide_ends = jnp.cumsum(slide_lengths[0])
    near_slides = slide_index(seq_place * row_count + row_steps, slide_ends)
    far_slides = slide_index(seq_place + seq_ways * row_steps, slide_ends)
    near_present = holes[0]
    strided_shape = (row_count // seq_ways, seq_ways)

    def to_strided(packed):
        moved, moved_mask = (
            lax.all_to_all(
                packed.reshape(strided_shape + (3 * D,)),
                "seq",
                split_axis=1,
                concat_axis=0,
                tiled=True,
            ),
            lax.all_to_all(
                near_present.astype(jnp.bfloat16).reshape(strided_shape + (1,)),
                "seq",
                split_axis=1,
                concat_axis=0,
                tiled=True,
            ),
        )
        return (moved.reshape(row_count, 3 * D), moved_mask.reshape(row_count).astype(jnp.int32))

    normed_one, inverse_one = normalize(inputs)
    normed = (normed_one * gain_rows[0] + shift_rows[0]).astype(jnp.bfloat16)
    projected = jnp.dot(normed, w_qkv, preferred_element_type=jnp.float32).astype(jnp.bfloat16)
    near_out, near_lse = attend(projected, near_slides, near_present)
    far_proj, far_present = to_strided(projected)
    far_local, far_local_lse = attend(far_proj, far_slides, far_present)
    returned = (
        lax.all_to_all(
            far_local.reshape(row_count, 1, D).astype(jnp.bfloat16),
            "seq",
            split_axis=0,
            concat_axis=1,
            tiled=True,
        ).astype(jnp.float32),
        lax.all_to_all(
            far_local_lse.reshape(row_count, 1, HEADS).astype(jnp.bfloat16),
            "seq",
            split_axis=0,
            concat_axis=1,
            tiled=True,
        ).astype(jnp.float32),
    )
    far_out = returned[0].reshape(row_count, D)
    far_lse = returned[1].reshape(row_count, HEADS)
    near_share = jax.nn.sigmoid(near_lse - far_lse)
    near_heads = near_out.reshape(row_count, HEADS, HEAD)
    far_heads = far_out.reshape(row_count, HEADS, HEAD)
    mixture = (
        (near_share[:, :, None] * near_heads + (1.0 - near_share[:, :, None]) * far_heads)
        .reshape(row_count, D)
        .astype(jnp.bfloat16)
    )
    middle = inputs + jnp.dot(mixture, w_out, preferred_element_type=jnp.float32)
    normed_two, inverse_two = normalize(middle)
    second_in = (normed_two * gain_rows[1] + shift_rows[1]).astype(jnp.bfloat16)
    hidden = jnp.dot(second_in, w_up, preferred_element_type=jnp.float32) + bias_up
    activated = jax.nn.gelu(hidden, approximate=True).astype(jnp.bfloat16)
    output = middle + jnp.dot(activated, w_down, preferred_element_type=jnp.float32) + shift_rows[2]
    upstream = cotangent[0].astype(jnp.float32)
    down_grad = upstream.astype(jnp.bfloat16)
    grad_act = contract_cols(down_grad, w_down)
    gelu_pull = jax.vjp(partial(jax.nn.gelu, approximate=True), hidden)[1]
    hidden_grad = gelu_pull(grad_act)[0].astype(jnp.bfloat16)
    second_grad = contract_cols(hidden_grad, w_up)
    grad_gain_two = jnp.sum(second_grad * normed_two, axis=0)
    grad_shift_two = jnp.sum(second_grad, axis=0)
    middle_grad = upstream + norm_back(second_grad * gain_rows[1], normed_two, inverse_two)
    attend_grad = middle_grad.astype(jnp.bfloat16)
    mix_grad = contract_cols(attend_grad, w_out).reshape(row_count, HEADS, HEAD)
    near_lse_grad = (
        near_share * (1.0 - near_share) * jnp.sum((near_heads - far_heads) * mix_grad, axis=-1)
    )
    near_grad = (near_share[:, :, None] * mix_grad).reshape(row_count, D).astype(jnp.bfloat16)
    far_grad = ((1.0 - near_share[:, :, None]) * mix_grad).reshape(row_count, D)
    sent = (
        lax.all_to_all(
            as_sent(far_grad.reshape(strided_shape + (D,))),
            "seq",
            split_axis=1,
            concat_axis=0,
            tiled=True,
        ),
        lax.all_to_all(
            as_sent((-near_lse_grad).reshape(strided_shape + (HEADS,))),
            "seq",
            split_axis=1,
            concat_axis=0,
            tiled=True,
        ),
    )
    far_back = sent[0].reshape(row_count, D).astype(jnp.bfloat16)
    far_lse_grad = sent[1].reshape(row_count, HEADS)
    again_proj, again_present = to_strided(projected)
    again_lse = attend(again_proj, far_slides, again_present)[1]
    far_proj_grad = attend_back(
        again_proj, far_slides, again_present, again_lse, far_back, far_lse_grad
    ).astype(jnp.bfloat16)
    far_home = lax.all_to_all(
        far_proj_grad.reshape(row_count, 1, 3 * D), "seq", split_axis=0, concat_axis=1, tiled=True
    ).reshape(row_count, 3 * D)
    near_proj_grad = attend_back(
        projected, near_slides, near_present, near_lse, near_grad, near_lse_grad
    )
    proj_grad = (near_proj_grad + far_home.astype(jnp.float32)).astype(jnp.bfloat16)
    first_grad = contract_cols(proj_grad, w_qkv)
    grad_gain_one = jnp.sum(first_grad * normed_one, axis=0)
    grad_shift_one = jnp.sum(first_grad, axis=0)
    input_grad = middle_grad + norm_back(first_grad * gain_rows[0], normed_one, inverse_one)
    both_rows = (
        lax.all_gather(normed, "grp", axis=0, tiled=True),
        lax.all_gather(mixture, "grp", axis=0, tiled=True),
        lax.all_gather(second_in, "grp", axis=0, tiled=True),
        lax.all_gather(activated, "grp", axis=0, tiled=True),
    )
    moved = (
        lax.all_to_all(column_halves(proj_grad), "grp", split_axis=1, concat_axis=0, tiled=True),
        lax.all_to_all(column_halves(attend_grad), "grp", split_axis=1, concat_axis=0, tiled=True),
        lax.all_to_all(column_halves(hidden_grad), "grp", split_axis=1, concat_axis=0, tiled=True),
        lax.all_to_all(column_halves(down_grad), "grp", split_axis=1, concat_axis=0, tiled=True),
    )
    proj_mine = moved[0].reshape(2 * row_count, 3 * D // 2)
    attend_mine = moved[1].reshape(2 * row_count, D // 2)
    hidden_mine = moved[2].reshape(2 * row_count, FF // 2)
    down_mine = moved[3].reshape(2 * row_count, D // 2)
    norm_sums = lax.psum(
        jnp.stack([grad_gain_one, grad_gain_two, grad_shift_one, grad_shift_two]), "grp"
    )
    half_width = D // 2
    norm_half = lax.dynamic_slice_in_dim(
        norm_sums, lax.axis_index("grp") * half_width, half_width, 1
    )
    grad_w_qkv = contract_rows(both_rows[0], proj_mine)
    grad_w_out = contract_rows(both_rows[1], attend_mine)
    grad_w_up = contract_rows(both_rows[2], hidden_mine)
    grad_w_down = contract_rows(both_rows[3], down_mine)
    grad_bias_down = jnp.sum(down_mine.astype(jnp.float32), axis=0)
    grad_bias_up = jnp.sum(hidden_mine.astype(jnp.float32), axis=0)
    gradient = jnp.concatenate(
        [
            grad_w_qkv.reshape(-1),
            grad_w_out.reshape(-1),
            grad_w_up.reshape(-1),
            grad_w_down.reshape(-1),
            norm_half[0],
            norm_half[1],
            norm_half[2],
            norm_half[3],
            grad_bias_down,
            grad_bias_up,
        ]
    )
    reduced = lax.psum_scatter(gradient, "seq", scatter_dimension=0, tiled=True)
    shard_size = master.shape[1]
    flat_index = lax.axis_index("seq") * shard_size + jnp.arange(shard_size, dtype=jnp.int32)
    new_moment, new_second, new_master = adam_update(
        master[0], first_moment[0], second_moment[0], reduced, flat_index
    )
    return (
        output[None].astype(jnp.bfloat16),
        input_grad[None],
        new_moment[None],
        new_second[None],
        new_master[None],
    )


LANES = 128
BF16 = jnp.bfloat16
F32 = jnp.float32
MAT_ROWS = (3 * D * D + D * D + D * FF + FF * D) // 2 // LANES
SMALL_ROWS = 32
UNIT = 576
PAIR = 2
TILES = (3 * D // 2 // LANES, D // 2 // LANES, FF // 2 // LANES, D // 2 // LANES)
DEPTHS = (D, D, D, FF)
MESH = pl.DeviceIdType.MESH
VMEM_BYTES = 60 * 2**20
NEG = -1000000000.0
ORDERS = ((1, 2, 3), (0, 2, 3), (0, 3, 1), (0, 2, 1))
PIECES = 2
LATE_ROWS = 160
LATE_OUT = (64, 128, 192, 192)


def matrix_starts():
    starts = [0]
    for tiles, depth in zip(TILES, DEPTHS):
        starts.append(starts[-1] + tiles * depth)
    return starts


def place():
    return lax.axis_index("seq"), lax.axis_index("grp")


def greet_all(ways):
    s, g = place()
    barrier = pltpu.get_barrier_semaphore()

    def greet(step, carry):
        pl.semaphore_signal(
            barrier, inc=1, device_id=(lax.rem(s + step, ways), g), device_id_type=MESH
        )
        return carry

    lax.fori_loop(1, ways, greet, 0)
    pl.semaphore_signal(barrier, inc=1, device_id=(s, 1 - g), device_id_type=MESH)
    return barrier


def remote(src, dst, send_sem, recv_sem, to):
    return pltpu.make_async_remote_copy(
        src_ref=src,
        dst_ref=dst,
        send_sem=send_sem,
        recv_sem=recv_sem,
        device_id=to,
        device_id_type=MESH,
    )


def unit_tiles(unit, body):
    edges = [start // UNIT for start in matrix_starts()]
    kinds = {}
    for index, tiles in enumerate(TILES):
        inside = (unit >= edges[index]) & (unit < edges[index + 1])
        kinds[tiles] = kinds[tiles] | inside if tiles in kinds else inside
    for tiles, inside in kinds.items():
        pl.when(inside)(lambda tiles=tiles: body(tiles))


def dot(left, right):
    return jnp.dot(left, right, preferred_element_type=F32)


def dot_cols(left, right):
    return contract_cols(left, right)


def dot_rows(left, right):
    return contract_rows(left, right)


def tile_view(ref, index):
    rows = 16 * TILES[index]
    start = matrix_starts()[index]
    return ref.reshape(ref.shape[:-2] + (MAT_ROWS // rows, rows, LANES)), start // rows


def tile_groups(index):
    tiles = TILES[index]
    groups, at = [], 0
    while at < tiles:
        width = 3 if tiles - at == 3 else 2
        groups.append((at, width))
        at += width
    return groups


def weight(ref, index, half, row, rows, tile, width):
    view, base = tile_view(ref, index)
    first = base + row // 16
    pieces = [
        view[half, first : first + rows // 16, 16 * t : 16 * t + 16, :].reshape(rows, LANES)
        for t in range(tile, tile + width)
    ]
    return jnp.concatenate(pieces, axis=1)


def heads_of(rows):
    row = lax.broadcasted_iota(jnp.int32, (rows, D), 0) * HEAD
    column = lax.broadcasted_iota(jnp.int32, (rows, D), 1)
    return ((column >= row) & (column < row + HEAD)).astype(F32)


def to_columns(per_head):
    return jnp.dot(
        per_head, heads_of(HEADS), precision=lax.Precision.HIGHEST, preferred_element_type=F32
    )


def to_heads(columns):
    return lax.dot_general(
        columns,
        heads_of(HEADS),
        (((1,), (1,)), ((), ())),
        precision=lax.Precision.HIGHEST,
        preferred_element_type=F32,
    )


def pack_blocks(ref, values, extra):
    blocks = values.shape[0] // 8
    split = values.reshape(blocks, 8, D)
    ref[:, :, : D // 2] = jnp.concatenate(
        [split[:, :, : D // 2], split[:, :, D // 2 :]], axis=1
    ).astype(BF16)
    if extra is not None:
        high = extra.astype(BF16).astype(F32)
        low = extra - high
        pieces = jnp.concatenate(
            [high.reshape(blocks, 8, HEADS), low.reshape(blocks, 8, HEADS)], axis=1
        )
        ref[:, :, D // 2 : D // 2 + HEADS] = pieces.astype(BF16)


def unpack_values(ref):
    blocks = ref.shape[0]
    values = ref[:, :, : D // 2].astype(F32)
    return jnp.concatenate(
        [values[:, :8, :].reshape(blocks * 8, D // 2), values[:, 8:, :].reshape(blocks * 8, D // 2)],
        axis=1,
    )


def unpack_extra(ref):
    blocks = ref.shape[0]
    pieces = ref[:, :, D // 2 :].astype(F32)
    both = pieces[:, :8, :] + pieces[:, 8:, :]
    return both.reshape(blocks * 8, LANES)[:, :HEADS]


def slide_masks(ends_ref, s, ways, near_keys, far_keys):
    rows = near_keys.shape[1]
    ends, end = [], 0
    for index in range(ends_ref.shape[1]):
        end = end + ends_ref[0, index]
        ends.append(end)

    def slides(positions):
        total = jnp.zeros(positions.shape, jnp.int32)
        for end in ends:
            total = total + (positions >= end).astype(jnp.int32)
        return total

    across = rows // ways
    result = []
    for far, keys in ((False, near_keys), (True, far_keys)):
        found = []
        for dim in (0, 1):
            at = lax.broadcasted_iota(jnp.int32, (rows, rows), dim)
            if far:
                position = s + ways * at
            else:
                position = rows * s + ways * lax.rem(at, across) + at // across
            found.append(slides(position))
        query = lax.broadcasted_iota(jnp.int32, (rows, rows), 0)
        key = lax.broadcasted_iota(jnp.int32, (rows, rows), 1)
        allowed = ((found[0] == found[1]) & (keys > 0.5)) | (query == key)
        result.append(allowed.astype(F32))
    return result


def step_kernel(
    ways, tokens, cotangent, holes, lengths, flat,
    output, input_grad, flat_grad,
    whole, grads, small, extended, aligned, tail,
    turning, send_blocks, recv_blocks, masks, normed, normed_hat, inverse, projected, attended, lses,
    mixture, second_in, activated, slope, second_hat, second_inverse, middle_grad,
    qkv_grad, out_grad, up_grad, down_grad, near_grad, far_grad, lse_grads,
    their_normed, their_mixture, their_second, their_activated,
    their_qkv, their_out, their_up, their_down, small_parts, their_small,
    by_x, by_y, by_z, by_late, total, laid, follow_rows, small_all,
    tail_sem, slot_send, slot_recv, late_send, late_recv, core_send, core_recv, small_send, small_recv,
    block_send, block_recv, pair_send, pair_recv,
    x_send, x_recv, y_send, y_recv, z_send, z_recv, late_out_send, late_out_recv, end_sem, sum_sem,
):
    s, g = place()
    planes = ways // 4
    z, y, x = s // 4, lax.rem(s // 2, 2), lax.rem(s, 2)
    own = MAT_ROWS // ways
    half_own = own // 2
    rows = tokens.shape[0]
    across = rows // ways
    tiles = D // LANES
    half_width = D // 2
    third_rows = half_width // LANES
    entries = (MAT_ROWS * LANES + bounds_total()) // ways - own * LANES
    shift = entries * s
    row_shift, lane_shift = shift // LANES, lax.rem(shift, LANES)

    def chip(plane, row, column):
        return ((plane * 2 + row) * 2 + column, g)

    def part_at(plane, row, column, part):
        first = ((plane * 2 + row) * 2 + column) * own + part * half_own
        return pl.ds(pl.multiple_of(first, 16), half_own)


    last_row, last_lanes = divmod(own * LANES + entries, LANES)
    step_rows = 176

    def follow_copy():
        return remote(
            tail, extended.at[pl.ds(0, SMALL_ROWS)], tail_sem.at[0], tail_sem.at[1],
            (lax.rem(s + 1, ways), g),
        )

    def send_tail():
        lanes = lax.broadcasted_iota(jnp.int32, (SMALL_ROWS, LANES), 1)
        gap = LANES - last_lanes
        older = pltpu.roll(flat[last_row - SMALL_ROWS : last_row, :], gap, 1)
        newer = pltpu.roll(flat[last_row - SMALL_ROWS + 1 : last_row + 1, :], gap, 1)
        tail[...] = jnp.where(lanes < gap, older, newer)
        follow_copy().start()

    def align_own():
        lanes = lax.broadcasted_iota(jnp.int32, (step_rows, LANES), 1)

        def align(source, start, to):
            here = source[pl.ds(start - row_shift, step_rows), :]
            before = source[pl.ds(start - row_shift - 1, step_rows), :]
            aligned[pl.ds(pl.multiple_of(to, 8), step_rows), :] = jnp.where(
                lanes >= lane_shift,
                pltpu.roll(here, lane_shift, 1),
                pltpu.roll(before, lane_shift, 1),
            )

        def align_step(step, carry):
            align(flat, step * step_rows, step * step_rows)
            return carry

        def fill(unit, carry):
            first = unit * UNIT

            def tiled(count):
                for group in range(UNIT // (16 * count)):
                    for tile in range(count):
                        block = aligned[pl.ds(first + group * 16 * count + tile, 16, stride=count), :]
                        at = s * own + first + 16 * (group * count + tile)
                        whole[g, pl.ds(pl.multiple_of(at, 16), 16), :] = block.astype(BF16)

            unit_tiles(s * (own // UNIT) + unit, tiled)
            return carry

        extended[SMALL_ROWS:, :] = flat[: extended.shape[0] - SMALL_ROWS, :]
        lax.fori_loop(1, (own + SMALL_ROWS) // step_rows, align_step, 0)
        lax.fori_loop(1, own // UNIT, fill, 0)
        follow_copy().wait()
        align(extended, SMALL_ROWS, 0)
        fill(0, 0)

    order = [z]
    for step in range(1, planes):
        plane = jnp.int32(ORDERS[0][step - 1])
        for at in range(1, planes):
            plane = jnp.where(z == at, ORDERS[at][step - 1], plane)
        order.append(plane)

    part_rows = half_own - LATE_ROWS
    late = PIECES

    def slot_copy(plane, row, column, part, piece, kind, to):
        if piece == late:
            first, count = 2 * part_rows + part * LATE_ROWS, LATE_ROWS
        else:
            count = part_rows // PIECES
            first = part * part_rows + piece * count
        first = ((plane * 2 + row) * 2 + column) * own + first
        where = whole.at[g, pl.ds(pl.multiple_of(first, 16), count)]
        return remote(
            where,
            where,
            slot_send.at[part, plane, kind, piece],
            slot_recv.at[part, (plane * 2 + row) * 2 + column, piece],
            to,
        )

    def line_up(plane, part, piece):
        return slot_copy(plane, y, x, part, piece, 0, chip(z + 1, y, x))

    def line_down(plane, part, piece):
        return slot_copy(plane, y, x, part, piece, 1, chip(z - 1, y, x))

    def to_x(plane, part, piece):
        return slot_copy(plane, y, x, part, piece, 2, chip(z, y, 1 - x))

    def to_y(plane, part, piece):
        return slot_copy(plane, y, x, part, piece, 3, chip(z, 1 - y, x))

    def early(plane, piece):
        to_y(plane, 0, piece).start()
        to_x(plane, 1, piece).start()

    def direct(plane, piece):
        to_x(plane, 0, piece).start()
        to_y(plane, 1, piece).start()

    def turned(plane, piece):
        return (
            slot_copy(plane, 1 - y, x, 0, piece, 4, chip(z, y, 1 - x)),
            slot_copy(plane, y, 1 - x, 1, piece, 4, chip(z, 1 - y, x)),
        )

    def turn_piece(plane, piece):
        for copy in turned(plane, piece):
            copy.wait_recv()
            copy.start()

    def come(plane, piece):
        slot_copy(plane, y, 1 - x, 0, piece, 0, chip(z, y, x)).wait_recv()
        slot_copy(plane, 1 - y, 1 - x, 0, piece, 0, chip(z, y, x)).wait_recv()
        slot_copy(plane, 1 - y, x, 1, piece, 0, chip(z, y, x)).wait_recv()
        slot_copy(plane, 1 - y, 1 - x, 1, piece, 0, chip(z, y, x)).wait_recv()

    def leave(piece, plane_one):
        for part in range(2):

            def up(part=part):
                line_up(z, part, piece).start()

            def down(part=part):
                line_down(z, part, piece).start()

            if plane_one:
                pl.when((z == 1) & (z < planes - 1))(up)
            else:
                pl.when((z != 1) & (z < planes - 1))(up)
                pl.when(z > 0)(down)

    def enter_plane(plane, piece):
        for part in range(2):
            slot_copy(plane, y, x, part, piece, 0, chip(z, y, x)).wait_recv()

            def up(part=part):
                line_up(plane, part, piece).start()

            def down(part=part):
                line_down(plane, part, piece).start()

            pl.when((z > plane) & (z < planes - 1))(up)
            pl.when((z < plane) & (z > 0))(down)

    def late_copy(plane, part, way):
        view = whole.reshape(2, ways, own, LANES)
        where = view.at[
            g, pl.ds(4 * plane, 4), pl.ds(2 * part_rows + part * LATE_ROWS, LATE_ROWS)
        ]
        return remote(
            where, where, late_send.at[way, plane, part], late_recv.at[plane, part],
            chip(z + 1 - 2 * way, y, x),
        )

    def late_own():
        come(z, late)
        for part in range(2):
            pl.when(z < planes - 1)(lambda part=part: late_copy(z, part, 0).start())
            pl.when(z > 0)(lambda part=part: late_copy(z, part, 1).start())

    def late_on(plane):
        for part in range(2):
            late_copy(plane, part, 0).wait_recv()
            pl.when((z > plane) & (z < planes - 1))(
                lambda part=part: late_copy(plane, part, 0).start()
            )
            pl.when((z < plane) & (z > 0))(lambda part=part: late_copy(plane, part, 1).start())

    def to_core(half, plane, part, piece):
        count = LATE_ROWS if piece == late else part_rows // PIECES
        first = 2 * part_rows + part * count if piece == late else part * part_rows + piece * count
        view = whole.reshape(2, ways, own, LANES)
        where = view.at[half, pl.ds(4 * plane, 4), pl.ds(first, count)]
        return remote(
            where, where, core_send.at[plane, part, piece], core_recv.at[plane, part, piece],
            (s, 1 - g),
        )

    def finish(plane, piece):
        if piece != late:
            come(plane, piece)
        for part in range(2):
            to_core(g, plane, part, piece).start()

    def arrived(plane):
        for part in range(2):
            for piece in range(PIECES + 1):
                to_core(1 - g, plane, part, piece).wait_recv()

    def gather_sent():
        for plane in range(planes):
            for part in range(2):
                for piece in range(PIECES):

                    def up(plane=plane, part=part, piece=piece):
                        line_up(plane, part, piece).wait_send()

                    def down(plane=plane, part=part, piece=piece):
                        line_down(plane, part, piece).wait_send()

                    pl.when((z >= plane) & (z < planes - 1))(up)
                    pl.when((z <= plane) & (z > 0))(down)
                    to_x(plane, part, piece).wait_send()
                    to_y(plane, part, piece).wait_send()
                    turned(plane, piece)[part].wait_send()
                to_own = (to_x(z, part, late), to_y(z, part, late), turned(z, late)[part])
                if plane == 0:
                    for copy in to_own:
                        copy.wait_send()
                pl.when((z >= plane) & (z < planes - 1))(
                    lambda plane=plane, part=part: late_copy(plane, part, 0).wait_send()
                )
                pl.when((z <= plane) & (z > 0))(
                    lambda plane=plane, part=part: late_copy(plane, part, 1).wait_send()
                )
            for part in range(2):
                for piece in range(PIECES + 1):
                    to_core(g, plane, part, piece).wait_send()

    def small_to(index):
        return remote(small.at[g], small.at[g], small_send.at[index], small_recv.at[0], (index, g))

    def small_across():
        return remote(
            small.at[g], small.at[g], small_send.at[ways - 1], small_recv.at[1], (s, 1 - g)
        )

    def small_out():
        def tell(index, carry):
            small_to(index).start()
            return carry

        @pl.when(s == ways - 1)
        def _():
            small[g] = aligned[own : own + SMALL_ROWS, :].astype(BF16)
            lax.fori_loop(0, ways - 1, tell, 0)

    def small_in():
        pl.when(s != ways - 1)(lambda: small_to(s).wait_recv())
        small_across().start()
        remote(
            small.at[1 - g], small.at[1 - g], small_send.at[ways - 1], small_recv.at[1], (s, 1 - g)
        ).wait_recv()

    def small_sent():
        def told(index, carry):
            small_to(index).wait_send()
            return carry

        @pl.when(s == ways - 1)
        def _():
            lax.fori_loop(0, ways - 1, told, 0)

        small_across().wait_send()


    def cut(plane, part, piece):
        if piece == late:
            return 2 * (half_own - LATE_OUT[plane]) + part * LATE_OUT[plane], LATE_OUT[plane]
        count = (half_own - LATE_OUT[plane]) // PIECES
        return part * (half_own - LATE_OUT[plane]) + piece * count, count

    def piece_at(plane, row, column, part, piece):
        first, count = cut(plane, part, piece)
        first = ((plane * 2 + row) * 2 + column) * own + first
        return pl.ds(pl.multiple_of(first, 16), count)

    def held(ref, plane, part, piece):
        return ref.at[pl.ds(0, cut(plane, part, piece)[1])]

    def first_copy(plane, part, k, piece):
        where = (k, 1 - x) if part == 0 else (1 - y, k)
        return remote(
            grads.at[piece_at(plane, *where, part, piece)],
            held(by_x.at[plane, part, k, piece], plane, part, piece),
            x_send.at[plane, part, k, piece], x_recv.at[plane, part, k, piece],
            chip(z, y, 1 - x) if part == 0 else chip(z, 1 - y, x),
        )

    def second_copy(plane, part, piece):
        where = (1 - y, x) if part == 0 else (y, 1 - x)
        return remote(
            grads.at[piece_at(plane, *where, part, piece)],
            held(by_y.at[plane, part, piece], plane, part, piece),
            y_send.at[plane, part, piece], y_recv.at[plane, part, piece],
            chip(z, 1 - y, x) if part == 0 else chip(z, y, 1 - x),
        )

    def line_copy(plane, part, piece, way):
        return remote(
            grads.at[piece_at(plane, y, x, part, piece)],
            held(by_z.at[way, plane, part, piece], plane, part, piece),
            z_send.at[plane, part, piece], z_recv.at[way, plane, part, piece],
            chip(z + 1 - 2 * way, y, x),
        )

    def late_out_copy(plane, part, way):
        first, count = cut(plane, part, late)
        view = grads.reshape(ways, own, LANES)
        return remote(
            view.at[pl.ds(4 * plane, 4), pl.ds(first, count)],
            by_late.at[way, plane, part, :, pl.ds(0, count)],
            late_out_send.at[plane, part], late_out_recv.at[way, plane, part],
            chip(z + 1 - 2 * way, y, x),
        )

    def add(where, block):
        grads[where, :] = (grads[where, :].astype(F32) + block[...].astype(F32)).astype(BF16)

    def at_home(plane, piece, act):
        if piece == late:
            pl.when(z == plane)(act)
        else:
            act()

    def out_ahead(plane, piece):
        def act():
            for part in range(2):
                first_copy(plane, part, (1 - y, 1 - x)[part], piece).start()

        at_home(plane, piece, act)

    def out_keep(plane, piece):
        def act():
            for part in range(2):
                first_copy(plane, part, (y, x)[part], piece).start()

        at_home(plane, piece, act)

    def out_pass(plane, piece):
        def act():
            for part in range(2):
                other = (1 - y, 1 - x)[part]
                first_copy(plane, part, other, piece).wait_recv()
                where = (other, x) if part == 0 else (y, other)
                add(
                    piece_at(plane, *where, part, piece),
                    held(by_x.at[plane, part, other, piece], plane, part, piece),
                )
                second_copy(plane, part, piece).start()

        at_home(plane, piece, act)

    def out_take(plane, piece):
        def act():
            for part in range(2):
                mine = (y, x)[part]
                first_copy(plane, part, mine, piece).wait_recv()
                add(
                    piece_at(plane, y, x, part, piece),
                    held(by_x.at[plane, part, mine, piece], plane, part, piece),
                )

        at_home(plane, piece, act)

    def out_join(plane, piece):
        def act():
            for part in range(2):
                second_copy(plane, part, piece).wait_recv()
                add(
                    piece_at(plane, y, x, part, piece),
                    held(by_y.at[plane, part, piece], plane, part, piece),
                )
                if piece != late and plane > 0:
                    pl.when(z == 0)(lambda part=part: line_copy(plane, part, piece, 0).start())
                if piece != late and plane < planes - 1:
                    pl.when(z == planes - 1)(
                        lambda part=part: line_copy(plane, part, piece, 1).start()
                    )

        at_home(plane, piece, act)

    def between(plane, act):
        if plane > 1:
            pl.when((z > 0) & (z < plane))(lambda: act(0))
        if plane < planes - 2:
            pl.when((z > plane) & (z < planes - 1))(lambda: act(1))

    def out_relay(plane, piece):
        for part in range(2):

            def act(way, part=part):
                line_copy(plane, part, piece, way).wait_recv()
                add(
                    piece_at(plane, y, x, part, piece),
                    held(by_z.at[way, plane, part, piece], plane, part, piece),
                )
                line_copy(plane, part, piece, way).start()

            between(plane, act)

    def late_add(plane, part, way):
        late_out_copy(plane, part, way).wait_recv()
        for k in range(4):
            add(
                piece_at(plane, k // 2, k % 2, part, late),
                by_late.at[way, plane, part, k, pl.ds(0, LATE_OUT[plane])],
            )

    def late_start(plane):
        for part in range(2):
            if plane > 0:
                pl.when(z == 0)(lambda part=part: late_out_copy(plane, part, 0).start())
            if plane < planes - 1:
                pl.when(z == planes - 1)(lambda part=part: late_out_copy(plane, part, 1).start())

    def late_relay(plane):
        for part in range(2):

            def act(way, part=part):
                late_add(plane, part, way)
                late_out_copy(plane, part, way).start()

            between(plane, act)

    def late_home(plane):
        @pl.when(z == plane)
        def _():
            for part in range(2):
                if plane > 0:
                    late_add(plane, part, 0)
                if plane < planes - 1:
                    late_add(plane, part, 1)

    def out_sent():
        for plane in range(planes):
            for piece in range(PIECES + (1 if LATE_OUT[plane] else 0)):

                def act(plane=plane, piece=piece):
                    for part in range(2):
                        for k in range(2):
                            first_copy(plane, part, k, piece).wait_send()
                        second_copy(plane, part, piece).wait_send()

                at_home(plane, piece, act)

            @pl.when(z != plane)
            def _(plane=plane):
                for part in range(2):
                    for piece in range(PIECES):
                        line_copy(plane, part, piece, 0).wait_send()
                    if LATE_OUT[plane]:
                        late_out_copy(plane, part, 0).wait_send()

    def out_last(parts):
        for plane in range(planes):

            @pl.when(z == plane)
            def _(plane=plane):
                for part, piece in parts:
                    first, count = cut(plane, part, piece)
                    if not count:
                        continue
                    found = grads[piece_at(plane, y, x, part, piece), :].astype(F32)
                    for way in range(2):
                        if piece != late and (plane > 0 if way == 0 else plane < planes - 1):
                            line_copy(plane, part, piece, way).wait_recv()
                            found = found + by_z[way, plane, part, piece, :count].astype(F32)
                    total[first : first + count, :] = found

    def small_home():
        return remote(
            small_parts.at[g], small_all.at[s], sum_sem.at[0], sum_sem.at[1], (ways - 1, g)
        )

    def lay_group(first, group, count):
        for tile in range(count):
            block = total[pl.ds(pl.multiple_of(first + 16 * (group * count + tile), 16), 16), :]
            laid[pl.ds(first + group * 16 * count + tile, 16, stride=count), :] = block

    def follow_back():
        return remote(
            laid.at[pl.ds(0, SMALL_ROWS)], follow_rows, end_sem.at[0], end_sem.at[1],
            (lax.rem(s + ways - 1, ways), g),
        )

    def settle_first():
        unit_tiles(s * (own // UNIT), lambda count: lay_group(0, 0, count))
        follow_back().start()

    def settle():
        def lay(unit, carry):
            def tiled(count):
                for group in range(1, UNIT // (16 * count)):
                    lay_group(unit * UNIT, group, count)

            def first_group(count):
                lay_group(unit * UNIT, 0, count)

            unit_tiles(s * (own // UNIT) + unit, tiled)
            pl.when(unit > 0)(lambda: unit_tiles(s * (own // UNIT) + unit, first_group))
            return carry

        lax.fori_loop(0, own // UNIT, lay, 0)

        @pl.when(s == ways - 1)
        def _():
            remote(
                small_all.at[pl.ds(0, ways - 1)], small_all.at[pl.ds(0, ways - 1)],
                sum_sem.at[0], sum_sem.at[1], (0, g),
            ).wait_recv()
            small_all[ways - 1] = small_parts[g]
            laid[own : own + SMALL_ROWS, :] = jnp.sum(small_all[...], axis=0)

        laid[own + SMALL_ROWS :, :] = jnp.zeros((laid.shape[0] - own - SMALL_ROWS, LANES), F32)
        follow_back().wait()

        @pl.when(s != ways - 1)
        def _():
            laid[own : own + SMALL_ROWS, :] = follow_rows[...]

        back = lax.rem(LANES - lane_shift, LANES)
        step_rows = 56
        lanes = lax.broadcasted_iota(jnp.int32, (step_rows, LANES), 1)

        def align(step, carry):
            start = step * step_rows
            here = laid[pl.ds(start + row_shift, step_rows), :]
            after = laid[pl.ds(start + row_shift + 1, step_rows), :]
            flat_grad[pl.ds(pl.multiple_of(start, 8), step_rows), :] = jnp.where(
                lanes < LANES - lane_shift, pltpu.roll(here, back, 1), pltpu.roll(after, back, 1)
            )
            return carry

        lax.fori_loop(0, flat_grad.shape[0] // step_rows, align, 0)


    widths = (half_width + LANES,) * 3 + (half_width,)

    def exchange(index):
        width = widths[index]

        def start(step, carry):
            to = lax.rem(s + step, ways)
            remote(
                send_blocks.at[index, to, :, pl.ds(0, width)],
                recv_blocks.at[index, s, :, pl.ds(0, width)],
                block_send.at[index],
                block_recv.at[index],
                (to, g),
            ).start()
            return carry

        recv_blocks[index, s] = send_blocks[index, s]
        lax.fori_loop(1, ways, start, 0)

    def exchanged(index):
        width = widths[index]
        remote(
            send_blocks.at[index, pl.ds(0, ways - 1), :, pl.ds(0, width)],
            recv_blocks.at[index, pl.ds(0, ways - 1), :, pl.ds(0, width)],
            block_send.at[index],
            block_recv.at[index],
            (s, 1 - g),
        ).wait()

    pairs = []

    def hand_over(src, dst):
        index = len(pairs)
        pairs.append(remote(src, dst, pair_send.at[index], pair_recv.at[index], (s, 1 - g)))
        pairs[index].start()
        return pairs[index]

    def by_residue(value):
        for tile in range(tiles):
            turning[tile] = value[:, tile * LANES : (tile + 1) * LANES]
        return jnp.concatenate(
            [
                jnp.concatenate(
                    [turning[tile, pl.ds(i, across, stride=ways), :] for i in range(ways)], axis=0
                )
                for tile in range(tiles)
            ],
            axis=1,
        )

    def in_order(value):
        for tile in range(tiles):
            for i in range(ways):
                turning[tile, pl.ds(i, across, stride=ways), :] = value[
                    across * i : across * (i + 1), tile * LANES : (tile + 1) * LANES
                ]
        return jnp.concatenate([turning[tile] for tile in range(tiles)], axis=1)

    def small_row(first, count):
        return jnp.concatenate(
            [small[half, first + r : first + r + 1, :] for half in range(2) for r in range(count)],
            axis=1,
        ).astype(F32)

    temper = HEAD ** (-0.5)

    def scores(which, head):
        at = slice(which * rows, (which + 1) * rows)
        query = projected[at, head * HEAD : (head + 1) * HEAD]
        key = projected[at, D + head * HEAD : D + (head + 1) * HEAD]
        value = projected[at, 2 * D + head * HEAD : 2 * D + (head + 1) * HEAD]
        found = jnp.where(masks[which] > 0.5, dot_cols(query, key) * temper, NEG)
        return query, key, value, found

    def attend_set(which):
        results, totals = [], []
        for head in range(HEADS):
            _, _, value, found = scores(which, head)
            top = jnp.max(found, axis=1, keepdims=True)
            weights = jnp.exp(found - top)
            summed = jnp.sum(weights, axis=1, keepdims=True)
            results.append(dot(weights.astype(BF16), value) * (1.0 / summed))
            totals.append(top + jnp.log(summed))
        attended[which] = jnp.concatenate(results, axis=1)
        lses[which] = jnp.concatenate(totals, axis=1)

    def attend_set_back(which, out_grads):
        lists = ([], [], [])
        for head in range(HEADS):
            query, key, value, found = scores(which, head)
            weights = jnp.exp(found - lses[which, :, head : head + 1])
            pulled = out_grads[:, head * HEAD : (head + 1) * HEAD]
            weight_grad = dot_cols(pulled, value)
            inner = jnp.sum(weights * weight_grad, axis=1, keepdims=True)
            extra = lse_grads[which, :, head : head + 1] - inner
            score_grad = (weights * (weight_grad + extra)).astype(BF16)
            lists[0].append(dot(score_grad, key) * temper)
            lists[1].append(dot_rows(score_grad, query) * temper)
            lists[2].append(dot_rows(weights.astype(BF16), pulled))
        at = slice(which * rows, (which + 1) * rows)
        query_grad, key_grad, value_grad = (jnp.concatenate(one, axis=1).astype(BF16) for one in lists)
        qkv_grad[0, at, :D] = query_grad
        qkv_grad[0, at, D:] = key_grad[:, :half_width]
        qkv_grad[1, at, :half_width] = key_grad[:, half_width:]
        qkv_grad[1, at, half_width:] = value_grad

    def weight_grad(index, mine, theirs, grad, their_grad, first, count):
        left = jnp.concatenate(
            [mine[:, first : first + count], theirs[:, first : first + count]], axis=0
        )
        view, base = tile_view(grads, index)
        at = base + first // 16
        for tile, width in tile_groups(index):
            to = slice(tile * LANES, (tile + width) * LANES)
            right = jnp.concatenate([grad[g, :, to], their_grad[:, to]], axis=0)
            found = dot_rows(left, right).astype(BF16)
            for t in range(width):
                view[at : at + count // 16, 16 * (tile + t) : 16 * (tile + t) + 16, :] = found[
                    :, t * LANES : (t + 1) * LANES
                ].reshape(count // 16, 16, LANES)


    kept = SimpleNamespace()
    barrier = greet_all(ways)
    inputs = by_residue(tokens[...].astype(F32))
    lane = lax.broadcasted_iota(jnp.int32, (rows, rows), 1)
    row = lax.broadcasted_iota(jnp.int32, (rows, rows), 0)
    flags = holes[...].astype(F32)
    to_column = (row == lane).astype(F32)
    own_column = jnp.sum(to_column * flags, axis=1, keepdims=True)
    turned_at = ways * lax.rem(row, across) + row // across
    turned_column = jnp.sum((turned_at == lane).astype(F32) * flags, axis=1, keepdims=True)
    turned_row_at = ways * lax.rem(lane, across) + lane // across
    turned_row = jnp.sum((turned_row_at == row).astype(F32) * own_column, axis=0, keepdims=True)
    pack_blocks(send_blocks.at[0], inputs, jnp.broadcast_to(turned_column, (rows, HEADS)) * 1.0)
    pl.semaphore_wait(barrier, ways)
    send_tail()
    exchange(0)
    align_own()
    small_out()
    upstream = by_residue(cotangent[...].astype(F32))
    for half in range(2):
        down_grad[half] = upstream[:, half * half_width : (half + 1) * half_width].astype(BF16)
    kept.down_grad_pair = hand_over(down_grad.at[1 - g], their_down)

    def norm():
        exchanged(0)
        far_inputs = unpack_values(recv_blocks.at[0])
        far_column = unpack_extra(recv_blocks.at[0])[:, :1]
        far_row = jnp.sum(to_column * far_column, axis=0, keepdims=True)
        near_mask, far_mask = slide_masks(lengths, s, ways, turned_row, far_row)
        masks[0] = near_mask
        masks[1] = far_mask
        hat, scale = normalize(jnp.concatenate([inputs, far_inputs], axis=0))
        small_in()
        count = third_rows
        kept.gain_one, kept.gain_two = small_row(0, count), small_row(count, count)
        kept.shift_one, kept.shift_two = small_row(2 * count, count), small_row(3 * count, count)
        kept.shift_down = small_row(4 * count, count)
        kept.bias_up = small_row(5 * count, FF // 2 // LANES)
        normed[...] = (hat * kept.gain_one + kept.shift_one).astype(BF16)
        normed_hat[...] = hat[:rows]
        inverse[...] = scale[:rows]
        kept.normed_pair = hand_over(normed, their_normed)

    def project():
        arrived(0)
        for half in range(2):
            for tile, width in tile_groups(0):
                at = half * 3 * half_width + tile * LANES
                projected[:, at : at + width * LANES] = dot(
                    normed[...], weight(whole, 0, half, 0, D, tile, width)
                ).astype(BF16)

    def attend_far():
        attend_set(1)
        pack_blocks(send_blocks.at[1], attended[1], lses[1])
        exchange(1)

    def mix():
        exchanged(1)
        far_out = unpack_values(recv_blocks.at[1])
        near_out = attended[0]
        kept.share = jax.nn.sigmoid(lses[0] - unpack_extra(recv_blocks.at[1]))
        kept.shares = to_columns(kept.share)
        kept.difference = near_out - far_out
        mixture[...] = (kept.shares * near_out + (1.0 - kept.shares) * far_out).astype(BF16)
        kept.mixture_pair = hand_over(mixture, their_mixture)

    def feed():
        arrived(1)
        arrived(2)
        kept.middle = inputs + jnp.concatenate(
            [dot(mixture[...], weight(whole, 1, half, 0, D, 0, third_rows)) for half in range(2)],
            axis=1,
        )
        hat, scale = normalize(kept.middle)
        second_hat[...] = hat
        second_inverse[...] = scale
        second_in[...] = (hat * kept.gain_two + kept.shift_two).astype(BF16)
        kept.second_in_pair = hand_over(second_in, their_second)
        root = (2.0 / 3.141592653589793) ** 0.5
        for half in range(2):
            for tile, width in tile_groups(2):
                at = half * FF // 2 + tile * LANES
                to = slice(at, at + width * LANES)
                v = dot(second_in[...], weight(whole, 2, half, 0, D, tile, width))
                v = v + kept.bias_up[:, to]
                square = v * v
                t = jnp.tanh(root * (v + 0.044715 * v * square))
                activated[:, to] = (0.5 * v * (1.0 + t)).astype(BF16)
                slope[:, to] = 0.5 * (1.0 + t) + 0.5 * v * (1.0 - t * t) * (
                    root * (1.0 + 3 * 0.044715 * square)
                )
        kept.activated_pair = hand_over(activated, their_activated)

    block = 256

    def feed_back():
        for plane in range(3, planes):
            arrived(plane)
        sums = []
        for start in range(0, FF, block):
            to = slice(start, start + block)
            pulled = sum(
                dot_cols(down_grad[half], weight(whole, 3, half, start, block, 0, third_rows))
                for half in range(2)
            )
            grad = (pulled * slope[:, to]).astype(BF16)
            half, at = divmod(start, FF // 2)
            up_grad[half, :, at : at + block] = grad
            sums.append(jnp.sum(grad.astype(F32), axis=0, keepdims=True))
        kept.up_sum = jnp.concatenate(sums, axis=1)
        kept.up_grad_pair = hand_over(up_grad.at[1 - g], their_up)

    def down_weights():
        kept.down_grad_pair.wait()
        kept.activated_pair.wait()
        for first in range(0, FF, D):
            weight_grad(3, activated, their_activated, down_grad, their_down, first, D)

    def through(left, index, tiles_to):
        return jnp.concatenate(
            [
                sum(
                    dot_cols(left[half], weight(whole, index, half, start, block, 0, tiles_to))
                    for half in range(2)
                )
                for start in range(0, D, block)
            ],
            axis=1,
        )

    def mix_back():
        second_grad = through(up_grad, 2, TILES[2])
        hat = second_hat[...]
        kept.gain_two_sum = jnp.sum(second_grad * hat, axis=0, keepdims=True)
        kept.shift_two_sum = jnp.sum(second_grad, axis=0, keepdims=True)
        gained = upstream + norm_back(second_grad * kept.gain_two, hat, second_inverse[...])
        middle_grad[...] = gained
        for half in range(2):
            out_grad[half] = gained[:, half * half_width : (half + 1) * half_width].astype(BF16)
        kept.out_grad_pair = hand_over(out_grad.at[1 - g], their_out)
        mix_grad = through(out_grad, 1, third_rows)
        share, shares = kept.share, kept.shares
        near_lse_grad = share * (1.0 - share) * to_heads(kept.difference * mix_grad)
        lse_grads[0] = near_lse_grad
        near_grad[...] = (shares * mix_grad).astype(BF16)
        pack_blocks(send_blocks.at[2], (1.0 - shares) * mix_grad, -near_lse_grad)
        exchange(2)

    def up_weights():
        kept.second_in_pair.wait()
        kept.up_grad_pair.wait()
        weight_grad(2, second_in, their_second, up_grad, their_up, 0, D)

    def out_weights():
        kept.mixture_pair.wait()
        kept.out_grad_pair.wait()
        weight_grad(1, mixture, their_mixture, out_grad, their_out, 0, D)

    def put_output():
        result = kept.middle + kept.shift_down + jnp.concatenate(
            [
                dot(activated[...], weight(whole, 3, half, 0, FF, 0, third_rows))
                for half in range(2)
            ],
            axis=1,
        )
        output[...] = in_order(result).astype(BF16)

    def far_back():
        exchanged(2)
        far_grad[...] = unpack_values(recv_blocks.at[2]).astype(BF16)
        lse_grads[1] = unpack_extra(recv_blocks.at[2])
        attend_set_back(1, far_grad)
        kept.qkv_grad_pair = hand_over(qkv_grad.at[1 - g], their_qkv)

    def project_back():
        kept.first_grad = through(qkv_grad, 0, TILES[0])
        pack_blocks(send_blocks.at[3], kept.first_grad[rows:], None)
        exchange(3)

    def qkv_weights():
        kept.normed_pair.wait()
        kept.qkv_grad_pair.wait()
        weight_grad(0, normed, their_normed, qkv_grad, their_qkv, 0, D)

    def put_input_grad():
        exchanged(3)
        first_grad = kept.first_grad[:rows] + unpack_values(recv_blocks.at[3])
        hat = normed_hat[...]
        kept.gain_one_sum = jnp.sum(first_grad * hat, axis=0, keepdims=True)
        kept.shift_one_sum = jnp.sum(first_grad, axis=0, keepdims=True)
        input_grad[...] = in_order(
            middle_grad[...] + norm_back(first_grad * kept.gain_one, hat, inverse[...])
        )

    def small_sums():
        for half in range(2):
            to = slice(half * half_width, (half + 1) * half_width)
            down_sum = jnp.sum(down_grad[half].astype(F32), axis=0, keepdims=True)
            sums = (kept.gain_one_sum, kept.gain_two_sum, kept.shift_one_sum, kept.shift_two_sum)
            listed = [one[:, to] for one in sums] + [down_sum]
            listed.append(kept.up_sum[:, half * FF // 2 : (half + 1) * FF // 2])
            at = 0
            for vector in listed:
                count = vector.shape[1] // LANES
                small_parts[half, at : at + count, :] = vector.reshape(count, LANES)
                at += count
            small_parts[half, at:, :] = jnp.zeros((SMALL_ROWS - at, LANES), F32)
        kept.small_pair = hand_over(small_parts.at[1 - g], their_small)
        kept.small_pair.wait()
        small_parts[g] = small_parts[g] + their_small[...]
        pl.when(s != ways - 1)(lambda: small_home().start())

    early(order[0], late)
    direct(order[0], late)
    early(order[0], 1)
    early(order[0], 0)
    leave(1, False)
    leave(0, False)
    leave(1, True)
    turn_piece(order[0], late)
    direct(order[0], 0)
    direct(order[0], 1)
    turn_piece(order[0], 1)
    enter_plane(order[1], 1)
    turn_piece(order[0], 0)
    early(order[1], 1)
    enter_plane(order[2], 1)
    enter_plane(order[1], 0)
    early(order[1], 0)
    finish(order[0], 1)
    late_own()
    turn_piece(order[1], 1)
    direct(order[1], 1)
    direct(order[1], 0)
    norm()
    enter_plane(order[2], 0)
    turn_piece(order[1], 0)
    finish(order[0], late)
    early(order[2], 0)
    direct(order[2], 1)
    enter_plane(order[3], 1)
    early(order[2], 1)
    early(order[3], 1)
    direct(order[3], 1)
    late_on(order[1])
    finish(order[1], 1)
    finish(order[1], late)
    finish(order[1], 0)
    leave(0, True)
    late_on(order[2])
    turn_piece(order[3], 1)
    turn_piece(order[2], 1)
    finish(order[0], 0)
    enter_plane(order[3], 0)
    early(order[3], 0)
    project()
    turn_piece(order[2], 0)
    direct(order[2], 0)
    attend_far()
    finish(order[2], late)
    finish(order[3], 1)
    finish(order[2], 1)
    direct(order[3], 0)
    attend_set(0)
    turn_piece(order[3], 0)
    late_on(order[3])
    finish(order[3], late)
    finish(order[2], 0)
    mix()
    finish(order[3], 0)
    feed()
    down_weights()
    late_start(3)
    out_ahead(3, 0)
    feed_back()
    out_ahead(3, 1)
    out_keep(3, 1)
    up_weights()
    out_ahead(2, 0)
    mix_back()
    out_ahead(2, 1)
    out_weights()
    out_ahead(1, 0)
    out_pass(3, 1)
    out_keep(3, 0)
    attend_set_back(0, near_grad)
    out_keep(2, 0)
    late_start(2)
    out_pass(3, 0)
    late_relay(3)
    late_start(1)
    out_pass(2, 0)
    out_pass(2, 1)
    out_keep(2, 1)
    far_back()
    late_relay(2)
    qkv_weights()
    late_relay(1)
    out_ahead(0, 0)
    out_keep(0, 0)
    out_take(3, 0)
    out_take(3, 1)
    out_ahead(0, 1)
    out_join(3, 1)
    project_back()
    out_join(3, 0)
    put_output()
    late_home(2)
    late_start(0)
    out_pass(0, 0)
    out_relay(3, 1)
    out_take(2, 0)
    out_keep(0, 1)
    out_take(2, 1)
    out_join(2, 0)
    out_take(0, 0)
    out_pass(0, 1)
    out_relay(3, 0)
    out_join(2, 1)
    out_ahead(1, 1)
    late_home(1)
    late_home(3)
    out_keep(1, 0)
    out_pass(1, 0)
    out_join(0, 0)
    out_keep(1, 1)
    late_relay(0)
    out_ahead(1, late)
    out_take(0, 1)
    out_relay(2, 1)
    out_relay(2, 0)
    out_relay(0, 0)
    late_home(0)
    out_keep(0, late)
    out_keep(1, late)
    out_join(0, 1)
    out_ahead(2, late)
    put_input_grad()
    out_ahead(0, late)
    out_relay(0, 1)
    out_take(1, late)
    out_take(1, 0)
    out_pass(1, late)
    out_keep(2, late)
    out_pass(1, 1)
    out_join(1, 0)
    small_sums()
    out_take(1, 1)
    out_pass(0, late)
    out_ahead(3, late)
    out_relay(1, 0)
    out_pass(2, late)
    out_take(2, late)
    out_keep(3, late)
    out_take(0, late)
    out_join(1, 1)
    out_pass(3, late)
    out_take(3, late)
    out_join(3, late)
    out_join(1, late)
    out_join(0, late)
    out_relay(1, 1)
    out_join(2, late)
    everything = [(part, piece) for piece in range(PIECES + 1) for part in range(2)]
    out_last(everything[:1])
    settle_first()
    out_last(everything[1:])
    settle()
    pl.when(s != ways - 1)(lambda: small_home().wait_send())
    gather_sent()
    small_sent()
    out_sent()


def bounds_total():
    return 5 * D // 2 + FF // 2


def run_step(tokens, cotangent, holes, lengths, flat, ways):
    rows = tokens.shape[0]
    own = MAT_ROWS // ways
    entries = (MAT_ROWS * LANES + bounds_total()) // ways
    half_own = own // 2
    planes = ways // 4
    vmem = pl.BlockSpec(memory_space=pltpu.VMEM)
    dma = pltpu.SemaphoreType.DMA
    half = D // 2
    shapes = [
        ((2, MAT_ROWS, LANES), BF16),
        ((MAT_ROWS, LANES), BF16),
        ((2, SMALL_ROWS, LANES), BF16),
        ((SMALL_ROWS + 184, LANES), F32),
        ((own + SMALL_ROWS, LANES), F32),
        ((SMALL_ROWS, LANES), F32),
        ((D // LANES, rows, LANES), F32),
        ((4, ways, 16, half + LANES), BF16),
        ((4, ways, 16, half + LANES), BF16),
        ((2, rows, rows), F32),
        ((2 * rows, D), BF16),
        ((rows, D), F32),
        ((rows, 1), F32),
        ((2 * rows, 3 * D), BF16),
        ((2, rows, D), F32),
        ((2, rows, HEADS), F32),
        ((rows, D), BF16),
        ((rows, D), BF16),
        ((rows, FF), BF16),
        ((rows, FF), F32),
        ((rows, D), F32),
        ((rows, 1), F32),
        ((rows, D), F32),
        ((2, 2 * rows, 3 * half), BF16),
        ((2, rows, half), BF16),
        ((2, rows, FF // 2), BF16),
        ((2, rows, half), BF16),
        ((rows, D), BF16),
        ((rows, D), BF16),
        ((2, rows, HEADS), F32),
        ((2 * rows, D), BF16),
        ((rows, D), BF16),
        ((rows, D), BF16),
        ((rows, FF), BF16),
        ((2 * rows, 3 * half), BF16),
        ((rows, half), BF16),
        ((rows, FF // 2), BF16),
        ((rows, half), BF16),
        ((2, SMALL_ROWS, LANES), F32),
        ((SMALL_ROWS, LANES), F32),
        ((planes, 2, 2, PIECES + 1, half_own // PIECES, LANES), BF16),
        ((planes, 2, PIECES + 1, half_own // PIECES, LANES), BF16),
        ((2, planes, 2, PIECES, half_own // PIECES, LANES), BF16),
        ((2, planes, 2, 4, max(LATE_OUT), LANES), BF16),
        ((own, LANES), F32),
        ((own + 2 * SMALL_ROWS, LANES), F32),
        ((SMALL_ROWS, LANES), F32),
        ((ways, SMALL_ROWS, LANES), F32),
    ]
    return pl.pallas_call(
        partial(step_kernel, ways),
        out_shape=(
            jax.ShapeDtypeStruct((rows, D), BF16),
            jax.ShapeDtypeStruct((rows, D), F32),
            jax.ShapeDtypeStruct((-(-entries // (8 * LANES)) * 8, LANES), F32),
        ),
        in_specs=[
            vmem, vmem, vmem, pl.BlockSpec(memory_space=pltpu.SMEM), vmem,
        ],
        out_specs=(vmem,) * 3,
        scratch_shapes=[pltpu.VMEM(*shape) for shape in shapes]
        + [
            dma((2,)),
            dma((2, planes, 5, PIECES + 1)), dma((2, ways, PIECES + 1)),
            dma((2, planes, 2)), dma((planes, 2)),
            dma((planes, 2, PIECES + 1)), dma((planes, 2, PIECES + 1)),
            dma((ways,)), dma((2,)),
            dma((4,)), dma((4,)), dma((9,)), dma((9,)),
            dma((planes, 2, 2, PIECES + 1)), dma((planes, 2, 2, PIECES + 1)),
            dma((planes, 2, PIECES + 1)), dma((planes, 2, PIECES + 1)),
            dma((planes, 2, PIECES)), dma((2, planes, 2, PIECES)),
            dma((planes, 2)), dma((2, planes, 2)),
            dma((2,)), dma((2,)),
        ],
        compiler_params=pltpu.CompilerParams(
            collective_id=1, has_side_effects=True, vmem_limit_bytes=VMEM_BYTES
        ),
        name="run_step",
    )(tokens, cotangent, holes, lengths, flat)


def rows_kernel(entries, flat, last, sems):
    full, rest = divmod(entries.shape[1], LANES)
    bulk = pltpu.make_async_copy(
        entries.at[:, pl.ds(0, full * LANES)].reshape(full, LANES), flat.at[pl.ds(0, full)], sems.at[0]
    )
    end = pltpu.make_async_copy(entries.at[:, pl.ds(full * LANES, rest)], last, sems.at[1])
    bulk.start()
    end.start()
    bulk.wait()
    end.wait()
    flat[full:, :] = jnp.zeros((flat.shape[0] - full, LANES), F32)
    flat[full : full + 1, :rest] = last[...]


def to_rows(entries, rows):
    size = entries.shape[1]
    return pl.pallas_call(
        rows_kernel,
        out_shape=jax.ShapeDtypeStruct((rows, LANES), F32),
        in_specs=[pl.BlockSpec(memory_space=pl.ANY)],
        out_specs=pl.BlockSpec(memory_space=pltpu.VMEM),
        scratch_shapes=[pltpu.VMEM((1, size % LANES), F32), pltpu.SemaphoreType.DMA((2,))],
        name="to_rows",
    )(entries)


def adam_kernel(
    gradient, master, first_moment, second_moment, layer_output, layer_grad,
    new_moment, new_second, new_master, output, input_grad, kept, last, kept_output, kept_grad,
    load_sem, store_sem, pass_sem,
):
    size = master.shape[1]
    full, rest = divmod(size, LANES)
    chunks, step = 3, 56
    chunk = -(-full // (step * chunks)) * step
    spans = [(c * chunk, min(chunk, full - c * chunk)) for c in range(chunks)]
    sources, targets = (first_moment, second_moment, master), (new_moment, new_second, new_master)

    def piece(array, first, count):
        return array.at[:, pl.ds(first * LANES, count * LANES)].reshape(count, LANES)

    def load(which, index):
        first, count = spans[index]
        if which == 3:
            span = pl.ds(first, -(-count // step) * step)
            return pltpu.make_async_copy(
                gradient.at[span], kept.at[3, span], load_sem.at[3, index]
            )
        return pltpu.make_async_copy(
            piece(sources[which], first, count), kept.at[which, pl.ds(first, count)],
            load_sem.at[which, index],
        )

    def store(which, index):
        first, count = spans[index]
        return pltpu.make_async_copy(
            kept.at[which, pl.ds(first, count)], piece(targets[which], first, count),
            store_sem.at[which, index],
        )

    def load_last(which):
        return pltpu.make_async_copy(
            sources[which].at[:, pl.ds(full * LANES, rest)], last.at[which], load_sem.at[which, chunks]
        )

    def store_last(which):
        return pltpu.make_async_copy(
            last.at[which], targets[which].at[:, pl.ds(full * LANES, rest)], store_sem.at[which, chunks]
        )

    passed = tuple(
        (
            pltpu.make_async_copy(source, through, pass_sem.at[index]),
            pltpu.make_async_copy(through, target, pass_sem.at[index]),
        )
        for index, (source, through, target) in enumerate(
            ((layer_output, kept_output, output), (layer_grad, kept_grad, input_grad))
        )
    )
    for index in range(chunks):
        for which in range(4):
            load(which, index).start()
    for which in range(3):
        load_last(which).start()
    for copy, _ in passed:
        copy.start()
    origin = lax.axis_index("seq") * size

    def update(first, count, moment, second, weights, gradients):
        at = (
            origin
            + (first + lax.broadcasted_iota(jnp.int32, (count, LANES), 0)) * LANES
            + lax.broadcasted_iota(jnp.int32, (count, LANES), 1)
        )
        return adam_update(weights, moment, second, gradients, at)

    for index, (first, count) in enumerate(spans):
        for which in range(4):
            load(which, index).wait()

        def run(at, carry, first=first):
            where = pl.multiple_of(first + at * step, 8)
            span = pl.ds(where, step)
            found = update(where, step, *(kept[which, span, :] for which in range(4)))
            for which in range(3):
                kept[which, span, :] = found[which]
            return carry

        lax.fori_loop(0, -(-count // step), run, 0)
        for which in range(3):
            store(which, index).start()
        if index == 0:
            for copy, onward in passed:
                copy.wait()
                onward.start()
    for which in range(3):
        load_last(which).wait()
    moment, second, weights = (last[which] for which in range(3))
    at = origin + full * LANES + lax.broadcasted_iota(jnp.int32, (1, rest), 1)
    found = adam_update(weights, moment, second, kept[3, full : full + 1, :rest], at)
    for which in range(3):
        last[which] = found[which]
        store_last(which).start()
    for which in range(3):
        for index in range(chunks):
            store(which, index).wait()
        store_last(which).wait()
    for _, copy in passed:
        copy.wait()


def run_adam(gradient, master, first_moment, second_moment, layer_output, layer_grad):
    size = master.shape[1]
    anywhere = pl.BlockSpec(memory_space=pl.ANY)
    return pl.pallas_call(
        adam_kernel,
        out_shape=(jax.ShapeDtypeStruct((1, size), F32),) * 3
        + tuple(jax.ShapeDtypeStruct(one.shape, one.dtype) for one in (layer_output, layer_grad)),
        in_specs=[anywhere] * 6,
        out_specs=(anywhere,) * 5,
        scratch_shapes=[
            pltpu.VMEM((4,) + gradient.shape, F32),
            pltpu.VMEM((3, 1, size % LANES), F32),
            pltpu.VMEM(layer_output.shape, layer_output.dtype),
            pltpu.VMEM(layer_grad.shape, layer_grad.dtype),
            pltpu.SemaphoreType.DMA((4, 5)),
            pltpu.SemaphoreType.DMA((3, 5)),
            pltpu.SemaphoreType.DMA((2,)),
        ],
        compiler_params=pltpu.CompilerParams(vmem_limit_bytes=VMEM_BYTES),
        name="run_adam",
    )(gradient, master, first_moment, second_moment, layer_output, layer_grad)


def on_device(tokens, cotangent, holes, slide_lengths, master, first_moment, second_moment):
    ways = lax.axis_size("seq")
    flat = to_rows(master, MAT_ROWS // ways + SMALL_ROWS)
    output, input_grad, gradient = run_step(tokens[0], cotangent[0], holes, slide_lengths, flat, ways)
    new_moment, new_second, new_master, output, input_grad = run_adam(
        gradient, master, first_moment, second_moment, output, input_grad
    )
    return (output[None], input_grad[None], new_moment, new_second, new_master)


def even(mesh):
    ways = mesh.shape["seq"]
    return ways % 4 == 0 and MAT_ROWS % (ways * UNIT) == 0 and ways * 8 == LANES


def solution(mesh):
    return jax.shard_map(
        on_device if even(mesh) else plain_on_device,
        mesh=mesh,
        in_specs=(
            P("grp", "seq", None),
            P("grp", "seq", None),
            P("grp", "seq"),
            P("grp", None),
            P("grp", "seq"),
            P("grp", "seq"),
            P("grp", "seq"),
        ),
        out_specs=(
            P("grp", "seq", None),
            P("grp", "seq", None),
            P("grp", "seq"),
            P("grp", "seq"),
            P("grp", "seq"),
        ),
        check_vma=False,
    )
```

```python
from functools import partial
from types import SimpleNamespace

import jax
import jax.numpy as jnp
from jax import lax
from jax.experimental import pallas as pl
from jax.experimental.pallas import tpu as pltpu
from jax.sharding import PartitionSpec as P

D = 768
FF = 3072
HEADS = 16
HEAD = 48
STEP = 10


EPS_NORM = 1e-05
EPS_ADAM = 1e-08
BETA_ONE = 0.9
BETA_TWO = 0.95


def as_sent(array):
    return jax.tree.map(lambda a: a.astype(jnp.bfloat16) if a.dtype == jnp.float32 else a, array)


def bounds():
    qkv_edge = 3 * D * D // 2
    out_edge = qkv_edge + D * D // 2
    up_edge = out_edge + D * FF // 2
    down_edge = up_edge + FF * D // 2
    gain_edge = down_edge + D
    return (qkv_edge, out_edge, up_edge, down_edge, gain_edge)


def per_segment(flat_index, values):
    edge_list = bounds()
    result = jnp.full(flat_index.shape, values[5], jnp.float32)
    for position in range(4, -1, -1):
        result = jnp.where(flat_index < edge_list[position], jnp.float32(values[position]), result)
    return result


def unpack(flat):
    edge_list = bounds()
    total = flat.shape[1]

    def joined(start, stop, shape):
        return jnp.concatenate(
            [flat[0, start:stop].reshape(shape), flat[1, start:stop].reshape(shape)], axis=-1
        )

    w_qkv = joined(0, edge_list[0], (D, 3 * D // 2))
    w_out = joined(edge_list[0], edge_list[1], (D, D // 2))
    w_up = joined(edge_list[1], edge_list[2], (D, FF // 2))
    w_down = joined(edge_list[2], edge_list[3], (FF, D // 2))
    gain_rows = joined(edge_list[3], edge_list[4], (2, D // 2))
    shift_rows = joined(edge_list[4], edge_list[4] + 3 * D // 2, (3, D // 2))
    bias_up = joined(edge_list[4] + 3 * D // 2, total, (FF // 2,))
    return (w_qkv, w_out, w_up, w_down, gain_rows, shift_rows, bias_up)


def normalize(values):
    centered = values - jnp.mean(values, axis=-1, keepdims=True)
    inverse = lax.rsqrt(jnp.mean(centered * centered, axis=-1, keepdims=True) + EPS_NORM)
    return (centered * inverse, inverse)


def norm_back(grad_hat, normed_hat, inverse):
    return inverse * (
        grad_hat
        - jnp.mean(grad_hat, axis=-1, keepdims=True)
        - normed_hat * jnp.mean(grad_hat * normed_hat, axis=-1, keepdims=True)
    )


def contract_rows(left, right):
    return lax.dot_general(
        left, right, (((0,), (0,)), ((), ())), preferred_element_type=jnp.float32
    )


def contract_cols(left, right):
    return lax.dot_general(
        left, right, (((1,), (1,)), ((), ())), preferred_element_type=jnp.float32
    )


def slide_index(positions, slide_ends):
    return jnp.sum((positions[:, None] >= slide_ends[None, :]).astype(jnp.int32), axis=1)


def split_heads(block_rows):
    return block_rows.reshape(block_rows.shape[0], HEADS, HEAD).transpose(1, 0, 2)


def join_heads(stacked):
    return stacked.transpose(1, 0, 2).reshape(stacked.shape[1], HEADS * HEAD)


def allowance(slides, present):
    token_count = slides.shape[0]
    same_slide = (slides[:, None] == slides[None, :]) & (present[None, :] > 0)
    return same_slide | jnp.eye(token_count, dtype=bool)


def attend(packed, slides, present):
    allowed = allowance(slides, present)
    scale = HEAD ** (-0.5)

    def one_head(pieces):
        query_head, key_head, value_head = pieces
        scores = contract_cols(query_head, key_head) * scale
        scores = jnp.where(allowed, scores, -1000000000.0)
        row_max = jnp.max(scores, axis=-1, keepdims=True)
        exponent = jnp.exp(scores - row_max)
        denominator = jnp.sum(exponent, axis=-1, keepdims=True)
        attention = (exponent / denominator).astype(jnp.bfloat16)
        result = jnp.dot(attention, value_head, preferred_element_type=jnp.float32)
        return (result, (row_max + jnp.log(denominator))[:, 0])

    outs, lses = lax.map(
        one_head,
        (
            split_heads(packed[:, :D]),
            split_heads(packed[:, D : 2 * D]),
            split_heads(packed[:, 2 * D :]),
        ),
    )
    return (join_heads(outs), lses.T)


def attend_back(packed, slides, present, lse_rows, out_grad, lse_grad):
    allowed = allowance(slides, present)
    scale = HEAD ** (-0.5)

    def one_head(pieces):
        query_head, key_head, value_head, lse_head, grad_head, extra_lse = pieces
        scores = contract_cols(query_head, key_head) * scale
        scores = jnp.where(allowed, scores, -1000000000.0)
        attention = jnp.exp(scores - lse_head[:, None])
        prob_grad = contract_cols(grad_head, value_head)
        inner_sum = jnp.sum(attention * prob_grad, axis=-1, keepdims=True)
        score_grad = (attention * (prob_grad - inner_sum + extra_lse[:, None])).astype(jnp.bfloat16)
        query_grad = jnp.dot(score_grad, key_head, preferred_element_type=jnp.float32) * scale
        key_grad = contract_rows(score_grad, query_head) * scale
        value_grad = contract_rows(attention.astype(jnp.bfloat16), grad_head)
        return (query_grad, key_grad, value_grad)

    query_grad, key_grad, value_grad = lax.map(
        one_head,
        (
            split_heads(packed[:, :D]),
            split_heads(packed[:, D : 2 * D]),
            split_heads(packed[:, 2 * D :]),
            lse_rows.T,
            split_heads(out_grad),
            lse_grad.T,
        ),
    )
    return jnp.concatenate(
        [join_heads(query_grad), join_heads(key_grad), join_heads(value_grad)], axis=1
    )


def adam_update(weights, moment, second, gradient, flat_index):
    step_rates = per_segment(
        flat_index,
        (
            0.7 * (2.0 / D) ** 0.5,
            0.7 * (24.0 / D) ** 0.5,
            0.7 * (1.0 / D) ** 0.5,
            0.7 * (1.0 / FF) ** 0.5,
            0.15,
            0.2,
        ),
    )
    decays = per_segment(flat_index, (0.1, 0.1, 0.1, 0.1, 0.0, 0.0))
    new_moment = BETA_ONE * moment + (1.0 - BETA_ONE) * gradient
    new_second = BETA_TWO * second + (1.0 - BETA_TWO) * gradient * gradient
    fix_one = 1.0 - BETA_ONE**STEP
    fix_two = 1.0 - BETA_TWO**STEP
    update = new_moment / fix_one / (jnp.sqrt(new_second / fix_two) + EPS_ADAM)
    return (new_moment, new_second, weights - step_rates * (update + decays * weights))


def column_halves(values):
    return values.reshape(values.shape[0], 2, values.shape[1] // 2)


def plain_on_device(tokens, cotangent, holes, slide_lengths, master, first_moment, second_moment):
    own_half = lax.all_gather(master.astype(jnp.bfloat16), "seq", axis=1, tiled=True)
    whole_flat = lax.all_gather(own_half, "grp", axis=0, tiled=True)
    w_qkv, w_out, w_up, w_down, gain_rows, shift_rows, bias_up = unpack(whole_flat)
    gain_rows = gain_rows.astype(jnp.float32)
    shift_rows = shift_rows.astype(jnp.float32)
    bias_up = bias_up.astype(jnp.float32)
    inputs = tokens[0].astype(jnp.float32)
    row_count = inputs.shape[0]
    seq_ways = lax.axis_size("seq")
    seq_place = lax.axis_index("seq")
    row_steps = jnp.arange(row_count, dtype=jnp.int32)
    slide_ends = jnp.cumsum(slide_lengths[0])
    near_slides = slide_index(seq_place * row_count + row_steps, slide_ends)
    far_slides = slide_index(seq_place + seq_ways * row_steps, slide_ends)
    near_present = holes[0]
    strided_shape = (row_count // seq_ways, seq_ways)

    def to_strided(packed):
        moved, moved_mask = (
            lax.all_to_all(
                packed.reshape(strided_shape + (3 * D,)),
                "seq",
                split_axis=1,
                concat_axis=0,
                tiled=True,
            ),
            lax.all_to_all(
                near_present.astype(jnp.bfloat16).reshape(strided_shape + (1,)),
                "seq",
                split_axis=1,
                concat_axis=0,
                tiled=True,
            ),
        )
        return (moved.reshape(row_count, 3 * D), moved_mask.reshape(row_count).astype(jnp.int32))

    normed_one, inverse_one = normalize(inputs)
    normed = (normed_one * gain_rows[0] + shift_rows[0]).astype(jnp.bfloat16)
    projected = jnp.dot(normed, w_qkv, preferred_element_type=jnp.float32).astype(jnp.bfloat16)
    near_out, near_lse = attend(projected, near_slides, near_present)
    far_proj, far_present = to_strided(projected)
    far_local, far_local_lse = attend(far_proj, far_slides, far_present)
    returned = (
        lax.all_to_all(
            far_local.reshape(row_count, 1, D).astype(jnp.bfloat16),
            "seq",
            split_axis=0,
            concat_axis=1,
            tiled=True,
        ).astype(jnp.float32),
        lax.all_to_all(
            far_local_lse.reshape(row_count, 1, HEADS).astype(jnp.bfloat16),
            "seq",
            split_axis=0,
            concat_axis=1,
            tiled=True,
        ).astype(jnp.float32),
    )
    far_out = returned[0].reshape(row_count, D)
    far_lse = returned[1].reshape(row_count, HEADS)
    near_share = jax.nn.sigmoid(near_lse - far_lse)
    near_heads = near_out.reshape(row_count, HEADS, HEAD)
    far_heads = far_out.reshape(row_count, HEADS, HEAD)
    mixture = (
        (near_share[:, :, None] * near_heads + (1.0 - near_share[:, :, None]) * far_heads)
        .reshape(row_count, D)
        .astype(jnp.bfloat16)
    )
    middle = inputs + jnp.dot(mixture, w_out, preferred_element_type=jnp.float32)
    normed_two, inverse_two = normalize(middle)
    second_in = (normed_two * gain_rows[1] + shift_rows[1]).astype(jnp.bfloat16)
    hidden = jnp.dot(second_in, w_up, preferred_element_type=jnp.float32) + bias_up
    activated = jax.nn.gelu(hidden, approximate=True).astype(jnp.bfloat16)
    output = middle + jnp.dot(activated, w_down, preferred_element_type=jnp.float32) + shift_rows[2]
    upstream = cotangent[0].astype(jnp.float32)
    down_grad = upstream.astype(jnp.bfloat16)
    grad_act = contract_cols(down_grad, w_down)
    gelu_pull = jax.vjp(partial(jax.nn.gelu, approximate=True), hidden)[1]
    hidden_grad = gelu_pull(grad_act)[0].astype(jnp.bfloat16)
    second_grad = contract_cols(hidden_grad, w_up)
    grad_gain_two = jnp.sum(second_grad * normed_two, axis=0)
    grad_shift_two = jnp.sum(second_grad, axis=0)
    middle_grad = upstream + norm_back(second_grad * gain_rows[1], normed_two, inverse_two)
    attend_grad = middle_grad.astype(jnp.bfloat16)
    mix_grad = contract_cols(attend_grad, w_out).reshape(row_count, HEADS, HEAD)
    near_lse_grad = (
        near_share * (1.0 - near_share) * jnp.sum((near_heads - far_heads) * mix_grad, axis=-1)
    )
    near_grad = (near_share[:, :, None] * mix_grad).reshape(row_count, D).astype(jnp.bfloat16)
    far_grad = ((1.0 - near_share[:, :, None]) * mix_grad).reshape(row_count, D)
    sent = (
        lax.all_to_all(
            as_sent(far_grad.reshape(strided_shape + (D,))),
            "seq",
            split_axis=1,
            concat_axis=0,
            tiled=True,
        ),
        lax.all_to_all(
            as_sent((-near_lse_grad).reshape(strided_shape + (HEADS,))),
            "seq",
            split_axis=1,
            concat_axis=0,
            tiled=True,
        ),
    )
    far_back = sent[0].reshape(row_count, D).astype(jnp.bfloat16)
    far_lse_grad = sent[1].reshape(row_count, HEADS)
    again_proj, again_present = to_strided(projected)
    again_lse = attend(again_proj, far_slides, again_present)[1]
    far_proj_grad = attend_back(
        again_proj, far_slides, again_present, again_lse, far_back, far_lse_grad
    ).astype(jnp.bfloat16)
    far_home = lax.all_to_all(
        far_proj_grad.reshape(row_count, 1, 3 * D), "seq", split_axis=0, concat_axis=1, tiled=True
    ).reshape(row_count, 3 * D)
    near_proj_grad = attend_back(
        projected, near_slides, near_present, near_lse, near_grad, near_lse_grad
    )
    proj_grad = (near_proj_grad + far_home.astype(jnp.float32)).astype(jnp.bfloat16)
    first_grad = contract_cols(proj_grad, w_qkv)
    grad_gain_one = jnp.sum(first_grad * normed_one, axis=0)
    grad_shift_one = jnp.sum(first_grad, axis=0)
    input_grad = middle_grad + norm_back(first_grad * gain_rows[0], normed_one, inverse_one)
    both_rows = (
        lax.all_gather(normed, "grp", axis=0, tiled=True),
        lax.all_gather(mixture, "grp", axis=0, tiled=True),
        lax.all_gather(second_in, "grp", axis=0, tiled=True),
        lax.all_gather(activated, "grp", axis=0, tiled=True),
    )
    moved = (
        lax.all_to_all(column_halves(proj_grad), "grp", split_axis=1, concat_axis=0, tiled=True),
        lax.all_to_all(column_halves(attend_grad), "grp", split_axis=1, concat_axis=0, tiled=True),
        lax.all_to_all(column_halves(hidden_grad), "grp", split_axis=1, concat_axis=0, tiled=True),
        lax.all_to_all(column_halves(down_grad), "grp", split_axis=1, concat_axis=0, tiled=True),
    )
    proj_mine = moved[0].reshape(2 * row_count, 3 * D // 2)
    attend_mine = moved[1].reshape(2 * row_count, D // 2)
    hidden_mine = moved[2].reshape(2 * row_count, FF // 2)
    down_mine = moved[3].reshape(2 * row_count, D // 2)
    norm_sums = lax.psum(
        jnp.stack([grad_gain_one, grad_gain_two, grad_shift_one, grad_shift_two]), "grp"
    )
    half_width = D // 2
    norm_half = lax.dynamic_slice_in_dim(
        norm_sums, lax.axis_index("grp") * half_width, half_width, 1
    )
    grad_w_qkv = contract_rows(both_rows[0], proj_mine)
    grad_w_out = contract_rows(both_rows[1], attend_mine)
    grad_w_up = contract_rows(both_rows[2], hidden_mine)
    grad_w_down = contract_rows(both_rows[3], down_mine)
    grad_bias_down = jnp.sum(down_mine.astype(jnp.float32), axis=0)
    grad_bias_up = jnp.sum(hidden_mine.astype(jnp.float32), axis=0)
    gradient = jnp.concatenate(
        [
            grad_w_qkv.reshape(-1),
            grad_w_out.reshape(-1),
            grad_w_up.reshape(-1),
            grad_w_down.reshape(-1),
            norm_half[0],
            norm_half[1],
            norm_half[2],
            norm_half[3],
            grad_bias_down,
            grad_bias_up,
        ]
    )
    reduced = lax.psum_scatter(gradient, "seq", scatter_dimension=0, tiled=True)
    shard_size = master.shape[1]
    flat_index = lax.axis_index("seq") * shard_size + jnp.arange(shard_size, dtype=jnp.int32)
    new_moment, new_second, new_master = adam_update(
        master[0], first_moment[0], second_moment[0], reduced, flat_index
    )
    return (
        output[None].astype(jnp.bfloat16),
        input_grad[None],
        new_moment[None],
        new_second[None],
        new_master[None],
    )


LANES = 128
BF16 = jnp.bfloat16
F32 = jnp.float32
MAT_ROWS = (3 * D * D + D * D + D * FF + FF * D) // 2 // LANES
SMALL_ROWS = 32
UNIT = 576
PAIR = 2
TILES = (3 * D // 2 // LANES, D // 2 // LANES, FF // 2 // LANES, D // 2 // LANES)
DEPTHS = (D, D, D, FF)
MESH = pl.DeviceIdType.MESH
VMEM_BYTES = 60 * 2**20
NEG = -1000000000.0
ORDERS = ((1, 2, 3), (0, 2, 3), (0, 3, 1), (0, 2, 1))
PIECES = 2
LATE_ROWS = 160
LATE_OUT = (128, 160, 192, 192)


def matrix_starts():
    starts = [0]
    for tiles, depth in zip(TILES, DEPTHS):
        starts.append(starts[-1] + tiles * depth)
    return starts


def place():
    return lax.axis_index("seq"), lax.axis_index("grp")


def greet_all(ways):
    s, g = place()
    barrier = pltpu.get_barrier_semaphore()

    def greet(step, carry):
        pl.semaphore_signal(
            barrier, inc=1, device_id=(lax.rem(s + step, ways), g), device_id_type=MESH
        )
        return carry

    lax.fori_loop(1, ways, greet, 0)
    pl.semaphore_signal(barrier, inc=1, device_id=(s, 1 - g), device_id_type=MESH)
    return barrier


def remote(src, dst, send_sem, recv_sem, to):
    return pltpu.make_async_remote_copy(
        src_ref=src,
        dst_ref=dst,
        send_sem=send_sem,
        recv_sem=recv_sem,
        device_id=to,
        device_id_type=MESH,
    )


def unit_tiles(unit, body):
    edges = [start // UNIT for start in matrix_starts()]
    kinds = {}
    for index, tiles in enumerate(TILES):
        inside = (unit >= edges[index]) & (unit < edges[index + 1])
        kinds[tiles] = kinds[tiles] | inside if tiles in kinds else inside
    for tiles, inside in kinds.items():
        pl.when(inside)(lambda tiles=tiles: body(tiles))


def dot(left, right):
    return jnp.dot(left, right, preferred_element_type=F32)


def dot_cols(left, right):
    return contract_cols(left, right)


def dot_rows(left, right):
    return contract_rows(left, right)


def tile_view(ref, index):
    rows = 16 * TILES[index]
    start = matrix_starts()[index]
    return ref.reshape(ref.shape[:-2] + (MAT_ROWS // rows, rows, LANES)), start // rows


def tile_groups(index):
    tiles = TILES[index]
    groups, at = [], 0
    while at < tiles:
        width = 3 if tiles - at == 3 else 2
        groups.append((at, width))
        at += width
    return groups


def weight(ref, index, half, row, rows, tile, width):
    view, base = tile_view(ref, index)
    first = base + row // 16
    pieces = [
        view[half, first : first + rows // 16, 16 * t : 16 * t + 16, :].reshape(rows, LANES)
        for t in range(tile, tile + width)
    ]
    return jnp.concatenate(pieces, axis=1)


def heads_of(rows):
    row = lax.broadcasted_iota(jnp.int32, (rows, D), 0) * HEAD
    column = lax.broadcasted_iota(jnp.int32, (rows, D), 1)
    return ((column >= row) & (column < row + HEAD)).astype(F32)


def to_columns(per_head):
    return jnp.dot(
        per_head, heads_of(HEADS), precision=lax.Precision.HIGHEST, preferred_element_type=F32
    )


def to_heads(columns):
    return lax.dot_general(
        columns,
        heads_of(HEADS),
        (((1,), (1,)), ((), ())),
        precision=lax.Precision.HIGHEST,
        preferred_element_type=F32,
    )


def pack_blocks(ref, values, extra):
    blocks = values.shape[0] // 8
    split = values.reshape(blocks, 8, D)
    ref[:, :, : D // 2] = jnp.concatenate(
        [split[:, :, : D // 2], split[:, :, D // 2 :]], axis=1
    ).astype(BF16)
    if extra is not None:
        high = extra.astype(BF16).astype(F32)
        low = extra - high
        pieces = jnp.concatenate(
            [high.reshape(blocks, 8, HEADS), low.reshape(blocks, 8, HEADS)], axis=1
        )
        ref[:, :, D // 2 : D // 2 + HEADS] = pieces.astype(BF16)


def unpack_values(ref):
    blocks = ref.shape[0]
    values = ref[:, :, : D // 2].astype(F32)
    return jnp.concatenate(
        [values[:, :8, :].reshape(blocks * 8, D // 2), values[:, 8:, :].reshape(blocks * 8, D // 2)],
        axis=1,
    )


def unpack_extra(ref):
    blocks = ref.shape[0]
    pieces = ref[:, :, D // 2 :].astype(F32)
    both = pieces[:, :8, :] + pieces[:, 8:, :]
    return both.reshape(blocks * 8, LANES)[:, :HEADS]


def slide_masks(ends_ref, s, ways, near_keys, far_keys):
    rows = near_keys.shape[1]
    ends, end = [], 0
    for index in range(ends_ref.shape[1]):
        end = end + ends_ref[0, index]
        ends.append(end)

    def slides(positions):
        total = jnp.zeros(positions.shape, jnp.int32)
        for end in ends:
            total = total + (positions >= end).astype(jnp.int32)
        return total

    across = rows // ways
    result = []
    for far, keys in ((False, near_keys), (True, far_keys)):
        found = []
        for dim in (0, 1):
            at = lax.broadcasted_iota(jnp.int32, (rows, rows), dim)
            if far:
                position = s + ways * at
            else:
                position = rows * s + ways * lax.rem(at, across) + at // across
            found.append(slides(position))
        query = lax.broadcasted_iota(jnp.int32, (rows, rows), 0)
        key = lax.broadcasted_iota(jnp.int32, (rows, rows), 1)
        allowed = ((found[0] == found[1]) & (keys > 0.5)) | (query == key)
        result.append(allowed.astype(F32))
    return result


def lay_group(tiled, laid, first, group, count, turn=None):
    for tile in range(count):
        block = tiled[pl.ds(pl.multiple_of(first + 16 * (group * count + tile), 16), 16), :]
        if turn is not None:
            block = pltpu.roll(block, turn, 1)
        laid[pl.ds(first + group * 16 * count + tile, 16, stride=count), :] = block


def step_kernel(
    ways, tokens, cotangent, holes, lengths, master,
    output, input_grad, total, after_rows,
    whole, grads, small, entries_here, entries_end, extended, aligned, tail,
    turning, send_blocks, recv_blocks, masks, normed, normed_hat, inverse, projected, attended, lses,
    mixture, second_in, activated, slope, second_hat, second_inverse, middle_grad,
    qkv_grad, out_grad, up_grad, down_grad, near_grad, far_grad, lse_grads,
    their_normed, their_mixture, their_second, their_activated,
    their_qkv, their_out, their_up, their_down, small_parts, their_small,
    by_x, by_y, by_z, by_late, laid, follow_rows, small_all,
    load_sem, tail_sem, slot_send, slot_recv, late_send, late_recv, core_send, core_recv, small_send, small_recv,
    block_send, block_recv, pair_send, pair_recv,
    x_send, x_recv, y_send, y_recv, z_send, z_recv, late_out_send, late_out_recv, end_sem, sum_sem,
):
    s, g = place()
    planes = ways // 4
    z, y, x = s // 4, lax.rem(s // 2, 2), lax.rem(s, 2)
    own = MAT_ROWS // ways
    half_own = own // 2
    rows = tokens.shape[0]
    across = rows // ways
    tiles = D // LANES
    half_width = D // 2
    third_rows = half_width // LANES
    entries = (MAT_ROWS * LANES + bounds_total()) // ways - own * LANES
    shift = entries * s
    row_shift, lane_shift = shift // LANES, lax.rem(shift, LANES)

    def chip(plane, row, column):
        return ((plane * 2 + row) * 2 + column, g)

    def part_at(plane, row, column, part):
        first = ((plane * 2 + row) * 2 + column) * own + part * half_own
        return pl.ds(pl.multiple_of(first, 16), half_own)


    last_row, last_lanes = divmod(own * LANES + entries, LANES)
    step_rows = 176
    full = last_row * LANES
    loads = (
        pltpu.make_async_copy(
            master.at[:, pl.ds(0, full)], entries_here.at[:, pl.ds(0, full)], load_sem.at[0]
        ),
        pltpu.make_async_copy(master.at[:, pl.ds(full, last_lanes)], entries_end, load_sem.at[1]),
    )

    def loaded():
        for load in loads:
            load.wait()
        entries_here[:, full:] = jnp.zeros((1, entries_here.shape[1] - full), F32)
        entries_here[:, full : full + last_lanes] = entries_end[...]

    def flat_rows(first, count):
        if not isinstance(first, int):
            first = pl.multiple_of(first * LANES, LANES)
        else:
            first = first * LANES
        return entries_here[:, pl.ds(first, count * LANES)].reshape(count, LANES)

    def follow_copy():
        return remote(
            tail, extended.at[pl.ds(0, SMALL_ROWS)], tail_sem.at[0], tail_sem.at[1],
            (lax.rem(s + 1, ways), g),
        )

    def make_tail():
        lanes = lax.broadcasted_iota(jnp.int32, (SMALL_ROWS, LANES), 1)
        gap = LANES - last_lanes
        older = pltpu.roll(flat_rows(last_row - SMALL_ROWS, SMALL_ROWS), gap, 1)
        newer = pltpu.roll(flat_rows(last_row - SMALL_ROWS + 1, SMALL_ROWS), gap, 1)
        tail[...] = jnp.where(lanes < gap, older, newer)

    def align(here, before, to):
        lanes = lax.broadcasted_iota(jnp.int32, (step_rows, LANES), 1)
        aligned[pl.ds(pl.multiple_of(to, 8), step_rows), :] = jnp.where(
            lanes >= lane_shift, pltpu.roll(here, lane_shift, 1), pltpu.roll(before, lane_shift, 1)
        )

    def fill(unit):
        first = unit * UNIT

        def tiled(count):
            for group in range(UNIT // (16 * count)):
                for tile in range(count):
                    block = aligned[pl.ds(first + group * 16 * count + tile, 16, stride=count), :]
                    at = s * own + first + 16 * (group * count + tile)
                    whole[g, pl.ds(pl.multiple_of(at, 16), 16), :] = block.astype(BF16)

        unit_tiles(s * (own // UNIT) + unit, tiled)

    def fill_most():
        def align_step(step, carry):
            first = step * step_rows - row_shift
            align(flat_rows(first, step_rows), flat_rows(first - 1, step_rows), step * step_rows)
            return carry

        def fill_unit(unit, carry):
            fill(unit)
            return carry

        extended[SMALL_ROWS:, :] = flat_rows(0, extended.shape[0] - SMALL_ROWS)
        lax.fori_loop(1, (own + SMALL_ROWS) // step_rows, align_step, 0)
        lax.fori_loop(1, own // UNIT, fill_unit, 0)

    def fill_first():
        follow_copy().wait()
        first = SMALL_ROWS - row_shift
        align(extended[pl.ds(first, step_rows), :], extended[pl.ds(first - 1, step_rows), :], 0)
        fill(0)

    order = [z]
    for step in range(1, planes):
        plane = jnp.int32(ORDERS[0][step - 1])
        for at in range(1, planes):
            plane = jnp.where(z == at, ORDERS[at][step - 1], plane)
        order.append(plane)

    part_rows = half_own - LATE_ROWS
    late = PIECES

    def slot_copy(plane, row, column, part, piece, kind, to):
        if piece == late:
            first, count = 2 * part_rows + part * LATE_ROWS, LATE_ROWS
        else:
            count = part_rows // PIECES
            first = part * part_rows + piece * count
        first = ((plane * 2 + row) * 2 + column) * own + first
        where = whole.at[g, pl.ds(pl.multiple_of(first, 16), count)]
        return remote(
            where,
            where,
            slot_send.at[part, plane, kind, piece],
            slot_recv.at[part, (plane * 2 + row) * 2 + column, piece],
            to,
        )

    def line_up(plane, part, piece):
        return slot_copy(plane, y, x, part, piece, 0, chip(z + 1, y, x))

    def line_down(plane, part, piece):
        return slot_copy(plane, y, x, part, piece, 1, chip(z - 1, y, x))

    def to_x(plane, part, piece):
        return slot_copy(plane, y, x, part, piece, 2, chip(z, y, 1 - x))

    def to_y(plane, part, piece):
        return slot_copy(plane, y, x, part, piece, 3, chip(z, 1 - y, x))

    def early(plane, piece):
        to_y(plane, 0, piece).start()
        to_x(plane, 1, piece).start()

    def direct(plane, piece):
        to_x(plane, 0, piece).start()
        to_y(plane, 1, piece).start()

    def turned(plane, piece):
        return (
            slot_copy(plane, 1 - y, x, 0, piece, 4, chip(z, y, 1 - x)),
            slot_copy(plane, y, 1 - x, 1, piece, 4, chip(z, 1 - y, x)),
        )

    def turn_piece(plane, piece):
        for copy in turned(plane, piece):
            copy.wait_recv()
            copy.start()

    def come(plane, piece):
        slot_copy(plane, y, 1 - x, 0, piece, 0, chip(z, y, x)).wait_recv()
        slot_copy(plane, 1 - y, 1 - x, 0, piece, 0, chip(z, y, x)).wait_recv()
        slot_copy(plane, 1 - y, x, 1, piece, 0, chip(z, y, x)).wait_recv()
        slot_copy(plane, 1 - y, 1 - x, 1, piece, 0, chip(z, y, x)).wait_recv()

    def leave(piece, plane_one):
        for part in range(2):

            def up(part=part):
                line_up(z, part, piece).start()

            def down(part=part):
                line_down(z, part, piece).start()

            if plane_one:
                pl.when((z == 1) & (z < planes - 1))(up)
            else:
                pl.when((z != 1) & (z < planes - 1))(up)
                pl.when(z > 0)(down)

    def enter_plane(plane, piece):
        for part in range(2):
            slot_copy(plane, y, x, part, piece, 0, chip(z, y, x)).wait_recv()

            def up(part=part):
                line_up(plane, part, piece).start()

            def down(part=part):
                line_down(plane, part, piece).start()

            pl.when((z > plane) & (z < planes - 1))(up)
            pl.when((z < plane) & (z > 0))(down)

    def late_copy(plane, part, way):
        view = whole.reshape(2, ways, own, LANES)
        where = view.at[
            g, pl.ds(4 * plane, 4), pl.ds(2 * part_rows + part * LATE_ROWS, LATE_ROWS)
        ]
        return remote(
            where, where, late_send.at[way, plane, part], late_recv.at[plane, part],
            chip(z + 1 - 2 * way, y, x),
        )

    def late_own():
        come(z, late)
        for part in range(2):
            pl.when(z < planes - 1)(lambda part=part: late_copy(z, part, 0).start())
            pl.when(z > 0)(lambda part=part: late_copy(z, part, 1).start())

    def late_on(plane):
        for part in range(2):
            late_copy(plane, part, 0).wait_recv()
            pl.when((z > plane) & (z < planes - 1))(
                lambda part=part: late_copy(plane, part, 0).start()
            )
            pl.when((z < plane) & (z > 0))(lambda part=part: late_copy(plane, part, 1).start())

    def to_core(half, plane, part, piece):
        count = LATE_ROWS if piece == late else part_rows // PIECES
        first = 2 * part_rows + part * count if piece == late else part * part_rows + piece * count
        view = whole.reshape(2, ways, own, LANES)
        where = view.at[half, pl.ds(4 * plane, 4), pl.ds(first, count)]
        return remote(
            where, where, core_send.at[plane, part, piece], core_recv.at[plane, part, piece],
            (s, 1 - g),
        )

    def finish(plane, piece):
        if piece != late:
            come(plane, piece)
        for part in range(2):
            to_core(g, plane, part, piece).start()

    def arrived(plane):
        for part in range(2):
            for piece in range(PIECES + 1):
                to_core(1 - g, plane, part, piece).wait_recv()

    def gather_sent():
        for plane in range(planes):
            for part in range(2):
                for piece in range(PIECES):

                    def up(plane=plane, part=part, piece=piece):
                        line_up(plane, part, piece).wait_send()

                    def down(plane=plane, part=part, piece=piece):
                        line_down(plane, part, piece).wait_send()

                    pl.when((z >= plane) & (z < planes - 1))(up)
                    pl.when((z <= plane) & (z > 0))(down)
                    to_x(plane, part, piece).wait_send()
                    to_y(plane, part, piece).wait_send()
                    turned(plane, piece)[part].wait_send()
                to_own = (to_x(z, part, late), to_y(z, part, late), turned(z, late)[part])
                if plane == 0:
                    for copy in to_own:
                        copy.wait_send()
                pl.when((z >= plane) & (z < planes - 1))(
                    lambda plane=plane, part=part: late_copy(plane, part, 0).wait_send()
                )
                pl.when((z <= plane) & (z > 0))(
                    lambda plane=plane, part=part: late_copy(plane, part, 1).wait_send()
                )
            for part in range(2):
                for piece in range(PIECES + 1):
                    to_core(g, plane, part, piece).wait_send()

    def small_to(index):
        return remote(small.at[g], small.at[g], small_send.at[index], small_recv.at[0], (index, g))

    def small_across():
        return remote(
            small.at[g], small.at[g], small_send.at[ways - 1], small_recv.at[1], (s, 1 - g)
        )

    def small_out():
        def tell(index, carry):
            small_to(index).start()
            return carry

        @pl.when(s == ways - 1)
        def _():
            small[g] = aligned[own : own + SMALL_ROWS, :].astype(BF16)
            lax.fori_loop(0, ways - 1, tell, 0)

    def small_in():
        pl.when(s != ways - 1)(lambda: small_to(s).wait_recv())
        small_across().start()
        remote(
            small.at[1 - g], small.at[1 - g], small_send.at[ways - 1], small_recv.at[1], (s, 1 - g)
        ).wait_recv()

    def small_sent():
        def told(index, carry):
            small_to(index).wait_send()
            return carry

        @pl.when(s == ways - 1)
        def _():
            lax.fori_loop(0, ways - 1, told, 0)

        small_across().wait_send()


    def cut(plane, part, piece):
        if piece == late:
            return 2 * (half_own - LATE_OUT[plane]) + part * LATE_OUT[plane], LATE_OUT[plane]
        count = (half_own - LATE_OUT[plane]) // PIECES
        return part * (half_own - LATE_OUT[plane]) + piece * count, count

    def piece_at(plane, row, column, part, piece):
        first, count = cut(plane, part, piece)
        first = ((plane * 2 + row) * 2 + column) * own + first
        return pl.ds(pl.multiple_of(first, 16), count)

    def held(ref, plane, part, piece):
        return ref.at[pl.ds(0, cut(plane, part, piece)[1])]

    def first_copy(plane, part, k, piece):
        where = (k, 1 - x) if part == 0 else (1 - y, k)
        return remote(
            grads.at[piece_at(plane, *where, part, piece)],
            held(by_x.at[plane, part, k, piece], plane, part, piece),
            x_send.at[plane, part, k, piece], x_recv.at[plane, part, k, piece],
            chip(z, y, 1 - x) if part == 0 else chip(z, 1 - y, x),
        )

    def second_copy(plane, part, piece):
        where = (1 - y, x) if part == 0 else (y, 1 - x)
        return remote(
            grads.at[piece_at(plane, *where, part, piece)],
            held(by_y.at[plane, part, piece], plane, part, piece),
            y_send.at[plane, part, piece], y_recv.at[plane, part, piece],
            chip(z, 1 - y, x) if part == 0 else chip(z, y, 1 - x),
        )

    def line_copy(plane, part, piece, way):
        return remote(
            grads.at[piece_at(plane, y, x, part, piece)],
            held(by_z.at[way, plane, part, piece], plane, part, piece),
            z_send.at[plane, part, piece], z_recv.at[way, plane, part, piece],
            chip(z + 1 - 2 * way, y, x),
        )

    def late_out_copy(plane, part, way):
        first, count = cut(plane, part, late)
        view = grads.reshape(ways, own, LANES)
        return remote(
            view.at[pl.ds(4 * plane, 4), pl.ds(first, count)],
            by_late.at[way, plane, part, :, pl.ds(0, count)],
            late_out_send.at[plane, part], late_out_recv.at[way, plane, part],
            chip(z + 1 - 2 * way, y, x),
        )

    def add(where, block):
        grads[where, :] = (grads[where, :].astype(F32) + block[...].astype(F32)).astype(BF16)

    def at_home(plane, piece, act):
        if piece == late:
            pl.when(z == plane)(act)
        else:
            act()

    def out_ahead(plane, piece):
        def act():
            for part in range(2):
                first_copy(plane, part, (1 - y, 1 - x)[part], piece).start()

        at_home(plane, piece, act)

    def out_keep(plane, piece):
        def act():
            for part in range(2):
                first_copy(plane, part, (y, x)[part], piece).start()

        at_home(plane, piece, act)

    def out_pass(plane, piece):
        def act():
            for part in range(2):
                other = (1 - y, 1 - x)[part]
                first_copy(plane, part, other, piece).wait_recv()
                where = (other, x) if part == 0 else (y, other)
                add(
                    piece_at(plane, *where, part, piece),
                    held(by_x.at[plane, part, other, piece], plane, part, piece),
                )
                second_copy(plane, part, piece).start()

        at_home(plane, piece, act)

    def out_take(plane, piece):
        def act():
            for part in range(2):
                mine = (y, x)[part]
                first_copy(plane, part, mine, piece).wait_recv()
                add(
                    piece_at(plane, y, x, part, piece),
                    held(by_x.at[plane, part, mine, piece], plane, part, piece),
                )

        at_home(plane, piece, act)

    def out_join(plane, piece):
        def act():
            for part in range(2):
                second_copy(plane, part, piece).wait_recv()
                add(
                    piece_at(plane, y, x, part, piece),
                    held(by_y.at[plane, part, piece], plane, part, piece),
                )
                if piece != late and plane > 0:
                    pl.when(z == 0)(lambda part=part: line_copy(plane, part, piece, 0).start())
                if piece != late and plane < planes - 1:
                    pl.when(z == planes - 1)(
                        lambda part=part: line_copy(plane, part, piece, 1).start()
                    )

        at_home(plane, piece, act)

    def between(plane, act):
        if plane > 1:
            pl.when((z > 0) & (z < plane))(lambda: act(0))
        if plane < planes - 2:
            pl.when((z > plane) & (z < planes - 1))(lambda: act(1))

    def out_relay(plane, piece):
        for part in range(2):

            def act(way, part=part):
                line_copy(plane, part, piece, way).wait_recv()
                add(
                    piece_at(plane, y, x, part, piece),
                    held(by_z.at[way, plane, part, piece], plane, part, piece),
                )
                line_copy(plane, part, piece, way).start()

            between(plane, act)

    def late_add(plane, part, way):
        late_out_copy(plane, part, way).wait_recv()
        for k in range(4):
            add(
                piece_at(plane, k // 2, k % 2, part, late),
                by_late.at[way, plane, part, k, pl.ds(0, LATE_OUT[plane])],
            )

    def late_start(plane):
        for part in range(2):
            if plane > 0:
                pl.when(z == 0)(lambda part=part: late_out_copy(plane, part, 0).start())
            if plane < planes - 1:
                pl.when(z == planes - 1)(lambda part=part: late_out_copy(plane, part, 1).start())

    def late_relay(plane):
        for part in range(2):

            def act(way, part=part):
                late_add(plane, part, way)
                late_out_copy(plane, part, way).start()

            between(plane, act)

    def late_home(plane):
        @pl.when(z == plane)
        def _():
            for part in range(2):
                if plane > 0:
                    late_add(plane, part, 0)
                if plane < planes - 1:
                    late_add(plane, part, 1)

    def out_sent():
        for plane in range(planes):
            for piece in range(PIECES + (1 if LATE_OUT[plane] else 0)):

                def act(plane=plane, piece=piece):
                    for part in range(2):
                        for k in range(2):
                            first_copy(plane, part, k, piece).wait_send()
                        second_copy(plane, part, piece).wait_send()

                at_home(plane, piece, act)

            @pl.when(z != plane)
            def _(plane=plane):
                for part in range(2):
                    for piece in range(PIECES):
                        line_copy(plane, part, piece, 0).wait_send()
                    if LATE_OUT[plane]:
                        late_out_copy(plane, part, 0).wait_send()

    def out_last(parts):
        for plane in range(planes):

            @pl.when(z == plane)
            def _(plane=plane):
                for part, piece in parts:
                    first, count = cut(plane, part, piece)
                    if not count:
                        continue
                    found = grads[piece_at(plane, y, x, part, piece), :].astype(F32)
                    for way in range(2):
                        if piece != late and (plane > 0 if way == 0 else plane < planes - 1):
                            line_copy(plane, part, piece, way).wait_recv()
                            found = found + by_z[way, plane, part, piece, :count].astype(F32)
                    total[first : first + count, :] = found

    def small_home():
        return remote(
            small_parts.at[g], small_all.at[s], sum_sem.at[0], sum_sem.at[1], (ways - 1, g)
        )

    def follow_back():
        return remote(
            laid.at[pl.ds(0, SMALL_ROWS)], follow_rows, end_sem.at[0], end_sem.at[1],
            (lax.rem(s + ways - 1, ways), g),
        )

    def settle_first():
        unit_tiles(s * (own // UNIT), lambda count: lay_group(total, laid, 0, 0, count))
        follow_back().start()

    def settle():
        follow_back().wait()

        @pl.when(s != ways - 1)
        def _():
            after_rows[...] = follow_rows[...]

        @pl.when(s == ways - 1)
        def _():
            remote(
                small_all.at[pl.ds(0, ways - 1)], small_all.at[pl.ds(0, ways - 1)],
                sum_sem.at[0], sum_sem.at[1], (0, g),
            ).wait_recv()
            small_all[ways - 1] = small_parts[g]
            after_rows[...] = jnp.sum(small_all[...], axis=0)


    widths = (half_width + LANES,) * 3 + (half_width,)

    def exchange(index):
        width = widths[index]

        def start(step, carry):
            to = lax.rem(s + step, ways)
            remote(
                send_blocks.at[index, to, :, pl.ds(0, width)],
                recv_blocks.at[index, s, :, pl.ds(0, width)],
                block_send.at[index],
                block_recv.at[index],
                (to, g),
            ).start()
            return carry

        recv_blocks[index, s] = send_blocks[index, s]
        lax.fori_loop(1, ways, start, 0)

    def exchanged(index):
        width = widths[index]
        remote(
            send_blocks.at[index, pl.ds(0, ways - 1), :, pl.ds(0, width)],
            recv_blocks.at[index, pl.ds(0, ways - 1), :, pl.ds(0, width)],
            block_send.at[index],
            block_recv.at[index],
            (s, 1 - g),
        ).wait()

    pairs = []

    def hand_over(src, dst):
        index = len(pairs)
        pairs.append(remote(src, dst, pair_send.at[index], pair_recv.at[index], (s, 1 - g)))
        pairs[index].start()
        return pairs[index]

    def by_residue(value):
        for tile in range(tiles):
            turning[tile] = value[:, tile * LANES : (tile + 1) * LANES]
        return jnp.concatenate(
            [
                jnp.concatenate(
                    [turning[tile, pl.ds(i, across, stride=ways), :] for i in range(ways)], axis=0
                )
                for tile in range(tiles)
            ],
            axis=1,
        )

    def in_order(value):
        for tile in range(tiles):
            for i in range(ways):
                turning[tile, pl.ds(i, across, stride=ways), :] = value[
                    across * i : across * (i + 1), tile * LANES : (tile + 1) * LANES
                ]
        return jnp.concatenate([turning[tile] for tile in range(tiles)], axis=1)

    def small_row(first, count):
        return jnp.concatenate(
            [small[half, first + r : first + r + 1, :] for half in range(2) for r in range(count)],
            axis=1,
        ).astype(F32)

    temper = HEAD ** (-0.5)

    def scores(which, head):
        at = slice(which * rows, (which + 1) * rows)
        query = projected[at, head * HEAD : (head + 1) * HEAD]
        key = projected[at, D + head * HEAD : D + (head + 1) * HEAD]
        value = projected[at, 2 * D + head * HEAD : 2 * D + (head + 1) * HEAD]
        found = jnp.where(masks[which] > 0.5, dot_cols(query, key) * temper, NEG)
        return query, key, value, found

    def attend_set(which):
        results, totals = [], []
        for head in range(HEADS):
            _, _, value, found = scores(which, head)
            top = jnp.max(found, axis=1, keepdims=True)
            weights = jnp.exp(found - top)
            summed = jnp.sum(weights, axis=1, keepdims=True)
            results.append(dot(weights.astype(BF16), value) * (1.0 / summed))
            totals.append(top + jnp.log(summed))
        attended[which] = jnp.concatenate(results, axis=1)
        lses[which] = jnp.concatenate(totals, axis=1)

    def attend_set_back(which, out_grads):
        lists = ([], [], [])
        for head in range(HEADS):
            query, key, value, found = scores(which, head)
            weights = jnp.exp(found - lses[which, :, head : head + 1])
            pulled = out_grads[:, head * HEAD : (head + 1) * HEAD]
            weight_grad = dot_cols(pulled, value)
            inner = jnp.sum(weights * weight_grad, axis=1, keepdims=True)
            extra = lse_grads[which, :, head : head + 1] - inner
            score_grad = (weights * (weight_grad + extra)).astype(BF16)
            lists[0].append(dot(score_grad, key) * temper)
            lists[1].append(dot_rows(score_grad, query) * temper)
            lists[2].append(dot_rows(weights.astype(BF16), pulled))
        at = slice(which * rows, (which + 1) * rows)
        query_grad, key_grad, value_grad = (jnp.concatenate(one, axis=1).astype(BF16) for one in lists)
        qkv_grad[0, at, :D] = query_grad
        qkv_grad[0, at, D:] = key_grad[:, :half_width]
        qkv_grad[1, at, :half_width] = key_grad[:, half_width:]
        qkv_grad[1, at, half_width:] = value_grad

    def weight_grad(index, mine, theirs, grad, their_grad, first, count):
        left = jnp.concatenate(
            [mine[:, first : first + count], theirs[:, first : first + count]], axis=0
        )
        view, base = tile_view(grads, index)
        at = base + first // 16
        for tile, width in tile_groups(index):
            to = slice(tile * LANES, (tile + width) * LANES)
            right = jnp.concatenate([grad[g, :, to], their_grad[:, to]], axis=0)
            found = dot_rows(left, right).astype(BF16)
            for t in range(width):
                view[at : at + count // 16, 16 * (tile + t) : 16 * (tile + t) + 16, :] = found[
                    :, t * LANES : (t + 1) * LANES
                ].reshape(count // 16, 16, LANES)


    kept = SimpleNamespace()
    barrier = greet_all(ways)
    for load in loads:
        load.start()
    inputs = by_residue(tokens[...].astype(F32))
    lane = lax.broadcasted_iota(jnp.int32, (rows, rows), 1)
    row = lax.broadcasted_iota(jnp.int32, (rows, rows), 0)
    flags = holes[...].astype(F32)
    to_column = (row == lane).astype(F32)
    own_column = jnp.sum(to_column * flags, axis=1, keepdims=True)
    turned_at = ways * lax.rem(row, across) + row // across
    turned_column = jnp.sum((turned_at == lane).astype(F32) * flags, axis=1, keepdims=True)
    turned_row_at = ways * lax.rem(lane, across) + lane // across
    turned_row = jnp.sum((turned_row_at == row).astype(F32) * own_column, axis=0, keepdims=True)
    pack_blocks(send_blocks.at[0], inputs, jnp.broadcast_to(turned_column, (rows, HEADS)) * 1.0)
    loaded()
    make_tail()
    fill_most()
    pl.semaphore_wait(barrier, ways)
    follow_copy().start()
    early(order[0], late)
    direct(order[0], late)
    exchange(0)
    small_out()
    fill_first()

    def norm():
        kept.upstream = by_residue(cotangent[...].astype(F32))
        for half in range(2):
            to = slice(half * half_width, (half + 1) * half_width)
            down_grad[half] = kept.upstream[:, to].astype(BF16)
        kept.down_grad_pair = hand_over(down_grad.at[1 - g], their_down)
        exchanged(0)
        far_inputs = unpack_values(recv_blocks.at[0])
        far_column = unpack_extra(recv_blocks.at[0])[:, :1]
        far_row = jnp.sum(to_column * far_column, axis=0, keepdims=True)
        near_mask, far_mask = slide_masks(lengths, s, ways, turned_row, far_row)
        masks[0] = near_mask
        masks[1] = far_mask
        hat, scale = normalize(jnp.concatenate([inputs, far_inputs], axis=0))
        small_in()
        count = third_rows
        kept.gain_one, kept.gain_two = small_row(0, count), small_row(count, count)
        kept.shift_one, kept.shift_two = small_row(2 * count, count), small_row(3 * count, count)
        kept.shift_down = small_row(4 * count, count)
        kept.bias_up = small_row(5 * count, FF // 2 // LANES)
        normed[...] = (hat * kept.gain_one + kept.shift_one).astype(BF16)
        normed_hat[...] = hat[:rows]
        inverse[...] = scale[:rows]
        kept.normed_pair = hand_over(normed, their_normed)

    def project():
        arrived(0)
        for half in range(2):
            for tile, width in tile_groups(0):
                at = half * 3 * half_width + tile * LANES
                projected[:, at : at + width * LANES] = dot(
                    normed[...], weight(whole, 0, half, 0, D, tile, width)
                ).astype(BF16)

    def attend_far():
        attend_set(1)
        pack_blocks(send_blocks.at[1], attended[1], lses[1])
        exchange(1)

    def mix():
        exchanged(1)
        far_out = unpack_values(recv_blocks.at[1])
        near_out = attended[0]
        kept.share = jax.nn.sigmoid(lses[0] - unpack_extra(recv_blocks.at[1]))
        kept.shares = to_columns(kept.share)
        kept.difference = near_out - far_out
        mixture[...] = (kept.shares * near_out + (1.0 - kept.shares) * far_out).astype(BF16)
        kept.mixture_pair = hand_over(mixture, their_mixture)

    def feed():
        arrived(1)
        arrived(2)
        kept.middle = inputs + jnp.concatenate(
            [dot(mixture[...], weight(whole, 1, half, 0, D, 0, third_rows)) for half in range(2)],
            axis=1,
        )
        hat, scale = normalize(kept.middle)
        second_hat[...] = hat
        second_inverse[...] = scale
        second_in[...] = (hat * kept.gain_two + kept.shift_two).astype(BF16)
        kept.second_in_pair = hand_over(second_in, their_second)
        root = (2.0 / 3.141592653589793) ** 0.5
        for half in range(2):
            for tile, width in tile_groups(2):
                at = half * FF // 2 + tile * LANES
                to = slice(at, at + width * LANES)
                v = dot(second_in[...], weight(whole, 2, half, 0, D, tile, width))
                v = v + kept.bias_up[:, to]
                square = v * v
                t = jnp.tanh(root * (v + 0.044715 * v * square))
                activated[:, to] = (0.5 * v * (1.0 + t)).astype(BF16)
                slope[:, to] = 0.5 * (1.0 + t) + 0.5 * v * (1.0 - t * t) * (
                    root * (1.0 + 3 * 0.044715 * square)
                )
        kept.activated_pair = hand_over(activated, their_activated)

    block = 256

    def feed_back():
        for plane in range(3, planes):
            arrived(plane)
        sums = []
        for start in range(0, FF, block):
            to = slice(start, start + block)
            pulled = sum(
                dot_cols(down_grad[half], weight(whole, 3, half, start, block, 0, third_rows))
                for half in range(2)
            )
            grad = (pulled * slope[:, to]).astype(BF16)
            half, at = divmod(start, FF // 2)
            up_grad[half, :, at : at + block] = grad
            sums.append(jnp.sum(grad.astype(F32), axis=0, keepdims=True))
        kept.up_sum = jnp.concatenate(sums, axis=1)
        kept.up_grad_pair = hand_over(up_grad.at[1 - g], their_up)

    def down_weights():
        kept.down_grad_pair.wait()
        kept.activated_pair.wait()
        for first in range(0, FF, D):
            weight_grad(3, activated, their_activated, down_grad, their_down, first, D)

    def through(left, index, tiles_to):
        return jnp.concatenate(
            [
                sum(
                    dot_cols(left[half], weight(whole, index, half, start, block, 0, tiles_to))
                    for half in range(2)
                )
                for start in range(0, D, block)
            ],
            axis=1,
        )

    def mix_back():
        second_grad = through(up_grad, 2, TILES[2])
        hat = second_hat[...]
        kept.gain_two_sum = jnp.sum(second_grad * hat, axis=0, keepdims=True)
        kept.shift_two_sum = jnp.sum(second_grad, axis=0, keepdims=True)
        gained = kept.upstream + norm_back(second_grad * kept.gain_two, hat, second_inverse[...])
        middle_grad[...] = gained
        for half in range(2):
            out_grad[half] = gained[:, half * half_width : (half + 1) * half_width].astype(BF16)
        kept.out_grad_pair = hand_over(out_grad.at[1 - g], their_out)
        mix_grad = through(out_grad, 1, third_rows)
        share, shares = kept.share, kept.shares
        near_lse_grad = share * (1.0 - share) * to_heads(kept.difference * mix_grad)
        lse_grads[0] = near_lse_grad
        near_grad[...] = (shares * mix_grad).astype(BF16)
        pack_blocks(send_blocks.at[2], (1.0 - shares) * mix_grad, -near_lse_grad)
        exchange(2)

    def up_weights():
        kept.second_in_pair.wait()
        kept.up_grad_pair.wait()
        weight_grad(2, second_in, their_second, up_grad, their_up, 0, D)

    def out_weights():
        kept.mixture_pair.wait()
        kept.out_grad_pair.wait()
        weight_grad(1, mixture, their_mixture, out_grad, their_out, 0, D)

    def put_output():
        result = kept.middle + kept.shift_down + jnp.concatenate(
            [
                dot(activated[...], weight(whole, 3, half, 0, FF, 0, third_rows))
                for half in range(2)
            ],
            axis=1,
        )
        output[...] = in_order(result).astype(BF16)

    def far_back():
        exchanged(2)
        far_grad[...] = unpack_values(recv_blocks.at[2]).astype(BF16)
        lse_grads[1] = unpack_extra(recv_blocks.at[2])
        attend_set_back(1, far_grad)
        kept.qkv_grad_pair = hand_over(qkv_grad.at[1 - g], their_qkv)

    def project_back():
        kept.first_grad = through(qkv_grad, 0, TILES[0])
        pack_blocks(send_blocks.at[3], kept.first_grad[rows:], None)
        exchange(3)

    def qkv_weights():
        kept.normed_pair.wait()
        kept.qkv_grad_pair.wait()
        weight_grad(0, normed, their_normed, qkv_grad, their_qkv, 0, D)

    def put_input_grad():
        exchanged(3)
        first_grad = kept.first_grad[:rows] + unpack_values(recv_blocks.at[3])
        hat = normed_hat[...]
        kept.gain_one_sum = jnp.sum(first_grad * hat, axis=0, keepdims=True)
        kept.shift_one_sum = jnp.sum(first_grad, axis=0, keepdims=True)
        input_grad[...] = in_order(
            middle_grad[...] + norm_back(first_grad * kept.gain_one, hat, inverse[...])
        )

    def small_sums():
        for half in range(2):
            to = slice(half * half_width, (half + 1) * half_width)
            down_sum = jnp.sum(down_grad[half].astype(F32), axis=0, keepdims=True)
            sums = (kept.gain_one_sum, kept.gain_two_sum, kept.shift_one_sum, kept.shift_two_sum)
            listed = [one[:, to] for one in sums] + [down_sum]
            listed.append(kept.up_sum[:, half * FF // 2 : (half + 1) * FF // 2])
            at = 0
            for vector in listed:
                count = vector.shape[1] // LANES
                small_parts[half, at : at + count, :] = vector.reshape(count, LANES)
                at += count
            small_parts[half, at:, :] = jnp.zeros((SMALL_ROWS - at, LANES), F32)
        kept.small_pair = hand_over(small_parts.at[1 - g], their_small)
        kept.small_pair.wait()
        small_parts[g] = small_parts[g] + their_small[...]
        pl.when(s != ways - 1)(lambda: small_home().start())

    leave(1, False)
    early(order[0], 1)
    early(order[0], 0)
    leave(1, True)
    leave(0, False)
    turn_piece(order[0], late)
    turn_piece(order[0], 1)
    direct(order[0], 1)
    direct(order[0], 0)
    enter_plane(order[1], 1)
    early(order[1], 1)
    turn_piece(order[0], 0)
    enter_plane(order[2], 1)
    enter_plane(order[1], 0)
    early(order[1], 0)
    early(order[2], 1)
    late_own()
    direct(order[1], 1)
    finish(order[0], late)
    turn_piece(order[1], 1)
    norm()
    direct(order[1], 0)
    enter_plane(order[2], 0)
    early(order[2], 0)
    turn_piece(order[1], 0)
    finish(order[0], 0)
    enter_plane(order[3], 1)
    early(order[3], 1)
    direct(order[2], 0)
    turn_piece(order[2], 1)
    direct(order[2], 1)
    finish(order[0], 1)
    late_on(order[1])
    finish(order[1], 1)
    leave(0, True)
    late_on(order[2])
    turn_piece(order[2], 0)
    finish(order[1], late)
    finish(order[1], 0)
    enter_plane(order[3], 0)
    early(order[3], 0)
    turn_piece(order[3], 1)
    direct(order[3], 1)
    project()
    attend_far()
    finish(order[2], late)
    finish(order[2], 1)
    attend_set(0)
    finish(order[2], 0)
    direct(order[3], 0)
    turn_piece(order[3], 0)
    late_on(order[3])
    finish(order[3], 1)
    finish(order[3], late)
    mix()
    finish(order[3], 0)
    feed()
    down_weights()
    late_start(3)
    out_keep(3, 0)
    out_ahead(3, 0)
    out_ahead(3, 1)
    feed_back()
    mix_back()
    up_weights()
    out_ahead(2, 1)
    late_start(2)
    out_ahead(2, 0)
    out_pass(3, 0)
    attend_set_back(0, near_grad)
    out_take(3, 0)
    out_weights()
    out_keep(3, 1)
    out_ahead(1, 0)
    late_start(1)
    out_keep(2, 1)
    late_relay(3)
    out_pass(3, 1)
    out_keep(2, 0)
    out_pass(2, 0)
    out_pass(2, 1)
    far_back()
    late_relay(2)
    out_take(3, 1)
    late_relay(1)
    qkv_weights()
    late_start(0)
    out_ahead(0, 1)
    late_home(3)
    out_join(3, 0)
    out_join(3, 1)
    out_take(2, 0)
    out_take(2, 1)
    out_ahead(0, 0)
    out_keep(0, 0)
    project_back()
    out_join(2, 0)
    out_pass(0, 0)
    out_keep(0, 1)
    out_relay(3, 0)
    put_output()
    out_take(0, 0)
    late_home(2)
    out_pass(0, 1)
    out_relay(3, 1)
    late_home(1)
    out_relay(2, 0)
    late_relay(0)
    out_join(2, 1)
    out_ahead(2, late)
    out_ahead(1, late)
    out_keep(1, 0)
    out_join(0, 0)
    put_input_grad()
    out_ahead(1, 1)
    out_relay(0, 0)
    out_pass(1, late)
    out_take(0, 1)
    out_relay(2, 1)
    out_keep(2, late)
    out_join(0, 1)
    out_keep(1, late)
    out_pass(1, 0)
    out_take(1, 0)
    out_relay(0, 1)
    out_keep(1, 1)
    out_pass(1, 1)
    small_sums()
    out_take(1, late)
    out_ahead(3, late)
    late_home(0)
    out_join(1, 0)
    out_keep(0, late)
    out_keep(3, late)
    out_ahead(0, late)
    out_pass(2, late)
    out_relay(1, 0)
    out_take(1, 1)
    out_join(1, 1)
    out_relay(1, 1)
    out_take(2, late)
    out_pass(3, late)
    out_join(2, late)
    out_pass(0, late)
    out_join(1, late)
    out_take(0, late)
    out_take(3, late)
    out_join(3, late)
    out_join(0, late)
    everything = [(part, piece) for piece in range(PIECES + 1) for part in range(2)]
    out_last(everything[:1])
    settle_first()
    out_last(everything[1:])
    settle()
    pl.when(s != ways - 1)(lambda: small_home().wait_send())
    gather_sent()
    small_sent()
    out_sent()


def bounds_total():
    return 5 * D // 2 + FF // 2


def run_step(tokens, cotangent, holes, lengths, master, ways):
    rows = tokens.shape[0]
    own = MAT_ROWS // ways
    entries = (MAT_ROWS * LANES + bounds_total()) // ways
    half_own = own // 2
    planes = ways // 4
    vmem = pl.BlockSpec(memory_space=pltpu.VMEM)
    dma = pltpu.SemaphoreType.DMA
    half = D // 2
    shapes = [
        ((2, MAT_ROWS, LANES), BF16),
        ((MAT_ROWS, LANES), BF16),
        ((2, SMALL_ROWS, LANES), BF16),
        ((1, (own + SMALL_ROWS) * LANES), F32),
        ((1, entries % LANES), F32),
        ((SMALL_ROWS + 184, LANES), F32),
        ((own + SMALL_ROWS, LANES), F32),
        ((SMALL_ROWS, LANES), F32),
        ((D // LANES, rows, LANES), F32),
        ((4, ways, 16, half + LANES), BF16),
        ((4, ways, 16, half + LANES), BF16),
        ((2, rows, rows), F32),
        ((2 * rows, D), BF16),
        ((rows, D), F32),
        ((rows, 1), F32),
        ((2 * rows, 3 * D), BF16),
        ((2, rows, D), F32),
        ((2, rows, HEADS), F32),
        ((rows, D), BF16),
        ((rows, D), BF16),
        ((rows, FF), BF16),
        ((rows, FF), F32),
        ((rows, D), F32),
        ((rows, 1), F32),
        ((rows, D), F32),
        ((2, 2 * rows, 3 * half), BF16),
        ((2, rows, half), BF16),
        ((2, rows, FF // 2), BF16),
        ((2, rows, half), BF16),
        ((rows, D), BF16),
        ((rows, D), BF16),
        ((2, rows, HEADS), F32),
        ((2 * rows, D), BF16),
        ((rows, D), BF16),
        ((rows, D), BF16),
        ((rows, FF), BF16),
        ((2 * rows, 3 * half), BF16),
        ((rows, half), BF16),
        ((rows, FF // 2), BF16),
        ((rows, half), BF16),
        ((2, SMALL_ROWS, LANES), F32),
        ((SMALL_ROWS, LANES), F32),
        ((planes, 2, 2, PIECES + 1, half_own // PIECES, LANES), BF16),
        ((planes, 2, PIECES + 1, half_own // PIECES, LANES), BF16),
        ((2, planes, 2, PIECES, half_own // PIECES, LANES), BF16),
        ((2, planes, 2, 4, max(LATE_OUT), LANES), BF16),
        ((16 * max(TILES), LANES), F32),
        ((SMALL_ROWS, LANES), F32),
        ((ways, SMALL_ROWS, LANES), F32),
    ]
    return pl.pallas_call(
        partial(step_kernel, ways),
        out_shape=(
            jax.ShapeDtypeStruct((rows, D), BF16),
            jax.ShapeDtypeStruct((rows, D), F32),
            jax.ShapeDtypeStruct((own, LANES), F32),
            jax.ShapeDtypeStruct((SMALL_ROWS, LANES), F32),
        ),
        in_specs=[
            vmem, vmem, vmem, pl.BlockSpec(memory_space=pltpu.SMEM), pl.BlockSpec(memory_space=pl.ANY),
        ],
        out_specs=(vmem,) * 4,
        scratch_shapes=[pltpu.VMEM(*shape) for shape in shapes]
        + [
            dma((2,)), dma((2,)),
            dma((2, planes, 5, PIECES + 1)), dma((2, ways, PIECES + 1)),
            dma((2, planes, 2)), dma((planes, 2)),
            dma((planes, 2, PIECES + 1)), dma((planes, 2, PIECES + 1)),
            dma((ways,)), dma((2,)),
            dma((4,)), dma((4,)), dma((9,)), dma((9,)),
            dma((planes, 2, 2, PIECES + 1)), dma((planes, 2, 2, PIECES + 1)),
            dma((planes, 2, PIECES + 1)), dma((planes, 2, PIECES + 1)),
            dma((planes, 2, PIECES)), dma((2, planes, 2, PIECES)),
            dma((planes, 2)), dma((2, planes, 2)),
            dma((2,)), dma((2,)),
        ],
        compiler_params=pltpu.CompilerParams(
            collective_id=1, has_side_effects=True, vmem_limit_bytes=VMEM_BYTES
        ),
        name="run_step",
    )(tokens, cotangent, holes, lengths, master)


def rates_at(at):
    values = (
        0.7 * (2.0 / D) ** 0.5, 0.7 * (24.0 / D) ** 0.5, 0.7 * (1.0 / D) ** 0.5, 0.7 * (1.0 / FF) ** 0.5,
        0.15, 0.2,
    )
    rates = values[5]
    for edge, value in reversed(list(zip(bounds(), values))):
        rates = jnp.where(at < edge, jnp.float32(value), rates)
    return rates, jnp.where(at < bounds()[3], jnp.float32(0.1), jnp.float32(0.0))


def adam_kernel(
    tiled, after_rows, master, first_moment, second_moment, layer_output, layer_grad,
    new_moment, new_second, new_master, output, input_grad, kept, last, kept_output, kept_grad,
    kept_tiled, laid, load_sem, store_sem, pass_sem, grad_sem,
):
    size = master.shape[1]
    full, rest = divmod(size, LANES)
    own, step = tiled.shape[0], 56
    chunks = own // UNIT
    edges = [(UNIT * c - SMALL_ROWS) // step * step for c in range(1, chunks)]
    edges = [0] + edges + [full]
    spans = [(first, end - first) for first, end in zip(edges, edges[1:])]
    sources, targets = (first_moment, second_moment, master), (new_moment, new_second, new_master)

    def piece(array, first, count):
        return array.at[:, pl.ds(first * LANES, count * LANES)].reshape(count, LANES)

    def load(which, index):
        first, count = spans[index]
        return pltpu.make_async_copy(
            piece(sources[which], first, count), kept.at[which, pl.ds(first, count)],
            load_sem.at[which, index],
        )

    def store(which, index):
        first, count = spans[index]
        return pltpu.make_async_copy(
            kept.at[which, pl.ds(first, count)], piece(targets[which], first, count),
            store_sem.at[which, index],
        )

    def load_last(which):
        return pltpu.make_async_copy(
            sources[which].at[:, pl.ds(full * LANES, rest)], last.at[which], load_sem.at[which, chunks]
        )

    def store_last(which):
        return pltpu.make_async_copy(
            last.at[which], targets[which].at[:, pl.ds(full * LANES, rest)], store_sem.at[which, chunks]
        )

    passed = tuple(
        (
            pltpu.make_async_copy(source, through, pass_sem.at[index]),
            pltpu.make_async_copy(through, target, pass_sem.at[index]),
        )
        for index, (source, through, target) in enumerate(
            ((layer_output, kept_output, output), (layer_grad, kept_grad, input_grad))
        )
    )
    after = pltpu.make_async_copy(
        after_rows, laid.at[pl.ds(own, SMALL_ROWS)], grad_sem.at[chunks]
    )

    def unit_in(unit):
        span = pl.ds(unit * UNIT, UNIT)
        return pltpu.make_async_copy(tiled.at[span], kept_tiled.at[span], grad_sem.at[unit])

    for index in range(chunks):
        unit_in(index).start()
        for which in range(3):
            load(which, index).start()
    after.start()
    for which in range(3):
        load_last(which).start()
    for copy, _ in passed:
        copy.start()
    s = lax.axis_index("seq")
    origin = s * size
    shift = s * (size - own * LANES)
    row_shift, lane_shift = shift // LANES, lax.rem(shift, LANES)
    back = lax.rem(LANES - lane_shift, LANES)

    def gradients(first, count):
        here = laid[pl.ds(first + row_shift, count), :]
        after = laid[pl.ds(first + row_shift + 1, count), :]
        lanes = lax.broadcasted_iota(jnp.int32, (count, LANES), 1)
        return jnp.where(lanes < LANES - lane_shift, here, after)


    def update(at, moment, second, weights, gradient):
        rates, decays = rates_at(at)
        moment = BETA_ONE * moment + (1.0 - BETA_ONE) * gradient
        second = BETA_TWO * second + (1.0 - BETA_TWO) * gradient * gradient
        scaled = moment * (1.0 / (1.0 - BETA_ONE**STEP))
        change = scaled / (jnp.sqrt(second * (1.0 / (1.0 - BETA_TWO**STEP))) + EPS_ADAM)
        return moment, second, weights - rates * (change + decays * weights)

    laid[own + SMALL_ROWS :, :] = jnp.zeros((laid.shape[0] - own - SMALL_ROWS, LANES), F32)

    def lay(unit):
        def groups(count):
            for group in range(UNIT // (16 * count)):
                lay_group(kept_tiled, laid, unit * UNIT, group, count, back)

        unit_tiles(s * (own // UNIT) + unit, groups)

    for index, (first, count) in enumerate(spans):
        unit_in(index).wait()
        lay(index)
        if index == chunks - 1:
            after.wait()
            laid[own : own + SMALL_ROWS, :] = pltpu.roll(laid[own : own + SMALL_ROWS, :], back, 1)
        for which in range(3):
            load(which, index).wait()

        def run(index, carry, first=first):
            where = pl.multiple_of(first + index * step, 8)
            span = pl.ds(where, step)
            start = origin + where * LANES
            end = start + step * LANES - 1
            edge_list = bounds()
            cut = (start < edge_list[0]) & (end >= edge_list[0])
            for edge in edge_list[1:]:
                cut = cut | ((start < edge) & (end >= edge))

            def put(at):
                found = update(at, *(kept[which, span, :] for which in range(3)), gradients(where, step))
                for which in range(3):
                    kept[which, span, :] = found[which]

            pl.when(jnp.logical_not(cut))(lambda: put(start))

            @pl.when(cut)
            def _():
                row = lax.broadcasted_iota(jnp.int32, (step, LANES), 0)
                put(start + row * LANES + lax.broadcasted_iota(jnp.int32, (step, LANES), 1))

            return carry

        lax.fori_loop(0, -(-count // step), run, 0)
        for which in range(3):
            store(which, index).start()
        if index == 0:
            for copy, onward in passed:
                copy.wait()
                onward.start()
    for which in range(3):
        load_last(which).wait()
    moment, second, weights = (last[which] for which in range(3))
    at = origin + full * LANES + lax.broadcasted_iota(jnp.int32, (1, rest), 1)
    found = update(at, moment, second, weights, gradients(full, 8)[:1, :rest])
    for which in range(3):
        last[which] = found[which]
        store_last(which).start()
    for which in range(3):
        for index in range(chunks):
            store(which, index).wait()
        store_last(which).wait()
    for _, copy in passed:
        copy.wait()


def run_adam(tiled, after_rows, master, first_moment, second_moment, layer_output, layer_grad):
    size = master.shape[1]
    anywhere = pl.BlockSpec(memory_space=pl.ANY)
    return pl.pallas_call(
        adam_kernel,
        out_shape=(jax.ShapeDtypeStruct((1, size), F32),) * 3
        + tuple(jax.ShapeDtypeStruct(one.shape, one.dtype) for one in (layer_output, layer_grad)),
        in_specs=[anywhere] * 7,
        out_specs=(anywhere,) * 5,
        scratch_shapes=[
            pltpu.VMEM((3, -(-size // (8 * LANES)) * 8, LANES), F32),
            pltpu.VMEM((3, 1, size % LANES), F32),
            pltpu.VMEM(layer_output.shape, layer_output.dtype),
            pltpu.VMEM(layer_grad.shape, layer_grad.dtype),
            pltpu.VMEM(tiled.shape, F32),
            pltpu.VMEM((tiled.shape[0] + 2 * SMALL_ROWS, LANES), F32),
            pltpu.SemaphoreType.DMA((3, tiled.shape[0] // UNIT + 1)),
            pltpu.SemaphoreType.DMA((3, tiled.shape[0] // UNIT + 1)),
            pltpu.SemaphoreType.DMA((2,)),
            pltpu.SemaphoreType.DMA((tiled.shape[0] // UNIT + 1,)),
        ],
        compiler_params=pltpu.CompilerParams(vmem_limit_bytes=VMEM_BYTES),
        name="run_adam",
    )(tiled, after_rows, master, first_moment, second_moment, layer_output, layer_grad)


def on_device(tokens, cotangent, holes, slide_lengths, master, first_moment, second_moment):
    ways = lax.axis_size("seq")
    output, input_grad, tiled, after_rows = run_step(
        tokens[0], cotangent[0], holes, slide_lengths, master, ways
    )
    new_moment, new_second, new_master, output, input_grad = run_adam(
        tiled, after_rows, master, first_moment, second_moment, output, input_grad
    )
    return (output[None], input_grad[None], new_moment, new_second, new_master)


def even(mesh):
    ways = mesh.shape["seq"]
    return ways % 4 == 0 and MAT_ROWS % (ways * UNIT) == 0 and ways * 8 == LANES


def solution(mesh):
    return jax.shard_map(
        on_device if even(mesh) else plain_on_device,
        mesh=mesh,
        in_specs=(
            P("grp", "seq", None),
            P("grp", "seq", None),
            P("grp", "seq"),
            P("grp", None),
            P("grp", "seq"),
            P("grp", "seq"),
            P("grp", "seq"),
        ),
        out_specs=(
            P("grp", "seq", None),
            P("grp", "seq", None),
            P("grp", "seq"),
            P("grp", "seq"),
            P("grp", "seq"),
        ),
        check_vma=False,
    )
```

```python
from functools import partial
from types import SimpleNamespace

import jax
import jax.numpy as jnp
from jax import lax
from jax.experimental import pallas as pl
from jax.experimental.pallas import tpu as pltpu
from jax.sharding import PartitionSpec as P

D = 768
FF = 3072
HEADS = 16
HEAD = 48
STEP = 10


EPS_NORM = 1e-05
EPS_ADAM = 1e-08
BETA_ONE = 0.9
BETA_TWO = 0.95


def as_sent(array):
    return jax.tree.map(lambda a: a.astype(jnp.bfloat16) if a.dtype == jnp.float32 else a, array)


def bounds():
    qkv_edge = 3 * D * D // 2
    out_edge = qkv_edge + D * D // 2
    up_edge = out_edge + D * FF // 2
    down_edge = up_edge + FF * D // 2
    gain_edge = down_edge + D
    return (qkv_edge, out_edge, up_edge, down_edge, gain_edge)


def per_segment(flat_index, values):
    edge_list = bounds()
    result = jnp.full(flat_index.shape, values[5], jnp.float32)
    for position in range(4, -1, -1):
        result = jnp.where(flat_index < edge_list[position], jnp.float32(values[position]), result)
    return result


def unpack(flat):
    edge_list = bounds()
    total = flat.shape[1]

    def joined(start, stop, shape):
        return jnp.concatenate(
            [flat[0, start:stop].reshape(shape), flat[1, start:stop].reshape(shape)], axis=-1
        )

    w_qkv = joined(0, edge_list[0], (D, 3 * D // 2))
    w_out = joined(edge_list[0], edge_list[1], (D, D // 2))
    w_up = joined(edge_list[1], edge_list[2], (D, FF // 2))
    w_down = joined(edge_list[2], edge_list[3], (FF, D // 2))
    gain_rows = joined(edge_list[3], edge_list[4], (2, D // 2))
    shift_rows = joined(edge_list[4], edge_list[4] + 3 * D // 2, (3, D // 2))
    bias_up = joined(edge_list[4] + 3 * D // 2, total, (FF // 2,))
    return (w_qkv, w_out, w_up, w_down, gain_rows, shift_rows, bias_up)


def normalize(values):
    centered = values - jnp.mean(values, axis=-1, keepdims=True)
    inverse = lax.rsqrt(jnp.mean(centered * centered, axis=-1, keepdims=True) + EPS_NORM)
    return (centered * inverse, inverse)


def norm_back(grad_hat, normed_hat, inverse):
    return inverse * (
        grad_hat
        - jnp.mean(grad_hat, axis=-1, keepdims=True)
        - normed_hat * jnp.mean(grad_hat * normed_hat, axis=-1, keepdims=True)
    )


def contract_rows(left, right):
    return lax.dot_general(
        left, right, (((0,), (0,)), ((), ())), preferred_element_type=jnp.float32
    )


def contract_cols(left, right):
    return lax.dot_general(
        left, right, (((1,), (1,)), ((), ())), preferred_element_type=jnp.float32
    )


def slide_index(positions, slide_ends):
    return jnp.sum((positions[:, None] >= slide_ends[None, :]).astype(jnp.int32), axis=1)


def split_heads(block_rows):
    return block_rows.reshape(block_rows.shape[0], HEADS, HEAD).transpose(1, 0, 2)


def join_heads(stacked):
    return stacked.transpose(1, 0, 2).reshape(stacked.shape[1], HEADS * HEAD)


def allowance(slides, present):
    token_count = slides.shape[0]
    same_slide = (slides[:, None] == slides[None, :]) & (present[None, :] > 0)
    return same_slide | jnp.eye(token_count, dtype=bool)


def attend(packed, slides, present):
    allowed = allowance(slides, present)
    scale = HEAD ** (-0.5)

    def one_head(pieces):
        query_head, key_head, value_head = pieces
        scores = contract_cols(query_head, key_head) * scale
        scores = jnp.where(allowed, scores, -1000000000.0)
        row_max = jnp.max(scores, axis=-1, keepdims=True)
        exponent = jnp.exp(scores - row_max)
        denominator = jnp.sum(exponent, axis=-1, keepdims=True)
        attention = (exponent / denominator).astype(jnp.bfloat16)
        result = jnp.dot(attention, value_head, preferred_element_type=jnp.float32)
        return (result, (row_max + jnp.log(denominator))[:, 0])

    outs, lses = lax.map(
        one_head,
        (
            split_heads(packed[:, :D]),
            split_heads(packed[:, D : 2 * D]),
            split_heads(packed[:, 2 * D :]),
        ),
    )
    return (join_heads(outs), lses.T)


def attend_back(packed, slides, present, lse_rows, out_grad, lse_grad):
    allowed = allowance(slides, present)
    scale = HEAD ** (-0.5)

    def one_head(pieces):
        query_head, key_head, value_head, lse_head, grad_head, extra_lse = pieces
        scores = contract_cols(query_head, key_head) * scale
        scores = jnp.where(allowed, scores, -1000000000.0)
        attention = jnp.exp(scores - lse_head[:, None])
        prob_grad = contract_cols(grad_head, value_head)
        inner_sum = jnp.sum(attention * prob_grad, axis=-1, keepdims=True)
        score_grad = (attention * (prob_grad - inner_sum + extra_lse[:, None])).astype(jnp.bfloat16)
        query_grad = jnp.dot(score_grad, key_head, preferred_element_type=jnp.float32) * scale
        key_grad = contract_rows(score_grad, query_head) * scale
        value_grad = contract_rows(attention.astype(jnp.bfloat16), grad_head)
        return (query_grad, key_grad, value_grad)

    query_grad, key_grad, value_grad = lax.map(
        one_head,
        (
            split_heads(packed[:, :D]),
            split_heads(packed[:, D : 2 * D]),
            split_heads(packed[:, 2 * D :]),
            lse_rows.T,
            split_heads(out_grad),
            lse_grad.T,
        ),
    )
    return jnp.concatenate(
        [join_heads(query_grad), join_heads(key_grad), join_heads(value_grad)], axis=1
    )


def adam_update(weights, moment, second, gradient, flat_index):
    step_rates = per_segment(
        flat_index,
        (
            0.7 * (2.0 / D) ** 0.5,
            0.7 * (24.0 / D) ** 0.5,
            0.7 * (1.0 / D) ** 0.5,
            0.7 * (1.0 / FF) ** 0.5,
            0.15,
            0.2,
        ),
    )
    decays = per_segment(flat_index, (0.1, 0.1, 0.1, 0.1, 0.0, 0.0))
    new_moment = BETA_ONE * moment + (1.0 - BETA_ONE) * gradient
    new_second = BETA_TWO * second + (1.0 - BETA_TWO) * gradient * gradient
    fix_one = 1.0 - BETA_ONE**STEP
    fix_two = 1.0 - BETA_TWO**STEP
    update = new_moment / fix_one / (jnp.sqrt(new_second / fix_two) + EPS_ADAM)
    return (new_moment, new_second, weights - step_rates * (update + decays * weights))


def column_halves(values):
    return values.reshape(values.shape[0], 2, values.shape[1] // 2)


def plain_on_device(tokens, cotangent, holes, slide_lengths, master, first_moment, second_moment):
    own_half = lax.all_gather(master.astype(jnp.bfloat16), "seq", axis=1, tiled=True)
    whole_flat = lax.all_gather(own_half, "grp", axis=0, tiled=True)
    w_qkv, w_out, w_up, w_down, gain_rows, shift_rows, bias_up = unpack(whole_flat)
    gain_rows = gain_rows.astype(jnp.float32)
    shift_rows = shift_rows.astype(jnp.float32)
    bias_up = bias_up.astype(jnp.float32)
    inputs = tokens[0].astype(jnp.float32)
    row_count = inputs.shape[0]
    seq_ways = lax.axis_size("seq")
    seq_place = lax.axis_index("seq")
    row_steps = jnp.arange(row_count, dtype=jnp.int32)
    slide_ends = jnp.cumsum(slide_lengths[0])
    near_slides = slide_index(seq_place * row_count + row_steps, slide_ends)
    far_slides = slide_index(seq_place + seq_ways * row_steps, slide_ends)
    near_present = holes[0]
    strided_shape = (row_count // seq_ways, seq_ways)

    def to_strided(packed):
        moved, moved_mask = (
            lax.all_to_all(
                packed.reshape(strided_shape + (3 * D,)),
                "seq",
                split_axis=1,
                concat_axis=0,
                tiled=True,
            ),
            lax.all_to_all(
                near_present.astype(jnp.bfloat16).reshape(strided_shape + (1,)),
                "seq",
                split_axis=1,
                concat_axis=0,
                tiled=True,
            ),
        )
        return (moved.reshape(row_count, 3 * D), moved_mask.reshape(row_count).astype(jnp.int32))

    normed_one, inverse_one = normalize(inputs)
    normed = (normed_one * gain_rows[0] + shift_rows[0]).astype(jnp.bfloat16)
    projected = jnp.dot(normed, w_qkv, preferred_element_type=jnp.float32).astype(jnp.bfloat16)
    near_out, near_lse = attend(projected, near_slides, near_present)
    far_proj, far_present = to_strided(projected)
    far_local, far_local_lse = attend(far_proj, far_slides, far_present)
    returned = (
        lax.all_to_all(
            far_local.reshape(row_count, 1, D).astype(jnp.bfloat16),
            "seq",
            split_axis=0,
            concat_axis=1,
            tiled=True,
        ).astype(jnp.float32),
        lax.all_to_all(
            far_local_lse.reshape(row_count, 1, HEADS).astype(jnp.bfloat16),
            "seq",
            split_axis=0,
            concat_axis=1,
            tiled=True,
        ).astype(jnp.float32),
    )
    far_out = returned[0].reshape(row_count, D)
    far_lse = returned[1].reshape(row_count, HEADS)
    near_share = jax.nn.sigmoid(near_lse - far_lse)
    near_heads = near_out.reshape(row_count, HEADS, HEAD)
    far_heads = far_out.reshape(row_count, HEADS, HEAD)
    mixture = (
        (near_share[:, :, None] * near_heads + (1.0 - near_share[:, :, None]) * far_heads)
        .reshape(row_count, D)
        .astype(jnp.bfloat16)
    )
    middle = inputs + jnp.dot(mixture, w_out, preferred_element_type=jnp.float32)
    normed_two, inverse_two = normalize(middle)
    second_in = (normed_two * gain_rows[1] + shift_rows[1]).astype(jnp.bfloat16)
    hidden = jnp.dot(second_in, w_up, preferred_element_type=jnp.float32) + bias_up
    activated = jax.nn.gelu(hidden, approximate=True).astype(jnp.bfloat16)
    output = middle + jnp.dot(activated, w_down, preferred_element_type=jnp.float32) + shift_rows[2]
    upstream = cotangent[0].astype(jnp.float32)
    down_grad = upstream.astype(jnp.bfloat16)
    grad_act = contract_cols(down_grad, w_down)
    gelu_pull = jax.vjp(partial(jax.nn.gelu, approximate=True), hidden)[1]
    hidden_grad = gelu_pull(grad_act)[0].astype(jnp.bfloat16)
    second_grad = contract_cols(hidden_grad, w_up)
    grad_gain_two = jnp.sum(second_grad * normed_two, axis=0)
    grad_shift_two = jnp.sum(second_grad, axis=0)
    middle_grad = upstream + norm_back(second_grad * gain_rows[1], normed_two, inverse_two)
    attend_grad = middle_grad.astype(jnp.bfloat16)
    mix_grad = contract_cols(attend_grad, w_out).reshape(row_count, HEADS, HEAD)
    near_lse_grad = (
        near_share * (1.0 - near_share) * jnp.sum((near_heads - far_heads) * mix_grad, axis=-1)
    )
    near_grad = (near_share[:, :, None] * mix_grad).reshape(row_count, D).astype(jnp.bfloat16)
    far_grad = ((1.0 - near_share[:, :, None]) * mix_grad).reshape(row_count, D)
    sent = (
        lax.all_to_all(
            as_sent(far_grad.reshape(strided_shape + (D,))),
            "seq",
            split_axis=1,
            concat_axis=0,
            tiled=True,
        ),
        lax.all_to_all(
            as_sent((-near_lse_grad).reshape(strided_shape + (HEADS,))),
            "seq",
            split_axis=1,
            concat_axis=0,
            tiled=True,
        ),
    )
    far_back = sent[0].reshape(row_count, D).astype(jnp.bfloat16)
    far_lse_grad = sent[1].reshape(row_count, HEADS)
    again_proj, again_present = to_strided(projected)
    again_lse = attend(again_proj, far_slides, again_present)[1]
    far_proj_grad = attend_back(
        again_proj, far_slides, again_present, again_lse, far_back, far_lse_grad
    ).astype(jnp.bfloat16)
    far_home = lax.all_to_all(
        far_proj_grad.reshape(row_count, 1, 3 * D), "seq", split_axis=0, concat_axis=1, tiled=True
    ).reshape(row_count, 3 * D)
    near_proj_grad = attend_back(
        projected, near_slides, near_present, near_lse, near_grad, near_lse_grad
    )
    proj_grad = (near_proj_grad + far_home.astype(jnp.float32)).astype(jnp.bfloat16)
    first_grad = contract_cols(proj_grad, w_qkv)
    grad_gain_one = jnp.sum(first_grad * normed_one, axis=0)
    grad_shift_one = jnp.sum(first_grad, axis=0)
    input_grad = middle_grad + norm_back(first_grad * gain_rows[0], normed_one, inverse_one)
    both_rows = (
        lax.all_gather(normed, "grp", axis=0, tiled=True),
        lax.all_gather(mixture, "grp", axis=0, tiled=True),
        lax.all_gather(second_in, "grp", axis=0, tiled=True),
        lax.all_gather(activated, "grp", axis=0, tiled=True),
    )
    moved = (
        lax.all_to_all(column_halves(proj_grad), "grp", split_axis=1, concat_axis=0, tiled=True),
        lax.all_to_all(column_halves(attend_grad), "grp", split_axis=1, concat_axis=0, tiled=True),
        lax.all_to_all(column_halves(hidden_grad), "grp", split_axis=1, concat_axis=0, tiled=True),
        lax.all_to_all(column_halves(down_grad), "grp", split_axis=1, concat_axis=0, tiled=True),
    )
    proj_mine = moved[0].reshape(2 * row_count, 3 * D // 2)
    attend_mine = moved[1].reshape(2 * row_count, D // 2)
    hidden_mine = moved[2].reshape(2 * row_count, FF // 2)
    down_mine = moved[3].reshape(2 * row_count, D // 2)
    norm_sums = lax.psum(
        jnp.stack([grad_gain_one, grad_gain_two, grad_shift_one, grad_shift_two]), "grp"
    )
    half_width = D // 2
    norm_half = lax.dynamic_slice_in_dim(
        norm_sums, lax.axis_index("grp") * half_width, half_width, 1
    )
    grad_w_qkv = contract_rows(both_rows[0], proj_mine)
    grad_w_out = contract_rows(both_rows[1], attend_mine)
    grad_w_up = contract_rows(both_rows[2], hidden_mine)
    grad_w_down = contract_rows(both_rows[3], down_mine)
    grad_bias_down = jnp.sum(down_mine.astype(jnp.float32), axis=0)
    grad_bias_up = jnp.sum(hidden_mine.astype(jnp.float32), axis=0)
    gradient = jnp.concatenate(
        [
            grad_w_qkv.reshape(-1),
            grad_w_out.reshape(-1),
            grad_w_up.reshape(-1),
            grad_w_down.reshape(-1),
            norm_half[0],
            norm_half[1],
            norm_half[2],
            norm_half[3],
            grad_bias_down,
            grad_bias_up,
        ]
    )
    reduced = lax.psum_scatter(gradient, "seq", scatter_dimension=0, tiled=True)
    shard_size = master.shape[1]
    flat_index = lax.axis_index("seq") * shard_size + jnp.arange(shard_size, dtype=jnp.int32)
    new_moment, new_second, new_master = adam_update(
        master[0], first_moment[0], second_moment[0], reduced, flat_index
    )
    return (
        output[None].astype(jnp.bfloat16),
        input_grad[None],
        new_moment[None],
        new_second[None],
        new_master[None],
    )


LANES = 128
BF16 = jnp.bfloat16
F32 = jnp.float32
MAT_ROWS = (3 * D * D + D * D + D * FF + FF * D) // 2 // LANES
SMALL_ROWS = 32
UNIT = 576
PAIR = 2
TILES = (3 * D // 2 // LANES, D // 2 // LANES, FF // 2 // LANES, D // 2 // LANES)
DEPTHS = (D, D, D, FF)
MESH = pl.DeviceIdType.MESH
VMEM_BYTES = 60 * 2**20
NEG = -1000000000.0
ORDERS = ((1, 2, 3), (0, 2, 3), (0, 3, 1), (0, 2, 1))
PIECES = 2
LATE_ROWS = 160
LATE_OUT = (128, 160, 192, 192)


def matrix_starts():
    starts = [0]
    for tiles, depth in zip(TILES, DEPTHS):
        starts.append(starts[-1] + tiles * depth)
    return starts


def place():
    return lax.axis_index("seq"), lax.axis_index("grp")


def greet_all(ways):
    s, g = place()
    barrier = pltpu.get_barrier_semaphore()

    def greet(step, carry):
        pl.semaphore_signal(
            barrier, inc=1, device_id=(lax.rem(s + step, ways), g), device_id_type=MESH
        )
        return carry

    lax.fori_loop(1, ways, greet, 0)
    pl.semaphore_signal(barrier, inc=1, device_id=(s, 1 - g), device_id_type=MESH)
    return barrier


def remote(src, dst, send_sem, recv_sem, to):
    return pltpu.make_async_remote_copy(
        src_ref=src,
        dst_ref=dst,
        send_sem=send_sem,
        recv_sem=recv_sem,
        device_id=to,
        device_id_type=MESH,
    )


def unit_tiles(unit, body):
    edges = [start // UNIT for start in matrix_starts()]
    kinds = {}
    for index, tiles in enumerate(TILES):
        inside = (unit >= edges[index]) & (unit < edges[index + 1])
        kinds[tiles] = kinds[tiles] | inside if tiles in kinds else inside
    for tiles, inside in kinds.items():
        pl.when(inside)(lambda tiles=tiles: body(tiles))


def dot(left, right):
    return jnp.dot(left, right, preferred_element_type=F32)


def dot_cols(left, right):
    return contract_cols(left, right)


def dot_rows(left, right):
    return contract_rows(left, right)


def tile_view(ref, index):
    rows = 16 * TILES[index]
    start = matrix_starts()[index]
    return ref.reshape(ref.shape[:-2] + (MAT_ROWS // rows, rows, LANES)), start // rows


def tile_groups(index):
    tiles = TILES[index]
    groups, at = [], 0
    while at < tiles:
        width = 3 if tiles - at == 3 else 2
        groups.append((at, width))
        at += width
    return groups


def weight(ref, index, half, row, rows, tile, width):
    view, base = tile_view(ref, index)
    first = base + row // 16
    pieces = [
        view[half, first : first + rows // 16, 16 * t : 16 * t + 16, :].reshape(rows, LANES)
        for t in range(tile, tile + width)
    ]
    return jnp.concatenate(pieces, axis=1)


def heads_of(rows):
    row = lax.broadcasted_iota(jnp.int32, (rows, D), 0) * HEAD
    column = lax.broadcasted_iota(jnp.int32, (rows, D), 1)
    return ((column >= row) & (column < row + HEAD)).astype(F32)


def to_columns(per_head):
    return jnp.dot(
        per_head, heads_of(HEADS), precision=lax.Precision.HIGHEST, preferred_element_type=F32
    )


def to_heads(columns):
    return lax.dot_general(
        columns,
        heads_of(HEADS),
        (((1,), (1,)), ((), ())),
        precision=lax.Precision.HIGHEST,
        preferred_element_type=F32,
    )


def pack_blocks(ref, values, extra):
    blocks = values.shape[0] // 8
    split = values.reshape(blocks, 8, D)
    ref[:, :, : D // 2] = jnp.concatenate(
        [split[:, :, : D // 2], split[:, :, D // 2 :]], axis=1
    ).astype(BF16)
    if extra is not None:
        high = extra.astype(BF16).astype(F32)
        low = extra - high
        pieces = jnp.concatenate(
            [high.reshape(blocks, 8, HEADS), low.reshape(blocks, 8, HEADS)], axis=1
        )
        ref[:, :, D // 2 : D // 2 + HEADS] = pieces.astype(BF16)


def unpack_values(ref):
    blocks = ref.shape[0]
    values = ref[:, :, : D // 2].astype(F32)
    return jnp.concatenate(
        [values[:, :8, :].reshape(blocks * 8, D // 2), values[:, 8:, :].reshape(blocks * 8, D // 2)],
        axis=1,
    )


def unpack_extra(ref):
    blocks = ref.shape[0]
    pieces = ref[:, :, D // 2 :].astype(F32)
    both = pieces[:, :8, :] + pieces[:, 8:, :]
    return both.reshape(blocks * 8, LANES)[:, :HEADS]


def slide_masks(ends_ref, s, ways, near_keys, far_keys):
    rows = near_keys.shape[1]
    ends, end = [], 0
    for index in range(ends_ref.shape[1]):
        end = end + ends_ref[0, index]
        ends.append(end)

    def slides(positions):
        total = jnp.zeros(positions.shape, jnp.int32)
        for end in ends:
            total = total + (positions >= end).astype(jnp.int32)
        return total

    across = rows // ways
    result = []
    for far, keys in ((False, near_keys), (True, far_keys)):
        found = []
        for dim in (0, 1):
            at = lax.broadcasted_iota(jnp.int32, (rows, rows), dim)
            if far:
                position = s + ways * at
            else:
                position = rows * s + ways * lax.rem(at, across) + at // across
            found.append(slides(position))
        query = lax.broadcasted_iota(jnp.int32, (rows, rows), 0)
        key = lax.broadcasted_iota(jnp.int32, (rows, rows), 1)
        allowed = ((found[0] == found[1]) & (keys > 0.5)) | (query == key)
        result.append(allowed.astype(F32))
    return result


def lay_group(tiled, laid, first, group, count, turn=None):
    for tile in range(count):
        block = tiled[pl.ds(pl.multiple_of(first + 16 * (group * count + tile), 16), 16), :]
        if turn is not None:
            block = pltpu.roll(block, turn, 1)
        laid[pl.ds(first + group * 16 * count + tile, 16, stride=count), :] = block


def step_kernel(
    ways, tokens, cotangent, holes, lengths, master,
    output, input_grad, total, after_rows,
    whole, grads, small, entries_here, entries_end, extended, aligned, tail,
    turning, send_blocks, recv_blocks, masks, normed, normed_hat, inverse, projected, attended, lses,
    mixture, second_in, activated, slope, second_hat, second_inverse, middle_grad,
    normed_t, mixture_t, second_t, activated_t,
    qkv_grad, out_grad, up_grad, down_grad, near_grad, far_grad, lse_grads,
    their_normed, their_mixture, their_second, their_activated,
    their_qkv, their_out, their_up, their_down, small_parts, their_small,
    by_x, by_y, by_z, by_late, laid, follow_rows, small_all,
    load_sem, tail_sem, slot_send, slot_recv, late_send, late_recv, core_send, core_recv, small_send, small_recv,
    block_send, block_recv, pair_send, pair_recv,
    x_send, x_recv, y_send, y_recv, z_send, z_recv, late_out_send, late_out_recv, end_sem, sum_sem,
):
    s, g = place()
    planes = ways // 4
    z, y, x = s // 4, lax.rem(s // 2, 2), lax.rem(s, 2)
    own = MAT_ROWS // ways
    half_own = own // 2
    rows = tokens.shape[0]
    across = rows // ways
    tiles = D // LANES
    half_width = D // 2
    third_rows = half_width // LANES
    entries = (MAT_ROWS * LANES + bounds_total()) // ways - own * LANES
    shift = entries * s
    row_shift, lane_shift = shift // LANES, lax.rem(shift, LANES)

    def chip(plane, row, column):
        return ((plane * 2 + row) * 2 + column, g)

    def part_at(plane, row, column, part):
        first = ((plane * 2 + row) * 2 + column) * own + part * half_own
        return pl.ds(pl.multiple_of(first, 16), half_own)


    last_row, last_lanes = divmod(own * LANES + entries, LANES)
    step_rows = 176
    full = last_row * LANES
    loads = (
        pltpu.make_async_copy(
            master.at[:, pl.ds(0, full)], entries_here.at[:, pl.ds(0, full)], load_sem.at[0]
        ),
        pltpu.make_async_copy(master.at[:, pl.ds(full, last_lanes)], entries_end, load_sem.at[1]),
    )

    def loaded():
        for load in loads:
            load.wait()
        entries_here[:, full:] = jnp.zeros((1, entries_here.shape[1] - full), F32)
        entries_here[:, full : full + last_lanes] = entries_end[...]

    def flat_rows(first, count):
        if not isinstance(first, int):
            first = pl.multiple_of(first * LANES, LANES)
        else:
            first = first * LANES
        return entries_here[:, pl.ds(first, count * LANES)].reshape(count, LANES)

    def follow_copy():
        return remote(
            tail, extended.at[pl.ds(0, SMALL_ROWS)], tail_sem.at[0], tail_sem.at[1],
            (lax.rem(s + 1, ways), g),
        )

    def make_tail():
        lanes = lax.broadcasted_iota(jnp.int32, (SMALL_ROWS, LANES), 1)
        gap = LANES - last_lanes
        older = pltpu.roll(flat_rows(last_row - SMALL_ROWS, SMALL_ROWS), gap, 1)
        newer = pltpu.roll(flat_rows(last_row - SMALL_ROWS + 1, SMALL_ROWS), gap, 1)
        tail[...] = jnp.where(lanes < gap, older, newer)

    def align(here, before, to):
        lanes = lax.broadcasted_iota(jnp.int32, (step_rows, LANES), 1)
        aligned[pl.ds(pl.multiple_of(to, 8), step_rows), :] = jnp.where(
            lanes >= lane_shift, pltpu.roll(here, lane_shift, 1), pltpu.roll(before, lane_shift, 1)
        )

    def fill(unit):
        first = unit * UNIT

        def tiled(count):
            for group in range(UNIT // (16 * count)):
                for tile in range(count):
                    block = aligned[pl.ds(first + group * 16 * count + tile, 16, stride=count), :]
                    at = s * own + first + 16 * (group * count + tile)
                    whole[g, pl.ds(pl.multiple_of(at, 16), 16), :] = block.astype(BF16)

        unit_tiles(s * (own // UNIT) + unit, tiled)

    def fill_most():
        def align_step(step, carry):
            first = step * step_rows - row_shift
            align(flat_rows(first, step_rows), flat_rows(first - 1, step_rows), step * step_rows)
            return carry

        def fill_unit(unit, carry):
            fill(unit)
            return carry

        extended[SMALL_ROWS:, :] = flat_rows(0, extended.shape[0] - SMALL_ROWS)
        lax.fori_loop(1, (own + SMALL_ROWS) // step_rows, align_step, 0)
        lax.fori_loop(1, own // UNIT, fill_unit, 0)

    def fill_first():
        follow_copy().wait()
        first = SMALL_ROWS - row_shift
        align(extended[pl.ds(first, step_rows), :], extended[pl.ds(first - 1, step_rows), :], 0)
        fill(0)

    order = [z]
    for step in range(1, planes):
        plane = jnp.int32(ORDERS[0][step - 1])
        for at in range(1, planes):
            plane = jnp.where(z == at, ORDERS[at][step - 1], plane)
        order.append(plane)

    part_rows = half_own - LATE_ROWS
    late = PIECES

    def slot_copy(plane, row, column, part, piece, kind, to):
        if piece == late:
            first, count = 2 * part_rows + part * LATE_ROWS, LATE_ROWS
        else:
            count = part_rows // PIECES
            first = part * part_rows + piece * count
        first = ((plane * 2 + row) * 2 + column) * own + first
        where = whole.at[g, pl.ds(pl.multiple_of(first, 16), count)]
        return remote(
            where,
            where,
            slot_send.at[part, plane, kind, piece],
            slot_recv.at[part, (plane * 2 + row) * 2 + column, piece],
            to,
        )

    def line_up(plane, part, piece):
        return slot_copy(plane, y, x, part, piece, 0, chip(z + 1, y, x))

    def line_down(plane, part, piece):
        return slot_copy(plane, y, x, part, piece, 1, chip(z - 1, y, x))

    def to_x(plane, part, piece):
        return slot_copy(plane, y, x, part, piece, 2, chip(z, y, 1 - x))

    def to_y(plane, part, piece):
        return slot_copy(plane, y, x, part, piece, 3, chip(z, 1 - y, x))

    def early(plane, piece):
        to_y(plane, 0, piece).start()
        to_x(plane, 1, piece).start()

    def direct(plane, piece):
        to_x(plane, 0, piece).start()
        to_y(plane, 1, piece).start()

    def turned(plane, piece):
        return (
            slot_copy(plane, 1 - y, x, 0, piece, 4, chip(z, y, 1 - x)),
            slot_copy(plane, y, 1 - x, 1, piece, 4, chip(z, 1 - y, x)),
        )

    def turn_piece(plane, piece):
        for copy in turned(plane, piece):
            copy.wait_recv()
            copy.start()

    def come(plane, piece):
        slot_copy(plane, y, 1 - x, 0, piece, 0, chip(z, y, x)).wait_recv()
        slot_copy(plane, 1 - y, 1 - x, 0, piece, 0, chip(z, y, x)).wait_recv()
        slot_copy(plane, 1 - y, x, 1, piece, 0, chip(z, y, x)).wait_recv()
        slot_copy(plane, 1 - y, 1 - x, 1, piece, 0, chip(z, y, x)).wait_recv()

    def leave(piece, plane_one):
        for part in range(2):

            def up(part=part):
                line_up(z, part, piece).start()

            def down(part=part):
                line_down(z, part, piece).start()

            if plane_one:
                pl.when((z == 1) & (z < planes - 1))(up)
            else:
                pl.when((z != 1) & (z < planes - 1))(up)
                pl.when(z > 0)(down)

    def enter_plane(plane, piece):
        for part in range(2):
            slot_copy(plane, y, x, part, piece, 0, chip(z, y, x)).wait_recv()

            def up(part=part):
                line_up(plane, part, piece).start()

            def down(part=part):
                line_down(plane, part, piece).start()

            pl.when((z > plane) & (z < planes - 1))(up)
            pl.when((z < plane) & (z > 0))(down)

    def late_copy(plane, part, way):
        view = whole.reshape(2, ways, own, LANES)
        where = view.at[
            g, pl.ds(4 * plane, 4), pl.ds(2 * part_rows + part * LATE_ROWS, LATE_ROWS)
        ]
        return remote(
            where, where, late_send.at[way, plane, part], late_recv.at[plane, part],
            chip(z + 1 - 2 * way, y, x),
        )

    def late_own():
        come(z, late)
        for part in range(2):
            pl.when(z < planes - 1)(lambda part=part: late_copy(z, part, 0).start())
            pl.when(z > 0)(lambda part=part: late_copy(z, part, 1).start())

    def late_on(plane):
        for part in range(2):
            late_copy(plane, part, 0).wait_recv()
            pl.when((z > plane) & (z < planes - 1))(
                lambda part=part: late_copy(plane, part, 0).start()
            )
            pl.when((z < plane) & (z > 0))(lambda part=part: late_copy(plane, part, 1).start())

    def to_core(half, plane, part, piece):
        count = LATE_ROWS if piece == late else part_rows // PIECES
        first = 2 * part_rows + part * count if piece == late else part * part_rows + piece * count
        view = whole.reshape(2, ways, own, LANES)
        where = view.at[half, pl.ds(4 * plane, 4), pl.ds(first, count)]
        return remote(
            where, where, core_send.at[plane, part, piece], core_recv.at[plane, part, piece],
            (s, 1 - g),
        )

    def finish(plane, piece):
        if piece != late:
            come(plane, piece)
        for part in range(2):
            to_core(g, plane, part, piece).start()

    def arrived(plane):
        for part in range(2):
            for piece in range(PIECES + 1):
                to_core(1 - g, plane, part, piece).wait_recv()

    def gather_sent():
        for plane in range(planes):
            for part in range(2):
                for piece in range(PIECES):

                    def up(plane=plane, part=part, piece=piece):
                        line_up(plane, part, piece).wait_send()

                    def down(plane=plane, part=part, piece=piece):
                        line_down(plane, part, piece).wait_send()

                    pl.when((z >= plane) & (z < planes - 1))(up)
                    pl.when((z <= plane) & (z > 0))(down)
                    to_x(plane, part, piece).wait_send()
                    to_y(plane, part, piece).wait_send()
                    turned(plane, piece)[part].wait_send()
                to_own = (to_x(z, part, late), to_y(z, part, late), turned(z, late)[part])
                if plane == 0:
                    for copy in to_own:
                        copy.wait_send()
                pl.when((z >= plane) & (z < planes - 1))(
                    lambda plane=plane, part=part: late_copy(plane, part, 0).wait_send()
                )
                pl.when((z <= plane) & (z > 0))(
                    lambda plane=plane, part=part: late_copy(plane, part, 1).wait_send()
                )
            for part in range(2):
                for piece in range(PIECES + 1):
                    to_core(g, plane, part, piece).wait_send()

    def small_to(index):
        return remote(small.at[g], small.at[g], small_send.at[index], small_recv.at[0], (index, g))

    def small_across():
        return remote(
            small.at[g], small.at[g], small_send.at[ways - 1], small_recv.at[1], (s, 1 - g)
        )

    def small_out():
        def tell(index, carry):
            small_to(index).start()
            return carry

        @pl.when(s == ways - 1)
        def _():
            small[g] = aligned[own : own + SMALL_ROWS, :].astype(BF16)
            lax.fori_loop(0, ways - 1, tell, 0)

    def small_in():
        pl.when(s != ways - 1)(lambda: small_to(s).wait_recv())
        small_across().start()
        remote(
            small.at[1 - g], small.at[1 - g], small_send.at[ways - 1], small_recv.at[1], (s, 1 - g)
        ).wait_recv()

    def small_sent():
        def told(index, carry):
            small_to(index).wait_send()
            return carry

        @pl.when(s == ways - 1)
        def _():
            lax.fori_loop(0, ways - 1, told, 0)

        small_across().wait_send()


    def cut(plane, part, piece):
        if piece == late:
            return 2 * (half_own - LATE_OUT[plane]) + part * LATE_OUT[plane], LATE_OUT[plane]
        count = (half_own - LATE_OUT[plane]) // PIECES
        return part * (half_own - LATE_OUT[plane]) + piece * count, count

    def piece_at(plane, row, column, part, piece):
        first, count = cut(plane, part, piece)
        first = ((plane * 2 + row) * 2 + column) * own + first
        return pl.ds(pl.multiple_of(first, 16), count)

    def held(ref, plane, part, piece):
        return ref.at[pl.ds(0, cut(plane, part, piece)[1])]

    def first_copy(plane, part, k, piece):
        where = (k, 1 - x) if part == 0 else (1 - y, k)
        return remote(
            grads.at[piece_at(plane, *where, part, piece)],
            held(by_x.at[plane, part, k, piece], plane, part, piece),
            x_send.at[plane, part, k, piece], x_recv.at[plane, part, k, piece],
            chip(z, y, 1 - x) if part == 0 else chip(z, 1 - y, x),
        )

    def second_copy(plane, part, piece):
        where = (1 - y, x) if part == 0 else (y, 1 - x)
        return remote(
            grads.at[piece_at(plane, *where, part, piece)],
            held(by_y.at[plane, part, piece], plane, part, piece),
            y_send.at[plane, part, piece], y_recv.at[plane, part, piece],
            chip(z, 1 - y, x) if part == 0 else chip(z, y, 1 - x),
        )

    def line_copy(plane, part, piece, way):
        return remote(
            grads.at[piece_at(plane, y, x, part, piece)],
            held(by_z.at[way, plane, part, piece], plane, part, piece),
            z_send.at[plane, part, piece], z_recv.at[way, plane, part, piece],
            chip(z + 1 - 2 * way, y, x),
        )

    def late_out_copy(plane, part, way):
        first, count = cut(plane, part, late)
        view = grads.reshape(ways, own, LANES)
        return remote(
            view.at[pl.ds(4 * plane, 4), pl.ds(first, count)],
            by_late.at[way, plane, part, :, pl.ds(0, count)],
            late_out_send.at[plane, part], late_out_recv.at[way, plane, part],
            chip(z + 1 - 2 * way, y, x),
        )

    def add(where, block):
        grads[where, :] = (grads[where, :].astype(F32) + block[...].astype(F32)).astype(BF16)

    def at_home(plane, piece, act):
        if piece == late:
            pl.when(z == plane)(act)
        else:
            act()

    def out_ahead(plane, piece):
        def act():
            for part in range(2):
                first_copy(plane, part, (1 - y, 1 - x)[part], piece).start()

        at_home(plane, piece, act)

    def out_keep(plane, piece):
        def act():
            for part in range(2):
                first_copy(plane, part, (y, x)[part], piece).start()

        at_home(plane, piece, act)

    def out_pass(plane, piece):
        def act():
            for part in range(2):
                other = (1 - y, 1 - x)[part]
                first_copy(plane, part, other, piece).wait_recv()
                where = (other, x) if part == 0 else (y, other)
                add(
                    piece_at(plane, *where, part, piece),
                    held(by_x.at[plane, part, other, piece], plane, part, piece),
                )
                second_copy(plane, part, piece).start()

        at_home(plane, piece, act)

    def out_take(plane, piece):
        def act():
            for part in range(2):
                mine = (y, x)[part]
                first_copy(plane, part, mine, piece).wait_recv()
                add(
                    piece_at(plane, y, x, part, piece),
                    held(by_x.at[plane, part, mine, piece], plane, part, piece),
                )

        at_home(plane, piece, act)

    def out_join(plane, piece):
        def act():
            for part in range(2):
                second_copy(plane, part, piece).wait_recv()
                add(
                    piece_at(plane, y, x, part, piece),
                    held(by_y.at[plane, part, piece], plane, part, piece),
                )
                if piece != late and plane > 0:
                    pl.when(z == 0)(lambda part=part: line_copy(plane, part, piece, 0).start())
                if piece != late and plane < planes - 1:
                    pl.when(z == planes - 1)(
                        lambda part=part: line_copy(plane, part, piece, 1).start()
                    )

        at_home(plane, piece, act)

    def between(plane, act):
        if plane > 1:
            pl.when((z > 0) & (z < plane))(lambda: act(0))
        if plane < planes - 2:
            pl.when((z > plane) & (z < planes - 1))(lambda: act(1))

    def out_relay(plane, piece):
        for part in range(2):

            def act(way, part=part):
                line_copy(plane, part, piece, way).wait_recv()
                add(
                    piece_at(plane, y, x, part, piece),
                    held(by_z.at[way, plane, part, piece], plane, part, piece),
                )
                line_copy(plane, part, piece, way).start()

            between(plane, act)

    def late_add(plane, part, way):
        late_out_copy(plane, part, way).wait_recv()
        for k in range(4):
            add(
                piece_at(plane, k // 2, k % 2, part, late),
                by_late.at[way, plane, part, k, pl.ds(0, LATE_OUT[plane])],
            )

    def late_start(plane):
        for part in range(2):
            if plane > 0:
                pl.when(z == 0)(lambda part=part: late_out_copy(plane, part, 0).start())
            if plane < planes - 1:
                pl.when(z == planes - 1)(lambda part=part: late_out_copy(plane, part, 1).start())

    def late_relay(plane):
        for part in range(2):

            def act(way, part=part):
                late_add(plane, part, way)
                late_out_copy(plane, part, way).start()

            between(plane, act)

    def late_home(plane):
        @pl.when(z == plane)
        def _():
            for part in range(2):
                if plane > 0:
                    late_add(plane, part, 0)
                if plane < planes - 1:
                    late_add(plane, part, 1)

    def out_sent():
        for plane in range(planes):
            for piece in range(PIECES + (1 if LATE_OUT[plane] else 0)):

                def act(plane=plane, piece=piece):
                    for part in range(2):
                        for k in range(2):
                            first_copy(plane, part, k, piece).wait_send()
                        second_copy(plane, part, piece).wait_send()

                at_home(plane, piece, act)

            @pl.when(z != plane)
            def _(plane=plane):
                for part in range(2):
                    for piece in range(PIECES):
                        line_copy(plane, part, piece, 0).wait_send()
                    if LATE_OUT[plane]:
                        late_out_copy(plane, part, 0).wait_send()

    def out_last(parts):
        for plane in range(planes):

            @pl.when(z == plane)
            def _(plane=plane):
                for part, piece in parts:
                    first, count = cut(plane, part, piece)
                    if not count:
                        continue
                    found = grads[piece_at(plane, y, x, part, piece), :].astype(F32)
                    for way in range(2):
                        if piece != late and (plane > 0 if way == 0 else plane < planes - 1):
                            line_copy(plane, part, piece, way).wait_recv()
                            found = found + by_z[way, plane, part, piece, :count].astype(F32)
                    total[first : first + count, :] = found

    def small_home():
        return remote(
            small_parts.at[g], small_all.at[s], sum_sem.at[0], sum_sem.at[1], (ways - 1, g)
        )

    def follow_back():
        return remote(
            laid.at[pl.ds(0, SMALL_ROWS)], follow_rows, end_sem.at[0], end_sem.at[1],
            (lax.rem(s + ways - 1, ways), g),
        )

    def settle_first():
        unit_tiles(s * (own // UNIT), lambda count: lay_group(total, laid, 0, 0, count))
        follow_back().start()

    def settle():
        follow_back().wait()

        @pl.when(s != ways - 1)
        def _():
            after_rows[...] = follow_rows[...]

        @pl.when(s == ways - 1)
        def _():
            remote(
                small_all.at[pl.ds(0, ways - 1)], small_all.at[pl.ds(0, ways - 1)],
                sum_sem.at[0], sum_sem.at[1], (0, g),
            ).wait_recv()
            small_all[ways - 1] = small_parts[g]
            after_rows[...] = jnp.sum(small_all[...], axis=0)


    widths = (half_width + LANES,) * 3 + (half_width,)

    def exchange(index):
        width = widths[index]

        def start(step, carry):
            to = lax.rem(s + step, ways)
            remote(
                send_blocks.at[index, to, :, pl.ds(0, width)],
                recv_blocks.at[index, s, :, pl.ds(0, width)],
                block_send.at[index],
                block_recv.at[index],
                (to, g),
            ).start()
            return carry

        recv_blocks[index, s] = send_blocks[index, s]
        lax.fori_loop(1, ways, start, 0)

    def exchanged(index):
        width = widths[index]
        remote(
            send_blocks.at[index, pl.ds(0, ways - 1), :, pl.ds(0, width)],
            recv_blocks.at[index, pl.ds(0, ways - 1), :, pl.ds(0, width)],
            block_send.at[index],
            block_recv.at[index],
            (s, 1 - g),
        ).wait()

    pairs = []

    def hand_over(src, dst):
        index = len(pairs)
        pairs.append(remote(src, dst, pair_send.at[index], pair_recv.at[index], (s, 1 - g)))
        pairs[index].start()
        return pairs[index]

    def by_residue(value):
        for tile in range(tiles):
            turning[tile] = value[:, tile * LANES : (tile + 1) * LANES]
        return jnp.concatenate(
            [
                jnp.concatenate(
                    [turning[tile, pl.ds(i, across, stride=ways), :] for i in range(ways)], axis=0
                )
                for tile in range(tiles)
            ],
            axis=1,
        )

    def in_order(value):
        for tile in range(tiles):
            for i in range(ways):
                turning[tile, pl.ds(i, across, stride=ways), :] = value[
                    across * i : across * (i + 1), tile * LANES : (tile + 1) * LANES
                ]
        return jnp.concatenate([turning[tile] for tile in range(tiles)], axis=1)

    def small_row(first, count):
        return jnp.concatenate(
            [small[half, first + r : first + r + 1, :] for half in range(2) for r in range(count)],
            axis=1,
        ).astype(F32)

    temper = HEAD ** (-0.5)

    def scores(which, head):
        at = slice(which * rows, (which + 1) * rows)
        query = projected[at, head * HEAD : (head + 1) * HEAD]
        key = projected[at, D + head * HEAD : D + (head + 1) * HEAD]
        value = projected[at, 2 * D + head * HEAD : 2 * D + (head + 1) * HEAD]
        found = jnp.where(masks[which] > 0.5, dot_cols(query, key) * temper, NEG)
        return query, key, value, found

    def attend_set(which, part):
        first = part * HEADS // 2
        results, totals = [], []
        for head in range(first, first + HEADS // 2):
            _, _, value, found = scores(which, head)
            top = jnp.max(found, axis=1, keepdims=True)
            weights = jnp.exp(found - top)
            summed = jnp.sum(weights, axis=1, keepdims=True)
            results.append(dot(weights.astype(BF16), value) * (1.0 / summed))
            totals.append(top + jnp.log(summed))
        to = slice(part * half_width, (part + 1) * half_width)
        attended[which, :, to] = jnp.concatenate(results, axis=1)
        lses[which, :, first : first + HEADS // 2] = jnp.concatenate(totals, axis=1)

    def attend_set_back(which, out_grads, part):
        first = part * HEADS // 2
        lists = ([], [], [])
        for head in range(first, first + HEADS // 2):
            query, key, value, found = scores(which, head)
            weights = jnp.exp(found - lses[which, :, head : head + 1])
            pulled = out_grads[:, head * HEAD : (head + 1) * HEAD]
            weight_grad = dot_cols(pulled, value)
            inner = jnp.sum(weights * weight_grad, axis=1, keepdims=True)
            extra = lse_grads[which, :, head : head + 1] - inner
            score_grad = (weights * (weight_grad + extra)).astype(BF16)
            lists[0].append(dot(score_grad, key) * temper)
            lists[1].append(dot_rows(score_grad, query) * temper)
            lists[2].append(dot_rows(weights.astype(BF16), pulled))
        at = slice(which * rows, (which + 1) * rows)
        for index, one in enumerate(lists):
            half, start = divmod(index * D + part * half_width, 3 * half_width)
            qkv_grad[half, at, start : start + half_width] = jnp.concatenate(one, axis=1).astype(BF16)

    def weight_grad(index, mine, theirs, grad, their_grad, first, count):
        left = jnp.concatenate(
            [mine[first : first + count, :], theirs[first : first + count, :]], axis=1
        )
        view, base = tile_view(grads, index)
        at = base + first // 16
        for tile, width in tile_groups(index):
            to = slice(tile * LANES, (tile + width) * LANES)
            right = jnp.concatenate([grad[g, :, to], their_grad[:, to]], axis=0)
            found = dot(left, right).astype(BF16)
            for t in range(width):
                view[at : at + count // 16, 16 * (tile + t) : 16 * (tile + t) + 16, :] = found[
                    :, t * LANES : (t + 1) * LANES
                ].reshape(count // 16, 16, LANES)


    kept = SimpleNamespace()
    barrier = greet_all(ways)
    for load in loads:
        load.start()
    inputs = by_residue(tokens[...].astype(F32))
    lane = lax.broadcasted_iota(jnp.int32, (rows, rows), 1)
    row = lax.broadcasted_iota(jnp.int32, (rows, rows), 0)
    flags = holes[...].astype(F32)
    to_column = (row == lane).astype(F32)
    own_column = jnp.sum(to_column * flags, axis=1, keepdims=True)
    turned_at = ways * lax.rem(row, across) + row // across
    turned_column = jnp.sum((turned_at == lane).astype(F32) * flags, axis=1, keepdims=True)
    turned_row_at = ways * lax.rem(lane, across) + lane // across
    turned_row = jnp.sum((turned_row_at == row).astype(F32) * own_column, axis=0, keepdims=True)
    pack_blocks(send_blocks.at[0], inputs, jnp.broadcast_to(turned_column, (rows, HEADS)) * 1.0)
    loaded()
    make_tail()
    fill_most()
    pl.semaphore_wait(barrier, ways)
    follow_copy().start()
    early(order[0], late)
    direct(order[0], late)
    exchange(0)
    small_out()
    fill_first()

    def norm():
        kept.upstream = by_residue(cotangent[...].astype(F32))
        for half in range(2):
            to = slice(half * half_width, (half + 1) * half_width)
            down_grad[half] = kept.upstream[:, to].astype(BF16)
        kept.down_grad_pair = hand_over(down_grad.at[1 - g], their_down)
        exchanged(0)
        far_inputs = unpack_values(recv_blocks.at[0])
        far_column = unpack_extra(recv_blocks.at[0])[:, :1]
        far_row = jnp.sum(to_column * far_column, axis=0, keepdims=True)
        near_mask, far_mask = slide_masks(lengths, s, ways, turned_row, far_row)
        masks[0] = near_mask
        masks[1] = far_mask
        hat, scale = normalize(jnp.concatenate([inputs, far_inputs], axis=0))
        small_in()
        count = third_rows
        kept.gain_one, kept.gain_two = small_row(0, count), small_row(count, count)
        kept.shift_one, kept.shift_two = small_row(2 * count, count), small_row(3 * count, count)
        kept.shift_down = small_row(4 * count, count)
        kept.bias_up = small_row(5 * count, FF // 2 // LANES)
        both = hat * kept.gain_one + kept.shift_one
        normed[...] = both.astype(BF16)
        normed_t[...] = both.T.astype(BF16)
        normed_hat[...] = hat[:rows]
        inverse[...] = scale[:rows]
        kept.normed_pair = hand_over(normed_t, their_normed)

    def project():
        arrived(0)
        for half in range(2):
            for tile, width in tile_groups(0):
                at = half * 3 * half_width + tile * LANES
                projected[:, at : at + width * LANES] = dot(
                    normed[...], weight(whole, 0, half, 0, D, tile, width)
                ).astype(BF16)

    def attend_far():
        attend_set(1, 0)
        attend_set(1, 1)
        pack_blocks(send_blocks.at[1], attended[1], lses[1])
        exchange(1)

    def mix():
        exchanged(1)
        far_out = unpack_values(recv_blocks.at[1])
        near_out = attended[0]
        kept.share = jax.nn.sigmoid(lses[0] - unpack_extra(recv_blocks.at[1]))
        kept.shares = to_columns(kept.share)
        kept.difference = near_out - far_out
        mixed = kept.shares * near_out + (1.0 - kept.shares) * far_out
        mixture[...] = mixed.astype(BF16)
        mixture_t[...] = mixed.T.astype(BF16)
        kept.mixture_pair = hand_over(mixture_t, their_mixture)

    def feed():
        arrived(1)
        arrived(2)
        kept.middle = inputs + jnp.concatenate(
            [dot(mixture[...], weight(whole, 1, half, 0, D, 0, third_rows)) for half in range(2)],
            axis=1,
        )
        hat, scale = normalize(kept.middle)
        second_hat[...] = hat
        second_inverse[...] = scale
        second = hat * kept.gain_two + kept.shift_two
        second_in[...] = second.astype(BF16)
        root = (2.0 / 3.141592653589793) ** 0.5
        kept.activated_pairs = []
        for half in range(2):
            for tile, width in tile_groups(2):
                at = half * FF // 2 + tile * LANES
                to = slice(at, at + width * LANES)
                v = dot(second_in[...], weight(whole, 2, half, 0, D, tile, width))
                v = v + kept.bias_up[:, to]
                square = v * v
                t = jnp.tanh(root * (v + 0.044715 * v * square))
                active = 0.5 * v * (1.0 + t)
                activated[:, to] = active.astype(BF16)
                activated_t[to, :] = active.T.astype(BF16)
                slope[:, to] = 0.5 * (1.0 + t) + 0.5 * v * (1.0 - t * t) * (
                    root * (1.0 + 3 * 0.044715 * square)
                )
                if (at + width * LANES) % D == 0:
                    span = pl.ds(at + width * LANES - D, D)
                    kept.activated_pairs.append(
                        hand_over(activated_t.at[span], their_activated.at[span])
                    )
        second_t[...] = second.T.astype(BF16)
        kept.second_in_pair = hand_over(second_t, their_second)

    block = 256

    def feed_back():
        for plane in range(3, planes):
            arrived(plane)
        sums = []
        for start in range(0, FF, block):
            to = slice(start, start + block)
            pulled = sum(
                dot_cols(down_grad[half], weight(whole, 3, half, start, block, 0, third_rows))
                for half in range(2)
            )
            grad = (pulled * slope[:, to]).astype(BF16)
            half, at = divmod(start, FF // 2)
            up_grad[half, :, at : at + block] = grad
            sums.append(jnp.sum(grad.astype(F32), axis=0, keepdims=True))
        kept.up_sum = jnp.concatenate(sums, axis=1)
        kept.up_grad_pair = hand_over(up_grad.at[1 - g], their_up)

    def down_weights():
        kept.down_grad_pair.wait()
        for first in range(0, FF, D):
            kept.activated_pairs[first // D].wait()
            weight_grad(3, activated_t, their_activated, down_grad, their_down, first, D)

    def through(left, index, tiles_to):
        return jnp.concatenate(
            [
                sum(
                    dot_cols(left[half], weight(whole, index, half, start, block, 0, tiles_to))
                    for half in range(2)
                )
                for start in range(0, D, block)
            ],
            axis=1,
        )

    def mix_back():
        second_grad = through(up_grad, 2, TILES[2])
        hat = second_hat[...]
        kept.gain_two_sum = jnp.sum(second_grad * hat, axis=0, keepdims=True)
        kept.shift_two_sum = jnp.sum(second_grad, axis=0, keepdims=True)
        gained = kept.upstream + norm_back(second_grad * kept.gain_two, hat, second_inverse[...])
        middle_grad[...] = gained
        for half in range(2):
            out_grad[half] = gained[:, half * half_width : (half + 1) * half_width].astype(BF16)
        kept.out_grad_pair = hand_over(out_grad.at[1 - g], their_out)
        mix_grad = through(out_grad, 1, third_rows)
        share, shares = kept.share, kept.shares
        near_lse_grad = share * (1.0 - share) * to_heads(kept.difference * mix_grad)
        lse_grads[0] = near_lse_grad
        near_grad[...] = (shares * mix_grad).astype(BF16)
        pack_blocks(send_blocks.at[2], (1.0 - shares) * mix_grad, -near_lse_grad)
        exchange(2)

    def up_weights():
        kept.second_in_pair.wait()
        kept.up_grad_pair.wait()
        weight_grad(2, second_t, their_second, up_grad, their_up, 0, D)

    def out_weights():
        kept.mixture_pair.wait()
        kept.out_grad_pair.wait()
        weight_grad(1, mixture_t, their_mixture, out_grad, their_out, 0, D)

    def put_output():
        result = kept.middle + kept.shift_down + jnp.concatenate(
            [
                dot(activated[...], weight(whole, 3, half, 0, FF, 0, third_rows))
                for half in range(2)
            ],
            axis=1,
        )
        output[...] = in_order(result).astype(BF16)

    def far_back_start():
        kept.qkv_near_pair = hand_over(
            qkv_grad.at[1 - g, pl.ds(0, rows)], their_qkv.at[pl.ds(0, rows)]
        )
        exchanged(2)
        far_grad[...] = unpack_values(recv_blocks.at[2]).astype(BF16)
        lse_grads[1] = unpack_extra(recv_blocks.at[2])
        attend_set_back(1, far_grad, 0)

    def far_back():
        attend_set_back(1, far_grad, 1)
        kept.qkv_far_pair = hand_over(
            qkv_grad.at[1 - g, pl.ds(rows, rows)], their_qkv.at[pl.ds(rows, rows)]
        )

    def project_back():
        kept.first_grad = through(qkv_grad, 0, TILES[0])
        pack_blocks(send_blocks.at[3], kept.first_grad[rows:], None)
        exchange(3)

    def qkv_weights():
        kept.normed_pair.wait()
        kept.qkv_near_pair.wait()
        kept.qkv_far_pair.wait()
        weight_grad(0, normed_t, their_normed, qkv_grad, their_qkv, 0, D)

    def put_input_grad():
        exchanged(3)
        first_grad = kept.first_grad[:rows] + unpack_values(recv_blocks.at[3])
        hat = normed_hat[...]
        kept.gain_one_sum = jnp.sum(first_grad * hat, axis=0, keepdims=True)
        kept.shift_one_sum = jnp.sum(first_grad, axis=0, keepdims=True)
        input_grad[...] = in_order(
            middle_grad[...] + norm_back(first_grad * kept.gain_one, hat, inverse[...])
        )

    def small_sums():
        for half in range(2):
            to = slice(half * half_width, (half + 1) * half_width)
            down_sum = jnp.sum(down_grad[half].astype(F32), axis=0, keepdims=True)
            sums = (kept.gain_one_sum, kept.gain_two_sum, kept.shift_one_sum, kept.shift_two_sum)
            listed = [one[:, to] for one in sums] + [down_sum]
            listed.append(kept.up_sum[:, half * FF // 2 : (half + 1) * FF // 2])
            at = 0
            for vector in listed:
                count = vector.shape[1] // LANES
                small_parts[half, at : at + count, :] = vector.reshape(count, LANES)
                at += count
            small_parts[half, at:, :] = jnp.zeros((SMALL_ROWS - at, LANES), F32)
        kept.small_pair = hand_over(small_parts.at[1 - g], their_small)
        kept.small_pair.wait()
        small_parts[g] = small_parts[g] + their_small[...]
        pl.when(s != ways - 1)(lambda: small_home().start())

    everything = [(part, piece) for piece in range(PIECES + 1) for part in range(2)]
    leave(1, False)
    early(order[0], 1)
    early(order[0], 0)
    leave(1, True)
    leave(0, False)
    turn_piece(order[0], late)
    turn_piece(order[0], 1)
    direct(order[0], 1)
    direct(order[0], 0)
    enter_plane(order[1], 1)
    early(order[1], 1)
    turn_piece(order[0], 0)
    enter_plane(order[2], 1)
    enter_plane(order[1], 0)
    early(order[1], 0)
    early(order[2], 1)
    late_own()
    direct(order[1], 1)
    finish(order[0], late)
    turn_piece(order[1], 1)
    norm()
    direct(order[1], 0)
    enter_plane(order[2], 0)
    early(order[2], 0)
    turn_piece(order[1], 0)
    finish(order[0], 0)
    enter_plane(order[3], 1)
    early(order[3], 1)
    direct(order[2], 0)
    turn_piece(order[2], 1)
    direct(order[2], 1)
    finish(order[0], 1)
    late_on(order[1])
    finish(order[1], 1)
    leave(0, True)
    late_on(order[2])
    turn_piece(order[2], 0)
    finish(order[1], late)
    finish(order[1], 0)
    enter_plane(order[3], 0)
    early(order[3], 0)
    turn_piece(order[3], 1)
    direct(order[3], 1)
    project()
    attend_far()
    finish(order[2], late)
    finish(order[2], 1)
    attend_set(0, 0)
    attend_set(0, 1)
    finish(order[2], 0)
    direct(order[3], 0)
    turn_piece(order[3], 0)
    late_on(order[3])
    finish(order[3], 1)
    finish(order[3], late)
    mix()
    finish(order[3], 0)
    feed()
    down_weights()
    late_start(3)
    out_keep(3, 0)
    out_ahead(3, 0)
    out_ahead(3, 1)
    feed_back()
    mix_back()
    up_weights()
    out_ahead(2, 1)
    late_start(2)
    out_ahead(2, 0)
    out_pass(3, 0)
    attend_set_back(0, near_grad, 0)
    attend_set_back(0, near_grad, 1)
    out_take(3, 0)
    out_weights()
    out_keep(3, 1)
    out_ahead(1, 0)
    late_start(1)
    out_keep(2, 1)
    late_relay(3)
    out_pass(3, 1)
    out_keep(2, 0)
    out_pass(2, 0)
    out_pass(2, 1)
    far_back_start()
    far_back()
    late_relay(2)
    out_take(3, 1)
    late_relay(1)
    qkv_weights()
    late_start(0)
    out_ahead(0, 1)
    late_home(3)
    out_join(3, 0)
    out_join(3, 1)
    out_take(2, 0)
    out_take(2, 1)
    out_ahead(0, 0)
    out_keep(0, 0)
    project_back()
    out_join(2, 0)
    out_pass(0, 0)
    out_keep(0, 1)
    out_relay(3, 0)
    put_output()
    out_take(0, 0)
    late_home(2)
    out_pass(0, 1)
    out_relay(3, 1)
    late_home(1)
    out_relay(2, 0)
    late_relay(0)
    out_join(2, 1)
    out_ahead(2, late)
    out_ahead(1, late)
    out_keep(1, 0)
    out_join(0, 0)
    out_ahead(1, 1)
    out_relay(0, 0)
    out_pass(1, late)
    out_take(0, 1)
    out_relay(2, 1)
    out_keep(2, late)
    out_join(0, 1)
    out_keep(1, late)
    out_pass(1, 0)
    out_take(1, 0)
    out_relay(0, 1)
    put_input_grad()
    out_keep(1, 1)
    out_pass(1, 1)
    small_sums()
    out_take(1, late)
    out_ahead(3, late)
    late_home(0)
    out_join(1, 0)
    out_keep(0, late)
    out_keep(3, late)
    out_ahead(0, late)
    out_pass(2, late)
    out_relay(1, 0)
    out_last(everything[:1])
    settle_first()
    out_take(1, 1)
    out_join(1, 1)
    out_relay(1, 1)
    out_take(2, late)
    out_pass(3, late)
    out_join(2, late)
    out_pass(0, late)
    out_join(1, late)
    out_take(0, late)
    out_take(3, late)
    out_join(3, late)
    out_join(0, late)
    out_last(everything[1:])
    settle()
    pl.when(s != ways - 1)(lambda: small_home().wait_send())
    gather_sent()
    small_sent()
    out_sent()


def bounds_total():
    return 5 * D // 2 + FF // 2


def run_step(tokens, cotangent, holes, lengths, master, ways):
    rows = tokens.shape[0]
    own = MAT_ROWS // ways
    entries = (MAT_ROWS * LANES + bounds_total()) // ways
    half_own = own // 2
    planes = ways // 4
    vmem = pl.BlockSpec(memory_space=pltpu.VMEM)
    dma = pltpu.SemaphoreType.DMA
    half = D // 2
    most = max((half_own - min(LATE_OUT)) // PIECES, max(LATE_OUT))
    shapes = [
        ((2, MAT_ROWS, LANES), BF16),
        ((MAT_ROWS, LANES), BF16),
        ((2, SMALL_ROWS, LANES), BF16),
        ((1, (own + SMALL_ROWS) * LANES), F32),
        ((1, entries % LANES), F32),
        ((SMALL_ROWS + 184, LANES), F32),
        ((own + SMALL_ROWS, LANES), F32),
        ((SMALL_ROWS, LANES), F32),
        ((D // LANES, rows, LANES), F32),
        ((4, ways, 16, half + LANES), BF16),
        ((4, ways, 16, half + LANES), BF16),
        ((2, rows, rows), F32),
        ((2 * rows, D), BF16),
        ((rows, D), F32),
        ((rows, 1), F32),
        ((2 * rows, 3 * D), BF16),
        ((2, rows, D), F32),
        ((2, rows, HEADS), F32),
        ((rows, D), BF16),
        ((rows, D), BF16),
        ((rows, FF), BF16),
        ((rows, FF), F32),
        ((rows, D), F32),
        ((rows, 1), F32),
        ((rows, D), F32),
        ((D, 2 * rows), BF16),
        ((D, rows), BF16),
        ((D, rows), BF16),
        ((FF, rows), BF16),
        ((2, 2 * rows, 3 * half), BF16),
        ((2, rows, half), BF16),
        ((2, rows, FF // 2), BF16),
        ((2, rows, half), BF16),
        ((rows, D), BF16),
        ((rows, D), BF16),
        ((2, rows, HEADS), F32),
        ((D, 2 * rows), BF16),
        ((D, rows), BF16),
        ((D, rows), BF16),
        ((FF, rows), BF16),
        ((2 * rows, 3 * half), BF16),
        ((rows, half), BF16),
        ((rows, FF // 2), BF16),
        ((rows, half), BF16),
        ((2, SMALL_ROWS, LANES), F32),
        ((SMALL_ROWS, LANES), F32),
        ((planes, 2, 2, PIECES + 1, most, LANES), BF16),
        ((planes, 2, PIECES + 1, most, LANES), BF16),
        ((2, planes, 2, PIECES, most, LANES), BF16),
        ((2, planes, 2, 4, max(LATE_OUT), LANES), BF16),
        ((16 * max(TILES), LANES), F32),
        ((SMALL_ROWS, LANES), F32),
        ((ways, SMALL_ROWS, LANES), F32),
    ]
    return pl.pallas_call(
        partial(step_kernel, ways),
        out_shape=(
            jax.ShapeDtypeStruct((rows, D), BF16),
            jax.ShapeDtypeStruct((rows, D), F32),
            jax.ShapeDtypeStruct((own, LANES), F32),
            jax.ShapeDtypeStruct((SMALL_ROWS, LANES), F32),
        ),
        in_specs=[
            vmem, vmem, vmem, pl.BlockSpec(memory_space=pltpu.SMEM), pl.BlockSpec(memory_space=pl.ANY),
        ],
        out_specs=(vmem,) * 4,
        scratch_shapes=[pltpu.VMEM(*shape) for shape in shapes]
        + [
            dma((2,)), dma((2,)),
            dma((2, planes, 5, PIECES + 1)), dma((2, ways, PIECES + 1)),
            dma((2, planes, 2)), dma((planes, 2)),
            dma((planes, 2, PIECES + 1)), dma((planes, 2, PIECES + 1)),
            dma((ways,)), dma((2,)),
            dma((4,)), dma((4,)), dma((13,)), dma((13,)),
            dma((planes, 2, 2, PIECES + 1)), dma((planes, 2, 2, PIECES + 1)),
            dma((planes, 2, PIECES + 1)), dma((planes, 2, PIECES + 1)),
            dma((planes, 2, PIECES)), dma((2, planes, 2, PIECES)),
            dma((planes, 2)), dma((2, planes, 2)),
            dma((2,)), dma((2,)),
        ],
        compiler_params=pltpu.CompilerParams(
            collective_id=1, has_side_effects=True, vmem_limit_bytes=VMEM_BYTES
        ),
        name="run_step",
    )(tokens, cotangent, holes, lengths, master)


def rates_at(at):
    values = (
        0.7 * (2.0 / D) ** 0.5, 0.7 * (24.0 / D) ** 0.5, 0.7 * (1.0 / D) ** 0.5, 0.7 * (1.0 / FF) ** 0.5,
        0.15, 0.2,
    )
    rates = values[5]
    for edge, value in reversed(list(zip(bounds(), values))):
        rates = jnp.where(at < edge, jnp.float32(value), rates)
    return rates, jnp.where(at < bounds()[3], jnp.float32(0.1), jnp.float32(0.0))


def adam_kernel(
    tiled, after_rows, master, first_moment, second_moment, layer_output, layer_grad,
    new_moment, new_second, new_master, output, input_grad, kept, last, kept_output, kept_grad,
    kept_tiled, laid, load_sem, store_sem, pass_sem, grad_sem,
):
    size = master.shape[1]
    full, rest = divmod(size, LANES)
    own, step = tiled.shape[0], 56
    chunks = own // UNIT
    edges = [(UNIT * c - SMALL_ROWS) // step * step for c in range(1, chunks)]
    edges = [0] + edges + [full]
    spans = [(first, end - first) for first, end in zip(edges, edges[1:])]
    sources, targets = (first_moment, second_moment, master), (new_moment, new_second, new_master)

    def piece(array, first, count):
        return array.at[:, pl.ds(first * LANES, count * LANES)].reshape(count, LANES)

    def load(which, index):
        first, count = spans[index]
        return pltpu.make_async_copy(
            piece(sources[which], first, count), kept.at[which, pl.ds(first, count)],
            load_sem.at[which, index],
        )

    def store(which, index):
        first, count = spans[index]
        return pltpu.make_async_copy(
            kept.at[which, pl.ds(first, count)], piece(targets[which], first, count),
            store_sem.at[which, index],
        )

    def load_last(which):
        return pltpu.make_async_copy(
            sources[which].at[:, pl.ds(full * LANES, rest)], last.at[which], load_sem.at[which, chunks]
        )

    def store_last(which):
        return pltpu.make_async_copy(
            last.at[which], targets[which].at[:, pl.ds(full * LANES, rest)], store_sem.at[which, chunks]
        )

    passed = tuple(
        (
            pltpu.make_async_copy(source, through, pass_sem.at[index]),
            pltpu.make_async_copy(through, target, pass_sem.at[index]),
        )
        for index, (source, through, target) in enumerate(
            ((layer_output, kept_output, output), (layer_grad, kept_grad, input_grad))
        )
    )
    after = pltpu.make_async_copy(
        after_rows, laid.at[pl.ds(own, SMALL_ROWS)], grad_sem.at[chunks]
    )

    def unit_in(unit):
        span = pl.ds(unit * UNIT, UNIT)
        return pltpu.make_async_copy(tiled.at[span], kept_tiled.at[span], grad_sem.at[unit])

    for index in range(chunks):
        unit_in(index).start()
        for which in range(3):
            load(which, index).start()
    after.start()
    for which in range(3):
        load_last(which).start()
    for copy, _ in passed:
        copy.start()
    s = lax.axis_index("seq")
    origin = s * size
    shift = s * (size - own * LANES)
    row_shift, lane_shift = shift // LANES, lax.rem(shift, LANES)
    back = lax.rem(LANES - lane_shift, LANES)

    def gradients(first, count):
        here = laid[pl.ds(first + row_shift, count), :]
        after = laid[pl.ds(first + row_shift + 1, count), :]
        lanes = lax.broadcasted_iota(jnp.int32, (count, LANES), 1)
        return jnp.where(lanes < LANES - lane_shift, here, after)


    def update(at, moment, second, weights, gradient):
        rates, decays = rates_at(at)
        moment = BETA_ONE * moment + (1.0 - BETA_ONE) * gradient
        second = BETA_TWO * second + (1.0 - BETA_TWO) * gradient * gradient
        scaled = moment * (1.0 / (1.0 - BETA_ONE**STEP))
        change = scaled / (jnp.sqrt(second * (1.0 / (1.0 - BETA_TWO**STEP))) + EPS_ADAM)
        return moment, second, weights - rates * (change + decays * weights)

    laid[own + SMALL_ROWS :, :] = jnp.zeros((laid.shape[0] - own - SMALL_ROWS, LANES), F32)

    def lay(unit):
        def groups(count):
            for group in range(UNIT // (16 * count)):
                lay_group(kept_tiled, laid, unit * UNIT, group, count, back)

        unit_tiles(s * (own // UNIT) + unit, groups)

    for index, (first, count) in enumerate(spans):
        unit_in(index).wait()
        lay(index)
        if index == chunks - 1:
            after.wait()
            laid[own : own + SMALL_ROWS, :] = pltpu.roll(laid[own : own + SMALL_ROWS, :], back, 1)
        for which in range(3):
            load(which, index).wait()

        def run(index, carry, first=first):
            where = pl.multiple_of(first + index * step, 8)
            span = pl.ds(where, step)
            start = origin + where * LANES
            end = start + step * LANES - 1
            edge_list = bounds()
            cut = (start < edge_list[0]) & (end >= edge_list[0])
            for edge in edge_list[1:]:
                cut = cut | ((start < edge) & (end >= edge))

            def put(at):
                found = update(at, *(kept[which, span, :] for which in range(3)), gradients(where, step))
                for which in range(3):
                    kept[which, span, :] = found[which]

            pl.when(jnp.logical_not(cut))(lambda: put(start))

            @pl.when(cut)
            def _():
                row = lax.broadcasted_iota(jnp.int32, (step, LANES), 0)
                put(start + row * LANES + lax.broadcasted_iota(jnp.int32, (step, LANES), 1))

            return carry

        lax.fori_loop(0, -(-count // step), run, 0)
        for which in range(3):
            store(which, index).start()
        if index == 0:
            for copy, onward in passed:
                copy.wait()
                onward.start()
    for which in range(3):
        load_last(which).wait()
    moment, second, weights = (last[which] for which in range(3))
    at = origin + full * LANES + lax.broadcasted_iota(jnp.int32, (1, rest), 1)
    found = update(at, moment, second, weights, gradients(full, 8)[:1, :rest])
    for which in range(3):
        last[which] = found[which]
        store_last(which).start()
    for which in range(3):
        for index in range(chunks):
            store(which, index).wait()
        store_last(which).wait()
    for _, copy in passed:
        copy.wait()


def run_adam(tiled, after_rows, master, first_moment, second_moment, layer_output, layer_grad):
    size = master.shape[1]
    anywhere = pl.BlockSpec(memory_space=pl.ANY)
    return pl.pallas_call(
        adam_kernel,
        out_shape=(jax.ShapeDtypeStruct((1, size), F32),) * 3
        + tuple(jax.ShapeDtypeStruct(one.shape, one.dtype) for one in (layer_output, layer_grad)),
        in_specs=[anywhere] * 7,
        out_specs=(anywhere,) * 5,
        scratch_shapes=[
            pltpu.VMEM((3, -(-size // (8 * LANES)) * 8, LANES), F32),
            pltpu.VMEM((3, 1, size % LANES), F32),
            pltpu.VMEM(layer_output.shape, layer_output.dtype),
            pltpu.VMEM(layer_grad.shape, layer_grad.dtype),
            pltpu.VMEM(tiled.shape, F32),
            pltpu.VMEM((tiled.shape[0] + 2 * SMALL_ROWS, LANES), F32),
            pltpu.SemaphoreType.DMA((3, tiled.shape[0] // UNIT + 1)),
            pltpu.SemaphoreType.DMA((3, tiled.shape[0] // UNIT + 1)),
            pltpu.SemaphoreType.DMA((2,)),
            pltpu.SemaphoreType.DMA((tiled.shape[0] // UNIT + 1,)),
        ],
        compiler_params=pltpu.CompilerParams(vmem_limit_bytes=VMEM_BYTES),
        name="run_adam",
    )(tiled, after_rows, master, first_moment, second_moment, layer_output, layer_grad)


def on_device(tokens, cotangent, holes, slide_lengths, master, first_moment, second_moment):
    ways = lax.axis_size("seq")
    output, input_grad, tiled, after_rows = run_step(
        tokens[0], cotangent[0], holes, slide_lengths, master, ways
    )
    new_moment, new_second, new_master, output, input_grad = run_adam(
        tiled, after_rows, master, first_moment, second_moment, output, input_grad
    )
    return (output[None], input_grad[None], new_moment, new_second, new_master)


def even(mesh):
    ways = mesh.shape["seq"]
    return ways % 4 == 0 and MAT_ROWS % (ways * UNIT) == 0 and ways * 8 == LANES


def solution(mesh):
    return jax.shard_map(
        on_device if even(mesh) else plain_on_device,
        mesh=mesh,
        in_specs=(
            P("grp", "seq", None),
            P("grp", "seq", None),
            P("grp", "seq"),
            P("grp", None),
            P("grp", "seq"),
            P("grp", "seq"),
            P("grp", "seq"),
        ),
        out_specs=(
            P("grp", "seq", None),
            P("grp", "seq", None),
            P("grp", "seq"),
            P("grp", "seq"),
            P("grp", "seq"),
        ),
        check_vma=False,
    )
```

```python
from functools import partial
from types import SimpleNamespace

import jax
import jax.numpy as jnp
from jax import lax
from jax.experimental import pallas as pl
from jax.experimental.pallas import tpu as pltpu
from jax.sharding import PartitionSpec as P

D = 768
FF = 3072
HEADS = 16
HEAD = 48
STEP = 10


EPS_NORM = 1e-05
EPS_ADAM = 1e-08
BETA_ONE = 0.9
BETA_TWO = 0.95


def as_sent(array):
    return jax.tree.map(lambda a: a.astype(jnp.bfloat16) if a.dtype == jnp.float32 else a, array)


def bounds():
    qkv_edge = 3 * D * D // 2
    out_edge = qkv_edge + D * D // 2
    up_edge = out_edge + D * FF // 2
    down_edge = up_edge + FF * D // 2
    gain_edge = down_edge + D
    return (qkv_edge, out_edge, up_edge, down_edge, gain_edge)


def per_segment(flat_index, values):
    edge_list = bounds()
    result = jnp.full(flat_index.shape, values[5], jnp.float32)
    for position in range(4, -1, -1):
        result = jnp.where(flat_index < edge_list[position], jnp.float32(values[position]), result)
    return result


def unpack(flat):
    edge_list = bounds()
    total = flat.shape[1]

    def joined(start, stop, shape):
        return jnp.concatenate(
            [flat[0, start:stop].reshape(shape), flat[1, start:stop].reshape(shape)], axis=-1
        )

    w_qkv = joined(0, edge_list[0], (D, 3 * D // 2))
    w_out = joined(edge_list[0], edge_list[1], (D, D // 2))
    w_up = joined(edge_list[1], edge_list[2], (D, FF // 2))
    w_down = joined(edge_list[2], edge_list[3], (FF, D // 2))
    gain_rows = joined(edge_list[3], edge_list[4], (2, D // 2))
    shift_rows = joined(edge_list[4], edge_list[4] + 3 * D // 2, (3, D // 2))
    bias_up = joined(edge_list[4] + 3 * D // 2, total, (FF // 2,))
    return (w_qkv, w_out, w_up, w_down, gain_rows, shift_rows, bias_up)


def normalize(values):
    centered = values - jnp.mean(values, axis=-1, keepdims=True)
    inverse = lax.rsqrt(jnp.mean(centered * centered, axis=-1, keepdims=True) + EPS_NORM)
    return (centered * inverse, inverse)


def norm_back(grad_hat, normed_hat, inverse):
    return inverse * (
        grad_hat
        - jnp.mean(grad_hat, axis=-1, keepdims=True)
        - normed_hat * jnp.mean(grad_hat * normed_hat, axis=-1, keepdims=True)
    )


def contract_rows(left, right):
    return lax.dot_general(
        left, right, (((0,), (0,)), ((), ())), preferred_element_type=jnp.float32
    )


def contract_cols(left, right):
    return lax.dot_general(
        left, right, (((1,), (1,)), ((), ())), preferred_element_type=jnp.float32
    )


def slide_index(positions, slide_ends):
    return jnp.sum((positions[:, None] >= slide_ends[None, :]).astype(jnp.int32), axis=1)


def split_heads(block_rows):
    return block_rows.reshape(block_rows.shape[0], HEADS, HEAD).transpose(1, 0, 2)


def join_heads(stacked):
    return stacked.transpose(1, 0, 2).reshape(stacked.shape[1], HEADS * HEAD)


def allowance(slides, present):
    token_count = slides.shape[0]
    same_slide = (slides[:, None] == slides[None, :]) & (present[None, :] > 0)
    return same_slide | jnp.eye(token_count, dtype=bool)


def attend(packed, slides, present):
    allowed = allowance(slides, present)
    scale = HEAD ** (-0.5)

    def one_head(pieces):
        query_head, key_head, value_head = pieces
        scores = contract_cols(query_head, key_head) * scale
        scores = jnp.where(allowed, scores, -1000000000.0)
        row_max = jnp.max(scores, axis=-1, keepdims=True)
        exponent = jnp.exp(scores - row_max)
        denominator = jnp.sum(exponent, axis=-1, keepdims=True)
        attention = (exponent / denominator).astype(jnp.bfloat16)
        result = jnp.dot(attention, value_head, preferred_element_type=jnp.float32)
        return (result, (row_max + jnp.log(denominator))[:, 0])

    outs, lses = lax.map(
        one_head,
        (
            split_heads(packed[:, :D]),
            split_heads(packed[:, D : 2 * D]),
            split_heads(packed[:, 2 * D :]),
        ),
    )
    return (join_heads(outs), lses.T)


def attend_back(packed, slides, present, lse_rows, out_grad, lse_grad):
    allowed = allowance(slides, present)
    scale = HEAD ** (-0.5)

    def one_head(pieces):
        query_head, key_head, value_head, lse_head, grad_head, extra_lse = pieces
        scores = contract_cols(query_head, key_head) * scale
        scores = jnp.where(allowed, scores, -1000000000.0)
        attention = jnp.exp(scores - lse_head[:, None])
        prob_grad = contract_cols(grad_head, value_head)
        inner_sum = jnp.sum(attention * prob_grad, axis=-1, keepdims=True)
        score_grad = (attention * (prob_grad - inner_sum + extra_lse[:, None])).astype(jnp.bfloat16)
        query_grad = jnp.dot(score_grad, key_head, preferred_element_type=jnp.float32) * scale
        key_grad = contract_rows(score_grad, query_head) * scale
        value_grad = contract_rows(attention.astype(jnp.bfloat16), grad_head)
        return (query_grad, key_grad, value_grad)

    query_grad, key_grad, value_grad = lax.map(
        one_head,
        (
            split_heads(packed[:, :D]),
            split_heads(packed[:, D : 2 * D]),
            split_heads(packed[:, 2 * D :]),
            lse_rows.T,
            split_heads(out_grad),
            lse_grad.T,
        ),
    )
    return jnp.concatenate(
        [join_heads(query_grad), join_heads(key_grad), join_heads(value_grad)], axis=1
    )


def adam_update(weights, moment, second, gradient, flat_index):
    step_rates = per_segment(
        flat_index,
        (
            0.7 * (2.0 / D) ** 0.5,
            0.7 * (24.0 / D) ** 0.5,
            0.7 * (1.0 / D) ** 0.5,
            0.7 * (1.0 / FF) ** 0.5,
            0.15,
            0.2,
        ),
    )
    decays = per_segment(flat_index, (0.1, 0.1, 0.1, 0.1, 0.0, 0.0))
    new_moment = BETA_ONE * moment + (1.0 - BETA_ONE) * gradient
    new_second = BETA_TWO * second + (1.0 - BETA_TWO) * gradient * gradient
    fix_one = 1.0 - BETA_ONE**STEP
    fix_two = 1.0 - BETA_TWO**STEP
    update = new_moment / fix_one / (jnp.sqrt(new_second / fix_two) + EPS_ADAM)
    return (new_moment, new_second, weights - step_rates * (update + decays * weights))


def column_halves(values):
    return values.reshape(values.shape[0], 2, values.shape[1] // 2)


def plain_on_device(tokens, cotangent, holes, slide_lengths, master, first_moment, second_moment):
    own_half = lax.all_gather(master.astype(jnp.bfloat16), "seq", axis=1, tiled=True)
    whole_flat = lax.all_gather(own_half, "grp", axis=0, tiled=True)
    w_qkv, w_out, w_up, w_down, gain_rows, shift_rows, bias_up = unpack(whole_flat)
    gain_rows = gain_rows.astype(jnp.float32)
    shift_rows = shift_rows.astype(jnp.float32)
    bias_up = bias_up.astype(jnp.float32)
    inputs = tokens[0].astype(jnp.float32)
    row_count = inputs.shape[0]
    seq_ways = lax.axis_size("seq")
    seq_place = lax.axis_index("seq")
    row_steps = jnp.arange(row_count, dtype=jnp.int32)
    slide_ends = jnp.cumsum(slide_lengths[0])
    near_slides = slide_index(seq_place * row_count + row_steps, slide_ends)
    far_slides = slide_index(seq_place + seq_ways * row_steps, slide_ends)
    near_present = holes[0]
    strided_shape = (row_count // seq_ways, seq_ways)

    def to_strided(packed):
        moved, moved_mask = (
            lax.all_to_all(
                packed.reshape(strided_shape + (3 * D,)),
                "seq",
                split_axis=1,
                concat_axis=0,
                tiled=True,
            ),
            lax.all_to_all(
                near_present.astype(jnp.bfloat16).reshape(strided_shape + (1,)),
                "seq",
                split_axis=1,
                concat_axis=0,
                tiled=True,
            ),
        )
        return (moved.reshape(row_count, 3 * D), moved_mask.reshape(row_count).astype(jnp.int32))

    normed_one, inverse_one = normalize(inputs)
    normed = (normed_one * gain_rows[0] + shift_rows[0]).astype(jnp.bfloat16)
    projected = jnp.dot(normed, w_qkv, preferred_element_type=jnp.float32).astype(jnp.bfloat16)
    near_out, near_lse = attend(projected, near_slides, near_present)
    far_proj, far_present = to_strided(projected)
    far_local, far_local_lse = attend(far_proj, far_slides, far_present)
    returned = (
        lax.all_to_all(
            far_local.reshape(row_count, 1, D).astype(jnp.bfloat16),
            "seq",
            split_axis=0,
            concat_axis=1,
            tiled=True,
        ).astype(jnp.float32),
        lax.all_to_all(
            far_local_lse.reshape(row_count, 1, HEADS).astype(jnp.bfloat16),
            "seq",
            split_axis=0,
            concat_axis=1,
            tiled=True,
        ).astype(jnp.float32),
    )
    far_out = returned[0].reshape(row_count, D)
    far_lse = returned[1].reshape(row_count, HEADS)
    near_share = jax.nn.sigmoid(near_lse - far_lse)
    near_heads = near_out.reshape(row_count, HEADS, HEAD)
    far_heads = far_out.reshape(row_count, HEADS, HEAD)
    mixture = (
        (near_share[:, :, None] * near_heads + (1.0 - near_share[:, :, None]) * far_heads)
        .reshape(row_count, D)
        .astype(jnp.bfloat16)
    )
    middle = inputs + jnp.dot(mixture, w_out, preferred_element_type=jnp.float32)
    normed_two, inverse_two = normalize(middle)
    second_in = (normed_two * gain_rows[1] + shift_rows[1]).astype(jnp.bfloat16)
    hidden = jnp.dot(second_in, w_up, preferred_element_type=jnp.float32) + bias_up
    activated = jax.nn.gelu(hidden, approximate=True).astype(jnp.bfloat16)
    output = middle + jnp.dot(activated, w_down, preferred_element_type=jnp.float32) + shift_rows[2]
    upstream = cotangent[0].astype(jnp.float32)
    down_grad = upstream.astype(jnp.bfloat16)
    grad_act = contract_cols(down_grad, w_down)
    gelu_pull = jax.vjp(partial(jax.nn.gelu, approximate=True), hidden)[1]
    hidden_grad = gelu_pull(grad_act)[0].astype(jnp.bfloat16)
    second_grad = contract_cols(hidden_grad, w_up)
    grad_gain_two = jnp.sum(second_grad * normed_two, axis=0)
    grad_shift_two = jnp.sum(second_grad, axis=0)
    middle_grad = upstream + norm_back(second_grad * gain_rows[1], normed_two, inverse_two)
    attend_grad = middle_grad.astype(jnp.bfloat16)
    mix_grad = contract_cols(attend_grad, w_out).reshape(row_count, HEADS, HEAD)
    near_lse_grad = (
        near_share * (1.0 - near_share) * jnp.sum((near_heads - far_heads) * mix_grad, axis=-1)
    )
    near_grad = (near_share[:, :, None] * mix_grad).reshape(row_count, D).astype(jnp.bfloat16)
    far_grad = ((1.0 - near_share[:, :, None]) * mix_grad).reshape(row_count, D)
    sent = (
        lax.all_to_all(
            as_sent(far_grad.reshape(strided_shape + (D,))),
            "seq",
            split_axis=1,
            concat_axis=0,
            tiled=True,
        ),
        lax.all_to_all(
            as_sent((-near_lse_grad).reshape(strided_shape + (HEADS,))),
            "seq",
            split_axis=1,
            concat_axis=0,
            tiled=True,
        ),
    )
    far_back = sent[0].reshape(row_count, D).astype(jnp.bfloat16)
    far_lse_grad = sent[1].reshape(row_count, HEADS)
    again_proj, again_present = to_strided(projected)
    again_lse = attend(again_proj, far_slides, again_present)[1]
    far_proj_grad = attend_back(
        again_proj, far_slides, again_present, again_lse, far_back, far_lse_grad
    ).astype(jnp.bfloat16)
    far_home = lax.all_to_all(
        far_proj_grad.reshape(row_count, 1, 3 * D), "seq", split_axis=0, concat_axis=1, tiled=True
    ).reshape(row_count, 3 * D)
    near_proj_grad = attend_back(
        projected, near_slides, near_present, near_lse, near_grad, near_lse_grad
    )
    proj_grad = (near_proj_grad + far_home.astype(jnp.float32)).astype(jnp.bfloat16)
    first_grad = contract_cols(proj_grad, w_qkv)
    grad_gain_one = jnp.sum(first_grad * normed_one, axis=0)
    grad_shift_one = jnp.sum(first_grad, axis=0)
    input_grad = middle_grad + norm_back(first_grad * gain_rows[0], normed_one, inverse_one)
    both_rows = (
        lax.all_gather(normed, "grp", axis=0, tiled=True),
        lax.all_gather(mixture, "grp", axis=0, tiled=True),
        lax.all_gather(second_in, "grp", axis=0, tiled=True),
        lax.all_gather(activated, "grp", axis=0, tiled=True),
    )
    moved = (
        lax.all_to_all(column_halves(proj_grad), "grp", split_axis=1, concat_axis=0, tiled=True),
        lax.all_to_all(column_halves(attend_grad), "grp", split_axis=1, concat_axis=0, tiled=True),
        lax.all_to_all(column_halves(hidden_grad), "grp", split_axis=1, concat_axis=0, tiled=True),
        lax.all_to_all(column_halves(down_grad), "grp", split_axis=1, concat_axis=0, tiled=True),
    )
    proj_mine = moved[0].reshape(2 * row_count, 3 * D // 2)
    attend_mine = moved[1].reshape(2 * row_count, D // 2)
    hidden_mine = moved[2].reshape(2 * row_count, FF // 2)
    down_mine = moved[3].reshape(2 * row_count, D // 2)
    norm_sums = lax.psum(
        jnp.stack([grad_gain_one, grad_gain_two, grad_shift_one, grad_shift_two]), "grp"
    )
    half_width = D // 2
    norm_half = lax.dynamic_slice_in_dim(
        norm_sums, lax.axis_index("grp") * half_width, half_width, 1
    )
    grad_w_qkv = contract_rows(both_rows[0], proj_mine)
    grad_w_out = contract_rows(both_rows[1], attend_mine)
    grad_w_up = contract_rows(both_rows[2], hidden_mine)
    grad_w_down = contract_rows(both_rows[3], down_mine)
    grad_bias_down = jnp.sum(down_mine.astype(jnp.float32), axis=0)
    grad_bias_up = jnp.sum(hidden_mine.astype(jnp.float32), axis=0)
    gradient = jnp.concatenate(
        [
            grad_w_qkv.reshape(-1),
            grad_w_out.reshape(-1),
            grad_w_up.reshape(-1),
            grad_w_down.reshape(-1),
            norm_half[0],
            norm_half[1],
            norm_half[2],
            norm_half[3],
            grad_bias_down,
            grad_bias_up,
        ]
    )
    reduced = lax.psum_scatter(gradient, "seq", scatter_dimension=0, tiled=True)
    shard_size = master.shape[1]
    flat_index = lax.axis_index("seq") * shard_size + jnp.arange(shard_size, dtype=jnp.int32)
    new_moment, new_second, new_master = adam_update(
        master[0], first_moment[0], second_moment[0], reduced, flat_index
    )
    return (
        output[None].astype(jnp.bfloat16),
        input_grad[None],
        new_moment[None],
        new_second[None],
        new_master[None],
    )


LANES = 128
BF16 = jnp.bfloat16
F32 = jnp.float32
MAT_ROWS = (3 * D * D + D * D + D * FF + FF * D) // 2 // LANES
SMALL_ROWS = 32
UNIT = 576
PAIR = 2
TILES = (3 * D // 2 // LANES, D // 2 // LANES, FF // 2 // LANES, D // 2 // LANES)
DEPTHS = (D, D, D, FF)
MESH = pl.DeviceIdType.MESH
VMEM_BYTES = 60 * 2**20
NEG = -1000000000.0
ORDERS = ((1, 2, 3), (0, 2, 3), (0, 3, 1), (0, 2, 1))
PIECES = 2
LATE_ROWS = 160
LATE_OUT = (128, 160, 192, 192)


def matrix_starts():
    starts = [0]
    for tiles, depth in zip(TILES, DEPTHS):
        starts.append(starts[-1] + tiles * depth)
    return starts


def place():
    return lax.axis_index("seq"), lax.axis_index("grp")


def greet_all(ways):
    s, g = place()
    barrier = pltpu.get_barrier_semaphore()

    def greet(step, carry):
        pl.semaphore_signal(
            barrier, inc=1, device_id=(lax.rem(s + step, ways), g), device_id_type=MESH
        )
        return carry

    lax.fori_loop(1, ways, greet, 0)
    pl.semaphore_signal(barrier, inc=1, device_id=(s, 1 - g), device_id_type=MESH)
    return barrier


def remote(src, dst, send_sem, recv_sem, to):
    return pltpu.make_async_remote_copy(
        src_ref=src,
        dst_ref=dst,
        send_sem=send_sem,
        recv_sem=recv_sem,
        device_id=to,
        device_id_type=MESH,
    )


def unit_tiles(unit, body):
    edges = [start // UNIT for start in matrix_starts()]
    kinds = {}
    for index, tiles in enumerate(TILES):
        inside = (unit >= edges[index]) & (unit < edges[index + 1])
        kinds[tiles] = kinds[tiles] | inside if tiles in kinds else inside
    for tiles, inside in kinds.items():
        pl.when(inside)(lambda tiles=tiles: body(tiles))


def dot(left, right):
    return jnp.dot(left, right, preferred_element_type=F32)


def dot_cols(left, right):
    return contract_cols(left, right)


def dot_rows(left, right):
    return contract_rows(left, right)


def tile_view(ref, index):
    rows = 16 * TILES[index]
    start = matrix_starts()[index]
    return ref.reshape(ref.shape[:-2] + (MAT_ROWS // rows, rows, LANES)), start // rows


def tile_groups(index):
    tiles = TILES[index]
    groups, at = [], 0
    while at < tiles:
        width = 3 if tiles - at == 3 else 2
        groups.append((at, width))
        at += width
    return groups


def weight(ref, index, half, row, rows, tile, width):
    view, base = tile_view(ref, index)
    first = base + row // 16
    pieces = [
        view[half, first : first + rows // 16, 16 * t : 16 * t + 16, :].reshape(rows, LANES)
        for t in range(tile, tile + width)
    ]
    return jnp.concatenate(pieces, axis=1)


def heads_of(rows):
    row = lax.broadcasted_iota(jnp.int32, (rows, D), 0) * HEAD
    column = lax.broadcasted_iota(jnp.int32, (rows, D), 1)
    return ((column >= row) & (column < row + HEAD)).astype(F32)


def to_columns(per_head):
    return jnp.dot(
        per_head, heads_of(HEADS), precision=lax.Precision.HIGHEST, preferred_element_type=F32
    )


def to_heads(columns):
    return lax.dot_general(
        columns,
        heads_of(HEADS),
        (((1,), (1,)), ((), ())),
        precision=lax.Precision.HIGHEST,
        preferred_element_type=F32,
    )


def pack_blocks(ref, values, extra):
    blocks = values.shape[0] // 8
    split = values.reshape(blocks, 8, D)
    ref[:, :, : D // 2] = jnp.concatenate(
        [split[:, :, : D // 2], split[:, :, D // 2 :]], axis=1
    ).astype(BF16)
    if extra is not None:
        high = extra.astype(BF16).astype(F32)
        low = extra - high
        pieces = jnp.concatenate(
            [high.reshape(blocks, 8, HEADS), low.reshape(blocks, 8, HEADS)], axis=1
        )
        ref[:, :, D // 2 : D // 2 + HEADS] = pieces.astype(BF16)


def unpack_values(ref):
    blocks = ref.shape[0]
    values = ref[:, :, : D // 2].astype(F32)
    return jnp.concatenate(
        [values[:, :8, :].reshape(blocks * 8, D // 2), values[:, 8:, :].reshape(blocks * 8, D // 2)],
        axis=1,
    )


def unpack_extra(ref):
    blocks = ref.shape[0]
    pieces = ref[:, :, D // 2 :].astype(F32)
    both = pieces[:, :8, :] + pieces[:, 8:, :]
    return both.reshape(blocks * 8, LANES)[:, :HEADS]


def slide_masks(ends_ref, s, ways, near_keys, far_keys):
    rows = near_keys.shape[1]
    ends, end = [], 0
    for index in range(ends_ref.shape[1]):
        end = end + ends_ref[0, index]
        ends.append(end)

    def slides(positions):
        total = jnp.zeros(positions.shape, jnp.int32)
        for end in ends:
            total = total + (positions >= end).astype(jnp.int32)
        return total

    across = rows // ways
    result = []
    for far, keys in ((False, near_keys), (True, far_keys)):
        found = []
        for dim in (0, 1):
            at = lax.broadcasted_iota(jnp.int32, (rows, rows), dim)
            if far:
                position = s + ways * at
            else:
                position = rows * s + ways * lax.rem(at, across) + at // across
            found.append(slides(position))
        query = lax.broadcasted_iota(jnp.int32, (rows, rows), 0)
        key = lax.broadcasted_iota(jnp.int32, (rows, rows), 1)
        allowed = ((found[0] == found[1]) & (keys > 0.5)) | (query == key)
        result.append(allowed.astype(F32))
    return result


def lay_group(tiled, laid, first, group, count, turn=None):
    for tile in range(count):
        block = tiled[pl.ds(pl.multiple_of(first + 16 * (group * count + tile), 16), 16), :]
        if turn is not None:
            block = pltpu.roll(block, turn, 1)
        laid[pl.ds(first + group * 16 * count + tile, 16, stride=count), :] = block


def step_kernel(
    ways, tokens, cotangent, holes, lengths, master,
    output, input_grad, total, after_rows,
    whole, grads, small, entries_here, entries_end, extended, aligned, tail,
    turning, send_blocks, recv_blocks, masks, normed, normed_hat, inverse, projected, attended, lses,
    mixture, second_in, activated, slope, second_hat, second_inverse, middle_grad,
    normed_t, mixture_t, second_t, activated_t,
    qkv_grad, out_grad, up_grad, down_grad, near_grad, far_grad, lse_grads,
    their_normed, their_mixture, their_second, their_activated,
    their_qkv, their_out, their_up, their_down, small_parts, their_small,
    by_x, by_y, by_z, by_late, laid, follow_rows, small_all,
    load_sem, tail_sem, slot_send, slot_recv, late_send, late_recv, core_send, core_recv, small_send, small_recv,
    block_send, block_recv, pair_send, pair_recv,
    x_send, x_recv, y_send, y_recv, z_send, z_recv, late_out_send, late_out_recv, end_sem, sum_sem,
):
    s, g = place()
    planes = ways // 4
    z, y, x = s // 4, lax.rem(s // 2, 2), lax.rem(s, 2)
    own = MAT_ROWS // ways
    half_own = own // 2
    rows = tokens.shape[0]
    across = rows // ways
    tiles = D // LANES
    half_width = D // 2
    third_rows = half_width // LANES
    entries = (MAT_ROWS * LANES + bounds_total()) // ways - own * LANES
    shift = entries * s
    row_shift, lane_shift = shift // LANES, lax.rem(shift, LANES)

    def chip(plane, row, column):
        return ((plane * 2 + row) * 2 + column, g)

    def part_at(plane, row, column, part):
        first = ((plane * 2 + row) * 2 + column) * own + part * half_own
        return pl.ds(pl.multiple_of(first, 16), half_own)


    last_row, last_lanes = divmod(own * LANES + entries, LANES)
    step_rows = 176
    full = last_row * LANES
    loads = (
        pltpu.make_async_copy(
            master.at[:, pl.ds(0, full)], entries_here.at[:, pl.ds(0, full)], load_sem.at[0]
        ),
        pltpu.make_async_copy(master.at[:, pl.ds(full, last_lanes)], entries_end, load_sem.at[1]),
    )

    def loaded():
        for load in loads:
            load.wait()
        entries_here[:, full:] = jnp.zeros((1, entries_here.shape[1] - full), F32)
        entries_here[:, full : full + last_lanes] = entries_end[...]

    def flat_rows(first, count):
        if not isinstance(first, int):
            first = pl.multiple_of(first * LANES, LANES)
        else:
            first = first * LANES
        return entries_here[:, pl.ds(first, count * LANES)].reshape(count, LANES)

    def follow_copy():
        return remote(
            tail, extended.at[pl.ds(0, SMALL_ROWS)], tail_sem.at[0], tail_sem.at[1],
            (lax.rem(s + 1, ways), g),
        )

    def make_tail():
        lanes = lax.broadcasted_iota(jnp.int32, (SMALL_ROWS, LANES), 1)
        gap = LANES - last_lanes
        older = pltpu.roll(flat_rows(last_row - SMALL_ROWS, SMALL_ROWS), gap, 1)
        newer = pltpu.roll(flat_rows(last_row - SMALL_ROWS + 1, SMALL_ROWS), gap, 1)
        tail[...] = jnp.where(lanes < gap, older, newer)

    def align(here, before, to):
        lanes = lax.broadcasted_iota(jnp.int32, (step_rows, LANES), 1)
        aligned[pl.ds(pl.multiple_of(to, 8), step_rows), :] = jnp.where(
            lanes >= lane_shift, pltpu.roll(here, lane_shift, 1), pltpu.roll(before, lane_shift, 1)
        )

    def fill(unit):
        first = unit * UNIT

        def tiled(count):
            for group in range(UNIT // (16 * count)):
                for tile in range(count):
                    block = aligned[pl.ds(first + group * 16 * count + tile, 16, stride=count), :]
                    at = s * own + first + 16 * (group * count + tile)
                    whole[g, pl.ds(pl.multiple_of(at, 16), 16), :] = block.astype(BF16)

        unit_tiles(s * (own // UNIT) + unit, tiled)

    def fill_most():
        def align_step(step, carry):
            first = step * step_rows - row_shift
            align(flat_rows(first, step_rows), flat_rows(first - 1, step_rows), step * step_rows)
            return carry

        def fill_unit(unit, carry):
            fill(unit)
            return carry

        extended[SMALL_ROWS:, :] = flat_rows(0, extended.shape[0] - SMALL_ROWS)
        lax.fori_loop(1, (own + SMALL_ROWS) // step_rows, align_step, 0)
        lax.fori_loop(1, own // UNIT, fill_unit, 0)

    def fill_first():
        follow_copy().wait()
        first = SMALL_ROWS - row_shift
        align(extended[pl.ds(first, step_rows), :], extended[pl.ds(first - 1, step_rows), :], 0)
        fill(0)

    order = [z]
    for step in range(1, planes):
        plane = jnp.int32(ORDERS[0][step - 1])
        for at in range(1, planes):
            plane = jnp.where(z == at, ORDERS[at][step - 1], plane)
        order.append(plane)

    part_rows = half_own - LATE_ROWS
    late = PIECES

    def slot_copy(plane, row, column, part, piece, kind, to):
        if piece == late:
            first, count = 2 * part_rows + part * LATE_ROWS, LATE_ROWS
        else:
            count = part_rows // PIECES
            first = part * part_rows + piece * count
        first = ((plane * 2 + row) * 2 + column) * own + first
        where = whole.at[g, pl.ds(pl.multiple_of(first, 16), count)]
        return remote(
            where,
            where,
            slot_send.at[part, plane, kind, piece],
            slot_recv.at[part, (plane * 2 + row) * 2 + column, piece],
            to,
        )

    def line_up(plane, part, piece):
        return slot_copy(plane, y, x, part, piece, 0, chip(z + 1, y, x))

    def line_down(plane, part, piece):
        return slot_copy(plane, y, x, part, piece, 1, chip(z - 1, y, x))

    def to_x(plane, part, piece):
        return slot_copy(plane, y, x, part, piece, 2, chip(z, y, 1 - x))

    def to_y(plane, part, piece):
        return slot_copy(plane, y, x, part, piece, 3, chip(z, 1 - y, x))

    def early(plane, piece):
        to_y(plane, 0, piece).start()
        to_x(plane, 1, piece).start()

    def direct(plane, piece):
        to_x(plane, 0, piece).start()
        to_y(plane, 1, piece).start()

    def turned(plane, piece):
        return (
            slot_copy(plane, 1 - y, x, 0, piece, 4, chip(z, y, 1 - x)),
            slot_copy(plane, y, 1 - x, 1, piece, 4, chip(z, 1 - y, x)),
        )

    def turn_piece(plane, piece):
        for copy in turned(plane, piece):
            copy.wait_recv()
            copy.start()

    def come(plane, piece):
        slot_copy(plane, y, 1 - x, 0, piece, 0, chip(z, y, x)).wait_recv()
        slot_copy(plane, 1 - y, 1 - x, 0, piece, 0, chip(z, y, x)).wait_recv()
        slot_copy(plane, 1 - y, x, 1, piece, 0, chip(z, y, x)).wait_recv()
        slot_copy(plane, 1 - y, 1 - x, 1, piece, 0, chip(z, y, x)).wait_recv()

    def leave(piece, plane_one):
        for part in range(2):

            def up(part=part):
                line_up(z, part, piece).start()

            def down(part=part):
                line_down(z, part, piece).start()

            if plane_one:
                pl.when((z == 1) & (z < planes - 1))(up)
            else:
                pl.when((z != 1) & (z < planes - 1))(up)
                pl.when(z > 0)(down)

    def enter_plane(plane, piece):
        for part in range(2):
            slot_copy(plane, y, x, part, piece, 0, chip(z, y, x)).wait_recv()

            def up(part=part):
                line_up(plane, part, piece).start()

            def down(part=part):
                line_down(plane, part, piece).start()

            pl.when((z > plane) & (z < planes - 1))(up)
            pl.when((z < plane) & (z > 0))(down)

    def late_copy(plane, part, way):
        view = whole.reshape(2, ways, own, LANES)
        where = view.at[
            g, pl.ds(4 * plane, 4), pl.ds(2 * part_rows + part * LATE_ROWS, LATE_ROWS)
        ]
        return remote(
            where, where, late_send.at[way, plane, part], late_recv.at[plane, part],
            chip(z + 1 - 2 * way, y, x),
        )

    def late_own():
        come(z, late)
        for part in range(2):
            pl.when(z < planes - 1)(lambda part=part: late_copy(z, part, 0).start())
            pl.when(z > 0)(lambda part=part: late_copy(z, part, 1).start())

    def late_on(plane):
        for part in range(2):
            late_copy(plane, part, 0).wait_recv()
            pl.when((z > plane) & (z < planes - 1))(
                lambda part=part: late_copy(plane, part, 0).start()
            )
            pl.when((z < plane) & (z > 0))(lambda part=part: late_copy(plane, part, 1).start())

    def to_core(half, plane, part, piece):
        count = LATE_ROWS if piece == late else part_rows // PIECES
        first = 2 * part_rows + part * count if piece == late else part * part_rows + piece * count
        view = whole.reshape(2, ways, own, LANES)
        where = view.at[half, pl.ds(4 * plane, 4), pl.ds(first, count)]
        return remote(
            where, where, core_send.at[plane, part, piece], core_recv.at[plane, part, piece],
            (s, 1 - g),
        )

    def finish(plane, piece):
        if piece != late:
            come(plane, piece)
        for part in range(2):
            to_core(g, plane, part, piece).start()

    def arrived(plane):
        for part in range(2):
            for piece in range(PIECES + 1):
                to_core(1 - g, plane, part, piece).wait_recv()

    def gather_sent():
        for plane in range(planes):
            for part in range(2):
                for piece in range(PIECES):

                    def up(plane=plane, part=part, piece=piece):
                        line_up(plane, part, piece).wait_send()

                    def down(plane=plane, part=part, piece=piece):
                        line_down(plane, part, piece).wait_send()

                    pl.when((z >= plane) & (z < planes - 1))(up)
                    pl.when((z <= plane) & (z > 0))(down)
                    to_x(plane, part, piece).wait_send()
                    to_y(plane, part, piece).wait_send()
                    turned(plane, piece)[part].wait_send()
                to_own = (to_x(z, part, late), to_y(z, part, late), turned(z, late)[part])
                if plane == 0:
                    for copy in to_own:
                        copy.wait_send()
                pl.when((z >= plane) & (z < planes - 1))(
                    lambda plane=plane, part=part: late_copy(plane, part, 0).wait_send()
                )
                pl.when((z <= plane) & (z > 0))(
                    lambda plane=plane, part=part: late_copy(plane, part, 1).wait_send()
                )
            for part in range(2):
                for piece in range(PIECES + 1):
                    to_core(g, plane, part, piece).wait_send()

    def small_to(index):
        return remote(small.at[g], small.at[g], small_send.at[index], small_recv.at[0], (index, g))

    def small_across():
        return remote(
            small.at[g], small.at[g], small_send.at[ways - 1], small_recv.at[1], (s, 1 - g)
        )

    def small_out():
        def tell(index, carry):
            small_to(index).start()
            return carry

        @pl.when(s == ways - 1)
        def _():
            small[g] = aligned[own : own + SMALL_ROWS, :].astype(BF16)
            lax.fori_loop(0, ways - 1, tell, 0)

    def small_in():
        pl.when(s != ways - 1)(lambda: small_to(s).wait_recv())
        small_across().start()
        remote(
            small.at[1 - g], small.at[1 - g], small_send.at[ways - 1], small_recv.at[1], (s, 1 - g)
        ).wait_recv()

    def small_sent():
        def told(index, carry):
            small_to(index).wait_send()
            return carry

        @pl.when(s == ways - 1)
        def _():
            lax.fori_loop(0, ways - 1, told, 0)

        small_across().wait_send()


    def cut(plane, part, piece):
        if piece == late:
            return 2 * (half_own - LATE_OUT[plane]) + part * LATE_OUT[plane], LATE_OUT[plane]
        count = (half_own - LATE_OUT[plane]) // PIECES
        return part * (half_own - LATE_OUT[plane]) + piece * count, count

    def piece_at(plane, row, column, part, piece):
        first, count = cut(plane, part, piece)
        first = ((plane * 2 + row) * 2 + column) * own + first
        return pl.ds(pl.multiple_of(first, 16), count)

    def held(ref, plane, part, piece):
        return ref.at[pl.ds(0, cut(plane, part, piece)[1])]

    def first_copy(plane, part, k, piece):
        where = (k, 1 - x) if part == 0 else (1 - y, k)
        return remote(
            grads.at[piece_at(plane, *where, part, piece)],
            held(by_x.at[plane, part, k, piece], plane, part, piece),
            x_send.at[plane, part, k, piece], x_recv.at[plane, part, k, piece],
            chip(z, y, 1 - x) if part == 0 else chip(z, 1 - y, x),
        )

    def second_copy(plane, part, piece):
        where = (1 - y, x) if part == 0 else (y, 1 - x)
        return remote(
            grads.at[piece_at(plane, *where, part, piece)],
            held(by_y.at[plane, part, piece], plane, part, piece),
            y_send.at[plane, part, piece], y_recv.at[plane, part, piece],
            chip(z, 1 - y, x) if part == 0 else chip(z, y, 1 - x),
        )

    def line_copy(plane, part, piece, way):
        return remote(
            grads.at[piece_at(plane, y, x, part, piece)],
            held(by_z.at[way, plane, part, piece], plane, part, piece),
            z_send.at[plane, part, piece], z_recv.at[way, plane, part, piece],
            chip(z + 1 - 2 * way, y, x),
        )

    def late_out_copy(plane, part, way):
        first, count = cut(plane, part, late)
        view = grads.reshape(ways, own, LANES)
        return remote(
            view.at[pl.ds(4 * plane, 4), pl.ds(first, count)],
            by_late.at[way, plane, part, :, pl.ds(0, count)],
            late_out_send.at[plane, part], late_out_recv.at[way, plane, part],
            chip(z + 1 - 2 * way, y, x),
        )

    def add(where, block):
        grads[where, :] = (grads[where, :].astype(F32) + block[...].astype(F32)).astype(BF16)

    def at_home(plane, piece, act):
        if piece == late:
            pl.when(z == plane)(act)
        else:
            act()

    def out_ahead(plane, piece):
        def act():
            for part in range(2):
                first_copy(plane, part, (1 - y, 1 - x)[part], piece).start()

        at_home(plane, piece, act)

    def out_keep(plane, piece):
        def act():
            for part in range(2):
                first_copy(plane, part, (y, x)[part], piece).start()

        at_home(plane, piece, act)

    def out_pass(plane, piece):
        def act():
            for part in range(2):
                other = (1 - y, 1 - x)[part]
                first_copy(plane, part, other, piece).wait_recv()
                where = (other, x) if part == 0 else (y, other)
                add(
                    piece_at(plane, *where, part, piece),
                    held(by_x.at[plane, part, other, piece], plane, part, piece),
                )
                second_copy(plane, part, piece).start()

        at_home(plane, piece, act)

    def out_take(plane, piece):
        def act():
            for part in range(2):
                mine = (y, x)[part]
                first_copy(plane, part, mine, piece).wait_recv()
                add(
                    piece_at(plane, y, x, part, piece),
                    held(by_x.at[plane, part, mine, piece], plane, part, piece),
                )

        at_home(plane, piece, act)

    def out_join(plane, piece):
        def act():
            for part in range(2):
                second_copy(plane, part, piece).wait_recv()
                add(
                    piece_at(plane, y, x, part, piece),
                    held(by_y.at[plane, part, piece], plane, part, piece),
                )
                if piece != late and plane > 0:
                    pl.when(z == 0)(lambda part=part: line_copy(plane, part, piece, 0).start())
                if piece != late and plane < planes - 1:
                    pl.when(z == planes - 1)(
                        lambda part=part: line_copy(plane, part, piece, 1).start()
                    )

        at_home(plane, piece, act)

    def between(plane, act):
        if plane > 1:
            pl.when((z > 0) & (z < plane))(lambda: act(0))
        if plane < planes - 2:
            pl.when((z > plane) & (z < planes - 1))(lambda: act(1))

    def out_relay(plane, piece):
        for part in range(2):

            def act(way, part=part):
                line_copy(plane, part, piece, way).wait_recv()
                add(
                    piece_at(plane, y, x, part, piece),
                    held(by_z.at[way, plane, part, piece], plane, part, piece),
                )
                line_copy(plane, part, piece, way).start()

            between(plane, act)

    def late_add(plane, part, way):
        late_out_copy(plane, part, way).wait_recv()
        for k in range(4):
            add(
                piece_at(plane, k // 2, k % 2, part, late),
                by_late.at[way, plane, part, k, pl.ds(0, LATE_OUT[plane])],
            )

    def late_start(plane):
        for part in range(2):
            if plane > 0:
                pl.when(z == 0)(lambda part=part: late_out_copy(plane, part, 0).start())
            if plane < planes - 1:
                pl.when(z == planes - 1)(lambda part=part: late_out_copy(plane, part, 1).start())

    def late_relay(plane):
        for part in range(2):

            def act(way, part=part):
                late_add(plane, part, way)
                late_out_copy(plane, part, way).start()

            between(plane, act)

    def late_home(plane):
        @pl.when(z == plane)
        def _():
            for part in range(2):
                if plane > 0:
                    late_add(plane, part, 0)
                if plane < planes - 1:
                    late_add(plane, part, 1)

    def out_sent():
        for plane in range(planes):
            for piece in range(PIECES + (1 if LATE_OUT[plane] else 0)):

                def act(plane=plane, piece=piece):
                    for part in range(2):
                        for k in range(2):
                            first_copy(plane, part, k, piece).wait_send()
                        second_copy(plane, part, piece).wait_send()

                at_home(plane, piece, act)

            @pl.when(z != plane)
            def _(plane=plane):
                for part in range(2):
                    for piece in range(PIECES):
                        line_copy(plane, part, piece, 0).wait_send()
                    if LATE_OUT[plane]:
                        late_out_copy(plane, part, 0).wait_send()

    def out_last(parts):
        for plane in range(planes):

            @pl.when(z == plane)
            def _(plane=plane):
                for part, piece in parts:
                    first, count = cut(plane, part, piece)
                    if not count:
                        continue
                    found = grads[piece_at(plane, y, x, part, piece), :].astype(F32)
                    for way in range(2):
                        if piece != late and (plane > 0 if way == 0 else plane < planes - 1):
                            line_copy(plane, part, piece, way).wait_recv()
                            found = found + by_z[way, plane, part, piece, :count].astype(F32)
                    total[first : first + count, :] = found

    def small_home():
        return remote(
            small_parts.at[g], small_all.at[s], sum_sem.at[0], sum_sem.at[1], (ways - 1, g)
        )

    def follow_back():
        return remote(
            laid.at[pl.ds(0, SMALL_ROWS)], follow_rows, end_sem.at[0], end_sem.at[1],
            (lax.rem(s + ways - 1, ways), g),
        )

    def settle_first():
        unit_tiles(s * (own // UNIT), lambda count: lay_group(total, laid, 0, 0, count))
        follow_back().start()

    def settle():
        follow_back().wait()

        @pl.when(s != ways - 1)
        def _():
            after_rows[...] = follow_rows[...]

        @pl.when(s == ways - 1)
        def _():
            remote(
                small_all.at[pl.ds(0, ways - 1)], small_all.at[pl.ds(0, ways - 1)],
                sum_sem.at[0], sum_sem.at[1], (0, g),
            ).wait_recv()
            small_all[ways - 1] = small_parts[g]
            after_rows[...] = jnp.sum(small_all[...], axis=0)


    widths = (half_width + LANES,) * 3 + (half_width,)

    def exchange(index):
        width = widths[index]

        def start(step, carry):
            apart = ways // 2 + (step // 2) * (1 - 2 * lax.rem(step, 2))
            to = lax.rem(s + apart, ways)
            remote(
                send_blocks.at[index, to, :, pl.ds(0, width)],
                recv_blocks.at[index, s, :, pl.ds(0, width)],
                block_send.at[index],
                block_recv.at[index],
                (to, g),
            ).start()
            return carry

        recv_blocks[index, s] = send_blocks[index, s]
        lax.fori_loop(1, ways, start, 0)

    def exchanged(index):
        width = widths[index]
        remote(
            send_blocks.at[index, pl.ds(0, ways - 1), :, pl.ds(0, width)],
            recv_blocks.at[index, pl.ds(0, ways - 1), :, pl.ds(0, width)],
            block_send.at[index],
            block_recv.at[index],
            (s, 1 - g),
        ).wait()

    pairs = []

    def hand_over(src, dst):
        index = len(pairs)
        pairs.append(remote(src, dst, pair_send.at[index], pair_recv.at[index], (s, 1 - g)))
        pairs[index].start()
        return pairs[index]

    def by_residue(value):
        for tile in range(tiles):
            turning[tile] = value[:, tile * LANES : (tile + 1) * LANES]
        return jnp.concatenate(
            [
                jnp.concatenate(
                    [turning[tile, pl.ds(i, across, stride=ways), :] for i in range(ways)], axis=0
                )
                for tile in range(tiles)
            ],
            axis=1,
        )

    def in_order(value):
        for tile in range(tiles):
            for i in range(ways):
                turning[tile, pl.ds(i, across, stride=ways), :] = value[
                    across * i : across * (i + 1), tile * LANES : (tile + 1) * LANES
                ]
        return jnp.concatenate([turning[tile] for tile in range(tiles)], axis=1)

    def small_row(first, count):
        return jnp.concatenate(
            [small[half, first + r : first + r + 1, :] for half in range(2) for r in range(count)],
            axis=1,
        ).astype(F32)

    temper = HEAD ** (-0.5)

    def scores(which, head):
        at = slice(which * rows, (which + 1) * rows)
        query = projected[at, head * HEAD : (head + 1) * HEAD]
        key = projected[at, D + head * HEAD : D + (head + 1) * HEAD]
        value = projected[at, 2 * D + head * HEAD : 2 * D + (head + 1) * HEAD]
        found = jnp.where(masks[which] > 0.5, dot_cols(query, key) * temper, NEG)
        return query, key, value, found

    def attend_set(which, part):
        first = part * HEADS // 2
        results, totals = [], []
        for head in range(first, first + HEADS // 2):
            _, _, value, found = scores(which, head)
            top = jnp.max(found, axis=1, keepdims=True)
            weights = jnp.exp(found - top)
            summed = jnp.sum(weights, axis=1, keepdims=True)
            results.append(dot(weights.astype(BF16), value) * (1.0 / summed))
            totals.append(top + jnp.log(summed))
        to = slice(part * half_width, (part + 1) * half_width)
        attended[which, :, to] = jnp.concatenate(results, axis=1)
        lses[which, :, first : first + HEADS // 2] = jnp.concatenate(totals, axis=1)

    def attend_set_back(which, out_grads, part):
        first = part * HEADS // 2
        lists = ([], [], [])
        for head in range(first, first + HEADS // 2):
            query, key, value, found = scores(which, head)
            weights = jnp.exp(found - lses[which, :, head : head + 1])
            pulled = out_grads[:, head * HEAD : (head + 1) * HEAD]
            weight_grad = dot_cols(pulled, value)
            inner = jnp.sum(weights * weight_grad, axis=1, keepdims=True)
            extra = lse_grads[which, :, head : head + 1] - inner
            score_grad = (weights * (weight_grad + extra)).astype(BF16)
            lists[0].append(dot(score_grad, key) * temper)
            lists[1].append(dot_rows(score_grad, query) * temper)
            lists[2].append(dot_rows(weights.astype(BF16), pulled))
        at = slice(which * rows, (which + 1) * rows)
        for index, one in enumerate(lists):
            half, start = divmod(index * D + part * half_width, 3 * half_width)
            qkv_grad[half, at, start : start + half_width] = jnp.concatenate(one, axis=1).astype(BF16)

    def weight_grad(index, mine, theirs, grad, their_grad, first, count):
        left = jnp.concatenate(
            [mine[first : first + count, :], theirs[first : first + count, :]], axis=1
        )
        view, base = tile_view(grads, index)
        at = base + first // 16
        for tile, width in tile_groups(index):
            to = slice(tile * LANES, (tile + width) * LANES)
            right = jnp.concatenate([grad[g, :, to], their_grad[:, to]], axis=0)
            found = dot(left, right).astype(BF16)
            for t in range(width):
                view[at : at + count // 16, 16 * (tile + t) : 16 * (tile + t) + 16, :] = found[
                    :, t * LANES : (t + 1) * LANES
                ].reshape(count // 16, 16, LANES)


    kept = SimpleNamespace()
    barrier = greet_all(ways)
    for load in loads:
        load.start()
    inputs = by_residue(tokens[...].astype(F32))
    lane = lax.broadcasted_iota(jnp.int32, (rows, rows), 1)
    row = lax.broadcasted_iota(jnp.int32, (rows, rows), 0)
    flags = holes[...].astype(F32)
    to_column = (row == lane).astype(F32)
    own_column = jnp.sum(to_column * flags, axis=1, keepdims=True)
    turned_at = ways * lax.rem(row, across) + row // across
    turned_column = jnp.sum((turned_at == lane).astype(F32) * flags, axis=1, keepdims=True)
    turned_row_at = ways * lax.rem(lane, across) + lane // across
    turned_row = jnp.sum((turned_row_at == row).astype(F32) * own_column, axis=0, keepdims=True)
    pack_blocks(send_blocks.at[0], inputs, jnp.broadcast_to(turned_column, (rows, HEADS)) * 1.0)
    loaded()
    make_tail()
    fill_most()
    pl.semaphore_wait(barrier, ways)
    follow_copy().start()
    early(order[0], late)
    direct(order[0], late)
    exchange(0)
    small_out()
    fill_first()

    def norm():
        kept.upstream = by_residue(cotangent[...].astype(F32))
        for half in range(2):
            to = slice(half * half_width, (half + 1) * half_width)
            down_grad[half] = kept.upstream[:, to].astype(BF16)
        kept.down_grad_pair = hand_over(down_grad.at[1 - g], their_down)
        exchanged(0)
        far_inputs = unpack_values(recv_blocks.at[0])
        far_column = unpack_extra(recv_blocks.at[0])[:, :1]
        far_row = jnp.sum(to_column * far_column, axis=0, keepdims=True)
        near_mask, far_mask = slide_masks(lengths, s, ways, turned_row, far_row)
        masks[0] = near_mask
        masks[1] = far_mask
        hat, scale = normalize(jnp.concatenate([inputs, far_inputs], axis=0))
        small_in()
        count = third_rows
        kept.gain_one, kept.gain_two = small_row(0, count), small_row(count, count)
        kept.shift_one, kept.shift_two = small_row(2 * count, count), small_row(3 * count, count)
        kept.shift_down = small_row(4 * count, count)
        kept.bias_up = small_row(5 * count, FF // 2 // LANES)
        both = hat * kept.gain_one + kept.shift_one
        normed[...] = both.astype(BF16)
        normed_t[...] = both.T.astype(BF16)
        normed_hat[...] = hat[:rows]
        inverse[...] = scale[:rows]
        kept.normed_pair = hand_over(normed_t, their_normed)

    def project():
        arrived(0)
        for half in range(2):
            for tile, width in tile_groups(0):
                at = half * 3 * half_width + tile * LANES
                projected[:, at : at + width * LANES] = dot(
                    normed[...], weight(whole, 0, half, 0, D, tile, width)
                ).astype(BF16)

    def attend_far():
        attend_set(1, 0)
        attend_set(1, 1)
        pack_blocks(send_blocks.at[1], attended[1], lses[1])
        exchange(1)

    def mix():
        exchanged(1)
        far_out = unpack_values(recv_blocks.at[1])
        near_out = attended[0]
        kept.share = jax.nn.sigmoid(lses[0] - unpack_extra(recv_blocks.at[1]))
        kept.shares = to_columns(kept.share)
        kept.difference = near_out - far_out
        mixed = kept.shares * near_out + (1.0 - kept.shares) * far_out
        mixture[...] = mixed.astype(BF16)
        mixture_t[...] = mixed.T.astype(BF16)
        kept.mixture_pair = hand_over(mixture_t, their_mixture)

    def feed():
        arrived(1)
        arrived(2)
        kept.middle = inputs + jnp.concatenate(
            [dot(mixture[...], weight(whole, 1, half, 0, D, 0, third_rows)) for half in range(2)],
            axis=1,
        )
        hat, scale = normalize(kept.middle)
        second_hat[...] = hat
        second_inverse[...] = scale
        second = hat * kept.gain_two + kept.shift_two
        second_in[...] = second.astype(BF16)
        root = (2.0 / 3.141592653589793) ** 0.5
        kept.activated_pairs = []
        for half in range(2):
            for tile, width in tile_groups(2):
                at = half * FF // 2 + tile * LANES
                to = slice(at, at + width * LANES)
                v = dot(second_in[...], weight(whole, 2, half, 0, D, tile, width))
                v = v + kept.bias_up[:, to]
                square = v * v
                t = jnp.tanh(root * (v + 0.044715 * v * square))
                active = 0.5 * v * (1.0 + t)
                activated[:, to] = active.astype(BF16)
                activated_t[to, :] = active.T.astype(BF16)
                slope[:, to] = 0.5 * (1.0 + t) + 0.5 * v * (1.0 - t * t) * (
                    root * (1.0 + 3 * 0.044715 * square)
                )
                if (at + width * LANES) % D == 0:
                    span = pl.ds(at + width * LANES - D, D)
                    kept.activated_pairs.append(
                        hand_over(activated_t.at[span], their_activated.at[span])
                    )
        second_t[...] = second.T.astype(BF16)
        kept.second_in_pair = hand_over(second_t, their_second)

    block = 256

    def feed_back():
        for plane in range(3, planes):
            arrived(plane)
        sums = []
        for start in range(0, FF, block):
            to = slice(start, start + block)
            pulled = sum(
                dot_cols(down_grad[half], weight(whole, 3, half, start, block, 0, third_rows))
                for half in range(2)
            )
            grad = (pulled * slope[:, to]).astype(BF16)
            half, at = divmod(start, FF // 2)
            up_grad[half, :, at : at + block] = grad
            sums.append(jnp.sum(grad.astype(F32), axis=0, keepdims=True))
        kept.up_sum = jnp.concatenate(sums, axis=1)
        kept.up_grad_pair = hand_over(up_grad.at[1 - g], their_up)

    def down_weights():
        kept.down_grad_pair.wait()
        for first in range(0, FF, D):
            kept.activated_pairs[first // D].wait()
            weight_grad(3, activated_t, their_activated, down_grad, their_down, first, D)

    def through(left, index, tiles_to):
        return jnp.concatenate(
            [
                sum(
                    dot_cols(left[half], weight(whole, index, half, start, block, 0, tiles_to))
                    for half in range(2)
                )
                for start in range(0, D, block)
            ],
            axis=1,
        )

    def mix_back():
        second_grad = through(up_grad, 2, TILES[2])
        hat = second_hat[...]
        kept.gain_two_sum = jnp.sum(second_grad * hat, axis=0, keepdims=True)
        kept.shift_two_sum = jnp.sum(second_grad, axis=0, keepdims=True)
        gained = kept.upstream + norm_back(second_grad * kept.gain_two, hat, second_inverse[...])
        middle_grad[...] = gained
        for half in range(2):
            out_grad[half] = gained[:, half * half_width : (half + 1) * half_width].astype(BF16)
        kept.out_grad_pair = hand_over(out_grad.at[1 - g], their_out)
        mix_grad = through(out_grad, 1, third_rows)
        share, shares = kept.share, kept.shares
        near_lse_grad = share * (1.0 - share) * to_heads(kept.difference * mix_grad)
        lse_grads[0] = near_lse_grad
        near_grad[...] = (shares * mix_grad).astype(BF16)
        pack_blocks(send_blocks.at[2], (1.0 - shares) * mix_grad, -near_lse_grad)
        exchange(2)

    def up_weights():
        kept.second_in_pair.wait()
        kept.up_grad_pair.wait()
        weight_grad(2, second_t, their_second, up_grad, their_up, 0, D)

    def out_weights():
        kept.mixture_pair.wait()
        kept.out_grad_pair.wait()
        weight_grad(1, mixture_t, their_mixture, out_grad, their_out, 0, D)

    def put_output():
        result = kept.middle + kept.shift_down + jnp.concatenate(
            [
                dot(activated[...], weight(whole, 3, half, 0, FF, 0, third_rows))
                for half in range(2)
            ],
            axis=1,
        )
        output[...] = in_order(result).astype(BF16)

    def far_back_start():
        kept.qkv_near_pair = hand_over(
            qkv_grad.at[1 - g, pl.ds(0, rows)], their_qkv.at[pl.ds(0, rows)]
        )
        exchanged(2)
        far_grad[...] = unpack_values(recv_blocks.at[2]).astype(BF16)
        lse_grads[1] = unpack_extra(recv_blocks.at[2])
        attend_set_back(1, far_grad, 0)

    def far_back():
        attend_set_back(1, far_grad, 1)
        kept.qkv_far_pair = hand_over(
            qkv_grad.at[1 - g, pl.ds(rows, rows)], their_qkv.at[pl.ds(rows, rows)]
        )

    def project_back():
        kept.first_grad = through(qkv_grad, 0, TILES[0])
        pack_blocks(send_blocks.at[3], kept.first_grad[rows:], None)
        exchange(3)

    def qkv_weights():
        kept.normed_pair.wait()
        kept.qkv_near_pair.wait()
        kept.qkv_far_pair.wait()
        weight_grad(0, normed_t, their_normed, qkv_grad, their_qkv, 0, D)

    def put_input_grad():
        exchanged(3)
        first_grad = kept.first_grad[:rows] + unpack_values(recv_blocks.at[3])
        hat = normed_hat[...]
        kept.gain_one_sum = jnp.sum(first_grad * hat, axis=0, keepdims=True)
        kept.shift_one_sum = jnp.sum(first_grad, axis=0, keepdims=True)
        input_grad[...] = in_order(
            middle_grad[...] + norm_back(first_grad * kept.gain_one, hat, inverse[...])
        )

    def small_sums():
        for half in range(2):
            to = slice(half * half_width, (half + 1) * half_width)
            down_sum = jnp.sum(down_grad[half].astype(F32), axis=0, keepdims=True)
            sums = (kept.gain_one_sum, kept.gain_two_sum, kept.shift_one_sum, kept.shift_two_sum)
            listed = [one[:, to] for one in sums] + [down_sum]
            listed.append(kept.up_sum[:, half * FF // 2 : (half + 1) * FF // 2])
            at = 0
            for vector in listed:
                count = vector.shape[1] // LANES
                small_parts[half, at : at + count, :] = vector.reshape(count, LANES)
                at += count
            small_parts[half, at:, :] = jnp.zeros((SMALL_ROWS - at, LANES), F32)
        kept.small_pair = hand_over(small_parts.at[1 - g], their_small)
        kept.small_pair.wait()
        small_parts[g] = small_parts[g] + their_small[...]
        pl.when(s != ways - 1)(lambda: small_home().start())

    everything = [(part, piece) for piece in range(PIECES + 1) for part in range(2)]
    leave(1, False)
    early(order[0], 1)
    early(order[0], 0)
    leave(1, True)
    leave(0, False)
    turn_piece(order[0], late)
    turn_piece(order[0], 1)
    direct(order[0], 1)
    direct(order[0], 0)
    enter_plane(order[1], 1)
    early(order[1], 1)
    turn_piece(order[0], 0)
    enter_plane(order[2], 1)
    enter_plane(order[1], 0)
    early(order[1], 0)
    early(order[2], 1)
    late_own()
    direct(order[1], 1)
    finish(order[0], late)
    turn_piece(order[1], 1)
    norm()
    direct(order[1], 0)
    enter_plane(order[2], 0)
    early(order[2], 0)
    turn_piece(order[1], 0)
    finish(order[0], 0)
    enter_plane(order[3], 1)
    early(order[3], 1)
    direct(order[2], 0)
    turn_piece(order[2], 1)
    direct(order[2], 1)
    finish(order[0], 1)
    late_on(order[1])
    finish(order[1], 1)
    leave(0, True)
    late_on(order[2])
    turn_piece(order[2], 0)
    finish(order[1], late)
    finish(order[1], 0)
    enter_plane(order[3], 0)
    early(order[3], 0)
    turn_piece(order[3], 1)
    direct(order[3], 1)
    project()
    attend_far()
    finish(order[2], late)
    finish(order[2], 1)
    attend_set(0, 0)
    attend_set(0, 1)
    finish(order[2], 0)
    direct(order[3], 0)
    turn_piece(order[3], 0)
    late_on(order[3])
    finish(order[3], 1)
    finish(order[3], late)
    mix()
    finish(order[3], 0)
    feed()
    down_weights()
    late_start(3)
    out_keep(3, 0)
    out_ahead(3, 0)
    out_ahead(3, 1)
    feed_back()
    mix_back()
    up_weights()
    out_ahead(2, 1)
    late_start(2)
    out_ahead(2, 0)
    out_pass(3, 0)
    attend_set_back(0, near_grad, 0)
    attend_set_back(0, near_grad, 1)
    out_take(3, 0)
    out_weights()
    out_keep(3, 1)
    out_ahead(1, 0)
    late_start(1)
    out_keep(2, 1)
    late_relay(3)
    out_pass(3, 1)
    out_keep(2, 0)
    out_pass(2, 0)
    out_pass(2, 1)
    far_back_start()
    far_back()
    late_relay(2)
    out_take(3, 1)
    late_relay(1)
    qkv_weights()
    late_start(0)
    out_ahead(0, 1)
    late_home(3)
    out_join(3, 0)
    out_join(3, 1)
    out_take(2, 0)
    out_take(2, 1)
    out_ahead(0, 0)
    out_keep(0, 0)
    project_back()
    out_join(2, 0)
    out_pass(0, 0)
    out_keep(0, 1)
    out_relay(3, 0)
    put_output()
    out_take(0, 0)
    late_home(2)
    out_pass(0, 1)
    out_relay(3, 1)
    late_home(1)
    out_relay(2, 0)
    late_relay(0)
    out_join(2, 1)
    out_ahead(2, late)
    out_ahead(1, late)
    out_keep(1, 0)
    out_join(0, 0)
    out_ahead(1, 1)
    out_relay(0, 0)
    out_pass(1, late)
    out_take(0, 1)
    out_relay(2, 1)
    out_keep(2, late)
    out_join(0, 1)
    out_keep(1, late)
    out_pass(1, 0)
    out_take(1, 0)
    out_relay(0, 1)
    put_input_grad()
    out_keep(1, 1)
    out_pass(1, 1)
    small_sums()
    out_take(1, late)
    out_ahead(3, late)
    late_home(0)
    out_join(1, 0)
    out_keep(0, late)
    out_keep(3, late)
    out_ahead(0, late)
    out_pass(2, late)
    out_relay(1, 0)
    out_last(everything[:1])
    settle_first()
    out_take(1, 1)
    out_join(1, 1)
    out_relay(1, 1)
    out_take(2, late)
    out_pass(3, late)
    out_join(2, late)
    out_pass(0, late)
    out_join(1, late)
    out_take(0, late)
    out_take(3, late)
    out_join(3, late)
    out_join(0, late)
    out_last(everything[1:])
    settle()
    pl.when(s != ways - 1)(lambda: small_home().wait_send())
    gather_sent()
    small_sent()
    out_sent()


def bounds_total():
    return 5 * D // 2 + FF // 2


def run_step(tokens, cotangent, holes, lengths, master, ways):
    rows = tokens.shape[0]
    own = MAT_ROWS // ways
    entries = (MAT_ROWS * LANES + bounds_total()) // ways
    half_own = own // 2
    planes = ways // 4
    vmem = pl.BlockSpec(memory_space=pltpu.VMEM)
    dma = pltpu.SemaphoreType.DMA
    half = D // 2
    most = max((half_own - min(LATE_OUT)) // PIECES, max(LATE_OUT))
    shapes = [
        ((2, MAT_ROWS, LANES), BF16),
        ((MAT_ROWS, LANES), BF16),
        ((2, SMALL_ROWS, LANES), BF16),
        ((1, (own + SMALL_ROWS) * LANES), F32),
        ((1, entries % LANES), F32),
        ((SMALL_ROWS + 184, LANES), F32),
        ((own + SMALL_ROWS, LANES), F32),
        ((SMALL_ROWS, LANES), F32),
        ((D // LANES, rows, LANES), F32),
        ((4, ways, 16, half + LANES), BF16),
        ((4, ways, 16, half + LANES), BF16),
        ((2, rows, rows), F32),
        ((2 * rows, D), BF16),
        ((rows, D), F32),
        ((rows, 1), F32),
        ((2 * rows, 3 * D), BF16),
        ((2, rows, D), F32),
        ((2, rows, HEADS), F32),
        ((rows, D), BF16),
        ((rows, D), BF16),
        ((rows, FF), BF16),
        ((rows, FF), F32),
        ((rows, D), F32),
        ((rows, 1), F32),
        ((rows, D), F32),
        ((D, 2 * rows), BF16),
        ((D, rows), BF16),
        ((D, rows), BF16),
        ((FF, rows), BF16),
        ((2, 2 * rows, 3 * half), BF16),
        ((2, rows, half), BF16),
        ((2, rows, FF // 2), BF16),
        ((2, rows, half), BF16),
        ((rows, D), BF16),
        ((rows, D), BF16),
        ((2, rows, HEADS), F32),
        ((D, 2 * rows), BF16),
        ((D, rows), BF16),
        ((D, rows), BF16),
        ((FF, rows), BF16),
        ((2 * rows, 3 * half), BF16),
        ((rows, half), BF16),
        ((rows, FF // 2), BF16),
        ((rows, half), BF16),
        ((2, SMALL_ROWS, LANES), F32),
        ((SMALL_ROWS, LANES), F32),
        ((planes, 2, 2, PIECES + 1, most, LANES), BF16),
        ((planes, 2, PIECES + 1, most, LANES), BF16),
        ((2, planes, 2, PIECES, most, LANES), BF16),
        ((2, planes, 2, 4, max(LATE_OUT), LANES), BF16),
        ((16 * max(TILES), LANES), F32),
        ((SMALL_ROWS, LANES), F32),
        ((ways, SMALL_ROWS, LANES), F32),
    ]
    return pl.pallas_call(
        partial(step_kernel, ways),
        out_shape=(
            jax.ShapeDtypeStruct((rows, D), BF16),
            jax.ShapeDtypeStruct((rows, D), F32),
            jax.ShapeDtypeStruct((own, LANES), F32),
            jax.ShapeDtypeStruct((SMALL_ROWS, LANES), F32),
        ),
        in_specs=[
            vmem, vmem, vmem, pl.BlockSpec(memory_space=pltpu.SMEM), pl.BlockSpec(memory_space=pl.ANY),
        ],
        out_specs=(vmem,) * 4,
        scratch_shapes=[pltpu.VMEM(*shape) for shape in shapes]
        + [
            dma((2,)), dma((2,)),
            dma((2, planes, 5, PIECES + 1)), dma((2, ways, PIECES + 1)),
            dma((2, planes, 2)), dma((planes, 2)),
            dma((planes, 2, PIECES + 1)), dma((planes, 2, PIECES + 1)),
            dma((ways,)), dma((2,)),
            dma((4,)), dma((4,)), dma((13,)), dma((13,)),
            dma((planes, 2, 2, PIECES + 1)), dma((planes, 2, 2, PIECES + 1)),
            dma((planes, 2, PIECES + 1)), dma((planes, 2, PIECES + 1)),
            dma((planes, 2, PIECES)), dma((2, planes, 2, PIECES)),
            dma((planes, 2)), dma((2, planes, 2)),
            dma((2,)), dma((2,)),
        ],
        compiler_params=pltpu.CompilerParams(
            collective_id=1, has_side_effects=True, vmem_limit_bytes=VMEM_BYTES
        ),
        name="run_step",
    )(tokens, cotangent, holes, lengths, master)


def rates_at(at):
    values = (
        0.7 * (2.0 / D) ** 0.5, 0.7 * (24.0 / D) ** 0.5, 0.7 * (1.0 / D) ** 0.5, 0.7 * (1.0 / FF) ** 0.5,
        0.15, 0.2,
    )
    rates = values[5]
    for edge, value in reversed(list(zip(bounds(), values))):
        rates = jnp.where(at < edge, jnp.float32(value), rates)
    return rates, jnp.where(at < bounds()[3], jnp.float32(0.1), jnp.float32(0.0))


def adam_kernel(
    tiled, after_rows, master, first_moment, second_moment, layer_output, layer_grad,
    new_moment, new_second, new_master, output, input_grad, kept, last, kept_output, kept_grad,
    kept_tiled, laid, load_sem, store_sem, pass_sem, grad_sem,
):
    size = master.shape[1]
    full, rest = divmod(size, LANES)
    own, step = tiled.shape[0], 56
    chunks = own // UNIT
    edges = [(UNIT * c - SMALL_ROWS) // step * step for c in range(1, chunks)]
    edges = [0] + edges + [full]
    spans = [(first, end - first) for first, end in zip(edges, edges[1:])]
    sources, targets = (first_moment, second_moment, master), (new_moment, new_second, new_master)

    def piece(array, first, count):
        return array.at[:, pl.ds(first * LANES, count * LANES)].reshape(count, LANES)

    def load(which, index):
        first, count = spans[index]
        return pltpu.make_async_copy(
            piece(sources[which], first, count), kept.at[which, pl.ds(first, count)],
            load_sem.at[which, index],
        )

    def store(which, index):
        first, count = spans[index]
        return pltpu.make_async_copy(
            kept.at[which, pl.ds(first, count)], piece(targets[which], first, count),
            store_sem.at[which, index],
        )

    def load_last(which):
        return pltpu.make_async_copy(
            sources[which].at[:, pl.ds(full * LANES, rest)], last.at[which], load_sem.at[which, chunks]
        )

    def store_last(which):
        return pltpu.make_async_copy(
            last.at[which], targets[which].at[:, pl.ds(full * LANES, rest)], store_sem.at[which, chunks]
        )

    passed = tuple(
        (
            pltpu.make_async_copy(source, through, pass_sem.at[index]),
            pltpu.make_async_copy(through, target, pass_sem.at[index]),
        )
        for index, (source, through, target) in enumerate(
            ((layer_output, kept_output, output), (layer_grad, kept_grad, input_grad))
        )
    )
    after = pltpu.make_async_copy(
        after_rows, laid.at[pl.ds(own, SMALL_ROWS)], grad_sem.at[chunks]
    )

    def unit_in(unit):
        span = pl.ds(unit * UNIT, UNIT)
        return pltpu.make_async_copy(tiled.at[span], kept_tiled.at[span], grad_sem.at[unit])

    for index in range(chunks):
        unit_in(index).start()
        for which in range(3):
            load(which, index).start()
    after.start()
    for which in range(3):
        load_last(which).start()
    for copy, _ in passed:
        copy.start()
    s = lax.axis_index("seq")
    origin = s * size
    shift = s * (size - own * LANES)
    row_shift, lane_shift = shift // LANES, lax.rem(shift, LANES)
    back = lax.rem(LANES - lane_shift, LANES)

    def gradients(first, count):
        here = laid[pl.ds(first + row_shift, count), :]
        after = laid[pl.ds(first + row_shift + 1, count), :]
        lanes = lax.broadcasted_iota(jnp.int32, (count, LANES), 1)
        return jnp.where(lanes < LANES - lane_shift, here, after)


    def update(at, moment, second, weights, gradient):
        rates, decays = rates_at(at)
        moment = BETA_ONE * moment + (1.0 - BETA_ONE) * gradient
        second = BETA_TWO * second + (1.0 - BETA_TWO) * gradient * gradient
        scaled = moment * (1.0 / (1.0 - BETA_ONE**STEP))
        change = scaled / (jnp.sqrt(second * (1.0 / (1.0 - BETA_TWO**STEP))) + EPS_ADAM)
        return moment, second, weights - rates * (change + decays * weights)

    laid[own + SMALL_ROWS :, :] = jnp.zeros((laid.shape[0] - own - SMALL_ROWS, LANES), F32)

    def lay(unit):
        def groups(count):
            for group in range(UNIT // (16 * count)):
                lay_group(kept_tiled, laid, unit * UNIT, group, count, back)

        unit_tiles(s * (own // UNIT) + unit, groups)

    for index, (first, count) in enumerate(spans):
        unit_in(index).wait()
        lay(index)
        if index == chunks - 1:
            after.wait()
            laid[own : own + SMALL_ROWS, :] = pltpu.roll(laid[own : own + SMALL_ROWS, :], back, 1)
        for which in range(3):
            load(which, index).wait()

        def run(index, carry, first=first):
            where = pl.multiple_of(first + index * step, 8)
            span = pl.ds(where, step)
            start = origin + where * LANES
            end = start + step * LANES - 1
            edge_list = bounds()
            cut = (start < edge_list[0]) & (end >= edge_list[0])
            for edge in edge_list[1:]:
                cut = cut | ((start < edge) & (end >= edge))

            def put(at):
                found = update(at, *(kept[which, span, :] for which in range(3)), gradients(where, step))
                for which in range(3):
                    kept[which, span, :] = found[which]

            pl.when(jnp.logical_not(cut))(lambda: put(start))

            @pl.when(cut)
            def _():
                row = lax.broadcasted_iota(jnp.int32, (step, LANES), 0)
                put(start + row * LANES + lax.broadcasted_iota(jnp.int32, (step, LANES), 1))

            return carry

        lax.fori_loop(0, -(-count // step), run, 0)
        for which in range(3):
            store(which, index).start()
        if index == 0:
            for copy, onward in passed:
                copy.wait()
                onward.start()
    for which in range(3):
        load_last(which).wait()
    moment, second, weights = (last[which] for which in range(3))
    at = origin + full * LANES + lax.broadcasted_iota(jnp.int32, (1, rest), 1)
    found = update(at, moment, second, weights, gradients(full, 8)[:1, :rest])
    for which in range(3):
        last[which] = found[which]
        store_last(which).start()
    for which in range(3):
        for index in range(chunks):
            store(which, index).wait()
        store_last(which).wait()
    for _, copy in passed:
        copy.wait()


def run_adam(tiled, after_rows, master, first_moment, second_moment, layer_output, layer_grad):
    size = master.shape[1]
    anywhere = pl.BlockSpec(memory_space=pl.ANY)
    return pl.pallas_call(
        adam_kernel,
        out_shape=(jax.ShapeDtypeStruct((1, size), F32),) * 3
        + tuple(jax.ShapeDtypeStruct(one.shape, one.dtype) for one in (layer_output, layer_grad)),
        in_specs=[anywhere] * 7,
        out_specs=(anywhere,) * 5,
        scratch_shapes=[
            pltpu.VMEM((3, -(-size // (8 * LANES)) * 8, LANES), F32),
            pltpu.VMEM((3, 1, size % LANES), F32),
            pltpu.VMEM(layer_output.shape, layer_output.dtype),
            pltpu.VMEM(layer_grad.shape, layer_grad.dtype),
            pltpu.VMEM(tiled.shape, F32),
            pltpu.VMEM((tiled.shape[0] + 2 * SMALL_ROWS, LANES), F32),
            pltpu.SemaphoreType.DMA((3, tiled.shape[0] // UNIT + 1)),
            pltpu.SemaphoreType.DMA((3, tiled.shape[0] // UNIT + 1)),
            pltpu.SemaphoreType.DMA((2,)),
            pltpu.SemaphoreType.DMA((tiled.shape[0] // UNIT + 1,)),
        ],
        compiler_params=pltpu.CompilerParams(vmem_limit_bytes=VMEM_BYTES),
        name="run_adam",
    )(tiled, after_rows, master, first_moment, second_moment, layer_output, layer_grad)


def on_device(tokens, cotangent, holes, slide_lengths, master, first_moment, second_moment):
    ways = lax.axis_size("seq")
    output, input_grad, tiled, after_rows = run_step(
        tokens[0], cotangent[0], holes, slide_lengths, master, ways
    )
    new_moment, new_second, new_master, output, input_grad = run_adam(
        tiled, after_rows, master, first_moment, second_moment, output, input_grad
    )
    return (output[None], input_grad[None], new_moment, new_second, new_master)


def even(mesh):
    ways = mesh.shape["seq"]
    return ways % 4 == 0 and MAT_ROWS % (ways * UNIT) == 0 and ways * 8 == LANES


def solution(mesh):
    return jax.shard_map(
        on_device if even(mesh) else plain_on_device,
        mesh=mesh,
        in_specs=(
            P("grp", "seq", None),
            P("grp", "seq", None),
            P("grp", "seq"),
            P("grp", None),
            P("grp", "seq"),
            P("grp", "seq"),
            P("grp", "seq"),
        ),
        out_specs=(
            P("grp", "seq", None),
            P("grp", "seq", None),
            P("grp", "seq"),
            P("grp", "seq"),
            P("grp", "seq"),
        ),
        check_vma=False,
    )
```
